32 devices in a mesh: freq: 16 (over z, y, x), blk: 2 (over core).
Axes of the slice: x: 2, y: 2, z: 4, core: 2. Of those that a mesh axis runs over, the one named last changes fastest.
Arguments:
- samples: bfloat16 [64, 267776], P(('blk', 'freq')), may hold values from -127 to 127, as said below
- slot_order: int32 [2, 32], P('blk'), may hold values from 0 to 31, each once within a row
- flags: int32 [64], P(('blk', 'freq')), may hold values 0 or 1
Outputs:
- visibilities: float32 [256, 2, 64, 64], P('freq', None, 'blk')
The draws below stay inside these ranges and needn't reach their ends.
Inputs may be any that keep to these rules, and one draw needn't show every extreme that they name: `samples`: every sample is a whole number.
All inputs are finite; a program needn't handle non-finite values. No bound on the sum of `flags` on one device may be relied on, other than what follows from the above.
Results may differ from the reference program's by a relative error of at most 0.0059.
Values may be sent and summed in bfloat16 or wider, within the bound.
No kernel may reach another device: no remote copies, remote signals or barrier semaphores. Data moves between devices by JAX's collectives and lax.ppermute only.
A program may use at most 64 MiB of HBM per device.

```python
import math
import jax
import jax.numpy as jnp
from jax import lax

CH = 256
TAPS = 12
SPEC = 512
NIN = 64
NSAMP = 267776
NBLOCKS = 2
BLOCK = 32


def draw_samples(key, part):
    key_amp, key_noise, key_sign = jax.random.split(key, 3)
    count = (SPEC + TAPS - 1) * 2 * CH
    amplitude = jax.random.randint(key_amp, (NIN, 1), 5, 57)
    raw_bits = jax.random.randint(key_noise, (NIN, count + 1), 0, 65536)
    noise = raw_bits % (2 * amplitude + 1) - amplitude
    polarity = jax.random.randint(key_sign, (NIN, 1), 0, 2) * 2 - 1
    values = noise[:, 1:] + polarity * (noise[:, :-1] // 2)
    return values.astype(jnp.float32).astype(jnp.bfloat16)


def place_ends(array, own_key, smallest, high):
    index_at = [jax.random.randint(jax.random.fold_in(own_key, axis), (), 0, length) for axis, length in enumerate(array.shape)]
    widest = array.shape.index(max(array.shape))
    next_to = index_at[:widest] + [(index_at[widest] + 1) % array.shape[widest]] + index_at[widest + 1:]
    return array.at[tuple(index_at)].set(smallest).at[tuple(next_to)].set(high)


def setup_inputs(seed: int = 0) -> dict:
    streams_of = jax.random.split(jax.random.key(seed), 4)
    return {
        "samples": draw_samples(jax.random.fold_in(streams_of[3], 71), 0),
        "slot_order": jax.vmap(lambda own: jax.random.permutation(own, BLOCK))(jax.random.split(streams_of[1], NBLOCKS)).reshape((NBLOCKS, BLOCK)).astype(jnp.int32),
        "flags": place_ends((jax.random.randint(streams_of[2], (NIN,), 0, 8) < 1).astype(jnp.int32), jax.random.fold_in(streams_of[2], 1), 0, 1),
    }


def prototype():
    count = TAPS * 2 * CH
    index = jnp.arange(count, dtype=jnp.float32)
    frame = 2.0 * CH
    shifted = (index + 0.5) / frame - TAPS / 2.0
    window = 0.5 - 0.5 * jnp.cos(2.0 * math.pi * (index + 0.5) / count)
    return (jnp.sinc(shifted) * window).astype(jnp.float32).reshape(TAPS, 2 * CH)

def twiddle():
    frame = 2 * CH
    chan = jnp.arange(CH, dtype=jnp.int32)[:, None]
    point = jnp.arange(frame, dtype=jnp.int32)[None, :]
    phase = (chan * point % frame).astype(jnp.float32) * (2.0 * math.pi / frame)
    table = jnp.stack([jnp.cos(phase), -jnp.sin(phase)], axis=1)
    return table.reshape(2 * CH, frame).astype(jnp.bfloat16)

def normalize(spectra, good):
    squares = lax.optimization_barrier(jnp.sum(spectra * spectra, axis=2))
    rows = squares.shape[1]
    power = lax.optimization_barrier(jnp.sum(squares.reshape(spectra.shape[0] // 2, 2, rows), axis=1)) / SPEC
    scale = good[None, :] / jnp.sqrt(power + 1e-05)
    return (spectra * jnp.repeat(scale, 2, axis=0)[:, :, None]).astype(jnp.bfloat16)

def channelize(group, good):
    taps = prototype()
    table = twiddle()
    frames = group.reshape(group.shape[0], SPEC + TAPS - 1, 2 * CH).astype(jnp.float32)
    total = jnp.zeros((group.shape[0], SPEC, 2 * CH), jnp.float32)
    for tap in range(TAPS):
        total = total + taps[tap][None, None, :] * frames[:, tap:tap + SPEC, :]
    fir = total.astype(jnp.bfloat16)
    spectra = jnp.einsum('kn,isn->kis', table.astype(jnp.float32), fir.astype(jnp.float32), precision=lax.Precision.HIGHEST)
    return normalize(spectra, good)

def correlate(pair):
    stacked = pair.reshape(2 * NIN, SPEC)
    gram = jnp.dot(stacked, stacked.T, preferred_element_type=jnp.float32)
    real_real = gram[:NIN, :NIN]
    real_imag = gram[:NIN, NIN:]
    imag_real = gram[NIN:, :NIN]
    imag_imag = gram[NIN:, NIN:]
    return jnp.stack([(real_real + imag_imag) / SPEC, (imag_real - real_imag) / SPEC], axis=0)

def reference(samples, slot_order, flags):
    group_size = math.gcd(NIN, 128)
    groups = NIN // group_size
    good = (1 - flags).astype(jnp.float32)
    quant = lax.map(lambda pair: channelize(pair[0], pair[1]), (samples.reshape(groups, group_size, NSAMP), good.reshape(groups, group_size)))
    quant = jnp.transpose(quant, (1, 0, 2, 3)).reshape(2 * CH, NIN, SPEC)
    quant = quant.reshape(CH, 2, NBLOCKS, BLOCK, SPEC)
    block_index = jnp.arange(NBLOCKS, dtype=jnp.int32)[:, None]
    slots = quant[:, :, block_index, slot_order, :].reshape(CH, 2, NIN, SPEC)
    return lax.map(correlate, slots)
```

```python
import math

import jax
import jax.numpy as jnp
from jax import lax
from jax.sharding import PartitionSpec as P

CH = 256
TAPS = 12
SPEC = 512


def prototype():
    count = TAPS * 2 * CH
    index = jnp.arange(count, dtype=jnp.float32)
    frame = 2.0 * CH
    shifted = (index + 0.5) / frame - TAPS / 2.0
    window = 0.5 - 0.5 * jnp.cos(2.0 * math.pi * (index + 0.5) / count)
    return (jnp.sinc(shifted) * window).astype(jnp.float32).reshape(TAPS, 2 * CH)


def twiddle():
    frame = 2 * CH
    chan = jnp.arange(CH, dtype=jnp.int32)[:, None]
    point = jnp.arange(frame, dtype=jnp.int32)[None, :]
    phase = (chan * point % frame).astype(jnp.float32) * (2.0 * math.pi / frame)
    table = jnp.stack([jnp.cos(phase), -jnp.sin(phase)], axis=1)
    return table.reshape(2 * CH, frame).astype(jnp.bfloat16)


def channelize(samples, flags):
    local_inputs = samples.shape[0]
    taps = prototype()
    table = twiddle()
    good = (1 - flags).astype(jnp.float32)
    frames = samples.reshape(local_inputs, SPEC + TAPS - 1, 2 * CH)
    total = jnp.zeros((local_inputs, SPEC, 2 * CH), jnp.float32)
    for tap in range(TAPS):
        total = total + taps[tap][None, None, :] * frames[:, tap : tap + SPEC, :].astype(
            jnp.float32
        )
    fir = total.astype(jnp.bfloat16)
    spectra = jnp.einsum("kn,isn->kis", table, fir, preferred_element_type=jnp.float32)
    squares = jnp.sum(spectra * spectra, axis=2)
    power = jnp.sum(squares.reshape(CH, 2, local_inputs), axis=1) / SPEC
    scale = good[None, :] / jnp.sqrt(power + 1e-05)
    return (spectra * jnp.repeat(scale, 2, axis=0)[:, :, None]).astype(jnp.bfloat16)


def gather_orders(slot_order, blocks):
    spread = jnp.broadcast_to(slot_order, (blocks, slot_order.shape[1]))
    return lax.all_to_all(spread, "blk", split_axis=0, concat_axis=0, tiled=True)


def gram_pairs(rows, other):
    dot = lambda u, v: jnp.einsum("cas,cbs->cab", u, v, preferred_element_type=jnp.float32)
    real = dot(rows[:, 0], other[:, 0]) + dot(rows[:, 1], other[:, 1])
    imag = dot(rows[:, 1], other[:, 0]) - dot(rows[:, 0], other[:, 1])
    return jnp.stack([real / SPEC, imag / SPEC], axis=1)


def split_channels(freq, blocks, samples, slot_order, flags):
    local_inputs = samples.shape[0]
    block = slot_order.shape[1]
    share = CH // (freq * blocks)
    orders = gather_orders(slot_order, blocks)
    quantized = channelize(samples, flags).reshape(2 * CH, local_inputs * SPEC)
    arrived = lax.all_to_all(quantized, ("freq", "blk"), split_axis=0, concat_axis=0, tiled=True)
    arrived = arrived.reshape(freq, blocks, share, 2, local_inputs, SPEC)
    arrived = arrived.transpose(2, 3, 1, 0, 4, 5).reshape(share, 2, blocks * block, SPEC)
    index = (orders + block * jnp.arange(blocks, dtype=jnp.int32)[:, None]).reshape(-1)
    slots = jnp.take(arrived, index, axis=2)
    tile = gram_pairs(slots, slots).reshape(share, 2, blocks, block, blocks * block)
    tile = tile.transpose(2, 0, 1, 3, 4)
    swapped = lax.all_to_all(tile, "blk", split_axis=0, concat_axis=0, tiled=True)
    return swapped.reshape(blocks * share, 2, block, blocks * block)


def gather_blocks(freq, blocks, samples, slot_order, flags):
    quantized = channelize(samples, flags)
    arrived = lax.all_to_all(quantized, "freq", split_axis=0, concat_axis=1, tiled=True)
    share = CH // freq
    block = slot_order.shape[1]
    own = jnp.take(arrived.reshape(share, 2, block, SPEC), slot_order[0], axis=2)
    piece = lax.all_gather(own, "blk", axis=2, tiled=True)
    return gram_pairs(own, piece)


def solution(mesh):
    freq, blocks = mesh.shape["freq"], mesh.shape["blk"]
    plan = split_channels if CH % (freq * blocks) == 0 else gather_blocks

    def body(samples, slot_order, flags):
        return plan(freq, blocks, samples, slot_order, flags)

    in_specs = (P(("blk", "freq"), None), P("blk", None), P(("blk", "freq")))
    out_specs = P("freq", None, "blk", None)
    return jax.shard_map(body, mesh=mesh, in_specs=in_specs, out_specs=out_specs, check_vma=False)
```

```python
import functools
import math

import jax
import jax.numpy as jnp
import numpy as np
from jax import lax
from jax.experimental import pallas as pl
from jax.experimental.pallas import tpu as pltpu
from jax.sharding import PartitionSpec as P

CH = 256
TAPS = 12
SPEC = 512
FRAME = 2 * CH
LANES = 128
SUB = 8
STEP = SPEC // SUB
SWAP = [(0, 1), (1, 0)]
VMEM_LIMIT = 40 * 1024 * 1024


def prototype():
    count = TAPS * FRAME
    index = np.arange(count, dtype=np.float64)
    shifted = (index + 0.5) / FRAME - TAPS / 2.0
    window = 0.5 - 0.5 * np.cos(2.0 * math.pi * (index + 0.5) / count)
    return (np.sinc(shifted) * window).astype(np.float32).reshape(TAPS, FRAME)


def twiddle():
    chan = np.arange(CH, dtype=np.int64)[:, None]
    point = np.arange(FRAME, dtype=np.int64)[None, :]
    phase = (chan * point % FRAME).astype(np.float64) * (2.0 * math.pi / FRAME)
    return np.stack([np.cos(phase), -np.sin(phase)], axis=1).astype(np.float32)


def channelize_kernel(flags_ref, x_ref, taps_ref, table_ref, out_ref, wide, fir):
    inputs = x_ref.shape[0]
    for i in range(inputs):
        for j in range(FRAME // LANES):
            cols = pl.ds(j * LANES, LANES)
            slot = i * (FRAME // LANES) + j
            wide[slot, : SPEC + TAPS - 1, :] = x_ref[i, :, cols].astype(jnp.float32)
            taps = [
                jnp.broadcast_to(taps_ref[pl.ds(t, 1), cols], (SUB, LANES)) for t in range(TAPS)
            ]
            window = [wide[slot, pl.ds(b, SUB, stride=STEP), :] for b in range(TAPS - 1)]
            pair = []
            for b in range(STEP):
                window.append(wide[slot, pl.ds(b + TAPS - 1, SUB, stride=STEP), :])
                total = taps[0] * window[b]
                for t in range(1, TAPS):
                    total = total + taps[t] * window[b + t]
                pair.append(total)
                if len(pair) == 2:
                    both = jnp.concatenate(pair, axis=0).astype(jnp.bfloat16)
                    fir[i, pl.ds((b - 1) * SUB, 2 * SUB), cols] = both
                    pair = []
        good = (1 - flags_ref[i]).astype(jnp.float32)
        rows = 128
        for r in range(0, FRAME, rows):
            spectra = lax.dot_general(
                table_ref[pl.ds(r, rows), :],
                fir[i],
                (((1,), (1,)), ((), ())),
                preferred_element_type=jnp.float32,
            ).reshape(rows // (2 * SUB), 2, SUB, SPEC)
            squares = jnp.sum(spectra * spectra, axis=1)
            power = jnp.sum(squares, axis=2, keepdims=True) / SPEC
            scale = good / jnp.sqrt(power + 1e-05)
            scaled = (spectra * scale[:, None]).astype(jnp.bfloat16)
            out_ref[pl.ds(r, rows), pl.ds(i * SPEC, SPEC)] = scaled.reshape(rows, SPEC)


def channelize(samples, flags, share):
    inputs = samples.shape[0]
    frames = samples.reshape(inputs, SPEC + TAPS - 1, FRAME)
    table = twiddle().reshape(CH // share, share, 2, FRAME).transpose(0, 2, 1, 3)
    table = jnp.asarray(table.reshape(FRAME, FRAME), dtype=jnp.bfloat16)
    taps = jnp.asarray(prototype())
    vmem = pl.BlockSpec(memory_space=pltpu.VMEM)
    return pl.pallas_call(
        channelize_kernel,
        out_shape=jax.ShapeDtypeStruct((FRAME, inputs * SPEC), jnp.bfloat16),
        in_specs=[pl.BlockSpec(memory_space=pltpu.SMEM), vmem, vmem, vmem],
        out_specs=vmem,
        scratch_shapes=[
            pltpu.VMEM((inputs * FRAME // LANES, SPEC + 16, LANES), jnp.float32),
            pltpu.VMEM((inputs, SPEC, FRAME), jnp.bfloat16),
        ],
        compiler_params=pltpu.CompilerParams(vmem_limit_bytes=VMEM_LIMIT),
        cost_estimate=pl.CostEstimate(
            flops=2 * inputs * SPEC * FRAME * (FRAME + TAPS),
            bytes_accessed=4 * inputs * SPEC * FRAME,
            transcendentals=0,
        ),
    )(flags, frames, taps, table)


def correlate_kernel(me_ref, target_ref, arrived_ref, own_ref, other_ref):
    share, _, block, width = own_ref.shape
    parts = 2 * width
    sources = arrived_ref.shape[0]
    inputs = arrived_ref.shape[1] // SPEC
    first = me_ref[0] == 0
    column = lax.broadcasted_iota(jnp.int32, (parts, sources), 1)
    target = [
        jnp.broadcast_to(target_ref[:, pl.ds(i, 1)], (parts, sources)) for i in range(inputs)
    ]
    for k in range(share):
        slots = None
        for i in range(inputs):
            pick = jnp.where(column == target[i] + k, 1.0, 0.0).astype(jnp.bfloat16)
            part = jnp.dot(
                pick,
                arrived_ref[:, pl.ds(i * SPEC, SPEC)],
                preferred_element_type=jnp.float32,
            )
            slots = part if slots is None else slots + part
        slots = slots.astype(jnp.bfloat16)
        gram = lax.dot_general(
            slots, slots, (((1,), (1,)), ((), ())), preferred_element_type=jnp.float32
        )
        real = (gram[:width, :width] + gram[width:, width:]) / SPEC
        imag = (gram[width:, :width] - gram[:width, width:]) / SPEC
        for p, part in enumerate((real, imag)):
            own_ref[k, p] = jnp.where(first, part[:block], part[block:])
            other_ref[k, p] = jnp.where(first, part[block:], part[:block])


def correlate(arrived, orders, me, share):
    blocks, block = orders.shape
    inputs = arrived.shape[1] // SPEC
    which = jnp.arange(blocks, dtype=jnp.int32)[:, None]
    source = (orders // inputs) * blocks + which
    row = (source * 2 * share).reshape(1, blocks * block)
    part = share * jnp.arange(2, dtype=jnp.int32)[:, None]
    place = (row + part).reshape(-1, 1)
    held = jnp.tile((orders % inputs).reshape(-1), 2)[:, None]
    lane = jnp.arange(inputs, dtype=jnp.int32)[None, :]
    target = jnp.where(held == lane, place, -FRAME)
    vmem = pl.BlockSpec(memory_space=pltpu.VMEM)
    tile = jax.ShapeDtypeStruct((share, 2, block, blocks * block), jnp.float32)
    return pl.pallas_call(
        correlate_kernel,
        out_shape=(tile, tile),
        in_specs=[pl.BlockSpec(memory_space=pltpu.SMEM), vmem, vmem],
        out_specs=(vmem, vmem),
        compiler_params=pltpu.CompilerParams(vmem_limit_bytes=VMEM_LIMIT),
        cost_estimate=pl.CostEstimate(
            flops=2 * share * 128 * arrived.size, bytes_accessed=2 * arrived.size, transcendentals=0
        ),
    )(me.reshape(1), target, arrived)


def split_channels(freq, blocks, samples, slot_order, flags):
    share = CH // (freq * blocks)
    me = lax.axis_index("blk").astype(jnp.int32)
    partner = lax.ppermute(slot_order, "blk", SWAP)
    orders = jnp.where(
        me == 0,
        jnp.concatenate([slot_order, partner]),
        jnp.concatenate([partner, slot_order]),
    )
    quantized = channelize(samples, flags, share)
    arrived = lax.all_to_all(quantized, ("freq", "blk"), split_axis=0, concat_axis=0, tiled=True)
    own, other = correlate(arrived, orders, me, share)
    received = lax.ppermute(other, "blk", SWAP)
    return jnp.where(
        me == 0,
        jnp.concatenate([own, received]),
        jnp.concatenate([received, own]),
    )


def gather_blocks(freq, samples, slot_order, flags):
    inputs = samples.shape[0]
    taps = jnp.asarray(prototype())
    table = jnp.asarray(twiddle().reshape(2 * CH, FRAME), dtype=jnp.bfloat16)
    good = (1 - flags).astype(jnp.float32)
    frames = samples.reshape(inputs, SPEC + TAPS - 1, FRAME)
    total = jnp.zeros((inputs, SPEC, FRAME), jnp.float32)
    for tap in range(TAPS):
        window = frames[:, tap : tap + SPEC, :].astype(jnp.float32)
        total = total + taps[tap][None, None, :] * window
    fir = total.astype(jnp.bfloat16)
    spectra = jnp.einsum("kn,isn->kis", table, fir, preferred_element_type=jnp.float32)
    squares = jnp.sum(spectra * spectra, axis=2)
    power = jnp.sum(squares.reshape(CH, 2, inputs), axis=1) / SPEC
    scale = good[None, :] / jnp.sqrt(power + 1e-05)
    quantized = (spectra * jnp.repeat(scale, 2, axis=0)[:, :, None]).astype(jnp.bfloat16)
    arrived = lax.all_to_all(quantized, "freq", split_axis=0, concat_axis=1, tiled=True)
    share = CH // freq
    block = slot_order.shape[1]
    own = jnp.take(arrived.reshape(share, 2, block, SPEC), slot_order[0], axis=2)
    piece = lax.all_gather(own, "blk", axis=2, tiled=True)
    dot = functools.partial(jnp.einsum, "cas,cbs->cab", preferred_element_type=jnp.float32)
    real = dot(own[:, 0], piece[:, 0]) + dot(own[:, 1], piece[:, 1])
    imag = dot(own[:, 1], piece[:, 0]) - dot(own[:, 0], piece[:, 1])
    return jnp.stack([real / SPEC, imag / SPEC], axis=1)


def solution(mesh):
    freq, blocks = mesh.shape["freq"], mesh.shape["blk"]

    def body(samples, slot_order, flags):
        if blocks == 2 and CH == SUB * freq * blocks:
            return split_channels(freq, blocks, samples, slot_order, flags)
        return gather_blocks(freq, samples, slot_order, flags)

    in_specs = (P(("blk", "freq"), None), P("blk", None), P(("blk", "freq")))
    out_specs = P("freq", None, "blk", None)
    return jax.shard_map(body, mesh=mesh, in_specs=in_specs, out_specs=out_specs, check_vma=False)
```

```python
import functools
import math

import jax
import jax.numpy as jnp
import numpy as np
from jax import lax
from jax.experimental import pallas as pl
from jax.experimental.pallas import tpu as pltpu
from jax.sharding import PartitionSpec as P

CH = 256
TAPS = 12
SPEC = 512
FRAME = 2 * CH
LANES = 128
SUB = 8
STEP = SPEC // SUB
STRIDE = STEP + 1
SWAP = [(0, 1), (1, 0)]
VMEM_LIMIT = 40 * 1024 * 1024


def prototype():
    count = TAPS * FRAME
    index = np.arange(count, dtype=np.float64)
    shifted = (index + 0.5) / FRAME - TAPS / 2.0
    window = 0.5 - 0.5 * np.cos(2.0 * math.pi * (index + 0.5) / count)
    return (np.sinc(shifted) * window).astype(np.float32).reshape(TAPS, FRAME)


def twiddle():
    chan = np.arange(CH, dtype=np.int64)[:, None]
    point = np.arange(FRAME, dtype=np.int64)[None, :]
    phase = (chan * point % FRAME).astype(np.float64) * (2.0 * math.pi / FRAME)
    return np.stack([np.cos(phase), -np.sin(phase)], axis=1).astype(np.float32)


def turns(count):
    half = count // 2
    return [m for pair in zip(range(half, count), [*range(1, half), 0]) for m in pair]


def channelize_kernel(
    me_ref, flags_ref, x_ref, taps_ref, table_ref, *refs, count
):
    outs, (wide, fir, spectra) = refs[:count], refs[count:]
    inputs = x_ref.shape[0]
    rows = FRAME // count
    half = rows // 2
    me = me_ref[0]
    last = lax.broadcasted_iota(jnp.int32, (SUB, LANES), 0) == SUB - 1
    for i in range(inputs):
        for j in range(FRAME // LANES):
            cols = pl.ds(j * LANES, LANES)
            slot = i * (FRAME // LANES) + j
            wide[slot, : SPEC + TAPS - 1, :] = x_ref[i, :, cols].astype(jnp.float32)
            taps = [
                jnp.broadcast_to(taps_ref[pl.ds(t, 1), cols], (SUB, LANES)) for t in range(TAPS)
            ]

            def load(b):
                return wide[slot, pl.ds(b, SUB, stride=STRIDE), :]

            def total(window):
                out = taps[0] * window[0]
                for t in range(1, TAPS):
                    out = out + taps[t] * window[t]
                return out

            extra = total([load(STEP + t) for t in range(TAPS)])
            window = [load(b) for b in range(TAPS - 1)]
            pair = []
            for b in range(STEP):
                window.append(load(b + TAPS - 1))
                row = total(window[b:])
                past = b - (STEP - SUB + 1)
                if past >= 0:
                    row = jnp.where(last, pltpu.roll(extra, SUB - 1 - past, 0), row)
                pair.append(row)
                if len(pair) == 2:
                    both = jnp.concatenate(pair, axis=0).astype(jnp.bfloat16)
                    fir[i, pl.ds((b - 1) * SUB, 2 * SUB), cols] = both
                    pair = []
        good = (1 - flags_ref[i]).astype(jnp.float32)
        spectra[i] = lax.dot_general(
            table_ref[...], fir[i], (((1,), (1,)), ((), ())), preferred_element_type=jnp.float32
        )
        for m, out in zip(turns(count), outs):
            start = pl.multiple_of(jnp.bitwise_xor(me, m) * rows, rows)
            real = spectra[i, pl.ds(start, half), :]
            imag = spectra[i, pl.ds(start + half, half), :]
            power = jnp.sum(real * real + imag * imag, axis=1, keepdims=True) / SPEC
            scale = good / jnp.sqrt(power + 1e-05)
            scaled = jnp.concatenate([real * scale, imag * scale], axis=0)
            out[:, pl.ds(i * SPEC, SPEC)] = scaled.astype(jnp.bfloat16)


def channelize(samples, flags, me, share):
    inputs = samples.shape[0]
    count = CH // share
    frames = samples.reshape(inputs, SPEC + TAPS - 1, FRAME)
    table = twiddle().reshape(count, share, 2, FRAME).transpose(0, 2, 1, 3)
    table = jnp.asarray(table.reshape(FRAME, FRAME), dtype=jnp.bfloat16)
    taps = jnp.asarray(prototype())
    smem = pl.BlockSpec(memory_space=pltpu.SMEM)
    vmem = pl.BlockSpec(memory_space=pltpu.VMEM)
    return pl.pallas_call(
        functools.partial(channelize_kernel, count=count),
        out_shape=[jax.ShapeDtypeStruct((2 * share, inputs * SPEC), jnp.bfloat16)] * count,
        in_specs=[smem, smem, vmem, vmem, vmem],
        out_specs=[vmem] * count,
        scratch_shapes=[
            pltpu.VMEM((inputs * FRAME // LANES, SPEC + 24, LANES), jnp.float32),
            pltpu.VMEM((inputs, SPEC, FRAME), jnp.bfloat16),
            pltpu.VMEM((inputs, FRAME, SPEC), jnp.float32),
        ],
        compiler_params=pltpu.CompilerParams(vmem_limit_bytes=VMEM_LIMIT),
        cost_estimate=pl.CostEstimate(
            flops=2 * inputs * SPEC * FRAME * (FRAME + TAPS),
            bytes_accessed=4 * inputs * SPEC * FRAME,
            transcendentals=0,
        ),
    )(me.reshape(1), flags, frames, taps, table)


def correlate_kernel(first_ref, target_ref, *refs):
    arrived_refs, (own_ref, other_ref) = refs[:-2], refs[-2:]
    share, _, block, width = own_ref.shape
    parts = 2 * width
    inputs = arrived_refs[0].shape[1] // SPEC
    arrived = [
        jnp.concatenate([ref[:, pl.ds(i * SPEC, SPEC)] for ref in arrived_refs], axis=0)
        for i in range(inputs)
    ]
    sources = arrived[0].shape[0]
    first = first_ref[0] == 0
    column = lax.broadcasted_iota(jnp.int32, (parts, sources), 1)
    target = [
        jnp.broadcast_to(target_ref[:, pl.ds(i, 1)], (parts, sources)) for i in range(inputs)
    ]
    for k in range(share):
        slots = None
        for i in range(inputs):
            pick = jnp.where(column == target[i] + k, 1.0, 0.0).astype(jnp.bfloat16)
            part = jnp.dot(pick, arrived[i], preferred_element_type=jnp.float32)
            slots = part if slots is None else slots + part
        slots = slots.astype(jnp.bfloat16)
        gram = lax.dot_general(
            slots, slots, (((1,), (1,)), ((), ())), preferred_element_type=jnp.float32
        )
        real = (gram[:width, :width] + gram[width:, width:]) / SPEC
        imag = (gram[width:, :width] - gram[:width, width:]) / SPEC
        for p, part in enumerate((real, imag)):
            own_ref[k, p] = jnp.where(first, part[:block], part[block:])
            other_ref[k, p] = jnp.where(first, part[block:], part[:block])


def correlate(arrived, orders, me, share):
    blocks, block = orders.shape
    inputs = arrived[0].shape[1] // SPEC
    which = jnp.arange(blocks, dtype=jnp.int32)[:, None]
    source = (orders // inputs) * blocks + which
    row = (jnp.bitwise_xor(source, me) * 2 * share).reshape(1, blocks * block)
    part = share * jnp.arange(2, dtype=jnp.int32)[:, None]
    place = (row + part).reshape(-1, 1)
    held = jnp.tile((orders % inputs).reshape(-1), 2)[:, None]
    lane = jnp.arange(inputs, dtype=jnp.int32)[None, :]
    target = jnp.where(held == lane, place, -FRAME)
    vmem = pl.BlockSpec(memory_space=pltpu.VMEM)
    tile = jax.ShapeDtypeStruct((share, 2, block, blocks * block), jnp.float32)
    size = len(arrived) * arrived[0].size
    return pl.pallas_call(
        correlate_kernel,
        out_shape=(tile, tile),
        in_specs=[pl.BlockSpec(memory_space=pltpu.SMEM), vmem] + [vmem] * len(arrived),
        out_specs=(vmem, vmem),
        compiler_params=pltpu.CompilerParams(vmem_limit_bytes=VMEM_LIMIT),
        cost_estimate=pl.CostEstimate(
            flops=2 * share * 128 * size, bytes_accessed=2 * size, transcendentals=0
        ),
    )((me % blocks).reshape(1), target, *arrived)


def split_channels(freq, blocks, samples, slot_order, flags):
    count = freq * blocks
    share = CH // count
    axes = ("freq", "blk")
    me = lax.axis_index(axes).astype(jnp.int32)
    first = me % blocks == 0
    partner = lax.ppermute(slot_order, "blk", SWAP)
    orders = jnp.where(
        first,
        jnp.concatenate([slot_order, partner]),
        jnp.concatenate([partner, slot_order]),
    )
    sent = channelize(samples, flags, me, share)
    arrived = [None] * count
    for m, part in zip(turns(count), sent):
        pairs = [(d, d ^ m) for d in range(count)]
        arrived[m] = lax.ppermute(part, axes, pairs) if m else part
    own, other = correlate(arrived, orders, me, share)
    received = lax.ppermute(other, "blk", SWAP)
    return jnp.where(
        first,
        jnp.concatenate([own, received]),
        jnp.concatenate([received, own]),
    )


def gather_blocks(freq, samples, slot_order, flags):
    inputs = samples.shape[0]
    taps = jnp.asarray(prototype())
    table = jnp.asarray(twiddle().reshape(2 * CH, FRAME), dtype=jnp.bfloat16)
    good = (1 - flags).astype(jnp.float32)
    frames = samples.reshape(inputs, SPEC + TAPS - 1, FRAME)
    total = jnp.zeros((inputs, SPEC, FRAME), jnp.float32)
    for tap in range(TAPS):
        window = frames[:, tap : tap + SPEC, :].astype(jnp.float32)
        total = total + taps[tap][None, None, :] * window
    fir = total.astype(jnp.bfloat16)
    spectra = jnp.einsum("kn,isn->kis", table, fir, preferred_element_type=jnp.float32)
    squares = jnp.sum(spectra * spectra, axis=2)
    power = jnp.sum(squares.reshape(CH, 2, inputs), axis=1) / SPEC
    scale = good[None, :] / jnp.sqrt(power + 1e-05)
    quantized = (spectra * jnp.repeat(scale, 2, axis=0)[:, :, None]).astype(jnp.bfloat16)
    arrived = lax.all_to_all(quantized, "freq", split_axis=0, concat_axis=1, tiled=True)
    share = CH // freq
    block = slot_order.shape[1]
    own = jnp.take(arrived.reshape(share, 2, block, SPEC), slot_order[0], axis=2)
    piece = lax.all_gather(own, "blk", axis=2, tiled=True)
    dot = functools.partial(jnp.einsum, "cas,cbs->cab", preferred_element_type=jnp.float32)
    real = dot(own[:, 0], piece[:, 0]) + dot(own[:, 1], piece[:, 1])
    imag = dot(own[:, 1], piece[:, 0]) - dot(own[:, 0], piece[:, 1])
    return jnp.stack([real / SPEC, imag / SPEC], axis=1)


def solution(mesh):
    freq, blocks = mesh.shape["freq"], mesh.shape["blk"]

    def body(samples, slot_order, flags):
        if blocks == 2 and CH == SUB * freq * blocks:
            return split_channels(freq, blocks, samples, slot_order, flags)
        return gather_blocks(freq, samples, slot_order, flags)

    in_specs = (P(("blk", "freq"), None), P("blk", None), P(("blk", "freq")))
    out_specs = P("freq", None, "blk", None)
    return jax.shard_map(body, mesh=mesh, in_specs=in_specs, out_specs=out_specs, check_vma=False)
```

```python
import functools
import math

import jax
import jax.numpy as jnp
import numpy as np
from jax import lax
from jax.experimental import pallas as pl
from jax.experimental.pallas import tpu as pltpu
from jax.sharding import PartitionSpec as P

CH = 256
TAPS = 12
SPEC = 512
FRAME = 2 * CH
LANES = 128
SUB = 8
STEP = SPEC // SUB
STRIDE = STEP + 1
SWAP = [(0, 1), (1, 0)]
VMEM_LIMIT = 40 * 1024 * 1024


def prototype():
    count = TAPS * FRAME
    index = np.arange(count, dtype=np.float64)
    shifted = (index + 0.5) / FRAME - TAPS / 2.0
    window = 0.5 - 0.5 * np.cos(2.0 * math.pi * (index + 0.5) / count)
    return (np.sinc(shifted) * window).astype(np.float32).reshape(TAPS, FRAME)


def twiddle():
    chan = np.arange(CH, dtype=np.int64)[:, None]
    point = np.arange(FRAME, dtype=np.int64)[None, :]
    phase = (chan * point % FRAME).astype(np.float64) * (2.0 * math.pi / FRAME)
    return np.stack([np.cos(phase), -np.sin(phase)], axis=1).astype(np.float32)


def channelize_kernel(
    flags_ref, x_ref, taps_ref, table_ref, out_ref, wide, fir, spectra, *, which
):
    half = SUB
    last = lax.broadcasted_iota(jnp.int32, (SUB, LANES), 0) == SUB - 1
    for j in range(FRAME // LANES):
        cols = pl.ds(j * LANES, LANES)
        wide[j, : SPEC + TAPS - 1, :] = x_ref[which, :, cols].astype(jnp.float32)
        taps = [jnp.broadcast_to(taps_ref[pl.ds(t, 1), cols], (SUB, LANES)) for t in range(TAPS)]

        def load(b):
            return wide[j, pl.ds(b, SUB, stride=STRIDE), :]

        def total(window):
            out = taps[0] * window[0]
            for t in range(1, TAPS):
                out = out + taps[t] * window[t]
            return out

        extra = total([load(STEP + t) for t in range(TAPS)])
        window = [load(b) for b in range(TAPS - 1)]
        pair = []
        for b in range(STEP):
            window.append(load(b + TAPS - 1))
            row = total(window[b:])
            past = b - (STEP - SUB + 1)
            if past >= 0:
                row = jnp.where(last, pltpu.roll(extra, SUB - 1 - past, 0), row)
            pair.append(row)
            if len(pair) == 2:
                both = jnp.concatenate(pair, axis=0).astype(jnp.bfloat16)
                fir[pl.ds((b - 1) * SUB, 2 * SUB), cols] = both
                pair = []
    good = (1 - flags_ref[which]).astype(jnp.float32)
    spectra[...] = lax.dot_general(
        table_ref[...], fir[...], (((1,), (1,)), ((), ())), preferred_element_type=jnp.float32
    )
    for start in range(0, FRAME, 2 * half):
        real = spectra[pl.ds(start, half), :]
        imag = spectra[pl.ds(start + half, half), :]
        power = jnp.sum(real * real + imag * imag, axis=1, keepdims=True) / SPEC
        scale = good / jnp.sqrt(power + 1e-05)
        scaled = jnp.concatenate([real * scale, imag * scale], axis=0)
        out_ref[pl.ds(start, 2 * half), :] = scaled.astype(jnp.bfloat16)


def channelize(frames, flags, which):
    table = twiddle().reshape(CH // SUB, SUB, 2, FRAME).transpose(0, 2, 1, 3)
    table = jnp.asarray(table.reshape(FRAME, FRAME), dtype=jnp.bfloat16)
    taps = jnp.asarray(prototype())
    smem = pl.BlockSpec(memory_space=pltpu.SMEM)
    vmem = pl.BlockSpec(memory_space=pltpu.VMEM)
    return pl.pallas_call(
        functools.partial(channelize_kernel, which=which),
        out_shape=jax.ShapeDtypeStruct((FRAME, SPEC), jnp.bfloat16),
        in_specs=[smem, vmem, vmem, vmem],
        out_specs=vmem,
        scratch_shapes=[
            pltpu.VMEM((FRAME // LANES, SPEC + 24, LANES), jnp.float32),
            pltpu.VMEM((SPEC, FRAME), jnp.bfloat16),
            pltpu.VMEM((FRAME, SPEC), jnp.float32),
        ],
        compiler_params=pltpu.CompilerParams(vmem_limit_bytes=VMEM_LIMIT),
        cost_estimate=pl.CostEstimate(
            flops=2 * SPEC * FRAME * (FRAME + TAPS),
            bytes_accessed=4 * SPEC * FRAME,
            transcendentals=0,
        ),
    )(flags, frames, taps, table)


def correlate_kernel(first_ref, target_ref, *refs):
    arrived_refs, (own_ref, other_ref) = refs[:-2], refs[-2:]
    share, _, block, width = own_ref.shape
    parts = 2 * width
    inputs = len(arrived_refs)
    sources = arrived_refs[0].shape[0]
    first = first_ref[0] == 0
    column = lax.broadcasted_iota(jnp.int32, (parts, sources), 1)
    target = [
        jnp.broadcast_to(target_ref[:, pl.ds(i, 1)], (parts, sources)) for i in range(inputs)
    ]
    for k in range(share):
        slots = None
        for i in range(inputs):
            pick = jnp.where(column == target[i] + k, 1.0, 0.0).astype(jnp.bfloat16)
            part = jnp.dot(pick, arrived_refs[i][...], preferred_element_type=jnp.float32)
            slots = part if slots is None else slots + part
        slots = slots.astype(jnp.bfloat16)
        gram = lax.dot_general(
            slots, slots, (((1,), (1,)), ((), ())), preferred_element_type=jnp.float32
        )
        real = (gram[:width, :width] + gram[width:, width:]) / SPEC
        imag = (gram[width:, :width] - gram[:width, width:]) / SPEC
        for p, part in enumerate((real, imag)):
            own_ref[k, p] = jnp.where(first, part[:block], part[block:])
            other_ref[k, p] = jnp.where(first, part[block:], part[:block])


def correlate(arrived, orders, me, share):
    blocks, block = orders.shape
    inputs = len(arrived)
    which = jnp.arange(blocks, dtype=jnp.int32)[:, None]
    source = (orders // inputs) * blocks + which
    row = (source * 2 * share).reshape(1, blocks * block)
    part = share * jnp.arange(2, dtype=jnp.int32)[:, None]
    place = (row + part).reshape(-1, 1)
    held = jnp.tile((orders % inputs).reshape(-1), 2)[:, None]
    lane = jnp.arange(inputs, dtype=jnp.int32)[None, :]
    target = jnp.where(held == lane, place, -FRAME)
    vmem = pl.BlockSpec(memory_space=pltpu.VMEM)
    tile = jax.ShapeDtypeStruct((share, 2, block, blocks * block), jnp.float32)
    size = inputs * arrived[0].size
    return pl.pallas_call(
        correlate_kernel,
        out_shape=(tile, tile),
        in_specs=[pl.BlockSpec(memory_space=pltpu.SMEM), vmem] + [vmem] * len(arrived),
        out_specs=(vmem, vmem),
        compiler_params=pltpu.CompilerParams(vmem_limit_bytes=VMEM_LIMIT),
        cost_estimate=pl.CostEstimate(
            flops=2 * share * 128 * size, bytes_accessed=2 * size, transcendentals=0
        ),
    )(me.reshape(1), target, *arrived)


def split_channels(freq, blocks, samples, slot_order, flags):
    share = CH // (freq * blocks)
    inputs = samples.shape[0]
    me = lax.axis_index("blk").astype(jnp.int32)
    first = me == 0
    partner = lax.ppermute(slot_order, "blk", SWAP)
    orders = jnp.where(
        first,
        jnp.concatenate([slot_order, partner]),
        jnp.concatenate([partner, slot_order]),
    )
    frames = samples.reshape(inputs, SPEC + TAPS - 1, FRAME)
    arrived = []
    for i in range(inputs):
        sent = channelize(frames, flags, i)
        turned = lax.all_to_all(sent, ("freq", "blk"), split_axis=0, concat_axis=0, tiled=True)
        arrived.append(turned)
    own, other = correlate(arrived, orders, me, share)
    received = lax.ppermute(other, "blk", SWAP)
    return jnp.where(
        first,
        jnp.concatenate([own, received]),
        jnp.concatenate([received, own]),
    )


def gather_blocks(freq, samples, slot_order, flags):
    inputs = samples.shape[0]
    taps = jnp.asarray(prototype())
    table = jnp.asarray(twiddle().reshape(2 * CH, FRAME), dtype=jnp.bfloat16)
    good = (1 - flags).astype(jnp.float32)
    frames = samples.reshape(inputs, SPEC + TAPS - 1, FRAME)
    total = jnp.zeros((inputs, SPEC, FRAME), jnp.float32)
    for tap in range(TAPS):
        window = frames[:, tap : tap + SPEC, :].astype(jnp.float32)
        total = total + taps[tap][None, None, :] * window
    fir = total.astype(jnp.bfloat16)
    spectra = jnp.einsum("kn,isn->kis", table, fir, preferred_element_type=jnp.float32)
    squares = jnp.sum(spectra * spectra, axis=2)
    power = jnp.sum(squares.reshape(CH, 2, inputs), axis=1) / SPEC
    scale = good[None, :] / jnp.sqrt(power + 1e-05)
    quantized = (spectra * jnp.repeat(scale, 2, axis=0)[:, :, None]).astype(jnp.bfloat16)
    arrived = lax.all_to_all(quantized, "freq", split_axis=0, concat_axis=1, tiled=True)
    share = CH // freq
    block = slot_order.shape[1]
    own = jnp.take(arrived.reshape(share, 2, block, SPEC), slot_order[0], axis=2)
    piece = lax.all_gather(own, "blk", axis=2, tiled=True)
    dot = functools.partial(jnp.einsum, "cas,cbs->cab", preferred_element_type=jnp.float32)
    real = dot(own[:, 0], piece[:, 0]) + dot(own[:, 1], piece[:, 1])
    imag = dot(own[:, 1], piece[:, 0]) - dot(own[:, 0], piece[:, 1])
    return jnp.stack([real / SPEC, imag / SPEC], axis=1)


def solution(mesh):
    freq, blocks = mesh.shape["freq"], mesh.shape["blk"]

    def body(samples, slot_order, flags):
        if blocks == 2 and CH == SUB * freq * blocks:
            return split_channels(freq, blocks, samples, slot_order, flags)
        return gather_blocks(freq, samples, slot_order, flags)

    in_specs = (P(("blk", "freq"), None), P("blk", None), P(("blk", "freq")))
    out_specs = P("freq", None, "blk", None)
    return jax.shard_map(body, mesh=mesh, in_specs=in_specs, out_specs=out_specs, check_vma=False)
```

```python
import functools
import math

import jax
import jax.numpy as jnp
import numpy as np
from jax import lax
from jax.experimental import pallas as pl
from jax.experimental.pallas import tpu as pltpu
from jax.sharding import Mesh
from jax.sharding import PartitionSpec as P

CH = 256
TAPS = 12
SPEC = 512
FRAME = 2 * CH
LANES = 128
SUB = 8
STEP = SPEC // SUB
STRIDE = STEP + 1
FAR = 4
SWAP = [(0, 1), (1, 0)]
VMEM_LIMIT = 40 * 1024 * 1024


def prototype():
    count = TAPS * FRAME
    index = np.arange(count, dtype=np.float64)
    shifted = (index + 0.5) / FRAME - TAPS / 2.0
    window = 0.5 - 0.5 * np.cos(2.0 * math.pi * (index + 0.5) / count)
    return (np.sinc(shifted) * window).astype(np.float32).reshape(TAPS, FRAME)


def twiddle():
    chan = np.arange(CH, dtype=np.int64)[:, None]
    point = np.arange(FRAME, dtype=np.int64)[None, :]
    phase = (chan * point % FRAME).astype(np.float64) * (2.0 * math.pi / FRAME)
    return np.stack([np.cos(phase), -np.sin(phase)], axis=1).astype(np.float32)


def channelize_kernel(
    flags_ref, x_ref, taps_ref, table_ref, out_ref, wide, fir, spectra, result, sems
):
    inputs = x_ref.shape[0]
    pieces = sems.shape[1]
    rows = FRAME // pieces
    last = lax.broadcasted_iota(jnp.int32, (SUB, LANES), 0) == SUB - 1
    copies = []
    for i in range(inputs):
        for j in range(FRAME // LANES):
            cols = pl.ds(j * LANES, LANES)
            slot = i * (FRAME // LANES) + j
            wide[slot, : SPEC + TAPS - 1, :] = x_ref[i, :, cols].astype(jnp.float32)
            taps = [
                jnp.broadcast_to(taps_ref[pl.ds(t, 1), cols], (SUB, LANES)) for t in range(TAPS)
            ]

            def load(b):
                return wide[slot, pl.ds(b, SUB, stride=STRIDE), :]

            def total(window):
                out = taps[0] * window[0]
                for t in range(1, TAPS):
                    out = out + taps[t] * window[t]
                return out

            extra = total([load(STEP + t) for t in range(TAPS)])
            window = [load(b) for b in range(TAPS - 1)]
            pair = []
            for b in range(STEP):
                window.append(load(b + TAPS - 1))
                row = total(window[b:])
                past = b - (STEP - SUB + 1)
                if past >= 0:
                    row = jnp.where(last, pltpu.roll(extra, SUB - 1 - past, 0), row)
                pair.append(row)
                if len(pair) == 2:
                    both = jnp.concatenate(pair, axis=0).astype(jnp.bfloat16)
                    fir[i, pl.ds((b - 1) * SUB, 2 * SUB), cols] = both
                    pair = []
        good = (1 - flags_ref[i]).astype(jnp.float32)
        spectra[i] = lax.dot_general(
            table_ref[...], fir[i], (((1,), (1,)), ((), ())), preferred_element_type=jnp.float32
        )
        for piece in range(pieces):
            place = (pl.ds(piece * rows, rows), pl.ds(i * SPEC, SPEC))
            pairs = spectra[i, pl.ds(piece * rows, rows), :]
            pairs = pairs.reshape(rows // (2 * SUB), 2, SUB, SPEC)
            squares = jnp.sum(pairs * pairs, axis=1)
            power = jnp.sum(squares, axis=2, keepdims=True) / SPEC
            scale = good / jnp.sqrt(power + 1e-05)
            scaled = (pairs * scale[:, None]).astype(jnp.bfloat16)
            result[place] = scaled.reshape(rows, SPEC)
            copy = pltpu.make_async_copy(result.at[place], out_ref.at[place], sems.at[i, piece])
            copy.start()
            copies.append(copy)
    for copy in copies:
        copy.wait()


def channelize(samples, flags, far, near, blocks):
    inputs = samples.shape[0]
    frames = samples.reshape(inputs, SPEC + TAPS - 1, FRAME)
    table = twiddle().reshape(far, near, blocks, SUB, 2, FRAME).transpose(2, 1, 0, 4, 3, 5)
    table = jnp.asarray(table.reshape(FRAME, FRAME), dtype=jnp.bfloat16)
    taps = jnp.asarray(prototype())
    smem = pl.BlockSpec(memory_space=pltpu.SMEM)
    vmem = pl.BlockSpec(memory_space=pltpu.VMEM)
    return pl.pallas_call(
        channelize_kernel,
        out_shape=jax.ShapeDtypeStruct((FRAME, inputs * SPEC), jnp.bfloat16),
        in_specs=[smem, vmem, vmem, vmem],
        out_specs=pl.BlockSpec(memory_space=pl.ANY),
        scratch_shapes=[
            pltpu.VMEM((inputs * FRAME // LANES, SPEC + 24, LANES), jnp.float32),
            pltpu.VMEM((inputs, SPEC, FRAME), jnp.bfloat16),
            pltpu.VMEM((inputs, FRAME, SPEC), jnp.float32),
            pltpu.VMEM((FRAME, inputs * SPEC), jnp.bfloat16),
            pltpu.SemaphoreType.DMA((inputs, 8)),
        ],
        compiler_params=pltpu.CompilerParams(vmem_limit_bytes=VMEM_LIMIT),
        cost_estimate=pl.CostEstimate(
            flops=2 * inputs * SPEC * FRAME * (FRAME + TAPS),
            bytes_accessed=4 * inputs * SPEC * FRAME,
            transcendentals=0,
        ),
    )(flags, frames, taps, table)


def correlate_kernel(first_ref, pick_ref, arrived_ref, own_ref, other_ref, slots):
    share, _, block, width = own_ref.shape
    blocks = pick_ref.shape[0]
    held = arrived_ref.shape[0] // blocks
    first = first_ref[0] == 0
    for n in range(blocks):
        rows = pl.ds(n * held, held)
        stacked = jnp.concatenate(
            [
                arrived_ref[rows, pl.ds(i * SPEC, SPEC)]
                for i in range(arrived_ref.shape[1] // SPEC)
            ],
            axis=0,
        )
        slots[n] = jnp.dot(
            pick_ref[n], stacked, preferred_element_type=jnp.float32
        ).astype(jnp.bfloat16)
    for k in range(share):
        pair = jnp.concatenate(
            [
                slots[n, pl.ds((2 * k + p) * block, block), :]
                for p in range(2)
                for n in range(blocks)
            ],
            axis=0,
        )
        gram = lax.dot_general(
            pair, pair, (((1,), (1,)), ((), ())), preferred_element_type=jnp.float32
        )
        real = (gram[:width, :width] + gram[width:, width:]) / SPEC
        imag = (gram[width:, :width] - gram[:width, width:]) / SPEC
        for p, part in enumerate((real, imag)):
            own_ref[k, p] = jnp.where(first, part[:block], part[block:])
            other_ref[k, p] = jnp.where(first, part[block:], part[:block])


def picks(orders, inputs, far, near, share):
    blocks, block = orders.shape
    device, held = orders // inputs, orders % inputs
    place = (device % near) * far + device // near
    start = ((held * far * near + place) * 2 * share)[:, None, None, :]
    chan = jnp.arange(share, dtype=jnp.int32)[:, None, None]
    part = jnp.arange(2, dtype=jnp.int32)[:, None]
    target = (start + part * share + chan).reshape(blocks, share * 2 * block, 1)
    column = lax.broadcasted_iota(jnp.int32, (1, 1, inputs * far * near * 2 * share), 2)
    return (column == target).astype(jnp.bfloat16)


def correlate(arrived, pick, me, share, block):
    blocks = pick.shape[0]
    smem = pl.BlockSpec(memory_space=pltpu.SMEM)
    vmem = pl.BlockSpec(memory_space=pltpu.VMEM)
    tile = jax.ShapeDtypeStruct((share, 2, block, blocks * block), jnp.float32)
    return pl.pallas_call(
        correlate_kernel,
        out_shape=(tile, tile),
        in_specs=[smem, vmem, vmem],
        out_specs=(vmem, vmem),
        scratch_shapes=[pltpu.VMEM((blocks, share * 2 * block, SPEC), jnp.bfloat16)],
        compiler_params=pltpu.CompilerParams(vmem_limit_bytes=VMEM_LIMIT),
        cost_estimate=pl.CostEstimate(
            flops=2 * pick.size * SPEC, bytes_accessed=4 * arrived.size, transcendentals=0
        ),
    )(me.reshape(1), pick, arrived)


def place_kernel(me_ref, own_ref, out_ref, sem):
    share = own_ref.shape[0]
    copy = pltpu.make_async_copy(own_ref, out_ref.at[pl.ds(me_ref[0] * share, share)], sem)
    copy.start()
    copy.wait()


def place_own(own, me, blocks):
    share = own.shape[0]
    return pl.pallas_call(
        place_kernel,
        out_shape=jax.ShapeDtypeStruct((blocks * share, *own.shape[1:]), own.dtype),
        in_specs=[
            pl.BlockSpec(memory_space=pltpu.SMEM),
            pl.BlockSpec(memory_space=pltpu.VMEM),
        ],
        out_specs=pl.BlockSpec(memory_space=pl.ANY),
        scratch_shapes=[pltpu.SemaphoreType.DMA],
        cost_estimate=pl.CostEstimate(flops=0, bytes_accessed=4 * own.size, transcendentals=0),
    )(me.reshape(1), own)


def split_channels(far, near, blocks, samples, slot_order, flags):
    share = CH // (far * near * blocks)
    inputs, block = samples.shape[0], slot_order.shape[1]
    axes = ("blk", "near", "far")
    me = lax.axis_index("blk").astype(jnp.int32)
    partner = lax.ppermute(slot_order, "blk", SWAP)
    orders = jnp.where(
        me == 0,
        jnp.concatenate([slot_order, partner]),
        jnp.concatenate([partner, slot_order]),
    )
    sent = channelize(samples, flags, far, near, blocks)
    arrived = lax.all_to_all(sent, axes, split_axis=0, concat_axis=0, tiled=True)
    pick = picks(orders, inputs, far, near, share)
    own, other = correlate(arrived, pick, me, share, block)
    received = lax.ppermute(other, "blk", SWAP)
    out = place_own(own, me, blocks)
    return lax.dynamic_update_slice(out, received, ((1 - me) * share, 0, 0, 0))


def gather_blocks(freq, samples, slot_order, flags):
    inputs = samples.shape[0]
    taps = jnp.asarray(prototype())
    table = jnp.asarray(twiddle().reshape(2 * CH, FRAME), dtype=jnp.bfloat16)
    good = (1 - flags).astype(jnp.float32)
    frames = samples.reshape(inputs, SPEC + TAPS - 1, FRAME)
    total = jnp.zeros((inputs, SPEC, FRAME), jnp.float32)
    for tap in range(TAPS):
        window = frames[:, tap : tap + SPEC, :].astype(jnp.float32)
        total = total + taps[tap][None, None, :] * window
    fir = total.astype(jnp.bfloat16)
    spectra = jnp.einsum("kn,isn->kis", table, fir, preferred_element_type=jnp.float32)
    squares = jnp.sum(spectra * spectra, axis=2)
    power = jnp.sum(squares.reshape(CH, 2, inputs), axis=1) / SPEC
    scale = good[None, :] / jnp.sqrt(power + 1e-05)
    quantized = (spectra * jnp.repeat(scale, 2, axis=0)[:, :, None]).astype(jnp.bfloat16)
    arrived = lax.all_to_all(quantized, ("far", "near"), split_axis=0, concat_axis=1, tiled=True)
    share = CH // freq
    block = slot_order.shape[1]
    own = jnp.take(arrived.reshape(share, 2, block, SPEC), slot_order[0], axis=2)
    piece = lax.all_gather(own, "blk", axis=2, tiled=True)
    dot = functools.partial(jnp.einsum, "cas,cbs->cab", preferred_element_type=jnp.float32)
    real = dot(own[:, 0], piece[:, 0]) + dot(own[:, 1], piece[:, 1])
    imag = dot(own[:, 1], piece[:, 0]) - dot(own[:, 0], piece[:, 1])
    return jnp.stack([real / SPEC, imag / SPEC], axis=1)


def solution(mesh):
    freq, blocks = mesh.shape["freq"], mesh.shape["blk"]
    far = math.gcd(freq, FAR)
    near = freq // far
    split = Mesh(mesh.devices.reshape(far, near, blocks), ("far", "near", "blk"))

    def body(samples, slot_order, flags):
        if blocks == 2 and CH == SUB * freq * blocks:
            return split_channels(far, near, blocks, samples, slot_order, flags)
        return gather_blocks(freq, samples, slot_order, flags)

    held = ("blk", "far", "near")
    in_specs = (P(held, None), P("blk", None), P(held))
    out_specs = P(("far", "near"), None, "blk", None)
    return jax.shard_map(body, mesh=split, in_specs=in_specs, out_specs=out_specs, check_vma=False)
```

```python
import functools
import math

import jax
import jax.numpy as jnp
import numpy as np
from jax import lax
from jax.experimental import pallas as pl
from jax.experimental.pallas import tpu as pltpu
from jax.sharding import Mesh
from jax.sharding import PartitionSpec as P

CH = 256
TAPS = 12
SPEC = 512
FRAME = 2 * CH
LANES = 128
SUB = 8
GROUP = 128
STEP = GROUP // SUB
STRIDE = STEP + 1
FAR = 4
SWAP = [(0, 1), (1, 0)]
VMEM_LIMIT = 40 * 1024 * 1024


def prototype():
    count = TAPS * FRAME
    index = np.arange(count, dtype=np.float64)
    shifted = (index + 0.5) / FRAME - TAPS / 2.0
    window = 0.5 - 0.5 * np.cos(2.0 * math.pi * (index + 0.5) / count)
    return (np.sinc(shifted) * window).astype(np.float32).reshape(TAPS, FRAME)


def twiddle():
    chan = np.arange(CH, dtype=np.int64)[:, None]
    point = np.arange(FRAME, dtype=np.int64)[None, :]
    phase = (chan * point % FRAME).astype(np.float64) * (2.0 * math.pi / FRAME)
    return np.stack([np.cos(phase), -np.sin(phase)], axis=1).astype(np.float32)


def channelize_kernel(
    flags_ref, x_ref, taps_ref, table_ref, out_ref, held, wide, fir, spectra, result, in_sems, sems
):
    inputs = held.shape[0]
    frames = SPEC + TAPS - 1
    pieces = sems.shape[1]
    rows = FRAME // pieces
    last = lax.broadcasted_iota(jnp.int32, (SUB, LANES), 0) == SUB - 1
    edges = [0] + [g * GROUP + TAPS - 1 for g in range(1, SPEC // GROUP)] + [frames]
    loads = []
    for g, (begin, end) in enumerate(zip(edges, edges[1:])):
        part = (slice(None), pl.ds(begin * FRAME, (end - begin) * FRAME))
        load = pltpu.make_async_copy(x_ref.at[part], held.at[part], in_sems.at[g])
        load.start()
        loads.append(load)

    def convert(g):
        for f in range(edges[g], edges[g + 1]):
            for j in range(FRAME // LANES):
                tile = held[:, pl.ds(f * FRAME + j * LANES, LANES)]
                wide[j, pl.ds(inputs * f, inputs), :] = tile.astype(jnp.float32)

    def filter_group(g, i, j):
        cols = pl.ds(j * LANES, LANES)
        taps = [jnp.broadcast_to(taps_ref[pl.ds(t, 1), cols], (SUB, LANES)) for t in range(TAPS)]

        def take(b):
            first = inputs * (g * GROUP + b) + i
            return wide[j, pl.ds(first, SUB, stride=inputs * STRIDE), :]

        def total(window):
            out = taps[0] * window[0]
            for t in range(1, TAPS):
                out = out + taps[t] * window[t]
            return out

        window = [take(b) for b in range(STEP + TAPS)]
        extra = total(window[STEP:])
        for b in range(0, STEP, 2):
            pair = []
            for c in (b, b + 1):
                row = total(window[c:])
                past = c - (STEP - SUB + 1)
                if past >= 0:
                    row = jnp.where(last, pltpu.roll(extra, SUB - 1 - past, 0), row)
                pair.append(row)
            both = jnp.concatenate(pair, axis=0).astype(jnp.bfloat16)
            fir[i, pl.ds(g * GROUP + b * SUB, 2 * SUB), cols] = both

    for g in range(SPEC // GROUP):
        loads[g].wait()
        convert(g)
        for i in range(inputs):
            for j in range(FRAME // LANES):
                filter_group(g, i, j)
    copies = []
    for i in range(inputs):
        spectra[i] = lax.dot_general(
            table_ref[...], fir[i], (((1,), (1,)), ((), ())), preferred_element_type=jnp.float32
        )
    for i in range(inputs):
        good = (1 - flags_ref[i]).astype(jnp.float32)
        for piece in range(pieces):
            place = (pl.ds(piece * rows, rows), pl.ds(i * SPEC, SPEC))
            pairs = spectra[i, pl.ds(piece * rows, rows), :]
            pairs = pairs.reshape(rows // (2 * SUB), 2, SUB, SPEC)
            squares = jnp.sum(pairs * pairs, axis=1)
            power = jnp.sum(squares, axis=2, keepdims=True) / SPEC
            scale = good / jnp.sqrt(power + 1e-05)
            scaled = (pairs * scale[:, None]).astype(jnp.bfloat16)
            result[place] = scaled.reshape(rows, SPEC)
            copy = pltpu.make_async_copy(result.at[place], out_ref.at[place], sems.at[i, piece])
            copy.start()
            copies.append(copy)
    for copy in copies:
        copy.wait()


def channelize(samples, flags, far, near, blocks):
    inputs = samples.shape[0]
    table = twiddle().reshape(far, near, blocks, SUB, 2, FRAME).transpose(2, 1, 0, 4, 3, 5)
    table = jnp.asarray(table.reshape(FRAME, FRAME), dtype=jnp.bfloat16)
    taps = jnp.asarray(prototype())
    smem = pl.BlockSpec(memory_space=pltpu.SMEM)
    vmem = pl.BlockSpec(memory_space=pltpu.VMEM)
    return pl.pallas_call(
        channelize_kernel,
        out_shape=jax.ShapeDtypeStruct((FRAME, inputs * SPEC), jnp.bfloat16),
        in_specs=[smem, pl.BlockSpec(memory_space=pltpu.HBM), vmem, vmem],
        out_specs=pl.BlockSpec(memory_space=pl.ANY),
        scratch_shapes=[
            pltpu.VMEM(samples.shape, jnp.bfloat16),
            pltpu.VMEM((FRAME // LANES, inputs * (SPEC + 24), LANES), jnp.float32),
            pltpu.VMEM((inputs, SPEC, FRAME), jnp.bfloat16),
            pltpu.VMEM((inputs, FRAME, SPEC), jnp.float32),
            pltpu.VMEM((FRAME, inputs * SPEC), jnp.bfloat16),
            pltpu.SemaphoreType.DMA((SPEC // GROUP,)),
            pltpu.SemaphoreType.DMA((inputs, 8)),
        ],
        compiler_params=pltpu.CompilerParams(vmem_limit_bytes=VMEM_LIMIT),
        cost_estimate=pl.CostEstimate(
            flops=2 * inputs * SPEC * FRAME * (FRAME + TAPS),
            bytes_accessed=4 * inputs * SPEC * FRAME,
            transcendentals=0,
        ),
    )(flags, samples, taps, table)


def correlate_kernel(first_ref, pick_ref, arrived_ref, own_ref, other_ref, slots):
    share, block, _ = own_ref.shape
    blocks = pick_ref.shape[0]
    width = blocks * block
    held = arrived_ref.shape[0] // blocks
    first = first_ref[0] == 0
    lane = lax.broadcasted_iota(jnp.int32, (width, 2 * width), 1)
    sign = jnp.where(lane < width, 1.0 / SPEC, -1.0 / SPEC)
    for n in range(blocks):
        rows = pl.ds(n * held, held)
        stacked = jnp.concatenate(
            [
                arrived_ref[rows, pl.ds(i * SPEC, SPEC)]
                for i in range(arrived_ref.shape[1] // SPEC)
            ],
            axis=0,
        )
        slots[n] = jnp.dot(
            pick_ref[n], stacked, preferred_element_type=jnp.float32
        ).astype(jnp.bfloat16)
    for k in range(share):
        pair = jnp.concatenate(
            [
                slots[n, pl.ds((2 * k + p) * block, block), :]
                for p in range(2)
                for n in range(blocks)
            ],
            axis=0,
        )
        gram = lax.dot_general(
            pair, pair, (((1,), (1,)), ((), ())), preferred_element_type=jnp.float32
        )
        part = gram[:width] * sign + pltpu.roll(gram[width:], width, 1) / SPEC
        own_ref[k] = jnp.where(first, part[:block], part[block:])
        other_ref[k] = jnp.where(first, part[block:], part[:block])


def picks(orders, inputs, far, near, share):
    blocks, block = orders.shape
    device, held = orders // inputs, orders % inputs
    place = (device % near) * far + device // near
    start = ((held * far * near + place) * 2 * share)[:, None, None, :]
    chan = jnp.arange(share, dtype=jnp.int32)[:, None, None]
    part = jnp.arange(2, dtype=jnp.int32)[:, None]
    target = (start + part * share + chan).reshape(blocks, share * 2 * block, 1)
    column = lax.broadcasted_iota(jnp.int32, (1, 1, inputs * far * near * 2 * share), 2)
    return (column == target).astype(jnp.bfloat16)


def correlate(arrived, pick, me, share, block):
    blocks = pick.shape[0]
    smem = pl.BlockSpec(memory_space=pltpu.SMEM)
    vmem = pl.BlockSpec(memory_space=pltpu.VMEM)
    tile = jax.ShapeDtypeStruct((share, block, 2 * blocks * block), jnp.float32)
    return pl.pallas_call(
        correlate_kernel,
        out_shape=(tile, tile),
        in_specs=[smem, vmem, vmem],
        out_specs=(vmem, vmem),
        scratch_shapes=[pltpu.VMEM((blocks, share * 2 * block, SPEC), jnp.bfloat16)],
        compiler_params=pltpu.CompilerParams(vmem_limit_bytes=VMEM_LIMIT),
        cost_estimate=pl.CostEstimate(
            flops=2 * pick.size * SPEC, bytes_accessed=4 * arrived.size, transcendentals=0
        ),
    )(me.reshape(1), pick, arrived)


def place_kernel(index_ref, packed_ref, *refs):
    out_ref, parts, sems = refs[-3:]
    share, _, _, width = parts.shape
    copies = []
    for k in range(share):
        parts[k, 0] = packed_ref[k, :, :width]
        parts[k, 1] = packed_ref[k, :, width:]
        where = index_ref[0] * share + k
        copies.append(pltpu.make_async_copy(parts.at[k], out_ref.at[where], sems.at[k]))
        copies[-1].start()
    for copy in copies:
        copy.wait()


def place(packed, index, blocks, base=None):
    share, block, lanes = packed.shape
    width = lanes // 2
    anywhere = pl.BlockSpec(memory_space=pl.ANY)
    return pl.pallas_call(
        place_kernel,
        out_shape=jax.ShapeDtypeStruct((blocks * share, 2, block, width), packed.dtype),
        in_specs=[
            pl.BlockSpec(memory_space=pltpu.SMEM),
            pl.BlockSpec(memory_space=pltpu.VMEM),
        ]
        + ([] if base is None else [anywhere]),
        out_specs=anywhere,
        scratch_shapes=[
            pltpu.VMEM((share, 2, block, width), packed.dtype),
            pltpu.SemaphoreType.DMA((share,)),
        ],
        input_output_aliases={} if base is None else {2: 0},
        compiler_params=pltpu.CompilerParams(vmem_limit_bytes=VMEM_LIMIT),
        cost_estimate=pl.CostEstimate(flops=0, bytes_accessed=8 * packed.size, transcendentals=0),
    )(index.reshape(1), packed, *([] if base is None else [base]))


def split_channels(far, near, blocks, samples, slot_order, flags):
    share = CH // (far * near * blocks)
    inputs, block = samples.shape[0], slot_order.shape[1]
    axes = ("blk", "near", "far")
    me = lax.axis_index("blk").astype(jnp.int32)
    partner = lax.ppermute(slot_order, "blk", SWAP)
    orders = jnp.where(
        me == 0,
        jnp.concatenate([slot_order, partner]),
        jnp.concatenate([partner, slot_order]),
    )
    sent = channelize(samples, flags, far, near, blocks)
    arrived = lax.all_to_all(sent, axes, split_axis=0, concat_axis=0, tiled=True)
    pick = picks(orders, inputs, far, near, share)
    own, other = correlate(arrived, pick, me, share, block)
    received = lax.ppermute(other, "blk", SWAP)
    return place(received, 1 - me, blocks, place(own, me, blocks))


def gather_blocks(freq, samples, slot_order, flags):
    inputs = samples.shape[0]
    taps = jnp.asarray(prototype())
    table = jnp.asarray(twiddle().reshape(2 * CH, FRAME), dtype=jnp.bfloat16)
    good = (1 - flags).astype(jnp.float32)
    frames = samples.reshape(inputs, SPEC + TAPS - 1, FRAME)
    total = jnp.zeros((inputs, SPEC, FRAME), jnp.float32)
    for tap in range(TAPS):
        window = frames[:, tap : tap + SPEC, :].astype(jnp.float32)
        total = total + taps[tap][None, None, :] * window
    fir = total.astype(jnp.bfloat16)
    spectra = jnp.einsum("kn,isn->kis", table, fir, preferred_element_type=jnp.float32)
    squares = jnp.sum(spectra * spectra, axis=2)
    power = jnp.sum(squares.reshape(CH, 2, inputs), axis=1) / SPEC
    scale = good[None, :] / jnp.sqrt(power + 1e-05)
    quantized = (spectra * jnp.repeat(scale, 2, axis=0)[:, :, None]).astype(jnp.bfloat16)
    arrived = lax.all_to_all(quantized, ("far", "near"), split_axis=0, concat_axis=1, tiled=True)
    share = CH // freq
    block = slot_order.shape[1]
    own = jnp.take(arrived.reshape(share, 2, block, SPEC), slot_order[0], axis=2)
    piece = lax.all_gather(own, "blk", axis=2, tiled=True)
    dot = functools.partial(jnp.einsum, "cas,cbs->cab", preferred_element_type=jnp.float32)
    real = dot(own[:, 0], piece[:, 0]) + dot(own[:, 1], piece[:, 1])
    imag = dot(own[:, 1], piece[:, 0]) - dot(own[:, 0], piece[:, 1])
    return jnp.stack([real / SPEC, imag / SPEC], axis=1)


def solution(mesh):
    freq, blocks = mesh.shape["freq"], mesh.shape["blk"]
    far = math.gcd(freq, FAR)
    near = freq // far
    split = Mesh(mesh.devices.reshape(far, near, blocks), ("far", "near", "blk"))

    def body(samples, slot_order, flags):
        if blocks == 2 and CH == SUB * freq * blocks:
            return split_channels(far, near, blocks, samples, slot_order, flags)
        return gather_blocks(freq, samples, slot_order, flags)

    held = ("blk", "far", "near")
    in_specs = (P(held, None), P("blk", None), P(held))
    out_specs = P(("far", "near"), None, "blk", None)
    return jax.shard_map(body, mesh=split, in_specs=in_specs, out_specs=out_specs, check_vma=False)
```

```python
import functools
import math

import jax
import jax.numpy as jnp
import numpy as np
from jax import lax
from jax.experimental import pallas as pl
from jax.experimental.pallas import tpu as pltpu
from jax.sharding import Mesh
from jax.sharding import PartitionSpec as P

CH = 256
TAPS = 12
SPEC = 512
FRAME = 2 * CH
LANES = 128
SUB = 8
GROUP = 256
STEP = GROUP // SUB
STRIDE = STEP + 1
FAR = 4
SWAP = [(0, 1), (1, 0)]
VMEM_LIMIT = 40 * 1024 * 1024


def prototype():
    count = TAPS * FRAME
    index = np.arange(count, dtype=np.float64)
    shifted = (index + 0.5) / FRAME - TAPS / 2.0
    window = 0.5 - 0.5 * np.cos(2.0 * math.pi * (index + 0.5) / count)
    return (np.sinc(shifted) * window).astype(np.float32).reshape(TAPS, FRAME)


def twiddle():
    chan = np.arange(CH, dtype=np.int64)[:, None]
    point = np.arange(FRAME, dtype=np.int64)[None, :]
    phase = (chan * point % FRAME).astype(np.float64) * (2.0 * math.pi / FRAME)
    return np.stack([np.cos(phase), -np.sin(phase)], axis=1).astype(np.float32)


def channelize_kernel(
    flags_hbm,
    x_hbm,
    taps_hbm,
    table_hbm,
    out_hbm,
    flags,
    taps_all,
    table,
    held,
    wide,
    fir,
    spectra,
    result,
    load_sems,
    sems,
):
    inputs = held.shape[0]
    frames = SPEC + TAPS - 1
    groups = SPEC // GROUP
    pieces = sems.shape[1]
    rows = FRAME // pieces
    last = lax.broadcasted_iota(jnp.int32, (SUB, LANES), 0) == SUB - 1
    edges = [0] + [g * GROUP + TAPS - 1 for g in range(1, groups)] + [frames]

    def load(source, target, n):
        copy = pltpu.make_async_copy(source, target, load_sems.at[n])
        copy.start()
        return copy

    def span(g):
        return slice(None), pl.ds(edges[g] * FRAME, (edges[g + 1] - edges[g]) * FRAME)

    loads = [load(x_hbm.at[span(g)], held.at[span(g)], g) for g in range(groups)]
    load_taps = load(taps_hbm, taps_all, groups)
    load_table = load(table_hbm, table, groups + 1)
    load_flags = load(flags_hbm, flags, groups + 2)

    def convert(g):
        for f in range(edges[g], edges[g + 1]):
            for j in range(FRAME // LANES):
                tile = held[:, pl.ds(f * FRAME + j * LANES, LANES)]
                wide[j, pl.ds(inputs * f, inputs), :] = tile.astype(jnp.float32)

    def filter_group(g, i, j):
        cols = pl.ds(j * LANES, LANES)
        taps = [jnp.broadcast_to(taps_all[pl.ds(t, 1), cols], (SUB, LANES)) for t in range(TAPS)]

        def take(b):
            first = inputs * (g * GROUP + b) + i
            return wide[j, pl.ds(first, SUB, stride=inputs * STRIDE), :]

        def total(window):
            out = taps[0] * window[0]
            for t in range(1, TAPS):
                out = out + taps[t] * window[t]
            return out

        extra = total([take(STEP + t) for t in range(TAPS)])
        window = [take(b) for b in range(TAPS - 1)]
        pair = []
        for b in range(STEP):
            window.append(take(b + TAPS - 1))
            row = total(window[b:])
            past = b - (STEP - SUB + 1)
            if past >= 0:
                row = jnp.where(last, pltpu.roll(extra, SUB - 1 - past, 0), row)
            pair.append(row)
            if len(pair) == 2:
                both = jnp.concatenate(pair, axis=0).astype(jnp.bfloat16)
                fir[i, pl.ds(g * GROUP + (b - 1) * SUB, 2 * SUB), cols] = both
                pair = []

    def transform(g, i):
        part = pl.ds(g * GROUP, GROUP)
        spectra[i, :, part] = lax.dot_general(
            table[...],
            fir[i, part, :],
            (((1,), (1,)), ((), ())),
            preferred_element_type=jnp.float32,
        )

    def normalise(i, piece):
        good = (1 - flags[i]).astype(jnp.float32)
        pairs = spectra[i, pl.ds(piece * rows, rows), :]
        pairs = pairs.reshape(rows // (2 * SUB), 2, SUB, SPEC)
        squares = jnp.sum(pairs * pairs, axis=1)
        power = jnp.sum(squares, axis=2, keepdims=True) / SPEC
        scale = good / jnp.sqrt(power + 1e-05)
        scaled = (pairs * scale[:, None]).astype(jnp.bfloat16)
        result[pl.ds(piece * rows, rows), pl.ds(i * SPEC, SPEC)] = scaled.reshape(rows, SPEC)

    def store(i, piece):
        place = (pl.ds(piece * rows, rows), pl.ds(i * SPEC, SPEC))
        copy = pltpu.make_async_copy(result.at[place], out_hbm.at[place], sems.at[i, piece])
        copy.start()
        return copy

    load_taps.wait()
    for g in range(groups):
        loads[g].wait()
        if g == 1:
            load_table.wait()
            load_flags.wait()
        for i in range(inputs):
            if g > 0:
                transform(g - 1, i)
        convert(g)
        for i in range(inputs):
            for j in range(FRAME // LANES):
                filter_group(g, i, j)
    transform(groups - 1, 0)
    copies = []
    for i in range(inputs):
        if i + 1 < inputs:
            transform(groups - 1, i + 1)
        for piece in range(pieces):
            normalise(i, piece)
            copies.append(store(i, piece))
    for copy in copies:
        copy.wait()


def channelize(samples, flags, far, near, blocks):
    inputs = samples.shape[0]
    table = twiddle().reshape(far, near, blocks, SUB, 2, FRAME).transpose(2, 1, 0, 4, 3, 5)
    table = jnp.asarray(table.reshape(FRAME, FRAME), dtype=jnp.bfloat16)
    taps = jnp.asarray(prototype())
    hbm = pl.BlockSpec(memory_space=pltpu.HBM)
    return pl.pallas_call(
        channelize_kernel,
        out_shape=jax.ShapeDtypeStruct((FRAME, inputs * SPEC), jnp.bfloat16),
        in_specs=[hbm] * 4,
        out_specs=hbm,
        scratch_shapes=[
            pltpu.SMEM(flags.shape, flags.dtype),
            pltpu.VMEM(taps.shape, taps.dtype),
            pltpu.VMEM(table.shape, table.dtype),
            pltpu.VMEM(samples.shape, samples.dtype),
            pltpu.VMEM((FRAME // LANES, inputs * (SPEC + 24), LANES), jnp.float32),
            pltpu.VMEM((inputs, SPEC, FRAME), jnp.bfloat16),
            pltpu.VMEM((inputs, FRAME, SPEC), jnp.float32),
            pltpu.VMEM((FRAME, inputs * SPEC), jnp.bfloat16),
            pltpu.SemaphoreType.DMA((SPEC // GROUP + 3,)),
            pltpu.SemaphoreType.DMA((inputs, 8)),
        ],
        cost_estimate=pl.CostEstimate(
            flops=2 * inputs * SPEC * FRAME * (FRAME + TAPS),
            bytes_accessed=4 * inputs * SPEC * FRAME,
            transcendentals=0,
        ),
    )(flags, samples, taps, table)


def correlate_kernel(pick_ref, arrived_ref, own_ref, other_ref, slots):
    share, block, _ = own_ref.shape
    blocks = pick_ref.shape[0]
    width = blocks * block
    held = arrived_ref.shape[0] // blocks
    first = lax.axis_index("blk") == 0
    lane = lax.broadcasted_iota(jnp.int32, (width, 2 * width), 1)
    sign = jnp.where(lane < width, 1.0 / SPEC, -1.0 / SPEC)
    for n in range(blocks):
        rows = pl.ds(n * held, held)
        stacked = jnp.concatenate(
            [
                arrived_ref[rows, pl.ds(i * SPEC, SPEC)]
                for i in range(arrived_ref.shape[1] // SPEC)
            ],
            axis=0,
        )
        slots[n] = jnp.dot(
            pick_ref[n], stacked, preferred_element_type=jnp.float32
        ).astype(jnp.bfloat16)
    for k in range(share):
        pair = jnp.concatenate(
            [
                slots[n, pl.ds((2 * k + p) * block, block), :]
                for p in range(2)
                for n in range(blocks)
            ],
            axis=0,
        )
        gram = lax.dot_general(
            pair, pair, (((1,), (1,)), ((), ())), preferred_element_type=jnp.float32
        )
        part = gram[:width] * sign + pltpu.roll(gram[width:], width, 1) / SPEC
        own_ref[k] = jnp.where(first, part[:block], part[block:])
        other_ref[k] = jnp.where(first, part[block:], part[:block])


def picks(orders, inputs, far, near, share):
    blocks, block = orders.shape
    device, held = orders // inputs, orders % inputs
    place = (device % near) * far + device // near
    start = ((held * far * near + place) * 2 * share)[:, None, None, :]
    chan = jnp.arange(share, dtype=jnp.int32)[:, None, None]
    part = jnp.arange(2, dtype=jnp.int32)[:, None]
    target = (start + part * share + chan).reshape(blocks, share * 2 * block, 1)
    column = lax.broadcasted_iota(jnp.int32, (1, 1, inputs * far * near * 2 * share), 2)
    return (column == target).astype(jnp.bfloat16)


def correlate(arrived, pick, share, block):
    blocks = pick.shape[0]
    vmem = pl.BlockSpec(memory_space=pltpu.VMEM)
    tile = jax.ShapeDtypeStruct((share, block, 2 * blocks * block), jnp.float32)
    return pl.pallas_call(
        correlate_kernel,
        out_shape=(tile, tile),
        in_specs=[vmem, vmem],
        out_specs=(vmem, vmem),
        scratch_shapes=[pltpu.VMEM((blocks, share * 2 * block, SPEC), jnp.bfloat16)],
        compiler_params=pltpu.CompilerParams(vmem_limit_bytes=VMEM_LIMIT),
        cost_estimate=pl.CostEstimate(
            flops=2 * pick.size * SPEC, bytes_accessed=4 * arrived.size, transcendentals=0
        ),
    )(pick, arrived)


def place_kernel(packed_ref, *refs, own):
    out_ref, parts, sems = refs[-3:]
    share, _, _, width = parts.shape
    me = lax.axis_index("blk")
    start = (me if own else 1 - me) * share
    copies = []
    for k in range(share):
        parts[k, 0] = packed_ref[k, :, :width]
        parts[k, 1] = packed_ref[k, :, width:]
        copies.append(pltpu.make_async_copy(parts.at[k], out_ref.at[start + k], sems.at[k]))
        copies[-1].start()
    for copy in copies:
        copy.wait()


def place(packed, blocks, base=None):
    share, block, lanes = packed.shape
    width = lanes // 2
    anywhere = pl.BlockSpec(memory_space=pl.ANY)
    return pl.pallas_call(
        functools.partial(place_kernel, own=base is None),
        out_shape=jax.ShapeDtypeStruct((blocks * share, 2, block, width), packed.dtype),
        in_specs=[pl.BlockSpec(memory_space=pltpu.VMEM)] + ([] if base is None else [anywhere]),
        out_specs=anywhere,
        scratch_shapes=[
            pltpu.VMEM((share, 2, block, width), packed.dtype),
            pltpu.SemaphoreType.DMA((share,)),
        ],
        input_output_aliases={} if base is None else {1: 0},
        compiler_params=pltpu.CompilerParams(vmem_limit_bytes=VMEM_LIMIT),
        cost_estimate=pl.CostEstimate(flops=0, bytes_accessed=8 * packed.size, transcendentals=0),
    )(packed, *([] if base is None else [base]))


def split_channels(far, near, blocks, samples, slot_order, flags):
    share = CH // (far * near * blocks)
    inputs, block = samples.shape[0], slot_order.shape[1]
    axes = ("blk", "near", "far")
    me = lax.axis_index("blk").astype(jnp.int32)
    partner = lax.ppermute(slot_order, "blk", SWAP)
    orders = jnp.where(
        me == 0,
        jnp.concatenate([slot_order, partner]),
        jnp.concatenate([partner, slot_order]),
    )
    sent = channelize(samples, flags, far, near, blocks)
    arrived = lax.all_to_all(sent, axes, split_axis=0, concat_axis=0, tiled=True)
    pick = picks(orders, inputs, far, near, share)
    own, other = correlate(arrived, pick, share, block)
    received = lax.ppermute(other, "blk", SWAP)
    return place(received, blocks, place(own, blocks))


def gather_blocks(freq, samples, slot_order, flags):
    inputs = samples.shape[0]
    taps = jnp.asarray(prototype())
    table = jnp.asarray(twiddle().reshape(2 * CH, FRAME), dtype=jnp.bfloat16)
    good = (1 - flags).astype(jnp.float32)
    frames = samples.reshape(inputs, SPEC + TAPS - 1, FRAME)
    total = jnp.zeros((inputs, SPEC, FRAME), jnp.float32)
    for tap in range(TAPS):
        window = frames[:, tap : tap + SPEC, :].astype(jnp.float32)
        total = total + taps[tap][None, None, :] * window
    fir = total.astype(jnp.bfloat16)
    spectra = jnp.einsum("kn,isn->kis", table, fir, preferred_element_type=jnp.float32)
    squares = jnp.sum(spectra * spectra, axis=2)
    power = jnp.sum(squares.reshape(CH, 2, inputs), axis=1) / SPEC
    scale = good[None, :] / jnp.sqrt(power + 1e-05)
    quantized = (spectra * jnp.repeat(scale, 2, axis=0)[:, :, None]).astype(jnp.bfloat16)
    arrived = lax.all_to_all(quantized, ("far", "near"), split_axis=0, concat_axis=1, tiled=True)
    share = CH // freq
    block = slot_order.shape[1]
    own = jnp.take(arrived.reshape(share, 2, block, SPEC), slot_order[0], axis=2)
    piece = lax.all_gather(own, "blk", axis=2, tiled=True)
    dot = functools.partial(jnp.einsum, "cas,cbs->cab", preferred_element_type=jnp.float32)
    real = dot(own[:, 0], piece[:, 0]) + dot(own[:, 1], piece[:, 1])
    imag = dot(own[:, 1], piece[:, 0]) - dot(own[:, 0], piece[:, 1])
    return jnp.stack([real / SPEC, imag / SPEC], axis=1)


def solution(mesh):
    freq, blocks = mesh.shape["freq"], mesh.shape["blk"]
    far = math.gcd(freq, FAR)
    near = freq // far
    split = Mesh(mesh.devices.reshape(far, near, blocks), ("far", "near", "blk"))

    def body(samples, slot_order, flags):
        if blocks == 2 and CH == SUB * freq * blocks:
            return split_channels(far, near, blocks, samples, slot_order, flags)
        return gather_blocks(freq, samples, slot_order, flags)

    held = ("blk", "far", "near")
    in_specs = (P(held, None), P("blk", None), P(held))
    out_specs = P(("far", "near"), None, "blk", None)
    return jax.shard_map(body, mesh=split, in_specs=in_specs, out_specs=out_specs, check_vma=False)
```

```python
import functools
import math

import jax
import jax.numpy as jnp
import numpy as np
from jax import lax
from jax.experimental import pallas as pl
from jax.experimental.pallas import tpu as pltpu
from jax.experimental.layout import Layout, with_layout_constraint
from jax.sharding import Mesh
from jax.sharding import PartitionSpec as P

CH = 256
TAPS = 12
SPEC = 512
FRAME = 2 * CH
LANES = 128
SUB = 8
GROUP = 256
STEP = GROUP // SUB
STRIDE = STEP + 1
PITCH = SPEC + 25
FAR = 4
SWAP = [(0, 1), (1, 0)]
VMEM_LIMIT = 40 * 1024 * 1024


def prototype():
    count = TAPS * FRAME
    index = np.arange(count, dtype=np.float64)
    shifted = (index + 0.5) / FRAME - TAPS / 2.0
    window = 0.5 - 0.5 * np.cos(2.0 * math.pi * (index + 0.5) / count)
    return (np.sinc(shifted) * window).astype(np.float32).reshape(TAPS, FRAME)


def twiddle():
    chan = np.arange(CH, dtype=np.int64)[:, None]
    point = np.arange(FRAME, dtype=np.int64)[None, :]
    phase = (chan * point % FRAME).astype(np.float64) * (2.0 * math.pi / FRAME)
    return np.stack([np.cos(phase), -np.sin(phase)], axis=1).astype(np.float32)


def channelize_kernel(
    flags_hbm,
    x_hbm,
    taps_hbm,
    table_hbm,
    out_hbm,
    flags,
    taps_all,
    table,
    held,
    wide,
    fir,
    spectra,
    result,
    load_sems,
    sems,
):
    inputs = fir.shape[0]
    frames = SPEC + TAPS - 1
    spread = inputs * FRAME // LANES
    groups = SPEC // GROUP
    pieces = sems.shape[1]
    rows = FRAME // pieces
    last = lax.broadcasted_iota(jnp.int32, (SUB, LANES), 0) == SUB - 1
    edges = [0, GROUP // 2] + [g * GROUP + TAPS for g in range(1, groups)] + [frames]

    def load(source, target, n):
        copy = pltpu.make_async_copy(source, target, load_sems.at[n])
        copy.start()
        return copy

    def span(n):
        return pl.ds(edges[n] * spread, (edges[n + 1] - edges[n]) * spread)

    chunks = len(edges) - 1
    loads = [load(x_hbm.at[span(n)], held.at[span(n)], n) for n in range(chunks)]
    load_taps = load(taps_hbm, taps_all, chunks)
    load_table = load(table_hbm, table, chunks + 1)
    load_flags = load(flags_hbm, flags, chunks + 2)

    def convert(n):
        for f in range(edges[n], edges[n + 1], 2):
            count = min(2, frames - f)
            tile = held[pl.ds(f * spread, count * spread), :].astype(jnp.float32)
            for c in range(count):
                part = tile[c * spread : (c + 1) * spread]
                wide[pl.ds(f + c, spread, stride=PITCH), :] = part

    def filter_group(g, i, j):
        cols = pl.ds(j * LANES, LANES)
        taps = [jnp.broadcast_to(taps_all[pl.ds(t, 1), cols], (SUB, LANES)) for t in range(TAPS)]

        def take(b):
            first = (inputs * j + i) * PITCH + g * GROUP + b
            return wide[pl.ds(first, SUB, stride=STRIDE), :]

        def total(window):
            out = taps[0] * window[0]
            for t in range(1, TAPS):
                out = out + taps[t] * window[t]
            return out

        extra = total([take(STEP + t) for t in range(TAPS)])
        window = [take(b) for b in range(TAPS - 1)]
        pair = []
        for b in range(STEP):
            window.append(take(b + TAPS - 1))
            row = total(window[b:])
            past = b - (STEP - SUB + 1)
            if past >= 0:
                row = jnp.where(last, pltpu.roll(extra, SUB - 1 - past, 0), row)
            pair.append(row)
            if len(pair) == 2:
                both = jnp.concatenate(pair, axis=0).astype(jnp.bfloat16)
                fir[i, pl.ds(g * GROUP + (b - 1) * SUB, 2 * SUB), cols] = both
                pair = []

    def transform(g, i):
        part = pl.ds(g * GROUP, GROUP)
        spectra[i, :, part] = lax.dot_general(
            table[...],
            fir[i, part, :],
            (((1,), (1,)), ((), ())),
            preferred_element_type=jnp.float32,
        )

    def normalise(i, piece):
        good = (1 - flags[i]).astype(jnp.float32)
        pairs = spectra[i, pl.ds(piece * rows, rows), :]
        pairs = pairs.reshape(rows // (2 * SUB), 2, SUB, SPEC)
        squares = jnp.sum(pairs * pairs, axis=1)
        power = jnp.sum(squares, axis=2, keepdims=True) / SPEC
        scale = good / jnp.sqrt(power + 1e-05)
        scaled = (pairs * scale[:, None]).astype(jnp.bfloat16)
        result[pl.ds(piece * rows, rows), pl.ds(i * SPEC, SPEC)] = scaled.reshape(rows, SPEC)

    def store(i, piece):
        place = (pl.ds(piece * rows, rows), pl.ds(i * SPEC, SPEC))
        copy = pltpu.make_async_copy(result.at[place], out_hbm.at[place], sems.at[i, piece])
        copy.start()
        return copy

    loads[0].wait()
    convert(0)
    load_taps.wait()
    for g in range(groups):
        loads[g + 1].wait()
        if g == 1:
            load_table.wait()
            load_flags.wait()
        for i in range(inputs):
            if g > 0:
                transform(g - 1, i)
        convert(g + 1)
        for i in range(inputs):
            for j in range(FRAME // LANES):
                filter_group(g, i, j)
    transform(groups - 1, 0)
    copies = []
    for i in range(inputs):
        if i + 1 < inputs:
            transform(groups - 1, i + 1)
        for piece in range(pieces):
            normalise(i, piece)
            copies.append(store(i, piece))
    for copy in copies:
        copy.wait()


def channelize(samples, flags, far, near, blocks):
    inputs = samples.shape[0]
    tiles = samples.reshape(inputs, -1, LANES)
    tiles = with_layout_constraint(tiles, Layout(major_to_minor=(1, 0, 2)))
    tiles = tiles.transpose(1, 0, 2)
    tiles = tiles.reshape(-1, LANES)
    table = twiddle().reshape(far, near, blocks, SUB, 2, FRAME).transpose(2, 1, 0, 4, 3, 5)
    table = jnp.asarray(table.reshape(FRAME, FRAME), dtype=jnp.bfloat16)
    taps = jnp.asarray(prototype())
    hbm = pl.BlockSpec(memory_space=pltpu.HBM)
    return pl.pallas_call(
        channelize_kernel,
        out_shape=jax.ShapeDtypeStruct((FRAME, inputs * SPEC), jnp.bfloat16),
        in_specs=[hbm] * 4,
        out_specs=hbm,
        scratch_shapes=[
            pltpu.SMEM(flags.shape, flags.dtype),
            pltpu.VMEM(taps.shape, taps.dtype),
            pltpu.VMEM(table.shape, table.dtype),
            pltpu.VMEM(tiles.shape, tiles.dtype),
            pltpu.VMEM((inputs * FRAME // LANES * PITCH, LANES), jnp.float32),
            pltpu.VMEM((inputs, SPEC, FRAME), jnp.bfloat16),
            pltpu.VMEM((inputs, FRAME, SPEC), jnp.float32),
            pltpu.VMEM((FRAME, inputs * SPEC), jnp.bfloat16),
            pltpu.SemaphoreType.DMA((SPEC // GROUP + 4,)),
            pltpu.SemaphoreType.DMA((inputs, 8)),
        ],
        cost_estimate=pl.CostEstimate(
            flops=2 * inputs * SPEC * FRAME * (FRAME + TAPS),
            bytes_accessed=4 * inputs * SPEC * FRAME,
            transcendentals=0,
        ),
    )(flags, tiles, taps, table)


def correlate_kernel(pick_ref, arrived_ref, own_ref, other_ref, slots):
    share, block, _ = own_ref.shape
    blocks = pick_ref.shape[0]
    width = blocks * block
    held = arrived_ref.shape[0] // blocks
    first = lax.axis_index("blk") == 0
    lane = lax.broadcasted_iota(jnp.int32, (width, 2 * width), 1)
    sign = jnp.where(lane < width, 1.0 / SPEC, -1.0 / SPEC)
    for n in range(blocks):
        rows = pl.ds(n * held, held)
        stacked = jnp.concatenate(
            [
                arrived_ref[rows, pl.ds(i * SPEC, SPEC)]
                for i in range(arrived_ref.shape[1] // SPEC)
            ],
            axis=0,
        )
        slots[n] = jnp.dot(
            pick_ref[n], stacked, preferred_element_type=jnp.float32
        ).astype(jnp.bfloat16)
    for k in range(share):
        pair = jnp.concatenate(
            [
                slots[n, pl.ds((2 * k + p) * block, block), :]
                for p in range(2)
                for n in range(blocks)
            ],
            axis=0,
        )
        gram = lax.dot_general(
            pair, pair, (((1,), (1,)), ((), ())), preferred_element_type=jnp.float32
        )
        part = gram[:width] * sign + pltpu.roll(gram[width:], width, 1) / SPEC
        own_ref[k] = jnp.where(first, part[:block], part[block:])
        other_ref[k] = jnp.where(first, part[block:], part[:block])


def picks(orders, inputs, far, near, share):
    blocks, block = orders.shape
    device, held = orders // inputs, orders % inputs
    place = (device % near) * far + device // near
    start = ((held * far * near + place) * 2 * share)[:, None, None, :]
    chan = jnp.arange(share, dtype=jnp.int32)[:, None, None]
    part = jnp.arange(2, dtype=jnp.int32)[:, None]
    target = (start + part * share + chan).reshape(blocks, share * 2 * block, 1)
    column = lax.broadcasted_iota(jnp.int32, (1, 1, inputs * far * near * 2 * share), 2)
    return (column == target).astype(jnp.bfloat16)


def correlate(arrived, pick, share, block):
    blocks = pick.shape[0]
    vmem = pl.BlockSpec(memory_space=pltpu.VMEM)
    tile = jax.ShapeDtypeStruct((share, block, 2 * blocks * block), jnp.float32)
    return pl.pallas_call(
        correlate_kernel,
        out_shape=(tile, tile),
        in_specs=[vmem, vmem],
        out_specs=(vmem, vmem),
        scratch_shapes=[pltpu.VMEM((blocks, share * 2 * block, SPEC), jnp.bfloat16)],
        compiler_params=pltpu.CompilerParams(vmem_limit_bytes=VMEM_LIMIT),
        cost_estimate=pl.CostEstimate(
            flops=2 * pick.size * SPEC, bytes_accessed=4 * arrived.size, transcendentals=0
        ),
    )(pick, arrived)


def place_kernel(packed_ref, *refs, own):
    out_ref, parts, sems = refs[-3:]
    share, _, _, width = parts.shape
    me = lax.axis_index("blk")
    start = (me if own else 1 - me) * share
    copies = []
    count = share // sems.shape[0]
    for n in range(sems.shape[0]):
        for k in range(n * count, (n + 1) * count):
            parts[k, 0] = packed_ref[k, :, :width]
            parts[k, 1] = packed_ref[k, :, width:]
        target = out_ref.at[pl.ds(start + n * count, count)]
        copies.append(pltpu.make_async_copy(parts.at[pl.ds(n * count, count)], target, sems.at[n]))
        copies[-1].start()
    for copy in copies:
        copy.wait()


def place(packed, blocks, base=None):
    share, block, lanes = packed.shape
    width = lanes // 2
    anywhere = pl.BlockSpec(memory_space=pl.ANY)
    return pl.pallas_call(
        functools.partial(place_kernel, own=base is None),
        out_shape=jax.ShapeDtypeStruct((blocks * share, 2, block, width), packed.dtype),
        in_specs=[pl.BlockSpec(memory_space=pltpu.VMEM)] + ([] if base is None else [anywhere]),
        out_specs=anywhere,
        scratch_shapes=[
            pltpu.VMEM((share, 2, block, width), packed.dtype),
            pltpu.SemaphoreType.DMA((2,)),
        ],
        input_output_aliases={} if base is None else {1: 0},
        compiler_params=pltpu.CompilerParams(vmem_limit_bytes=VMEM_LIMIT),
        cost_estimate=pl.CostEstimate(flops=0, bytes_accessed=8 * packed.size, transcendentals=0),
    )(packed, *([] if base is None else [base]))


def split_channels(far, near, blocks, samples, slot_order, flags):
    share = CH // (far * near * blocks)
    inputs, block = samples.shape[0], slot_order.shape[1]
    axes = ("blk", "near", "far")
    me = lax.axis_index("blk").astype(jnp.int32)
    partner = lax.ppermute(slot_order, "blk", SWAP)
    orders = jnp.where(
        me == 0,
        jnp.concatenate([slot_order, partner]),
        jnp.concatenate([partner, slot_order]),
    )
    sent = channelize(samples, flags, far, near, blocks)
    arrived = lax.all_to_all(sent, axes, split_axis=0, concat_axis=0, tiled=True)
    pick = picks(orders, inputs, far, near, share)
    own, other = correlate(arrived, pick, share, block)
    received = lax.ppermute(other, "blk", SWAP)
    return place(received, blocks, place(own, blocks))


def gather_blocks(freq, samples, slot_order, flags):
    inputs = samples.shape[0]
    taps = jnp.asarray(prototype())
    table = jnp.asarray(twiddle().reshape(2 * CH, FRAME), dtype=jnp.bfloat16)
    good = (1 - flags).astype(jnp.float32)
    frames = samples.reshape(inputs, SPEC + TAPS - 1, FRAME)
    total = jnp.zeros((inputs, SPEC, FRAME), jnp.float32)
    for tap in range(TAPS):
        window = frames[:, tap : tap + SPEC, :].astype(jnp.float32)
        total = total + taps[tap][None, None, :] * window
    fir = total.astype(jnp.bfloat16)
    spectra = jnp.einsum("kn,isn->kis", table, fir, preferred_element_type=jnp.float32)
    squares = jnp.sum(spectra * spectra, axis=2)
    power = jnp.sum(squares.reshape(CH, 2, inputs), axis=1) / SPEC
    scale = good[None, :] / jnp.sqrt(power + 1e-05)
    quantized = (spectra * jnp.repeat(scale, 2, axis=0)[:, :, None]).astype(jnp.bfloat16)
    arrived = lax.all_to_all(quantized, ("far", "near"), split_axis=0, concat_axis=1, tiled=True)
    share = CH // freq
    block = slot_order.shape[1]
    own = jnp.take(arrived.reshape(share, 2, block, SPEC), slot_order[0], axis=2)
    piece = lax.all_gather(own, "blk", axis=2, tiled=True)
    dot = functools.partial(jnp.einsum, "cas,cbs->cab", preferred_element_type=jnp.float32)
    real = dot(own[:, 0], piece[:, 0]) + dot(own[:, 1], piece[:, 1])
    imag = dot(own[:, 1], piece[:, 0]) - dot(own[:, 0], piece[:, 1])
    return jnp.stack([real / SPEC, imag / SPEC], axis=1)


def solution(mesh):
    freq, blocks = mesh.shape["freq"], mesh.shape["blk"]
    far = math.gcd(freq, FAR)
    near = freq // far
    split = Mesh(mesh.devices.reshape(far, near, blocks), ("far", "near", "blk"))

    def body(samples, slot_order, flags):
        if blocks == 2 and CH == SUB * freq * blocks:
            return split_channels(far, near, blocks, samples, slot_order, flags)
        return gather_blocks(freq, samples, slot_order, flags)

    held = ("blk", "far", "near")
    in_specs = (P(held, None), P("blk", None), P(held))
    out_specs = P(("far", "near"), None, "blk", None)
    return jax.shard_map(body, mesh=split, in_specs=in_specs, out_specs=out_specs, check_vma=False)
```

```python
import functools
import math

import jax
import jax.numpy as jnp
import numpy as np
from jax import lax
from jax.experimental import pallas as pl
from jax.experimental.pallas import tpu as pltpu
from jax.experimental.layout import Layout, with_layout_constraint
from jax.sharding import Mesh
from jax.sharding import PartitionSpec as P

CH = 256
TAPS = 12
SPEC = 512
FRAME = 2 * CH
LANES = 128
SUB = 8
GROUP = 256
STEP = GROUP // SUB
STRIDE = STEP + 1
PITCH = SPEC + 25
FAR = 4
SWAP = [(0, 1), (1, 0)]
VMEM_LIMIT = 40 * 1024 * 1024


def prototype():
    count = TAPS * FRAME
    index = np.arange(count, dtype=np.float64)
    shifted = (index + 0.5) / FRAME - TAPS / 2.0
    window = 0.5 - 0.5 * np.cos(2.0 * math.pi * (index + 0.5) / count)
    return (np.sinc(shifted) * window).astype(np.float32).reshape(TAPS, FRAME)


def twiddle():
    chan = np.arange(CH, dtype=np.int64)[:, None]
    point = np.arange(FRAME, dtype=np.int64)[None, :]
    phase = (chan * point % FRAME).astype(np.float64) * (2.0 * math.pi / FRAME)
    return np.stack([np.cos(phase), -np.sin(phase)], axis=1).astype(np.float32)


def channelize_kernel(
    flags_hbm,
    x_hbm,
    taps_hbm,
    table_hbm,
    out_hbm,
    flags,
    taps_all,
    table,
    held,
    wide,
    fir,
    spectra,
    result,
    load_sems,
    sems,
):
    inputs = fir.shape[0]
    frames = SPEC + TAPS - 1
    spread = inputs * FRAME // LANES
    groups = SPEC // GROUP
    pieces = sems.shape[0]
    rows = FRAME // pieces
    last = lax.broadcasted_iota(jnp.int32, (SUB, LANES), 0) == SUB - 1
    edges = [0, GROUP // 2] + [g * GROUP + TAPS for g in range(1, groups)] + [frames]

    def load(source, target, n):
        copy = pltpu.make_async_copy(source, target, load_sems.at[n])
        copy.start()
        return copy

    def span(n):
        return pl.ds(edges[n] * spread, (edges[n + 1] - edges[n]) * spread)

    chunks = len(edges) - 1
    loads = [load(x_hbm.at[span(n)], held.at[span(n)], n) for n in range(chunks)]
    load_taps = load(taps_hbm, taps_all, chunks)
    load_flags = load(flags_hbm, flags, chunks + 2)

    def convert(n):
        for f in range(edges[n], edges[n + 1], 2):
            count = min(2, frames - f)
            tile = held[pl.ds(f * spread, count * spread), :].astype(jnp.float32)
            for c in range(count):
                part = tile[c * spread : (c + 1) * spread]
                wide[pl.ds(f + c, spread, stride=PITCH), :] = part

    def filter_group(g, i, j):
        cols = pl.ds(j * LANES, LANES)
        taps = [jnp.broadcast_to(taps_all[pl.ds(t, 1), cols], (SUB, LANES)) for t in range(TAPS)]

        def take(b):
            first = (inputs * j + i) * PITCH + g * GROUP + b
            return wide[pl.ds(first, SUB, stride=STRIDE), :]

        def total(window):
            out = taps[0] * window[0]
            for t in range(1, TAPS):
                out = out + taps[t] * window[t]
            return out

        extra = total([take(STEP + t) for t in range(TAPS)])
        window = [take(b) for b in range(TAPS - 1)]
        pair = []
        for b in range(STEP):
            window.append(take(b + TAPS - 1))
            row = total(window[b:])
            past = b - (STEP - SUB + 1)
            if past >= 0:
                row = jnp.where(last, pltpu.roll(extra, SUB - 1 - past, 0), row)
            pair.append(row)
            if len(pair) == 2:
                both = jnp.concatenate(pair, axis=0).astype(jnp.bfloat16)
                fir[i, pl.ds(g * GROUP + (b - 1) * SUB, 2 * SUB), cols] = both
                pair = []

    def transform(g, i):
        part = pl.ds(g * GROUP, GROUP)
        spectra[i, :, part] = lax.dot_general(
            table[...],
            fir[i, part, :],
            (((1,), (1,)), ((), ())),
            preferred_element_type=jnp.float32,
        )

    def scaled(i, piece):
        good = (1 - flags[i]).astype(jnp.float32)
        pairs = spectra[i, pl.ds(piece * rows, rows), :]
        pairs = pairs.reshape(rows // (2 * SUB), 2, SUB, SPEC)
        squares = jnp.sum(pairs * pairs, axis=1)
        power = jnp.sum(squares, axis=2, keepdims=True) / SPEC
        scale = good / jnp.sqrt(power + 1e-05)
        return pairs * scale[:, None]

    def pack(piece, parts):
        place = pl.ds(piece * rows, rows)
        for p in range(2):
            both = jnp.concatenate([part[:, p] for part in parts], axis=1)
            result[place, pl.ds(p * SPEC, SPEC)] = both.astype(jnp.bfloat16).reshape(rows, SPEC)
        copy = pltpu.make_async_copy(result.at[place], out_hbm.at[place], sems.at[piece])
        copy.start()
        return copy

    loads[0].wait()
    convert(0)
    load_taps.wait()
    loads[1].wait()
    load_table = load(table_hbm, table, chunks + 1)
    convert(1)
    for i in range(inputs):
        for j in range(FRAME // LANES):
            filter_group(0, i, j)
    loads[2].wait()
    load_table.wait()
    load_flags.wait()
    for i in range(inputs):
        transform(0, i)
    convert(2)
    for i in range(inputs):
        if i > 0:
            transform(1, i - 1)
        for j in range(FRAME // LANES):
            filter_group(1, i, j)
    transform(1, inputs - 1)
    for piece in range(pieces):
        part = scaled(0, piece)
        spectra[0, pl.ds(piece * rows, rows), :] = part.reshape(rows, SPEC)
    copies = []
    for piece in range(pieces):
        held_part = spectra[0, pl.ds(piece * rows, rows), :]
        held_part = held_part.reshape(rows // (2 * SUB), 2, SUB, SPEC)
        copies.append(pack(piece, [held_part, scaled(1, piece)]))
    for copy in copies:
        copy.wait()


def channelize(samples, flags, far, near, blocks):
    inputs = samples.shape[0]
    tiles = samples.reshape(inputs, -1, LANES)
    tiles = with_layout_constraint(tiles, Layout(major_to_minor=(1, 0, 2)))
    tiles = tiles.transpose(1, 0, 2)
    tiles = tiles.reshape(-1, LANES)
    table = twiddle().reshape(far, near, blocks, SUB, 2, FRAME).transpose(2, 1, 0, 4, 3, 5)
    table = jnp.asarray(table.reshape(FRAME, FRAME), dtype=jnp.bfloat16)
    taps = jnp.asarray(prototype())
    hbm = pl.BlockSpec(memory_space=pltpu.HBM)
    return pl.pallas_call(
        channelize_kernel,
        out_shape=jax.ShapeDtypeStruct((FRAME, inputs * SPEC), jnp.bfloat16),
        in_specs=[hbm] * 4,
        out_specs=hbm,
        scratch_shapes=[
            pltpu.SMEM(flags.shape, flags.dtype),
            pltpu.VMEM(taps.shape, taps.dtype),
            pltpu.VMEM(table.shape, table.dtype),
            pltpu.VMEM(tiles.shape, tiles.dtype),
            pltpu.VMEM((inputs * FRAME // LANES * PITCH, LANES), jnp.float32),
            pltpu.VMEM((inputs, SPEC, FRAME), jnp.bfloat16),
            pltpu.VMEM((inputs, FRAME, SPEC), jnp.float32),
            pltpu.VMEM((FRAME, inputs * SPEC), jnp.bfloat16),
            pltpu.SemaphoreType.DMA((SPEC // GROUP + 4,)),
            pltpu.SemaphoreType.DMA((8,)),
        ],
        cost_estimate=pl.CostEstimate(
            flops=2 * inputs * SPEC * FRAME * (FRAME + TAPS),
            bytes_accessed=4 * inputs * SPEC * FRAME,
            transcendentals=0,
        ),
    )(flags, tiles, taps, table)


def correlate_kernel(pick_ref, arrived_ref, own_ref, other_ref, slots):
    share, block, _ = own_ref.shape
    blocks = pick_ref.shape[0]
    width = blocks * block
    held = arrived_ref.shape[0] // blocks
    first = lax.axis_index("blk") == 0
    lane = lax.broadcasted_iota(jnp.int32, (width, 2 * width), 1)
    sign = jnp.where(lane < width, 1.0 / SPEC, -1.0 / SPEC)
    for n in range(blocks):
        rows = pl.ds(n * held, held)
        slots[n] = jnp.dot(
            pick_ref[n], arrived_ref[rows, :], preferred_element_type=jnp.float32
        ).astype(jnp.bfloat16)
    for k in range(share):
        pair = jnp.concatenate(
            [
                slots[n, pl.ds(k * block, block), pl.ds(p * SPEC, SPEC)]
                for p in range(2)
                for n in range(blocks)
            ],
            axis=0,
        )
        gram = lax.dot_general(
            pair, pair, (((1,), (1,)), ((), ())), preferred_element_type=jnp.float32
        )
        part = gram[:width] * sign + pltpu.roll(gram[width:], width, 1) / SPEC
        own_ref[k] = jnp.where(first, part[:block], part[block:])
        other_ref[k] = jnp.where(first, part[block:], part[:block])


def picks(orders, inputs, far, near, share):
    blocks, block = orders.shape
    device, held = orders // inputs, orders % inputs
    place = (device % near) * far + device // near
    start = ((place * inputs + held) * share)[:, None, :]
    chan = jnp.arange(share, dtype=jnp.int32)[:, None]
    target = (start + chan).reshape(blocks, share * block, 1)
    column = lax.broadcasted_iota(jnp.int32, (1, 1, far * near * inputs * share), 2)
    return (column == target).astype(jnp.bfloat16)


def correlate(arrived, pick, share, block):
    blocks = pick.shape[0]
    vmem = pl.BlockSpec(memory_space=pltpu.VMEM)
    tile = jax.ShapeDtypeStruct((share, block, 2 * blocks * block), jnp.float32)
    return pl.pallas_call(
        correlate_kernel,
        out_shape=(tile, tile),
        in_specs=[vmem, vmem],
        out_specs=(vmem, vmem),
        scratch_shapes=[pltpu.VMEM((blocks, share * block, 2 * SPEC), jnp.bfloat16)],
        compiler_params=pltpu.CompilerParams(vmem_limit_bytes=VMEM_LIMIT),
        cost_estimate=pl.CostEstimate(
            flops=4 * pick.size * SPEC, bytes_accessed=4 * arrived.size, transcendentals=0
        ),
    )(pick, arrived)


def place_kernel(packed_ref, *refs, own):
    out_ref, parts, sems = refs[-3:]
    share, _, _, width = parts.shape
    me = lax.axis_index("blk")
    start = (me if own else 1 - me) * share
    copies = []
    count = share // sems.shape[0]
    for n in range(sems.shape[0]):
        for k in range(n * count, (n + 1) * count):
            parts[k, 0] = packed_ref[k, :, :width]
            parts[k, 1] = packed_ref[k, :, width:]
        target = out_ref.at[pl.ds(start + n * count, count)]
        copies.append(pltpu.make_async_copy(parts.at[pl.ds(n * count, count)], target, sems.at[n]))
        copies[-1].start()
    for copy in copies:
        copy.wait()


def place(packed, blocks, base=None):
    share, block, lanes = packed.shape
    width = lanes // 2
    anywhere = pl.BlockSpec(memory_space=pl.ANY)
    return pl.pallas_call(
        functools.partial(place_kernel, own=base is None),
        out_shape=jax.ShapeDtypeStruct((blocks * share, 2, block, width), packed.dtype),
        in_specs=[pl.BlockSpec(memory_space=pltpu.VMEM)] + ([] if base is None else [anywhere]),
        out_specs=anywhere,
        scratch_shapes=[
            pltpu.VMEM((share, 2, block, width), packed.dtype),
            pltpu.SemaphoreType.DMA((2,)),
        ],
        input_output_aliases={} if base is None else {1: 0},
        compiler_params=pltpu.CompilerParams(vmem_limit_bytes=VMEM_LIMIT),
        cost_estimate=pl.CostEstimate(flops=0, bytes_accessed=8 * packed.size, transcendentals=0),
    )(packed, *([] if base is None else [base]))


def split_channels(far, near, blocks, samples, slot_order, flags):
    share = CH // (far * near * blocks)
    inputs, block = samples.shape[0], slot_order.shape[1]
    axes = ("blk", "near", "far")
    me = lax.axis_index("blk").astype(jnp.int32)
    partner = lax.ppermute(slot_order, "blk", SWAP)
    orders = jnp.where(
        me == 0,
        jnp.concatenate([slot_order, partner]),
        jnp.concatenate([partner, slot_order]),
    )
    sent = channelize(samples, flags, far, near, blocks)
    arrived = lax.all_to_all(sent, axes, split_axis=0, concat_axis=0, tiled=True)
    pick = picks(orders, inputs, far, near, share)
    own, other = correlate(arrived, pick, share, block)
    received = lax.ppermute(other, "blk", SWAP)
    return place(received, blocks, place(own, blocks))


def gather_blocks(freq, samples, slot_order, flags):
    inputs = samples.shape[0]
    taps = jnp.asarray(prototype())
    table = jnp.asarray(twiddle().reshape(2 * CH, FRAME), dtype=jnp.bfloat16)
    good = (1 - flags).astype(jnp.float32)
    frames = samples.reshape(inputs, SPEC + TAPS - 1, FRAME)
    total = jnp.zeros((inputs, SPEC, FRAME), jnp.float32)
    for tap in range(TAPS):
        window = frames[:, tap : tap + SPEC, :].astype(jnp.float32)
        total = total + taps[tap][None, None, :] * window
    fir = total.astype(jnp.bfloat16)
    spectra = jnp.einsum("kn,isn->kis", table, fir, preferred_element_type=jnp.float32)
    squares = jnp.sum(spectra * spectra, axis=2)
    power = jnp.sum(squares.reshape(CH, 2, inputs), axis=1) / SPEC
    scale = good[None, :] / jnp.sqrt(power + 1e-05)
    quantized = (spectra * jnp.repeat(scale, 2, axis=0)[:, :, None]).astype(jnp.bfloat16)
    arrived = lax.all_to_all(quantized, ("far", "near"), split_axis=0, concat_axis=1, tiled=True)
    share = CH // freq
    block = slot_order.shape[1]
    own = jnp.take(arrived.reshape(share, 2, block, SPEC), slot_order[0], axis=2)
    piece = lax.all_gather(own, "blk", axis=2, tiled=True)
    dot = functools.partial(jnp.einsum, "cas,cbs->cab", preferred_element_type=jnp.float32)
    real = dot(own[:, 0], piece[:, 0]) + dot(own[:, 1], piece[:, 1])
    imag = dot(own[:, 1], piece[:, 0]) - dot(own[:, 0], piece[:, 1])
    return jnp.stack([real / SPEC, imag / SPEC], axis=1)


def solution(mesh):
    freq, blocks = mesh.shape["freq"], mesh.shape["blk"]
    far = math.gcd(freq, FAR)
    near = freq // far
    split = Mesh(mesh.devices.reshape(far, near, blocks), ("far", "near", "blk"))

    def body(samples, slot_order, flags):
        if blocks == 2 and CH == SUB * freq * blocks:
            return split_channels(far, near, blocks, samples, slot_order, flags)
        return gather_blocks(freq, samples, slot_order, flags)

    held = ("blk", "far", "near")
    in_specs = (P(held, None), P("blk", None), P(held))
    out_specs = P(("far", "near"), None, "blk", None)
    return jax.shard_map(body, mesh=split, in_specs=in_specs, out_specs=out_specs, check_vma=False)
```

```python
import functools
import math

import jax
import jax.numpy as jnp
import numpy as np
from jax import lax
from jax.experimental import pallas as pl
from jax.experimental.pallas import tpu as pltpu
from jax.experimental.layout import Layout, with_layout_constraint
from jax.sharding import Mesh
from jax.sharding import PartitionSpec as P

CH = 256
TAPS = 12
SPEC = 512
FRAME = 2 * CH
LANES = 128
SUB = 8
GROUP = 256
STEP = GROUP // SUB
STRIDE = STEP + 1
PITCH = SPEC + 25
FAR = 4
SWAP = [(0, 1), (1, 0)]
VMEM_LIMIT = 40 * 1024 * 1024


def prototype():
    count = TAPS * FRAME
    index = np.arange(count, dtype=np.float64)
    shifted = (index + 0.5) / FRAME - TAPS / 2.0
    window = 0.5 - 0.5 * np.cos(2.0 * math.pi * (index + 0.5) / count)
    return (np.sinc(shifted) * window).astype(np.float32).reshape(TAPS, FRAME)


def twiddle():
    chan = np.arange(CH, dtype=np.int64)[:, None]
    point = np.arange(FRAME, dtype=np.int64)[None, :]
    phase = (chan * point % FRAME).astype(np.float64) * (2.0 * math.pi / FRAME)
    return np.stack([np.cos(phase), -np.sin(phase)], axis=1).astype(np.float32)


def channelize_kernel(
    flags_hbm,
    x_hbm,
    taps_hbm,
    table_hbm,
    out_hbm,
    flags,
    taps_all,
    table,
    held,
    wide,
    fir,
    spectra,
    result,
    load_sems,
    sems,
):
    inputs = fir.shape[0]
    frames = SPEC + TAPS - 1
    spread = inputs * FRAME // LANES
    groups = SPEC // GROUP
    pieces = sems.shape[0]
    rows = FRAME // pieces
    last = lax.broadcasted_iota(jnp.int32, (SUB, LANES), 0) == SUB - 1
    edges = [0, GROUP // 2] + [g * GROUP + TAPS for g in range(1, groups)] + [frames]

    def load(source, target, n):
        copy = pltpu.make_async_copy(source, target, load_sems.at[n])
        copy.start()
        return copy

    def span(n):
        return pl.ds(edges[n] * spread, (edges[n + 1] - edges[n]) * spread)

    chunks = len(edges) - 1
    loads = [load(x_hbm.at[span(n)], held.at[span(n)], n) for n in range(chunks)]
    load_taps = load(taps_hbm, taps_all, chunks)
    load_flags = load(flags_hbm, flags, chunks + 2)

    def convert(n):
        for f in range(edges[n], edges[n + 1], 2):
            count = min(2, frames - f)
            tile = held[pl.ds(f * spread, count * spread), :].astype(jnp.float32)
            for c in range(count):
                part = tile[c * spread : (c + 1) * spread]
                wide[pl.ds(f + c, spread, stride=PITCH), :] = part

    def filter_group(g, i, j):
        cols = pl.ds(j * LANES, LANES)
        taps = [jnp.broadcast_to(taps_all[pl.ds(t, 1), cols], (SUB, LANES)) for t in range(TAPS)]

        def take(b):
            first = (inputs * j + i) * PITCH + g * GROUP + b
            return wide[pl.ds(first, SUB, stride=STRIDE), :]

        def total(first, count):
            window = [take(first + b) for b in range(count + TAPS - 1)]
            out = [taps[0] * window[b] for b in range(count)]
            for t in range(1, TAPS):
                out = [out[b] + taps[t] * window[b + t] for b in range(count)]
            return out

        extra = total(STEP, 1)[0]
        for first in range(0, STEP, SUB):
            out = total(first, SUB)
            for b in range(SUB):
                past = first + b - (STEP - SUB + 1)
                if past >= 0:
                    out[b] = jnp.where(last, pltpu.roll(extra, SUB - 1 - past, 0), out[b])
            for b in range(0, SUB, 2):
                both = jnp.concatenate(out[b : b + 2], axis=0).astype(jnp.bfloat16)
                fir[i, pl.ds(g * GROUP + (first + b) * SUB, 2 * SUB), cols] = both

    def transform(g, i):
        part = pl.ds(g * GROUP, GROUP)
        spectra[i, :, part] = lax.dot_general(
            table[...],
            fir[i, part, :],
            (((1,), (1,)), ((), ())),
            preferred_element_type=jnp.float32,
        )

    def scaled(i, piece):
        good = (1 - flags[i]).astype(jnp.float32)
        pairs = spectra[i, pl.ds(piece * rows, rows), :]
        pairs = pairs.reshape(rows // (2 * SUB), 2, SUB, SPEC)
        squares = jnp.sum(pairs * pairs, axis=1)
        power = jnp.sum(squares, axis=2, keepdims=True) / SPEC
        scale = good / jnp.sqrt(power + 1e-05)
        return pairs * scale[:, None]

    def pack(piece, parts):
        place = pl.ds(piece * rows, rows)
        for p in range(2):
            both = jnp.concatenate([part[:, p] for part in parts], axis=1)
            result[place, pl.ds(p * SPEC, SPEC)] = both.astype(jnp.bfloat16).reshape(rows, SPEC)
        copy = pltpu.make_async_copy(result.at[place], out_hbm.at[place], sems.at[piece])
        copy.start()
        return copy

    loads[0].wait()
    convert(0)
    load_taps.wait()
    loads[1].wait()
    load_table = load(table_hbm, table, chunks + 1)
    convert(1)
    for i in range(inputs):
        for j in range(FRAME // LANES):
            filter_group(0, i, j)
    loads[2].wait()
    load_table.wait()
    load_flags.wait()
    for i in range(inputs):
        transform(0, i)
    convert(2)
    for i in range(inputs):
        if i > 0:
            transform(1, i - 1)
        for j in range(FRAME // LANES):
            filter_group(1, i, j)
    transform(1, inputs - 1)
    for piece in range(pieces):
        part = scaled(0, piece)
        spectra[0, pl.ds(piece * rows, rows), :] = part.reshape(rows, SPEC)
    copies = []
    for piece in range(pieces):
        held_part = spectra[0, pl.ds(piece * rows, rows), :]
        held_part = held_part.reshape(rows // (2 * SUB), 2, SUB, SPEC)
        copies.append(pack(piece, [held_part, scaled(1, piece)]))
    for copy in copies:
        copy.wait()


def channelize(samples, flags, far, near, blocks):
    inputs = samples.shape[0]
    tiles = samples.reshape(inputs, -1, LANES)
    tiles = with_layout_constraint(tiles, Layout(major_to_minor=(1, 0, 2)))
    tiles = tiles.transpose(1, 0, 2)
    tiles = tiles.reshape(-1, LANES)
    table = twiddle().reshape(far, near, blocks, SUB, 2, FRAME).transpose(2, 1, 0, 4, 3, 5)
    table = jnp.asarray(table.reshape(FRAME, FRAME), dtype=jnp.bfloat16)
    taps = jnp.asarray(prototype())
    hbm = pl.BlockSpec(memory_space=pltpu.HBM)
    return pl.pallas_call(
        channelize_kernel,
        out_shape=jax.ShapeDtypeStruct((FRAME, inputs * SPEC), jnp.bfloat16),
        in_specs=[hbm] * 4,
        out_specs=hbm,
        scratch_shapes=[
            pltpu.SMEM(flags.shape, flags.dtype),
            pltpu.VMEM(taps.shape, taps.dtype),
            pltpu.VMEM(table.shape, table.dtype),
            pltpu.VMEM(tiles.shape, tiles.dtype),
            pltpu.VMEM((inputs * FRAME // LANES * PITCH, LANES), jnp.float32),
            pltpu.VMEM((inputs, SPEC, FRAME), jnp.bfloat16),
            pltpu.VMEM((inputs, FRAME, SPEC), jnp.float32),
            pltpu.VMEM((FRAME, inputs * SPEC), jnp.bfloat16),
            pltpu.SemaphoreType.DMA((SPEC // GROUP + 4,)),
            pltpu.SemaphoreType.DMA((8,)),
        ],
        cost_estimate=pl.CostEstimate(
            flops=2 * inputs * SPEC * FRAME * (FRAME + TAPS),
            bytes_accessed=4 * inputs * SPEC * FRAME,
            transcendentals=0,
        ),
    )(flags, tiles, taps, table)


def correlate_kernel(pick_ref, arrived_ref, own_ref, other_ref, slots):
    share, block, _ = own_ref.shape
    blocks = pick_ref.shape[0]
    width = blocks * block
    held = arrived_ref.shape[0] // blocks
    first = lax.axis_index("blk") == 0
    lane = lax.broadcasted_iota(jnp.int32, (width, 2 * width), 1)
    sign = jnp.where(lane < width, 1.0 / SPEC, -1.0 / SPEC)
    for n in range(blocks):
        rows = pl.ds(n * held, held)
        slots[n] = jnp.dot(
            pick_ref[n], arrived_ref[rows, :], preferred_element_type=jnp.float32
        ).astype(jnp.bfloat16)
    for k in range(share):
        pair = jnp.concatenate(
            [
                slots[n, pl.ds(k * block, block), pl.ds(p * SPEC, SPEC)]
                for p in range(2)
                for n in range(blocks)
            ],
            axis=0,
        )
        gram = lax.dot_general(
            pair, pair, (((1,), (1,)), ((), ())), preferred_element_type=jnp.float32
        )
        part = gram[:width] * sign + pltpu.roll(gram[width:], width, 1) / SPEC
        own_ref[k] = jnp.where(first, part[:block], part[block:])
        other_ref[k] = jnp.where(first, part[block:], part[:block])


def picks(orders, inputs, far, near, share):
    blocks, block = orders.shape
    device, held = orders // inputs, orders % inputs
    place = (device % near) * far + device // near
    start = ((place * inputs + held) * share)[:, None, :]
    chan = jnp.arange(share, dtype=jnp.int32)[:, None]
    target = (start + chan).reshape(blocks, share * block, 1)
    column = lax.broadcasted_iota(jnp.int32, (1, 1, far * near * inputs * share), 2)
    return (column == target).astype(jnp.bfloat16)


def correlate(arrived, pick, share, block):
    blocks = pick.shape[0]
    vmem = pl.BlockSpec(memory_space=pltpu.VMEM)
    tile = jax.ShapeDtypeStruct((share, block, 2 * blocks * block), jnp.float32)
    return pl.pallas_call(
        correlate_kernel,
        out_shape=(tile, tile),
        in_specs=[vmem, vmem],
        out_specs=(vmem, vmem),
        scratch_shapes=[pltpu.VMEM((blocks, share * block, 2 * SPEC), jnp.bfloat16)],
        compiler_params=pltpu.CompilerParams(vmem_limit_bytes=VMEM_LIMIT),
        cost_estimate=pl.CostEstimate(
            flops=4 * pick.size * SPEC, bytes_accessed=4 * arrived.size, transcendentals=0
        ),
    )(pick, arrived)


def place_kernel(packed_ref, *refs, own):
    out_ref, parts, sems = refs[-3:]
    share, _, _, width = parts.shape
    me = lax.axis_index("blk")
    start = (me if own else 1 - me) * share
    copies = []
    count = share // sems.shape[0]
    for n in range(sems.shape[0]):
        for k in range(n * count, (n + 1) * count):
            parts[k, 0] = packed_ref[k, :, :width]
            parts[k, 1] = packed_ref[k, :, width:]
        target = out_ref.at[pl.ds(start + n * count, count)]
        copies.append(pltpu.make_async_copy(parts.at[pl.ds(n * count, count)], target, sems.at[n]))
        copies[-1].start()
    for copy in copies:
        copy.wait()


def place(packed, blocks, base=None):
    share, block, lanes = packed.shape
    width = lanes // 2
    anywhere = pl.BlockSpec(memory_space=pl.ANY)
    return pl.pallas_call(
        functools.partial(place_kernel, own=base is None),
        out_shape=jax.ShapeDtypeStruct((blocks * share, 2, block, width), packed.dtype),
        in_specs=[pl.BlockSpec(memory_space=pltpu.VMEM)] + ([] if base is None else [anywhere]),
        out_specs=anywhere,
        scratch_shapes=[
            pltpu.VMEM((share, 2, block, width), packed.dtype),
            pltpu.SemaphoreType.DMA((2,)),
        ],
        input_output_aliases={} if base is None else {1: 0},
        compiler_params=pltpu.CompilerParams(vmem_limit_bytes=VMEM_LIMIT),
        cost_estimate=pl.CostEstimate(flops=0, bytes_accessed=8 * packed.size, transcendentals=0),
    )(packed, *([] if base is None else [base]))


def split_channels(far, near, blocks, samples, slot_order, flags):
    share = CH // (far * near * blocks)
    inputs, block = samples.shape[0], slot_order.shape[1]
    axes = ("blk", "near", "far")
    me = lax.axis_index("blk").astype(jnp.int32)
    partner = lax.ppermute(slot_order, "blk", SWAP)
    orders = jnp.where(
        me == 0,
        jnp.concatenate([slot_order, partner]),
        jnp.concatenate([partner, slot_order]),
    )
    sent = channelize(samples, flags, far, near, blocks)
    arrived = lax.all_to_all(sent, axes, split_axis=0, concat_axis=0, tiled=True)
    pick = picks(orders, inputs, far, near, share)
    own, other = correlate(arrived, pick, share, block)
    received = lax.ppermute(other, "blk", SWAP)
    return place(received, blocks, place(own, blocks))


def gather_blocks(freq, samples, slot_order, flags):
    inputs = samples.shape[0]
    taps = jnp.asarray(prototype())
    table = jnp.asarray(twiddle().reshape(2 * CH, FRAME), dtype=jnp.bfloat16)
    good = (1 - flags).astype(jnp.float32)
    frames = samples.reshape(inputs, SPEC + TAPS - 1, FRAME)
    total = jnp.zeros((inputs, SPEC, FRAME), jnp.float32)
    for tap in range(TAPS):
        window = frames[:, tap : tap + SPEC, :].astype(jnp.float32)
        total = total + taps[tap][None, None, :] * window
    fir = total.astype(jnp.bfloat16)
    spectra = jnp.einsum("kn,isn->kis", table, fir, preferred_element_type=jnp.float32)
    squares = jnp.sum(spectra * spectra, axis=2)
    power = jnp.sum(squares.reshape(CH, 2, inputs), axis=1) / SPEC
    scale = good[None, :] / jnp.sqrt(power + 1e-05)
    quantized = (spectra * jnp.repeat(scale, 2, axis=0)[:, :, None]).astype(jnp.bfloat16)
    arrived = lax.all_to_all(quantized, ("far", "near"), split_axis=0, concat_axis=1, tiled=True)
    share = CH // freq
    block = slot_order.shape[1]
    own = jnp.take(arrived.reshape(share, 2, block, SPEC), slot_order[0], axis=2)
    piece = lax.all_gather(own, "blk", axis=2, tiled=True)
    dot = functools.partial(jnp.einsum, "cas,cbs->cab", preferred_element_type=jnp.float32)
    real = dot(own[:, 0], piece[:, 0]) + dot(own[:, 1], piece[:, 1])
    imag = dot(own[:, 1], piece[:, 0]) - dot(own[:, 0], piece[:, 1])
    return jnp.stack([real / SPEC, imag / SPEC], axis=1)


def solution(mesh):
    freq, blocks = mesh.shape["freq"], mesh.shape["blk"]
    far = math.gcd(freq, FAR)
    near = freq // far
    split = Mesh(mesh.devices.reshape(far, near, blocks), ("far", "near", "blk"))

    def body(samples, slot_order, flags):
        if blocks == 2 and CH == SUB * freq * blocks:
            return split_channels(far, near, blocks, samples, slot_order, flags)
        return gather_blocks(freq, samples, slot_order, flags)

    held = ("blk", "far", "near")
    in_specs = (P(held, None), P("blk", None), P(held))
    out_specs = P(("far", "near"), None, "blk", None)
    return jax.shard_map(body, mesh=split, in_specs=in_specs, out_specs=out_specs, check_vma=False)
```

```python
import functools
import math

import jax
import jax.numpy as jnp
import numpy as np
from jax import lax
from jax.experimental import pallas as pl
from jax.experimental.pallas import tpu as pltpu
from jax.experimental.layout import Layout, with_layout_constraint
from jax.sharding import Mesh
from jax.sharding import PartitionSpec as P

CH = 256
TAPS = 12
SPEC = 512
FRAME = 2 * CH
LANES = 128
SUB = 8
GROUP = 256
STEP = GROUP // SUB
STRIDE = STEP + 1
PITCH = SPEC + 25
FAR = 4
SWAP = [(0, 1), (1, 0)]
VMEM_LIMIT = 40 * 1024 * 1024


def prototype():
    count = TAPS * FRAME
    index = np.arange(count, dtype=np.float64)
    shifted = (index + 0.5) / FRAME - TAPS / 2.0
    window = 0.5 - 0.5 * np.cos(2.0 * math.pi * (index + 0.5) / count)
    return (np.sinc(shifted) * window).astype(np.float32).reshape(TAPS, FRAME)


def twiddle():
    chan = np.arange(CH, dtype=np.int64)[:, None]
    point = np.arange(FRAME, dtype=np.int64)[None, :]
    phase = (chan * point % FRAME).astype(np.float64) * (2.0 * math.pi / FRAME)
    return np.stack([np.cos(phase), -np.sin(phase)], axis=1).astype(np.float32)


def channelize_kernel(
    flags_hbm,
    x_hbm,
    taps_hbm,
    table_hbm,
    out_hbm,
    flags,
    taps_all,
    table,
    held,
    wide,
    fir,
    spectra,
    result,
    load_sems,
    sems,
):
    inputs = fir.shape[0]
    frames = SPEC + TAPS - 1
    spread = inputs * FRAME // LANES
    groups = SPEC // GROUP
    pieces = sems.shape[0]
    rows = FRAME // pieces
    last = lax.broadcasted_iota(jnp.int32, (SUB, LANES), 0) == SUB - 1
    edges = [0, GROUP // 2] + [g * GROUP + TAPS for g in range(1, groups)] + [frames]

    def load(source, target, n):
        copy = pltpu.make_async_copy(source, target, load_sems.at[n])
        copy.start()
        return copy

    def span(n):
        return pl.ds(edges[n] * spread, (edges[n + 1] - edges[n]) * spread)

    chunks = len(edges) - 1
    loads = [load(x_hbm.at[span(n)], held.at[span(n)], n) for n in range(chunks)]
    load_taps = load(taps_hbm, taps_all, chunks)
    load_flags = load(flags_hbm, flags, chunks + 2)

    def convert(n):
        for f in range(edges[n], edges[n + 1], 2):
            count = min(2, frames - f)
            tile = held[pl.ds(f * spread, count * spread), :].astype(jnp.float32)
            for c in range(count):
                part = tile[c * spread : (c + 1) * spread]
                wide[pl.ds(f + c, spread, stride=PITCH), :] = part

    def filter_group(g, i, j):
        cols = pl.ds(pl.multiple_of(j * LANES, LANES), LANES)
        taps = [jnp.broadcast_to(taps_all[pl.ds(t, 1), cols], (SUB, LANES)) for t in range(TAPS)]

        def take(b):
            first = (inputs * j + i) * PITCH + (g * GROUP + b)
            return wide[pl.ds(first, SUB, stride=STRIDE), :]

        def total(first, count):
            window = [take(first + b) for b in range(count + TAPS - 1)]
            out = [taps[0] * window[b] for b in range(count)]
            for t in range(1, TAPS):
                out = [out[b] + taps[t] * window[b + t] for b in range(count)]
            return out

        extra = total(STEP, 1)[0]
        for first in range(0, STEP, SUB):
            out = total(first, SUB)
            for b in range(SUB):
                past = first + b - (STEP - SUB + 1)
                if past >= 0:
                    out[b] = jnp.where(last, pltpu.roll(extra, SUB - 1 - past, 0), out[b])
            for b in range(0, SUB, 2):
                both = jnp.concatenate(out[b : b + 2], axis=0).astype(jnp.bfloat16)
                fir[i, pl.ds(g * GROUP + (first + b) * SUB, 2 * SUB), cols] = both

    def transform(g, i, start=0, count=FRAME):
        part = pl.ds(g * GROUP, GROUP)
        out = pl.ds(start, count)
        spectra[i, out, part] = lax.dot_general(
            table[out, :],
            fir[i, part, :],
            (((1,), (1,)), ((), ())),
            preferred_element_type=jnp.float32,
        )

    def scaled(i, piece):
        good = (1 - flags[i]).astype(jnp.float32)
        pairs = spectra[i, pl.ds(piece * rows, rows), :]
        pairs = pairs.reshape(rows // (2 * SUB), 2, SUB, SPEC)
        squares = jnp.sum(pairs * pairs, axis=1)
        power = jnp.sum(squares, axis=2, keepdims=True) / SPEC
        scale = good / jnp.sqrt(power + 1e-05)
        return pairs * scale[:, None]

    def pack(piece, parts):
        place = pl.ds(piece * rows, rows)
        for p in range(2):
            both = jnp.concatenate([part[:, p] for part in parts], axis=1)
            result[place, pl.ds(p * SPEC, SPEC)] = both.astype(jnp.bfloat16).reshape(rows, SPEC)
        copy = pltpu.make_async_copy(result.at[place], out_hbm.at[place], sems.at[piece])
        copy.start()
        return copy

    loads[0].wait()
    convert(0)
    load_taps.wait()
    loads[1].wait()
    load_table = load(table_hbm, table, chunks + 1)
    convert(1)
    columns = FRAME // LANES

    @pl.loop(0, columns)
    def _(j):
        for i in range(inputs):
            filter_group(0, i, j)

    loads[2].wait()
    load_table.wait()
    load_flags.wait()
    convert(2)
    count = FRAME // columns

    @pl.loop(0, columns)
    def _(j):
        for i in range(inputs):
            transform(0, i, pl.multiple_of(j * count, count), count)
            filter_group(1, i, j)

    for i in range(inputs):
        transform(1, i)
    for piece in range(pieces):
        part = scaled(0, piece)
        spectra[0, pl.ds(piece * rows, rows), :] = part.reshape(rows, SPEC)
    copies = []
    for piece in range(pieces):
        held_part = spectra[0, pl.ds(piece * rows, rows), :]
        held_part = held_part.reshape(rows // (2 * SUB), 2, SUB, SPEC)
        copies.append(pack(piece, [held_part, scaled(1, piece)]))
    for copy in copies:
        copy.wait()


def channelize(samples, flags, far, near, blocks):
    inputs = samples.shape[0]
    tiles = samples.reshape(inputs, -1, LANES)
    tiles = with_layout_constraint(tiles, Layout(major_to_minor=(1, 0, 2)))
    tiles = tiles.transpose(1, 0, 2)
    tiles = tiles.reshape(-1, LANES)
    table = twiddle().reshape(far, near, blocks, SUB, 2, FRAME).transpose(2, 1, 0, 4, 3, 5)
    table = jnp.asarray(table.reshape(FRAME, FRAME), dtype=jnp.bfloat16)
    taps = jnp.asarray(prototype())
    hbm = pl.BlockSpec(memory_space=pltpu.HBM)
    return pl.pallas_call(
        channelize_kernel,
        out_shape=jax.ShapeDtypeStruct((FRAME, inputs * SPEC), jnp.bfloat16),
        in_specs=[hbm] * 4,
        out_specs=hbm,
        scratch_shapes=[
            pltpu.SMEM(flags.shape, flags.dtype),
            pltpu.VMEM(taps.shape, taps.dtype),
            pltpu.VMEM(table.shape, table.dtype),
            pltpu.VMEM(tiles.shape, tiles.dtype),
            pltpu.VMEM((inputs * FRAME // LANES * PITCH, LANES), jnp.float32),
            pltpu.VMEM((inputs, SPEC, FRAME), jnp.bfloat16),
            pltpu.VMEM((inputs, FRAME, SPEC), jnp.float32),
            pltpu.VMEM((FRAME, inputs * SPEC), jnp.bfloat16),
            pltpu.SemaphoreType.DMA((SPEC // GROUP + 4,)),
            pltpu.SemaphoreType.DMA((8,)),
        ],
        cost_estimate=pl.CostEstimate(
            flops=2 * inputs * SPEC * FRAME * (FRAME + TAPS),
            bytes_accessed=4 * inputs * SPEC * FRAME,
            transcendentals=0,
        ),
    )(flags, tiles, taps, table)


def correlate_kernel(pick_ref, arrived_ref, own_ref, other_ref, slots):
    share, block, _ = own_ref.shape
    blocks = pick_ref.shape[0]
    width = blocks * block
    held = arrived_ref.shape[0] // blocks
    first = lax.axis_index("blk") == 0
    lane = lax.broadcasted_iota(jnp.int32, (width, 2 * width), 1)
    sign = jnp.where(lane < width, 1.0 / SPEC, -1.0 / SPEC)
    for n in range(blocks):
        rows = pl.ds(n * held, held)
        slots[n] = jnp.dot(
            pick_ref[n], arrived_ref[rows, :], preferred_element_type=jnp.float32
        ).astype(jnp.bfloat16)
    for k in range(share):
        pair = jnp.concatenate(
            [
                slots[n, pl.ds(k * block, block), pl.ds(p * SPEC, SPEC)]
                for p in range(2)
                for n in range(blocks)
            ],
            axis=0,
        )
        gram = lax.dot_general(
            pair, pair, (((1,), (1,)), ((), ())), preferred_element_type=jnp.float32
        )
        part = gram[:width] * sign + pltpu.roll(gram[width:], width, 1) / SPEC
        own_ref[k] = jnp.where(first, part[:block], part[block:])
        other_ref[k] = jnp.where(first, part[block:], part[:block])


def picks(orders, inputs, far, near, share):
    blocks, block = orders.shape
    device, held = orders // inputs, orders % inputs
    place = (device % near) * far + device // near
    start = ((place * inputs + held) * share)[:, None, :]
    chan = jnp.arange(share, dtype=jnp.int32)[:, None]
    target = (start + chan).reshape(blocks, share * block, 1)
    column = lax.broadcasted_iota(jnp.int32, (1, 1, far * near * inputs * share), 2)
    return (column == target).astype(jnp.bfloat16)


def correlate(arrived, pick, share, block):
    blocks = pick.shape[0]
    vmem = pl.BlockSpec(memory_space=pltpu.VMEM)
    tile = jax.ShapeDtypeStruct((share, block, 2 * blocks * block), jnp.float32)
    return pl.pallas_call(
        correlate_kernel,
        out_shape=(tile, tile),
        in_specs=[vmem, vmem],
        out_specs=(vmem, vmem),
        scratch_shapes=[pltpu.VMEM((blocks, share * block, 2 * SPEC), jnp.bfloat16)],
        compiler_params=pltpu.CompilerParams(vmem_limit_bytes=VMEM_LIMIT),
        cost_estimate=pl.CostEstimate(
            flops=4 * pick.size * SPEC, bytes_accessed=4 * arrived.size, transcendentals=0
        ),
    )(pick, arrived)


def place_kernel(packed_ref, *refs, own):
    out_ref, parts, sems = refs[-3:]
    share, _, _, width = parts.shape
    me = lax.axis_index("blk")
    start = (me if own else 1 - me) * share
    copies = []
    count = share // sems.shape[0]
    for n in range(sems.shape[0]):
        for k in range(n * count, (n + 1) * count):
            parts[k, 0] = packed_ref[k, :, :width]
            parts[k, 1] = packed_ref[k, :, width:]
        target = out_ref.at[pl.ds(start + n * count, count)]
        copies.append(pltpu.make_async_copy(parts.at[pl.ds(n * count, count)], target, sems.at[n]))
        copies[-1].start()
    for copy in copies:
        copy.wait()


def place(packed, blocks, base=None):
    share, block, lanes = packed.shape
    width = lanes // 2
    anywhere = pl.BlockSpec(memory_space=pl.ANY)
    return pl.pallas_call(
        functools.partial(place_kernel, own=base is None),
        out_shape=jax.ShapeDtypeStruct((blocks * share, 2, block, width), packed.dtype),
        in_specs=[pl.BlockSpec(memory_space=pltpu.VMEM)] + ([] if base is None else [anywhere]),
        out_specs=anywhere,
        scratch_shapes=[
            pltpu.VMEM((share, 2, block, width), packed.dtype),
            pltpu.SemaphoreType.DMA((2,)),
        ],
        input_output_aliases={} if base is None else {1: 0},
        compiler_params=pltpu.CompilerParams(vmem_limit_bytes=VMEM_LIMIT),
        cost_estimate=pl.CostEstimate(flops=0, bytes_accessed=8 * packed.size, transcendentals=0),
    )(packed, *([] if base is None else [base]))


def split_channels(far, near, blocks, samples, slot_order, flags):
    share = CH // (far * near * blocks)
    inputs, block = samples.shape[0], slot_order.shape[1]
    axes = ("blk", "near", "far")
    me = lax.axis_index("blk").astype(jnp.int32)
    partner = lax.ppermute(slot_order, "blk", SWAP)
    orders = jnp.where(
        me == 0,
        jnp.concatenate([slot_order, partner]),
        jnp.concatenate([partner, slot_order]),
    )
    sent = channelize(samples, flags, far, near, blocks)
    arrived = lax.all_to_all(sent, axes, split_axis=0, concat_axis=0, tiled=True)
    pick = picks(orders, inputs, far, near, share)
    own, other = correlate(arrived, pick, share, block)
    received = lax.ppermute(other, "blk", SWAP)
    return place(received, blocks, place(own, blocks))


def gather_blocks(freq, samples, slot_order, flags):
    inputs = samples.shape[0]
    taps = jnp.asarray(prototype())
    table = jnp.asarray(twiddle().reshape(2 * CH, FRAME), dtype=jnp.bfloat16)
    good = (1 - flags).astype(jnp.float32)
    frames = samples.reshape(inputs, SPEC + TAPS - 1, FRAME)
    total = jnp.zeros((inputs, SPEC, FRAME), jnp.float32)
    for tap in range(TAPS):
        window = frames[:, tap : tap + SPEC, :].astype(jnp.float32)
        total = total + taps[tap][None, None, :] * window
    fir = total.astype(jnp.bfloat16)
    spectra = jnp.einsum("kn,isn->kis", table, fir, preferred_element_type=jnp.float32)
    squares = jnp.sum(spectra * spectra, axis=2)
    power = jnp.sum(squares.reshape(CH, 2, inputs), axis=1) / SPEC
    scale = good[None, :] / jnp.sqrt(power + 1e-05)
    quantized = (spectra * jnp.repeat(scale, 2, axis=0)[:, :, None]).astype(jnp.bfloat16)
    arrived = lax.all_to_all(quantized, ("far", "near"), split_axis=0, concat_axis=1, tiled=True)
    share = CH // freq
    block = slot_order.shape[1]
    own = jnp.take(arrived.reshape(share, 2, block, SPEC), slot_order[0], axis=2)
    piece = lax.all_gather(own, "blk", axis=2, tiled=True)
    dot = functools.partial(jnp.einsum, "cas,cbs->cab", preferred_element_type=jnp.float32)
    real = dot(own[:, 0], piece[:, 0]) + dot(own[:, 1], piece[:, 1])
    imag = dot(own[:, 1], piece[:, 0]) - dot(own[:, 0], piece[:, 1])
    return jnp.stack([real / SPEC, imag / SPEC], axis=1)


def solution(mesh):
    freq, blocks = mesh.shape["freq"], mesh.shape["blk"]
    far = math.gcd(freq, FAR)
    near = freq // far
    split = Mesh(mesh.devices.reshape(far, near, blocks), ("far", "near", "blk"))

    def body(samples, slot_order, flags):
        if blocks == 2 and CH == SUB * freq * blocks:
            return split_channels(far, near, blocks, samples, slot_order, flags)
        return gather_blocks(freq, samples, slot_order, flags)

    held = ("blk", "far", "near")
    in_specs = (P(held, None), P("blk", None), P(held))
    out_specs = P(("far", "near"), None, "blk", None)
    return jax.shard_map(body, mesh=split, in_specs=in_specs, out_specs=out_specs, check_vma=False)
```

```python
import functools
import math

import jax
import jax.numpy as jnp
import numpy as np
from jax import lax
from jax.experimental import pallas as pl
from jax.experimental.pallas import tpu as pltpu
from jax.experimental.layout import Layout, with_layout_constraint
from jax.sharding import Mesh
from jax.sharding import PartitionSpec as P

CH = 256
TAPS = 12
SPEC = 512
FRAME = 2 * CH
LANES = 128
SUB = 8
GROUP = 256
STEP = GROUP // SUB
STRIDE = STEP + 1
PITCH = SPEC + 25
FAR = 4
SWAP = [(0, 1), (1, 0)]
VMEM_LIMIT = 40 * 1024 * 1024


def prototype():
    count = TAPS * FRAME
    index = np.arange(count, dtype=np.float64)
    shifted = (index + 0.5) / FRAME - TAPS / 2.0
    window = 0.5 - 0.5 * np.cos(2.0 * math.pi * (index + 0.5) / count)
    return (np.sinc(shifted) * window).astype(np.float32).reshape(TAPS, FRAME)


def twiddle():
    chan = np.arange(CH, dtype=np.int64)[:, None]
    point = np.arange(FRAME, dtype=np.int64)[None, :]
    phase = (chan * point % FRAME).astype(np.float64) * (2.0 * math.pi / FRAME)
    return np.stack([np.cos(phase), -np.sin(phase)], axis=1).astype(np.float32)


def channelize_kernel(
    flags_hbm,
    x_hbm,
    taps_hbm,
    table_hbm,
    out_hbm,
    flags,
    taps_all,
    table,
    held,
    wide,
    fir,
    spectra,
    scales,
    result,
    load_sems,
    sems,
):
    inputs = fir.shape[0]
    frames = SPEC + TAPS - 1
    spread = inputs * FRAME // LANES
    groups = SPEC // GROUP
    pieces = sems.shape[0]
    rows = FRAME // pieces
    last = lax.broadcasted_iota(jnp.int32, (SUB, LANES), 0) == SUB - 1
    edges = [0, GROUP // 2] + [g * GROUP + TAPS for g in range(1, groups)] + [frames]

    def load(source, target, n):
        copy = pltpu.make_async_copy(source, target, load_sems.at[n])
        copy.start()
        return copy

    def span(n):
        return pl.ds(edges[n] * spread, (edges[n + 1] - edges[n]) * spread)

    chunks = len(edges) - 1
    loads = [load(x_hbm.at[span(n)], held.at[span(n)], n) for n in range(chunks)]
    load_taps = load(taps_hbm, taps_all, chunks)
    load_flags = load(flags_hbm, flags, chunks + 2)

    def convert(n):
        for f in range(edges[n], edges[n + 1], 2):
            count = min(2, frames - f)
            tile = held[pl.ds(f * spread, count * spread), :].astype(jnp.float32)
            for c in range(count):
                part = tile[c * spread : (c + 1) * spread]
                wide[pl.ds(f + c, spread, stride=PITCH), :] = part

    def filter_group(g, i, j):
        cols = pl.ds(j * LANES, LANES)
        taps = [jnp.broadcast_to(taps_all[pl.ds(t, 1), cols], (SUB, LANES)) for t in range(TAPS)]

        def take(b):
            first = (inputs * j + i) * PITCH + g * GROUP + b
            return wide[pl.ds(first, SUB, stride=STRIDE), :]

        def total(first, count):
            window = [take(first + b) for b in range(count + TAPS - 1)]
            out = [taps[0] * window[b] for b in range(count)]
            for t in range(1, TAPS):
                out = [out[b] + taps[t] * window[b + t] for b in range(count)]
            return out

        extra = total(STEP, 1)[0]
        for first in range(0, STEP, SUB):
            out = total(first, SUB)
            for b in range(SUB):
                past = first + b - (STEP - SUB + 1)
                if past >= 0:
                    out[b] = jnp.where(last, pltpu.roll(extra, SUB - 1 - past, 0), out[b])
            for b in range(0, SUB, 2):
                both = jnp.concatenate(out[b : b + 2], axis=0).astype(jnp.bfloat16)
                fir[i, pl.ds(g * GROUP + (first + b) * SUB, 2 * SUB), cols] = both

    def transform(g, i):
        part = pl.ds(g * GROUP, GROUP)
        spectra[i, :, part] = lax.dot_general(
            table[...],
            fir[i, part, :],
            (((1,), (1,)), ((), ())),
            preferred_element_type=jnp.float32,
        )

    def rate(i):
        good = (1 - flags[i]).astype(jnp.float32)
        for piece in range(pieces):
            pairs = spectra[i, pl.ds(piece * rows, rows), :]
            pairs = pairs.reshape(rows // (2 * SUB), 2, SUB, SPEC)
            squares = jnp.sum(pairs * pairs, axis=1)
            power = jnp.sum(squares, axis=2, keepdims=True) / SPEC
            scale = good / jnp.sqrt(power + 1e-05)
            place = pl.ds(piece * rows // 2, rows // 2)
            scales[i, place, :] = jnp.broadcast_to(scale.reshape(rows // 2, 1), (rows // 2, LANES))

    def scaled(i, piece):
        pairs = spectra[i, pl.ds(piece * rows, rows), :]
        pairs = pairs.reshape(rows // (2 * SUB), 2, SUB, SPEC)
        scale = scales[i, pl.ds(piece * rows // 2, rows // 2), :]
        scale = jnp.concatenate([scale] * (SPEC // LANES), axis=1)
        return pairs * scale.reshape(rows // (2 * SUB), 1, SUB, SPEC)

    def pack(piece):
        place = pl.ds(piece * rows, rows)
        parts = [scaled(i, piece) for i in range(inputs)]
        for p in range(2):
            both = jnp.concatenate([part[:, p] for part in parts], axis=1)
            result[place, pl.ds(p * SPEC, SPEC)] = both.astype(jnp.bfloat16).reshape(rows, SPEC)
        copy = pltpu.make_async_copy(result.at[place], out_hbm.at[place], sems.at[piece])
        copy.start()
        return copy

    loads[0].wait()
    convert(0)
    load_taps.wait()
    loads[1].wait()
    load_table = load(table_hbm, table, chunks + 1)
    convert(1)
    for i in range(inputs):
        for j in range(FRAME // LANES):
            filter_group(0, i, j)
    loads[2].wait()
    load_table.wait()
    load_flags.wait()
    for i in range(inputs):
        transform(0, i)
    convert(2)
    for i in range(inputs):
        if i > 0:
            transform(1, i - 1)
        for j in range(FRAME // LANES):
            filter_group(1, i, j)
    transform(1, inputs - 1)
    for i in range(inputs):
        rate(i)
    copies = [pack(piece) for piece in range(pieces)]
    for copy in copies:
        copy.wait()


def channelize(samples, flags, far, near, blocks):
    inputs = samples.shape[0]
    tiles = samples.reshape(inputs, -1, LANES)
    tiles = with_layout_constraint(tiles, Layout(major_to_minor=(1, 0, 2)))
    tiles = tiles.transpose(1, 0, 2)
    tiles = tiles.reshape(-1, LANES)
    table = twiddle().reshape(far, near, blocks, SUB, 2, FRAME).transpose(2, 1, 0, 4, 3, 5)
    table = jnp.asarray(table.reshape(FRAME, FRAME), dtype=jnp.bfloat16)
    taps = jnp.asarray(prototype())
    hbm = pl.BlockSpec(memory_space=pltpu.HBM)
    return pl.pallas_call(
        channelize_kernel,
        out_shape=jax.ShapeDtypeStruct((FRAME, inputs * SPEC), jnp.bfloat16),
        in_specs=[hbm] * 4,
        out_specs=hbm,
        scratch_shapes=[
            pltpu.SMEM(flags.shape, flags.dtype),
            pltpu.VMEM(taps.shape, taps.dtype),
            pltpu.VMEM(table.shape, table.dtype),
            pltpu.VMEM(tiles.shape, tiles.dtype),
            pltpu.VMEM((inputs * FRAME // LANES * PITCH, LANES), jnp.float32),
            pltpu.VMEM((inputs, SPEC, FRAME), jnp.bfloat16),
            pltpu.VMEM((inputs, FRAME, SPEC), jnp.float32),
            pltpu.VMEM((inputs, CH, LANES), jnp.float32),
            pltpu.VMEM((FRAME, inputs * SPEC), jnp.bfloat16),
            pltpu.SemaphoreType.DMA((SPEC // GROUP + 4,)),
            pltpu.SemaphoreType.DMA((8,)),
        ],
        cost_estimate=pl.CostEstimate(
            flops=2 * inputs * SPEC * FRAME * (FRAME + TAPS),
            bytes_accessed=4 * inputs * SPEC * FRAME,
            transcendentals=0,
        ),
    )(flags, tiles, taps, table)


def correlate_kernel(pick_ref, arrived_ref, own_ref, other_ref, slots):
    share, block, _ = own_ref.shape
    blocks = pick_ref.shape[0]
    width = blocks * block
    held = arrived_ref.shape[0] // blocks
    first = lax.axis_index("blk") == 0
    lane = lax.broadcasted_iota(jnp.int32, (width, 2 * width), 1)
    sign = jnp.where(lane < width, 1.0 / SPEC, -1.0 / SPEC)
    for n in range(blocks):
        rows = pl.ds(n * held, held)
        slots[n] = jnp.dot(
            pick_ref[n], arrived_ref[rows, :], preferred_element_type=jnp.float32
        ).astype(jnp.bfloat16)
    for k in range(share):
        pair = jnp.concatenate(
            [
                slots[n, pl.ds(k * block, block), pl.ds(p * SPEC, SPEC)]
                for p in range(2)
                for n in range(blocks)
            ],
            axis=0,
        )
        gram = lax.dot_general(
            pair, pair, (((1,), (1,)), ((), ())), preferred_element_type=jnp.float32
        )
        part = gram[:width] * sign + pltpu.roll(gram[width:], width, 1) / SPEC
        own_ref[k] = jnp.where(first, part[:block], part[block:])
        other_ref[k] = jnp.where(first, part[block:], part[:block])


def picks(orders, inputs, far, near, share):
    blocks, block = orders.shape
    device, held = orders // inputs, orders % inputs
    place = (device % near) * far + device // near
    start = ((place * inputs + held) * share)[:, None, :]
    chan = jnp.arange(share, dtype=jnp.int32)[:, None]
    target = (start + chan).reshape(blocks, share * block, 1)
    column = lax.broadcasted_iota(jnp.int32, (1, 1, far * near * inputs * share), 2)
    return (column == target).astype(jnp.bfloat16)


def correlate(arrived, pick, share, block):
    blocks = pick.shape[0]
    vmem = pl.BlockSpec(memory_space=pltpu.VMEM)
    tile = jax.ShapeDtypeStruct((share, block, 2 * blocks * block), jnp.float32)
    return pl.pallas_call(
        correlate_kernel,
        out_shape=(tile, tile),
        in_specs=[vmem, vmem],
        out_specs=(vmem, vmem),
        scratch_shapes=[pltpu.VMEM((blocks, share * block, 2 * SPEC), jnp.bfloat16)],
        compiler_params=pltpu.CompilerParams(vmem_limit_bytes=VMEM_LIMIT),
        cost_estimate=pl.CostEstimate(
            flops=4 * pick.size * SPEC, bytes_accessed=4 * arrived.size, transcendentals=0
        ),
    )(pick, arrived)


def place_kernel(packed_ref, *refs, own):
    out_ref, parts, sems = refs[-3:]
    share, _, _, width = parts.shape
    me = lax.axis_index("blk")
    start = (me if own else 1 - me) * share
    copies = []
    count = share // sems.shape[0]
    for n in range(sems.shape[0]):
        for k in range(n * count, (n + 1) * count):
            parts[k, 0] = packed_ref[k, :, :width]
            parts[k, 1] = packed_ref[k, :, width:]
        target = out_ref.at[pl.ds(start + n * count, count)]
        copies.append(pltpu.make_async_copy(parts.at[pl.ds(n * count, count)], target, sems.at[n]))
        copies[-1].start()
    for copy in copies:
        copy.wait()


def place(packed, blocks, base=None):
    share, block, lanes = packed.shape
    width = lanes // 2
    anywhere = pl.BlockSpec(memory_space=pl.ANY)
    return pl.pallas_call(
        functools.partial(place_kernel, own=base is None),
        out_shape=jax.ShapeDtypeStruct((blocks * share, 2, block, width), packed.dtype),
        in_specs=[pl.BlockSpec(memory_space=pltpu.VMEM)] + ([] if base is None else [anywhere]),
        out_specs=anywhere,
        scratch_shapes=[
            pltpu.VMEM((share, 2, block, width), packed.dtype),
            pltpu.SemaphoreType.DMA((2,)),
        ],
        input_output_aliases={} if base is None else {1: 0},
        compiler_params=pltpu.CompilerParams(vmem_limit_bytes=VMEM_LIMIT),
        cost_estimate=pl.CostEstimate(flops=0, bytes_accessed=8 * packed.size, transcendentals=0),
    )(packed, *([] if base is None else [base]))


def split_channels(far, near, blocks, samples, slot_order, flags):
    share = CH // (far * near * blocks)
    inputs, block = samples.shape[0], slot_order.shape[1]
    axes = ("blk", "near", "far")
    me = lax.axis_index("blk").astype(jnp.int32)
    partner = lax.ppermute(slot_order, "blk", SWAP)
    orders = jnp.where(
        me == 0,
        jnp.concatenate([slot_order, partner]),
        jnp.concatenate([partner, slot_order]),
    )
    sent = channelize(samples, flags, far, near, blocks)
    arrived = lax.all_to_all(sent, axes, split_axis=0, concat_axis=0, tiled=True)
    pick = picks(orders, inputs, far, near, share)
    own, other = correlate(arrived, pick, share, block)
    received = lax.ppermute(other, "blk", SWAP)
    return place(received, blocks, place(own, blocks))


def gather_blocks(freq, samples, slot_order, flags):
    inputs = samples.shape[0]
    taps = jnp.asarray(prototype())
    table = jnp.asarray(twiddle().reshape(2 * CH, FRAME), dtype=jnp.bfloat16)
    good = (1 - flags).astype(jnp.float32)
    frames = samples.reshape(inputs, SPEC + TAPS - 1, FRAME)
    total = jnp.zeros((inputs, SPEC, FRAME), jnp.float32)
    for tap in range(TAPS):
        window = frames[:, tap : tap + SPEC, :].astype(jnp.float32)
        total = total + taps[tap][None, None, :] * window
    fir = total.astype(jnp.bfloat16)
    spectra = jnp.einsum("kn,isn->kis", table, fir, preferred_element_type=jnp.float32)
    squares = jnp.sum(spectra * spectra, axis=2)
    power = jnp.sum(squares.reshape(CH, 2, inputs), axis=1) / SPEC
    scale = good[None, :] / jnp.sqrt(power + 1e-05)
    quantized = (spectra * jnp.repeat(scale, 2, axis=0)[:, :, None]).astype(jnp.bfloat16)
    arrived = lax.all_to_all(quantized, ("far", "near"), split_axis=0, concat_axis=1, tiled=True)
    share = CH // freq
    block = slot_order.shape[1]
    own = jnp.take(arrived.reshape(share, 2, block, SPEC), slot_order[0], axis=2)
    piece = lax.all_gather(own, "blk", axis=2, tiled=True)
    dot = functools.partial(jnp.einsum, "cas,cbs->cab", preferred_element_type=jnp.float32)
    real = dot(own[:, 0], piece[:, 0]) + dot(own[:, 1], piece[:, 1])
    imag = dot(own[:, 1], piece[:, 0]) - dot(own[:, 0], piece[:, 1])
    return jnp.stack([real / SPEC, imag / SPEC], axis=1)


def solution(mesh):
    freq, blocks = mesh.shape["freq"], mesh.shape["blk"]
    far = math.gcd(freq, FAR)
    near = freq // far
    split = Mesh(mesh.devices.reshape(far, near, blocks), ("far", "near", "blk"))

    def body(samples, slot_order, flags):
        if blocks == 2 and CH == SUB * freq * blocks:
            return split_channels(far, near, blocks, samples, slot_order, flags)
        return gather_blocks(freq, samples, slot_order, flags)

    held = ("blk", "far", "near")
    in_specs = (P(held, None), P("blk", None), P(held))
    out_specs = P(("far", "near"), None, "blk", None)
    return jax.shard_map(body, mesh=split, in_specs=in_specs, out_specs=out_specs, check_vma=False)
```

```python
import functools
import math

import jax
import jax.numpy as jnp
import numpy as np
from jax import lax
from jax.experimental import pallas as pl
from jax.experimental.pallas import tpu as pltpu
from jax.experimental.layout import Layout, with_layout_constraint
from jax.sharding import Mesh
from jax.sharding import PartitionSpec as P

CH = 256
TAPS = 12
SPEC = 512
FRAME = 2 * CH
LANES = 128
SUB = 8
GROUP = 256
STEP = GROUP // SUB
STRIDE = STEP + 1
PITCH = SPEC + 25
FAR = 4
SWAP = [(0, 1), (1, 0)]
VMEM_LIMIT = 40 * 1024 * 1024


def prototype():
    count = TAPS * FRAME
    index = np.arange(count, dtype=np.float64)
    shifted = (index + 0.5) / FRAME - TAPS / 2.0
    window = 0.5 - 0.5 * np.cos(2.0 * math.pi * (index + 0.5) / count)
    return (np.sinc(shifted) * window).astype(np.float32).reshape(TAPS, FRAME)


def twiddle():
    chan = np.arange(CH, dtype=np.int64)[:, None]
    point = np.arange(FRAME, dtype=np.int64)[None, :]
    phase = (chan * point % FRAME).astype(np.float64) * (2.0 * math.pi / FRAME)
    return np.stack([np.cos(phase), -np.sin(phase)], axis=1).astype(np.float32)


def channelize_kernel(
    flags_hbm,
    x_hbm,
    taps_hbm,
    table_hbm,
    out_hbm,
    flags,
    taps_all,
    table,
    held,
    wide,
    fir,
    spectra,
    result,
    load_sems,
    sems,
):
    inputs = fir.shape[0]
    frames = SPEC + TAPS - 1
    spread = inputs * FRAME // LANES
    groups = SPEC // GROUP
    pieces = sems.shape[1]
    rows = FRAME // pieces
    last = lax.broadcasted_iota(jnp.int32, (SUB, LANES), 0) == SUB - 1
    edges = [0, GROUP // 2] + [g * GROUP + TAPS for g in range(1, groups)] + [frames]

    def load(source, target, n):
        copy = pltpu.make_async_copy(source, target, load_sems.at[n])
        copy.start()
        return copy

    def span(n):
        return pl.ds(edges[n] * spread, (edges[n + 1] - edges[n]) * spread)

    chunks = len(edges) - 1
    loads = [load(x_hbm.at[span(n)], held.at[span(n)], n) for n in range(chunks)]
    load_taps = load(taps_hbm, taps_all, chunks)
    load_flags = load(flags_hbm, flags, chunks + 2)

    def convert(n):
        for f in range(edges[n], edges[n + 1], 2):
            count = min(2, frames - f)
            tile = held[pl.ds(f * spread, count * spread), :].astype(jnp.float32)
            for c in range(count):
                part = tile[c * spread : (c + 1) * spread]
                wide[pl.ds(f + c, spread, stride=PITCH), :] = part

    def filter_group(g, i, j):
        cols = pl.ds(j * LANES, LANES)
        good = (1 - flags[i]).astype(jnp.float32)
        taps = [
            jnp.broadcast_to(taps_all[pl.ds(t, 1), cols] * good, (SUB, LANES)) for t in range(TAPS)
        ]

        def take(b):
            first = (inputs * j + i) * PITCH + g * GROUP + b
            return wide[pl.ds(first, SUB, stride=STRIDE), :]

        def total(first, count):
            window = [take(first + b) for b in range(count + TAPS - 1)]
            out = [taps[0] * window[b] for b in range(count)]
            for t in range(1, TAPS):
                out = [out[b] + taps[t] * window[b + t] for b in range(count)]
            return out

        extra = total(STEP, 1)[0]
        for first in range(0, STEP, SUB):
            out = total(first, SUB)
            for b in range(SUB):
                past = first + b - (STEP - SUB + 1)
                if past >= 0:
                    out[b] = jnp.where(last, pltpu.roll(extra, SUB - 1 - past, 0), out[b])
            for b in range(0, SUB, 2):
                both = jnp.concatenate(out[b : b + 2], axis=0).astype(jnp.bfloat16)
                fir[i, pl.ds(g * GROUP + (first + b) * SUB, 2 * SUB), cols] = both

    def transform(g, i):
        part = pl.ds(g * GROUP, GROUP)
        spectra[g, i] = lax.dot_general(
            table[...],
            fir[i, part, :],
            (((1,), (1,)), ((), ())),
            preferred_element_type=jnp.float32,
        )

    def pack(g, piece):
        place = pl.ds(piece * rows, rows)
        shape = (rows // (2 * SUB), 2, SUB, GROUP)
        parts = [spectra[g, i, place, :].reshape(shape) for i in range(inputs)]
        for p in range(2):
            both = jnp.concatenate([part[:, p] for part in parts], axis=1)
            cols = pl.ds(p * SPEC + g * GROUP, GROUP)
            result[place, cols] = both.astype(jnp.bfloat16).reshape(rows, GROUP)

    def store(g, piece):
        copies = []
        for p in range(2):
            place = (pl.ds(piece * rows, rows), pl.ds(p * SPEC + g * GROUP, GROUP))
            sem = sems.at[g, piece, p]
            copies.append(pltpu.make_async_copy(result.at[place], out_hbm.at[place], sem))
            copies[-1].start()
        return copies

    loads[0].wait()
    convert(0)
    load_taps.wait()
    load_flags.wait()
    loads[1].wait()
    load_table = load(table_hbm, table, chunks + 1)
    convert(1)
    for i in range(inputs):
        for j in range(FRAME // LANES):
            filter_group(0, i, j)
    loads[2].wait()
    load_table.wait()
    for i in range(inputs):
        transform(0, i)
    convert(2)
    for i in range(inputs):
        if i > 0:
            transform(1, i - 1)
        for j in range(FRAME // LANES):
            filter_group(1, i, j)
        if i == 0:
            for piece in range(pieces):
                pack(0, piece)
    copies = []
    for piece in range(pieces):
        copies += store(0, piece)
    transform(1, inputs - 1)
    for piece in range(pieces):
        pack(1, piece)
        copies += store(1, piece)
    for copy in copies:
        copy.wait()


def channelize(samples, flags, far, near, blocks):
    inputs = samples.shape[0]
    tiles = samples.reshape(inputs, -1, LANES)
    tiles = with_layout_constraint(tiles, Layout(major_to_minor=(1, 0, 2)))
    tiles = tiles.transpose(1, 0, 2)
    tiles = tiles.reshape(-1, LANES)
    table = twiddle().reshape(far, near, blocks, SUB, 2, FRAME).transpose(2, 1, 0, 4, 3, 5)
    table = jnp.asarray(table.reshape(FRAME, FRAME), dtype=jnp.bfloat16)
    taps = jnp.asarray(prototype())
    hbm = pl.BlockSpec(memory_space=pltpu.HBM)
    return pl.pallas_call(
        channelize_kernel,
        out_shape=jax.ShapeDtypeStruct((FRAME, inputs * SPEC), jnp.bfloat16),
        in_specs=[hbm] * 4,
        out_specs=hbm,
        scratch_shapes=[
            pltpu.SMEM(flags.shape, flags.dtype),
            pltpu.VMEM(taps.shape, taps.dtype),
            pltpu.VMEM(table.shape, table.dtype),
            pltpu.VMEM(tiles.shape, tiles.dtype),
            pltpu.VMEM((inputs * FRAME // LANES * PITCH, LANES), jnp.float32),
            pltpu.VMEM((inputs, SPEC, FRAME), jnp.bfloat16),
            pltpu.VMEM((SPEC // GROUP, inputs, FRAME, GROUP), jnp.float32),
            pltpu.VMEM((FRAME, inputs * SPEC), jnp.bfloat16),
            pltpu.SemaphoreType.DMA((SPEC // GROUP + 4,)),
            pltpu.SemaphoreType.DMA((SPEC // GROUP, 4, 2)),
        ],
        cost_estimate=pl.CostEstimate(
            flops=2 * inputs * SPEC * FRAME * (FRAME + TAPS),
            bytes_accessed=4 * inputs * SPEC * FRAME,
            transcendentals=0,
        ),
    )(flags, tiles, taps, table)


def correlate_kernel(pick_ref, arrived_ref, own_ref, other_ref, slots):
    share, block, _ = own_ref.shape
    blocks = pick_ref.shape[0]
    width = blocks * block
    held = arrived_ref.shape[0] // blocks
    first = lax.axis_index("blk") == 0
    lane = lax.broadcasted_iota(jnp.int32, (width, 2 * width), 1)
    sign = jnp.where(lane < width, 1.0, -1.0)
    diagonal = lane == lax.broadcasted_iota(jnp.int32, (width, 2 * width), 0)
    for n in range(blocks):
        rows = pl.ds(n * held, held)
        slots[n] = jnp.dot(
            pick_ref[n], arrived_ref[rows, :], preferred_element_type=jnp.float32
        ).astype(jnp.bfloat16)
    for k in range(share):
        pair = jnp.concatenate(
            [
                slots[n, pl.ds(k * block, block), pl.ds(p * SPEC, SPEC)]
                for p in range(2)
                for n in range(blocks)
            ],
            axis=0,
        )
        gram = lax.dot_general(
            pair, pair, (((1,), (1,)), ((), ())), preferred_element_type=jnp.float32
        )
        part = gram[:width] * sign + pltpu.roll(gram[width:], width, 1)
        square = jnp.where(diagonal, part, 0.0)
        across = jnp.sum(square, axis=0, keepdims=True)
        across = across + pltpu.roll(across, width, 1)
        down = jnp.sum(square, axis=1, keepdims=True)
        part = part * (1.0 / jnp.sqrt(across / SPEC + 1e-05) / SPEC)
        part = part * (1.0 / jnp.sqrt(down / SPEC + 1e-05))
        own_ref[k] = jnp.where(first, part[:block], part[block:])
        other_ref[k] = jnp.where(first, part[block:], part[:block])


def picks(orders, inputs, far, near, share):
    blocks, block = orders.shape
    device, held = orders // inputs, orders % inputs
    place = (device % near) * far + device // near
    start = ((place * inputs + held) * share)[:, None, :]
    chan = jnp.arange(share, dtype=jnp.int32)[:, None]
    target = (start + chan).reshape(blocks, share * block, 1)
    column = lax.broadcasted_iota(jnp.int32, (1, 1, far * near * inputs * share), 2)
    return (column == target).astype(jnp.bfloat16)


def correlate(arrived, pick, share, block):
    blocks = pick.shape[0]
    vmem = pl.BlockSpec(memory_space=pltpu.VMEM)
    tile = jax.ShapeDtypeStruct((share, block, 2 * blocks * block), jnp.float32)
    return pl.pallas_call(
        correlate_kernel,
        out_shape=(tile, tile),
        in_specs=[vmem, vmem],
        out_specs=(vmem, vmem),
        scratch_shapes=[pltpu.VMEM((blocks, share * block, 2 * SPEC), jnp.bfloat16)],
        compiler_params=pltpu.CompilerParams(vmem_limit_bytes=VMEM_LIMIT),
        cost_estimate=pl.CostEstimate(
            flops=4 * pick.size * SPEC, bytes_accessed=4 * arrived.size, transcendentals=0
        ),
    )(pick, arrived)


def place_kernel(packed_ref, *refs, own):
    out_ref, parts, sems = refs[-3:]
    share, _, _, width = parts.shape
    me = lax.axis_index("blk")
    start = (me if own else 1 - me) * share
    copies = []
    count = share // sems.shape[0]
    for n in range(sems.shape[0]):
        for k in range(n * count, (n + 1) * count):
            parts[k, 0] = packed_ref[k, :, :width]
            parts[k, 1] = packed_ref[k, :, width:]
        target = out_ref.at[pl.ds(start + n * count, count)]
        copies.append(pltpu.make_async_copy(parts.at[pl.ds(n * count, count)], target, sems.at[n]))
        copies[-1].start()
    for copy in copies:
        copy.wait()


def place(packed, blocks, base=None):
    share, block, lanes = packed.shape
    width = lanes // 2
    anywhere = pl.BlockSpec(memory_space=pl.ANY)
    return pl.pallas_call(
        functools.partial(place_kernel, own=base is None),
        out_shape=jax.ShapeDtypeStruct((blocks * share, 2, block, width), packed.dtype),
        in_specs=[pl.BlockSpec(memory_space=pltpu.VMEM)] + ([] if base is None else [anywhere]),
        out_specs=anywhere,
        scratch_shapes=[
            pltpu.VMEM((share, 2, block, width), packed.dtype),
            pltpu.SemaphoreType.DMA((2,)),
        ],
        input_output_aliases={} if base is None else {1: 0},
        compiler_params=pltpu.CompilerParams(vmem_limit_bytes=VMEM_LIMIT),
        cost_estimate=pl.CostEstimate(flops=0, bytes_accessed=8 * packed.size, transcendentals=0),
    )(packed, *([] if base is None else [base]))


def split_channels(far, near, blocks, samples, slot_order, flags):
    share = CH // (far * near * blocks)
    inputs, block = samples.shape[0], slot_order.shape[1]
    axes = ("blk", "near", "far")
    me = lax.axis_index("blk").astype(jnp.int32)
    partner = lax.ppermute(slot_order, "blk", SWAP)
    orders = jnp.where(
        me == 0,
        jnp.concatenate([slot_order, partner]),
        jnp.concatenate([partner, slot_order]),
    )
    sent = channelize(samples, flags, far, near, blocks)
    arrived = lax.all_to_all(sent, axes, split_axis=0, concat_axis=0, tiled=True)
    pick = picks(orders, inputs, far, near, share)
    own, other = correlate(arrived, pick, share, block)
    received = lax.ppermute(other, "blk", SWAP)
    return place(received, blocks, place(own, blocks))


def gather_blocks(freq, samples, slot_order, flags):
    inputs = samples.shape[0]
    taps = jnp.asarray(prototype())
    table = jnp.asarray(twiddle().reshape(2 * CH, FRAME), dtype=jnp.bfloat16)
    good = (1 - flags).astype(jnp.float32)
    frames = samples.reshape(inputs, SPEC + TAPS - 1, FRAME)
    total = jnp.zeros((inputs, SPEC, FRAME), jnp.float32)
    for tap in range(TAPS):
        window = frames[:, tap : tap + SPEC, :].astype(jnp.float32)
        total = total + taps[tap][None, None, :] * window
    fir = total.astype(jnp.bfloat16)
    spectra = jnp.einsum("kn,isn->kis", table, fir, preferred_element_type=jnp.float32)
    squares = jnp.sum(spectra * spectra, axis=2)
    power = jnp.sum(squares.reshape(CH, 2, inputs), axis=1) / SPEC
    scale = good[None, :] / jnp.sqrt(power + 1e-05)
    quantized = (spectra * jnp.repeat(scale, 2, axis=0)[:, :, None]).astype(jnp.bfloat16)
    arrived = lax.all_to_all(quantized, ("far", "near"), split_axis=0, concat_axis=1, tiled=True)
    share = CH // freq
    block = slot_order.shape[1]
    own = jnp.take(arrived.reshape(share, 2, block, SPEC), slot_order[0], axis=2)
    piece = lax.all_gather(own, "blk", axis=2, tiled=True)
    dot = functools.partial(jnp.einsum, "cas,cbs->cab", preferred_element_type=jnp.float32)
    real = dot(own[:, 0], piece[:, 0]) + dot(own[:, 1], piece[:, 1])
    imag = dot(own[:, 1], piece[:, 0]) - dot(own[:, 0], piece[:, 1])
    return jnp.stack([real / SPEC, imag / SPEC], axis=1)


def solution(mesh):
    freq, blocks = mesh.shape["freq"], mesh.shape["blk"]
    far = math.gcd(freq, FAR)
    near = freq // far
    split = Mesh(mesh.devices.reshape(far, near, blocks), ("far", "near", "blk"))

    def body(samples, slot_order, flags):
        if blocks == 2 and CH == SUB * freq * blocks:
            return split_channels(far, near, blocks, samples, slot_order, flags)
        return gather_blocks(freq, samples, slot_order, flags)

    held = ("blk", "far", "near")
    in_specs = (P(held, None), P("blk", None), P(held))
    out_specs = P(("far", "near"), None, "blk", None)
    return jax.shard_map(body, mesh=split, in_specs=in_specs, out_specs=out_specs, check_vma=False)
```

```python
import functools
import math

import jax
import jax.numpy as jnp
import numpy as np
from jax import lax
from jax.experimental import pallas as pl
from jax.experimental.pallas import tpu as pltpu
from jax.experimental.layout import Layout, with_layout_constraint
from jax.sharding import Mesh
from jax.sharding import PartitionSpec as P

CH = 256
TAPS = 12
SPEC = 512
FRAME = 2 * CH
LANES = 128
SUB = 8
GROUP = 256
STEP = GROUP // SUB
STRIDE = STEP + 1
PITCH = SPEC + 25
FAR = 4
SWAP = [(0, 1), (1, 0)]
VMEM_LIMIT = 40 * 1024 * 1024


def prototype():
    count = TAPS * FRAME
    index = np.arange(count, dtype=np.float64)
    shifted = (index + 0.5) / FRAME - TAPS / 2.0
    window = 0.5 - 0.5 * np.cos(2.0 * math.pi * (index + 0.5) / count)
    return (np.sinc(shifted) * window).astype(np.float32).reshape(TAPS, FRAME)


def twiddle():
    chan = np.arange(CH, dtype=np.int64)[:, None]
    point = np.arange(FRAME, dtype=np.int64)[None, :]
    phase = (chan * point % FRAME).astype(np.float64) * (2.0 * math.pi / FRAME)
    return np.stack([np.cos(phase), -np.sin(phase)], axis=1).astype(np.float32)


def channelize_kernel(
    flags_hbm,
    x_hbm,
    taps_hbm,
    table_hbm,
    out_hbm,
    flags,
    taps_all,
    table,
    held,
    wide,
    fir,
    spectra,
    scales,
    result,
    load_sems,
    sems,
):
    inputs = fir.shape[0]
    frames = SPEC + TAPS - 1
    spread = inputs * FRAME // LANES
    groups = SPEC // GROUP
    pieces = sems.shape[0]
    rows = FRAME // pieces
    last = lax.broadcasted_iota(jnp.int32, (SUB, LANES), 0) == SUB - 1
    edges = [0, GROUP // 2] + [g * GROUP + TAPS for g in range(1, groups)] + [frames]

    def load(source, target, n):
        copy = pltpu.make_async_copy(source, target, load_sems.at[n])
        copy.start()
        return copy

    def span(n):
        return pl.ds(edges[n] * spread, (edges[n + 1] - edges[n]) * spread)

    chunks = len(edges) - 1
    loads = [load(x_hbm.at[span(n)], held.at[span(n)], n) for n in range(chunks)]
    load_taps = load(taps_hbm, taps_all, chunks)
    load_flags = load(flags_hbm, flags, chunks + 2)

    def convert(n):
        for f in range(edges[n], edges[n + 1], 2):
            count = min(2, frames - f)
            tile = held[pl.ds(f * spread, count * spread), :].astype(jnp.float32)
            for c in range(count):
                part = tile[c * spread : (c + 1) * spread]
                wide[pl.ds(f + c, spread, stride=PITCH), :] = part

    def filter_group(g, i, j):
        cols = pl.ds(j * LANES, LANES)
        taps = [jnp.broadcast_to(taps_all[pl.ds(t, 1), cols], (SUB, LANES)) for t in range(TAPS)]

        def take(b):
            first = (inputs * j + i) * PITCH + g * GROUP + b
            return wide[pl.ds(first, SUB, stride=STRIDE), :]

        def total(first, count):
            window = [take(first + b) for b in range(count + TAPS - 1)]
            out = [taps[0] * window[b] for b in range(count)]
            for t in range(1, TAPS):
                out = [out[b] + taps[t] * window[b + t] for b in range(count)]
            return out

        extra = total(STEP, 1)[0]
        for first in range(0, STEP, SUB):
            out = total(first, SUB)
            for b in range(SUB):
                past = first + b - (STEP - SUB + 1)
                if past >= 0:
                    out[b] = jnp.where(last, pltpu.roll(extra, SUB - 1 - past, 0), out[b])
            for b in range(0, SUB, 2):
                both = jnp.concatenate(out[b : b + 2], axis=0).astype(jnp.bfloat16)
                fir[i, pl.ds(g * GROUP + (first + b) * SUB, 2 * SUB), cols] = both

    def transform(g, i):
        part = pl.ds(g * GROUP, GROUP)
        spectra[i, :, part] = lax.dot_general(
            table[...],
            fir[i, part, :],
            (((1,), (1,)), ((), ())),
            preferred_element_type=jnp.float32,
        )

    def rate(i):
        good = (1 - flags[i]).astype(jnp.float32)
        for piece in range(pieces):
            pairs = spectra[i, pl.ds(piece * rows, rows), :]
            pairs = pairs.reshape(rows // (2 * SUB), 2, SUB, SPEC)
            squares = jnp.sum(pairs * pairs, axis=1)
            power = jnp.sum(squares, axis=2, keepdims=True) / SPEC
            scale = good / jnp.sqrt(power + 1e-05)
            place = pl.ds(piece * rows // 2, rows // 2)
            scales[i, place, :] = jnp.broadcast_to(scale.reshape(rows // 2, 1), (rows // 2, LANES))

    def scaled(i, piece):
        pairs = spectra[i, pl.ds(piece * rows, rows), :]
        pairs = pairs.reshape(rows // (2 * SUB), 2, SUB, SPEC)
        scale = scales[i, pl.ds(piece * rows // 2, rows // 2), :]
        scale = jnp.concatenate([scale] * (SPEC // LANES), axis=1)
        return pairs * scale.reshape(rows // (2 * SUB), 1, SUB, SPEC)

    def pack(piece):
        place = pl.ds(piece * rows, rows)
        parts = [scaled(i, piece) for i in range(inputs)]
        for p in range(2):
            both = jnp.concatenate([part[:, p] for part in parts], axis=1)
            result[place, pl.ds(p * SPEC, SPEC)] = both.astype(jnp.bfloat16).reshape(rows, SPEC)
        copy = pltpu.make_async_copy(result.at[place], out_hbm.at[place], sems.at[piece])
        copy.start()
        return copy

    loads[0].wait()
    convert(0)
    load_taps.wait()
    loads[1].wait()
    load_table = load(table_hbm, table, chunks + 1)
    convert(1)
    for i in range(inputs):
        for j in range(FRAME // LANES):
            filter_group(0, i, j)
    loads[2].wait()
    load_table.wait()
    load_flags.wait()
    for i in range(inputs):
        transform(0, i)
    convert(2)
    for i in range(inputs):
        if i > 0:
            transform(1, i - 1)
        for j in range(FRAME // LANES):
            filter_group(1, i, j)
    transform(1, inputs - 1)
    for i in range(inputs):
        rate(i)
    copies = [pack(piece) for piece in range(pieces)]
    for copy in copies:
        copy.wait()


def channelize(samples, flags, far, near, blocks):
    inputs = samples.shape[0]
    tiles = samples.reshape(inputs, -1, LANES)
    tiles = with_layout_constraint(tiles, Layout(major_to_minor=(1, 0, 2)))
    tiles = tiles.transpose(1, 0, 2)
    tiles = tiles.reshape(-1, LANES)
    table = twiddle().reshape(far, near, blocks, SUB, 2, FRAME).transpose(2, 1, 0, 4, 3, 5)
    table = table.reshape(far * near * blocks, 2 * SUB, FRAME)[::-1]
    table = jnp.asarray(table.reshape(FRAME, FRAME), dtype=jnp.bfloat16)
    taps = jnp.asarray(prototype())
    hbm = pl.BlockSpec(memory_space=pltpu.HBM)
    return pl.pallas_call(
        channelize_kernel,
        out_shape=jax.ShapeDtypeStruct((FRAME, inputs * SPEC), jnp.bfloat16),
        in_specs=[hbm] * 4,
        out_specs=hbm,
        scratch_shapes=[
            pltpu.SMEM(flags.shape, flags.dtype),
            pltpu.VMEM(taps.shape, taps.dtype),
            pltpu.VMEM(table.shape, table.dtype),
            pltpu.VMEM(tiles.shape, tiles.dtype),
            pltpu.VMEM((inputs * FRAME // LANES * PITCH, LANES), jnp.float32),
            pltpu.VMEM((inputs, SPEC, FRAME), jnp.bfloat16),
            pltpu.VMEM((inputs, FRAME, SPEC), jnp.float32),
            pltpu.VMEM((inputs, CH, LANES), jnp.float32),
            pltpu.VMEM((FRAME, inputs * SPEC), jnp.bfloat16),
            pltpu.SemaphoreType.DMA((SPEC // GROUP + 4,)),
            pltpu.SemaphoreType.DMA((8,)),
        ],
        cost_estimate=pl.CostEstimate(
            flops=2 * inputs * SPEC * FRAME * (FRAME + TAPS),
            bytes_accessed=4 * inputs * SPEC * FRAME,
            transcendentals=0,
        ),
    )(flags, tiles, taps, table)


def correlate_kernel(pick_ref, arrived_ref, own_ref, other_ref, slots):
    share, block, _ = own_ref.shape
    blocks = pick_ref.shape[0]
    width = blocks * block
    held = arrived_ref.shape[0] // blocks
    first = lax.axis_index("blk") == 0
    lane = lax.broadcasted_iota(jnp.int32, (width, 2 * width), 1)
    sign = jnp.where(lane < width, 1.0 / SPEC, -1.0 / SPEC)
    for n in range(blocks):
        rows = pl.ds((blocks - 1 - n) * held, held)
        slots[n] = jnp.dot(
            pick_ref[n], arrived_ref[rows, :], preferred_element_type=jnp.float32
        ).astype(jnp.bfloat16)
    for k in range(share):
        pair = jnp.concatenate(
            [
                slots[n, pl.ds(k * block, block), pl.ds(p * SPEC, SPEC)]
                for p in range(2)
                for n in range(blocks)
            ],
            axis=0,
        )
        gram = lax.dot_general(
            pair, pair, (((1,), (1,)), ((), ())), preferred_element_type=jnp.float32
        )
        part = gram[:width] * sign + pltpu.roll(gram[width:], width, 1) / SPEC
        own_ref[k] = jnp.where(first, part[:block], part[block:])
        other_ref[k] = jnp.where(first, part[block:], part[:block])


def picks(orders, inputs, far, near, share):
    blocks, block = orders.shape
    device, held = orders // inputs, orders % inputs
    place = far * near - 1 - ((device % near) * far + device // near)
    start = ((place * inputs + held) * share)[:, None, :]
    chan = jnp.arange(share, dtype=jnp.int32)[:, None]
    target = (start + chan).reshape(blocks, share * block, 1)
    column = lax.broadcasted_iota(jnp.int32, (1, 1, far * near * inputs * share), 2)
    return (column == target).astype(jnp.bfloat16)


def correlate(arrived, pick, share, block):
    blocks = pick.shape[0]
    vmem = pl.BlockSpec(memory_space=pltpu.VMEM)
    tile = jax.ShapeDtypeStruct((share, block, 2 * blocks * block), jnp.float32)
    return pl.pallas_call(
        correlate_kernel,
        out_shape=(tile, tile),
        in_specs=[vmem, vmem],
        out_specs=(vmem, vmem),
        scratch_shapes=[pltpu.VMEM((blocks, share * block, 2 * SPEC), jnp.bfloat16)],
        compiler_params=pltpu.CompilerParams(vmem_limit_bytes=VMEM_LIMIT),
        cost_estimate=pl.CostEstimate(
            flops=4 * pick.size * SPEC, bytes_accessed=4 * arrived.size, transcendentals=0
        ),
    )(pick, arrived)


def place_kernel(packed_ref, *refs, own):
    out_ref, parts, sems = refs[-3:]
    share, _, _, width = parts.shape
    me = lax.axis_index("blk")
    start = (me if own else 1 - me) * share
    copies = []
    count = share // sems.shape[0]
    for n in range(sems.shape[0]):
        for k in range(n * count, (n + 1) * count):
            parts[k, 0] = packed_ref[k, :, :width]
            parts[k, 1] = packed_ref[k, :, width:]
        target = out_ref.at[pl.ds(start + n * count, count)]
        copies.append(pltpu.make_async_copy(parts.at[pl.ds(n * count, count)], target, sems.at[n]))
        copies[-1].start()
    for copy in copies:
        copy.wait()


def place(packed, blocks, base=None):
    share, block, lanes = packed.shape
    width = lanes // 2
    anywhere = pl.BlockSpec(memory_space=pl.ANY)
    return pl.pallas_call(
        functools.partial(place_kernel, own=base is None),
        out_shape=jax.ShapeDtypeStruct((blocks * share, 2, block, width), packed.dtype),
        in_specs=[pl.BlockSpec(memory_space=pltpu.VMEM)] + ([] if base is None else [anywhere]),
        out_specs=anywhere,
        scratch_shapes=[
            pltpu.VMEM((share, 2, block, width), packed.dtype),
            pltpu.SemaphoreType.DMA((2,)),
        ],
        input_output_aliases={} if base is None else {1: 0},
        compiler_params=pltpu.CompilerParams(vmem_limit_bytes=VMEM_LIMIT),
        cost_estimate=pl.CostEstimate(flops=0, bytes_accessed=8 * packed.size, transcendentals=0),
    )(packed, *([] if base is None else [base]))


def split_channels(far, near, blocks, samples, slot_order, flags):
    share = CH // (far * near * blocks)
    inputs, block = samples.shape[0], slot_order.shape[1]
    axes = ("blk", "near", "far")
    me = lax.axis_index("blk").astype(jnp.int32)
    partner = lax.ppermute(slot_order, "blk", SWAP)
    orders = jnp.where(
        me == 0,
        jnp.concatenate([slot_order, partner]),
        jnp.concatenate([partner, slot_order]),
    )
    sent = channelize(samples, flags, far, near, blocks)
    order = list(reversed(range(blocks * near * far)))
    arrived = lax.all_to_all(
        sent, axes, split_axis=0, concat_axis=0, axis_index_groups=[order], tiled=True
    )
    pick = picks(orders, inputs, far, near, share)
    own, other = correlate(arrived, pick, share, block)
    received = lax.ppermute(other, "blk", SWAP)
    return place(received, blocks, place(own, blocks))


def gather_blocks(freq, samples, slot_order, flags):
    inputs = samples.shape[0]
    taps = jnp.asarray(prototype())
    table = jnp.asarray(twiddle().reshape(2 * CH, FRAME), dtype=jnp.bfloat16)
    good = (1 - flags).astype(jnp.float32)
    frames = samples.reshape(inputs, SPEC + TAPS - 1, FRAME)
    total = jnp.zeros((inputs, SPEC, FRAME), jnp.float32)
    for tap in range(TAPS):
        window = frames[:, tap : tap + SPEC, :].astype(jnp.float32)
        total = total + taps[tap][None, None, :] * window
    fir = total.astype(jnp.bfloat16)
    spectra = jnp.einsum("kn,isn->kis", table, fir, preferred_element_type=jnp.float32)
    squares = jnp.sum(spectra * spectra, axis=2)
    power = jnp.sum(squares.reshape(CH, 2, inputs), axis=1) / SPEC
    scale = good[None, :] / jnp.sqrt(power + 1e-05)
    quantized = (spectra * jnp.repeat(scale, 2, axis=0)[:, :, None]).astype(jnp.bfloat16)
    arrived = lax.all_to_all(quantized, ("far", "near"), split_axis=0, concat_axis=1, tiled=True)
    share = CH // freq
    block = slot_order.shape[1]
    own = jnp.take(arrived.reshape(share, 2, block, SPEC), slot_order[0], axis=2)
    piece = lax.all_gather(own, "blk", axis=2, tiled=True)
    dot = functools.partial(jnp.einsum, "cas,cbs->cab", preferred_element_type=jnp.float32)
    real = dot(own[:, 0], piece[:, 0]) + dot(own[:, 1], piece[:, 1])
    imag = dot(own[:, 1], piece[:, 0]) - dot(own[:, 0], piece[:, 1])
    return jnp.stack([real / SPEC, imag / SPEC], axis=1)


def solution(mesh):
    freq, blocks = mesh.shape["freq"], mesh.shape["blk"]
    far = math.gcd(freq, FAR)
    near = freq // far
    split = Mesh(mesh.devices.reshape(far, near, blocks), ("far", "near", "blk"))

    def body(samples, slot_order, flags):
        if blocks == 2 and CH == SUB * freq * blocks:
            return split_channels(far, near, blocks, samples, slot_order, flags)
        return gather_blocks(freq, samples, slot_order, flags)

    held = ("blk", "far", "near")
    in_specs = (P(held, None), P("blk", None), P(held))
    out_specs = P(("far", "near"), None, "blk", None)
    return jax.shard_map(body, mesh=split, in_specs=in_specs, out_specs=out_specs, check_vma=False)
```

```python
import functools
import math

import jax
import jax.numpy as jnp
import numpy as np
from jax import lax
from jax.experimental import pallas as pl
from jax.experimental.pallas import tpu as pltpu
from jax.experimental.layout import Layout, with_layout_constraint
from jax.sharding import PartitionSpec as P

CH = 256
TAPS = 12
SPEC = 512
FRAME = 2 * CH
LANES = 128
SUB = 8
GROUP = 256
STEP = GROUP // SUB
STRIDE = STEP + 1
PITCH = SPEC + 25
SWAP = [(0, 1), (1, 0)]
VMEM_LIMIT = 40 * 1024 * 1024


def prototype():
    count = TAPS * FRAME
    index = np.arange(count, dtype=np.float64)
    shifted = (index + 0.5) / FRAME - TAPS / 2.0
    window = 0.5 - 0.5 * np.cos(2.0 * math.pi * (index + 0.5) / count)
    return (np.sinc(shifted) * window).astype(np.float32).reshape(TAPS, FRAME)


def twiddle():
    chan = np.arange(CH, dtype=np.int64)[:, None]
    point = np.arange(FRAME, dtype=np.int64)[None, :]
    phase = (chan * point % FRAME).astype(np.float64) * (2.0 * math.pi / FRAME)
    return np.stack([np.cos(phase), -np.sin(phase)], axis=1).astype(np.float32)


def channelize_kernel(
    flags_hbm,
    x_hbm,
    taps_hbm,
    table_hbm,
    out_hbm,
    flags,
    taps_all,
    table,
    held,
    wide,
    fir,
    spectra,
    scales,
    result,
    load_sems,
    sems,
):
    inputs = fir.shape[0]
    frames = SPEC + TAPS - 1
    spread = inputs * FRAME // LANES
    groups = SPEC // GROUP
    pieces = sems.shape[0]
    rows = FRAME // pieces
    last = lax.broadcasted_iota(jnp.int32, (SUB, LANES), 0) == SUB - 1
    edges = [0, GROUP // 2] + [g * GROUP + TAPS for g in range(1, groups)] + [frames]

    def load(source, target, n):
        copy = pltpu.make_async_copy(source, target, load_sems.at[n])
        copy.start()
        return copy

    def span(n):
        return pl.ds(edges[n] * spread, (edges[n + 1] - edges[n]) * spread)

    chunks = len(edges) - 1
    loads = [load(x_hbm.at[span(n)], held.at[span(n)], n) for n in range(chunks)]
    load_taps = load(taps_hbm, taps_all, chunks)
    load_flags = load(flags_hbm, flags, chunks + 2)

    def convert(n):
        for f in range(edges[n], edges[n + 1], 2):
            count = min(2, frames - f)
            tile = held[pl.ds(f * spread, count * spread), :].astype(jnp.float32)
            for c in range(count):
                part = tile[c * spread : (c + 1) * spread]
                wide[pl.ds(f + c, spread, stride=PITCH), :] = part

    def filter_group(g, i, j):
        cols = pl.ds(j * LANES, LANES)
        taps = [jnp.broadcast_to(taps_all[pl.ds(t, 1), cols], (SUB, LANES)) for t in range(TAPS)]

        def take(b):
            first = (inputs * j + i) * PITCH + g * GROUP + b
            return wide[pl.ds(first, SUB, stride=STRIDE), :]

        def total(first, count):
            window = [take(first + b) for b in range(count + TAPS - 1)]
            out = [taps[0] * window[b] for b in range(count)]
            for t in range(1, TAPS):
                out = [out[b] + taps[t] * window[b + t] for b in range(count)]
            return out

        extra = total(STEP, 1)[0]
        for first in range(0, STEP, SUB):
            out = total(first, SUB)
            for b in range(SUB):
                past = first + b - (STEP - SUB + 1)
                if past >= 0:
                    out[b] = jnp.where(last, pltpu.roll(extra, SUB - 1 - past, 0), out[b])
            for b in range(0, SUB, 2):
                both = jnp.concatenate(out[b : b + 2], axis=0).astype(jnp.bfloat16)
                fir[i, pl.ds(g * GROUP + (first + b) * SUB, 2 * SUB), cols] = both

    def transform(g, i):
        part = pl.ds(g * GROUP, GROUP)
        spectra[i, :, part] = lax.dot_general(
            table[...],
            fir[i, part, :],
            (((1,), (1,)), ((), ())),
            preferred_element_type=jnp.float32,
        )

    def rate(i):
        good = (1 - flags[i]).astype(jnp.float32)
        for piece in range(pieces):
            pairs = spectra[i, pl.ds(piece * rows, rows), :]
            pairs = pairs.reshape(rows // (2 * SUB), 2, SUB, SPEC)
            squares = jnp.sum(pairs * pairs, axis=1)
            power = jnp.sum(squares, axis=2, keepdims=True) / SPEC
            scale = good / jnp.sqrt(power + 1e-05)
            place = pl.ds(piece * rows // 2, rows // 2)
            scales[i, place, :] = jnp.broadcast_to(scale.reshape(rows // 2, 1), (rows // 2, LANES))

    def scaled(i, piece):
        pairs = spectra[i, pl.ds(piece * rows, rows), :]
        pairs = pairs.reshape(rows // (2 * SUB), 2, SUB, SPEC)
        scale = scales[i, pl.ds(piece * rows // 2, rows // 2), :]
        scale = jnp.concatenate([scale] * (SPEC // LANES), axis=1)
        return pairs * scale.reshape(rows // (2 * SUB), 1, SUB, SPEC)

    def pack(piece):
        place = pl.ds(piece * rows, rows)
        parts = [scaled(i, piece) for i in range(inputs)]
        for p in range(2):
            both = jnp.concatenate([part[:, p] for part in parts], axis=1)
            result[place, pl.ds(p * SPEC, SPEC)] = both.astype(jnp.bfloat16).reshape(rows, SPEC)
        copy = pltpu.make_async_copy(result.at[place], out_hbm.at[place], sems.at[piece])
        copy.start()
        return copy

    loads[0].wait()
    convert(0)
    load_taps.wait()
    loads[1].wait()
    load_table = load(table_hbm, table, chunks + 1)
    convert(1)
    for i in range(inputs):
        for j in range(FRAME // LANES):
            filter_group(0, i, j)
    loads[2].wait()
    load_table.wait()
    load_flags.wait()
    for i in range(inputs):
        transform(0, i)
    convert(2)
    for i in range(inputs):
        if i > 0:
            transform(1, i - 1)
        for j in range(FRAME // LANES):
            filter_group(1, i, j)
    transform(1, inputs - 1)
    for i in range(inputs):
        rate(i)
    copies = [pack(piece) for piece in range(pieces)]
    for copy in copies:
        copy.wait()


def channelize(samples, flags, order):
    inputs = samples.shape[0]
    tiles = samples.reshape(inputs, -1, LANES)
    tiles = with_layout_constraint(tiles, Layout(major_to_minor=(1, 0, 2)))
    tiles = tiles.transpose(1, 0, 2)
    tiles = tiles.reshape(-1, LANES)
    table = twiddle().reshape(len(order), SUB, 2, FRAME)[np.asarray(order)].transpose(0, 2, 1, 3)
    table = jnp.asarray(table.reshape(FRAME, FRAME), dtype=jnp.bfloat16)
    taps = jnp.asarray(prototype())
    hbm = pl.BlockSpec(memory_space=pltpu.HBM)
    return pl.pallas_call(
        channelize_kernel,
        out_shape=jax.ShapeDtypeStruct((FRAME, inputs * SPEC), jnp.bfloat16),
        in_specs=[hbm] * 4,
        out_specs=hbm,
        scratch_shapes=[
            pltpu.SMEM(flags.shape, flags.dtype),
            pltpu.VMEM(taps.shape, taps.dtype),
            pltpu.VMEM(table.shape, table.dtype),
            pltpu.VMEM(tiles.shape, tiles.dtype),
            pltpu.VMEM((inputs * FRAME // LANES * PITCH, LANES), jnp.float32),
            pltpu.VMEM((inputs, SPEC, FRAME), jnp.bfloat16),
            pltpu.VMEM((inputs, FRAME, SPEC), jnp.float32),
            pltpu.VMEM((inputs, CH, LANES), jnp.float32),
            pltpu.VMEM((FRAME, inputs * SPEC), jnp.bfloat16),
            pltpu.SemaphoreType.DMA((SPEC // GROUP + 4,)),
            pltpu.SemaphoreType.DMA((8,)),
        ],
        cost_estimate=pl.CostEstimate(
            flops=2 * inputs * SPEC * FRAME * (FRAME + TAPS),
            bytes_accessed=4 * inputs * SPEC * FRAME,
            transcendentals=0,
        ),
    )(flags, tiles, taps, table)


def correlate_kernel(pick_ref, arrived_ref, own_ref, other_ref, slots, *, order):
    share, block, _ = own_ref.shape
    blocks = pick_ref.shape[0]
    width = blocks * block
    held = arrived_ref.shape[0] // len(order)
    first = lax.axis_index("blk") == 0
    lane = lax.broadcasted_iota(jnp.int32, (width, 2 * width), 1)
    sign = jnp.where(lane < width, 1.0 / SPEC, -1.0 / SPEC)
    for n in range(blocks):
        places = [place for place, device in enumerate(order) if device % blocks == n]
        rows = [arrived_ref[pl.ds(place * held, held), :] for place in places]
        slots[n] = jnp.dot(
            pick_ref[n], jnp.concatenate(rows, axis=0), preferred_element_type=jnp.float32
        ).astype(jnp.bfloat16)
    for k in range(share):
        pair = jnp.concatenate(
            [
                slots[n, pl.ds(k * block, block), pl.ds(p * SPEC, SPEC)]
                for p in range(2)
                for n in range(blocks)
            ],
            axis=0,
        )
        gram = lax.dot_general(
            pair, pair, (((1,), (1,)), ((), ())), preferred_element_type=jnp.float32
        )
        part = gram[:width] * sign + pltpu.roll(gram[width:], width, 1) / SPEC
        own_ref[k] = jnp.where(first, part[:block], part[block:])
        other_ref[k] = jnp.where(first, part[block:], part[:block])


def picks(orders, inputs, order, share):
    blocks, block = orders.shape
    device, held = orders // inputs, orders % inputs
    rank = [np.argsort([d for d in order if d % blocks == n]) for n in range(blocks)]
    known = jnp.asarray(np.stack(rank), dtype=jnp.int32)
    match = device[:, :, None] == jnp.arange(known.shape[1], dtype=jnp.int32)
    place = jnp.sum(jnp.where(match, known[:, None, :], 0), axis=2)
    start = ((place * inputs + held) * share)[:, None, :]
    chan = jnp.arange(share, dtype=jnp.int32)[:, None]
    target = (start + chan).reshape(blocks, share * block, 1)
    column = lax.broadcasted_iota(jnp.int32, (1, 1, known.shape[1] * inputs * share), 2)
    return (column == target).astype(jnp.bfloat16)


def correlate(arrived, pick, order, share, block):
    blocks = pick.shape[0]
    vmem = pl.BlockSpec(memory_space=pltpu.VMEM)
    tile = jax.ShapeDtypeStruct((share, block, 2 * blocks * block), jnp.float32)
    return pl.pallas_call(
        functools.partial(correlate_kernel, order=order),
        out_shape=(tile, tile),
        in_specs=[vmem, vmem],
        out_specs=(vmem, vmem),
        scratch_shapes=[pltpu.VMEM((blocks, share * block, 2 * SPEC), jnp.bfloat16)],
        compiler_params=pltpu.CompilerParams(vmem_limit_bytes=VMEM_LIMIT),
        cost_estimate=pl.CostEstimate(
            flops=4 * pick.size * SPEC, bytes_accessed=4 * arrived.size, transcendentals=0
        ),
    )(pick, arrived)


def place_kernel(packed_ref, *refs, own):
    out_ref, parts, sems = refs[-3:]
    share, _, _, width = parts.shape
    me = lax.axis_index("blk")
    start = (me if own else 1 - me) * share
    copies = []
    count = share // sems.shape[0]
    for n in range(sems.shape[0]):
        for k in range(n * count, (n + 1) * count):
            parts[k, 0] = packed_ref[k, :, :width]
            parts[k, 1] = packed_ref[k, :, width:]
        target = out_ref.at[pl.ds(start + n * count, count)]
        copies.append(pltpu.make_async_copy(parts.at[pl.ds(n * count, count)], target, sems.at[n]))
        copies[-1].start()
    for copy in copies:
        copy.wait()


def place(packed, blocks, base=None):
    share, block, lanes = packed.shape
    width = lanes // 2
    anywhere = pl.BlockSpec(memory_space=pl.ANY)
    return pl.pallas_call(
        functools.partial(place_kernel, own=base is None),
        out_shape=jax.ShapeDtypeStruct((blocks * share, 2, block, width), packed.dtype),
        in_specs=[pl.BlockSpec(memory_space=pltpu.VMEM)] + ([] if base is None else [anywhere]),
        out_specs=anywhere,
        scratch_shapes=[
            pltpu.VMEM((share, 2, block, width), packed.dtype),
            pltpu.SemaphoreType.DMA((2,)),
        ],
        input_output_aliases={} if base is None else {1: 0},
        compiler_params=pltpu.CompilerParams(vmem_limit_bytes=VMEM_LIMIT),
        cost_estimate=pl.CostEstimate(flops=0, bytes_accessed=8 * packed.size, transcendentals=0),
    )(packed, *([] if base is None else [base]))


def split_channels(freq, blocks, samples, slot_order, flags):
    share = CH // (freq * blocks)
    inputs, block = samples.shape[0], slot_order.shape[1]
    axes = ("freq", "blk")
    order = list(reversed(range(freq * blocks)))
    me = lax.axis_index("blk").astype(jnp.int32)
    partner = lax.ppermute(slot_order, "blk", SWAP)
    orders = jnp.where(
        me == 0,
        jnp.concatenate([slot_order, partner]),
        jnp.concatenate([partner, slot_order]),
    )
    sent = channelize(samples, flags, order)
    arrived = lax.all_to_all(
        sent, axes, split_axis=0, concat_axis=0, axis_index_groups=[order], tiled=True
    )
    pick = picks(orders, inputs, order, share)
    own, other = correlate(arrived, pick, order, share, block)
    received = lax.ppermute(other, "blk", SWAP)
    return place(received, blocks, place(own, blocks))


def gather_blocks(freq, samples, slot_order, flags):
    inputs = samples.shape[0]
    taps = jnp.asarray(prototype())
    table = jnp.asarray(twiddle().reshape(2 * CH, FRAME), dtype=jnp.bfloat16)
    good = (1 - flags).astype(jnp.float32)
    frames = samples.reshape(inputs, SPEC + TAPS - 1, FRAME)
    total = jnp.zeros((inputs, SPEC, FRAME), jnp.float32)
    for tap in range(TAPS):
        window = frames[:, tap : tap + SPEC, :].astype(jnp.float32)
        total = total + taps[tap][None, None, :] * window
    fir = total.astype(jnp.bfloat16)
    spectra = jnp.einsum("kn,isn->kis", table, fir, preferred_element_type=jnp.float32)
    squares = jnp.sum(spectra * spectra, axis=2)
    power = jnp.sum(squares.reshape(CH, 2, inputs), axis=1) / SPEC
    scale = good[None, :] / jnp.sqrt(power + 1e-05)
    quantized = (spectra * jnp.repeat(scale, 2, axis=0)[:, :, None]).astype(jnp.bfloat16)
    arrived = lax.all_to_all(quantized, "freq", split_axis=0, concat_axis=1, tiled=True)
    share = CH // freq
    block = slot_order.shape[1]
    own = jnp.take(arrived.reshape(share, 2, block, SPEC), slot_order[0], axis=2)
    piece = lax.all_gather(own, "blk", axis=2, tiled=True)
    dot = functools.partial(jnp.einsum, "cas,cbs->cab", preferred_element_type=jnp.float32)
    real = dot(own[:, 0], piece[:, 0]) + dot(own[:, 1], piece[:, 1])
    imag = dot(own[:, 1], piece[:, 0]) - dot(own[:, 0], piece[:, 1])
    return jnp.stack([real / SPEC, imag / SPEC], axis=1)


def solution(mesh):
    freq, blocks = mesh.shape["freq"], mesh.shape["blk"]

    def body(samples, slot_order, flags):
        if blocks == 2 and CH == SUB * freq * blocks:
            return split_channels(freq, blocks, samples, slot_order, flags)
        return gather_blocks(freq, samples, slot_order, flags)

    in_specs = (P(("blk", "freq"), None), P("blk", None), P(("blk", "freq")))
    out_specs = P("freq", None, "blk", None)
    return jax.shard_map(body, mesh=mesh, in_specs=in_specs, out_specs=out_specs, check_vma=False)
```

```python
import functools
import math

import jax
import jax.numpy as jnp
import numpy as np
from jax import lax
from jax.experimental import pallas as pl
from jax.experimental.pallas import tpu as pltpu
from jax.experimental.layout import Layout, with_layout_constraint
from jax.sharding import PartitionSpec as P

CH = 256
TAPS = 12
SPEC = 512
FRAME = 2 * CH
LANES = 128
SUB = 8
GROUP = 256
STEP = GROUP // SUB
STRIDE = STEP + 1
PITCH = SPEC + 25
SWAP = [(0, 1), (1, 0)]
VMEM_LIMIT = 40 * 1024 * 1024


def prototype():
    count = TAPS * FRAME
    index = np.arange(count, dtype=np.float64)
    shifted = (index + 0.5) / FRAME - TAPS / 2.0
    window = 0.5 - 0.5 * np.cos(2.0 * math.pi * (index + 0.5) / count)
    return (np.sinc(shifted) * window).astype(np.float32).reshape(TAPS, FRAME)


def twiddle():
    chan = np.arange(CH, dtype=np.int64)[:, None]
    point = np.arange(FRAME, dtype=np.int64)[None, :]
    phase = (chan * point % FRAME).astype(np.float64) * (2.0 * math.pi / FRAME)
    return np.stack([np.cos(phase), -np.sin(phase)], axis=1).astype(np.float32)


def channelize_kernel(
    flags_hbm,
    x_hbm,
    taps_hbm,
    table_hbm,
    out_hbm,
    flags,
    taps_all,
    table,
    held,
    wide,
    fir,
    spectra,
    scales,
    result,
    load_sems,
    sems,
):
    inputs = fir.shape[0]
    frames = SPEC + TAPS - 1
    spread = inputs * FRAME // LANES
    groups = SPEC // GROUP
    pieces = sems.shape[0]
    rows = FRAME // pieces
    last = lax.broadcasted_iota(jnp.int32, (SUB, LANES), 0) == SUB - 1
    edges = [0, GROUP // 2] + [g * GROUP + TAPS for g in range(1, groups)] + [frames]

    def load(source, target, n):
        copy = pltpu.make_async_copy(source, target, load_sems.at[n])
        copy.start()
        return copy

    def span(n):
        return pl.ds(edges[n] * spread, (edges[n + 1] - edges[n]) * spread)

    chunks = len(edges) - 1
    loads = [load(x_hbm.at[span(n)], held.at[span(n)], n) for n in range(chunks)]
    load_taps = load(taps_hbm, taps_all, chunks)
    load_flags = load(flags_hbm, flags, chunks + 2)

    def convert(n):
        for f in range(edges[n], edges[n + 1], 2):
            count = min(2, frames - f)
            tile = held[pl.ds(f * spread, count * spread), :].astype(jnp.float32)
            for c in range(count):
                part = tile[c * spread : (c + 1) * spread]
                wide[pl.ds(f + c, spread, stride=PITCH), :] = part

    def filter_group(g, i, j):
        cols = pl.ds(j * LANES, LANES)
        taps = [jnp.broadcast_to(taps_all[pl.ds(t, 1), cols], (SUB, LANES)) for t in range(TAPS)]

        def take(b):
            first = (inputs * j + i) * PITCH + g * GROUP + b
            return wide[pl.ds(first, SUB, stride=STRIDE), :]

        def total(first, count):
            window = [take(first + b) for b in range(count + TAPS - 1)]
            out = [taps[0] * window[b] for b in range(count)]
            for t in range(1, TAPS):
                out = [out[b] + taps[t] * window[b + t] for b in range(count)]
            return out

        extra = total(STEP, 1)[0]
        for first in range(0, STEP, SUB):
            out = total(first, SUB)
            for b in range(SUB):
                past = first + b - (STEP - SUB + 1)
                if past >= 0:
                    out[b] = jnp.where(last, pltpu.roll(extra, SUB - 1 - past, 0), out[b])
            for b in range(0, SUB, 2):
                both = jnp.concatenate(out[b : b + 2], axis=0).astype(jnp.bfloat16)
                fir[i, pl.ds(g * GROUP + (first + b) * SUB, 2 * SUB), cols] = both

    def transform(g, i):
        part = pl.ds(g * GROUP, GROUP)
        spectra[i, :, part] = lax.dot_general(
            table[...],
            fir[i, part, :],
            (((1,), (1,)), ((), ())),
            preferred_element_type=jnp.float32,
        )

    def rate(i):
        good = (1 - flags[i]).astype(jnp.float32)
        for piece in range(pieces):
            pairs = spectra[i, pl.ds(piece * rows, rows), :]
            pairs = pairs.reshape(rows // (2 * SUB), 2, SUB, SPEC)
            squares = jnp.sum(pairs * pairs, axis=1)
            power = jnp.sum(squares, axis=2, keepdims=True) / SPEC
            scale = good / jnp.sqrt(power + 1e-05)
            place = pl.ds(piece * rows // 2, rows // 2)
            scales[i, place, :] = jnp.broadcast_to(scale.reshape(rows // 2, 1), (rows // 2, LANES))

    def scaled(i, piece):
        pairs = spectra[i, pl.ds(piece * rows, rows), :]
        pairs = pairs.reshape(rows // (2 * SUB), 2, SUB, SPEC)
        scale = scales[i, pl.ds(piece * rows // 2, rows // 2), :]
        scale = jnp.concatenate([scale] * (SPEC // LANES), axis=1)
        return pairs * scale.reshape(rows // (2 * SUB), 1, SUB, SPEC)

    def pack(piece):
        place = pl.ds(piece * rows, rows)
        parts = [scaled(i, piece) for i in range(inputs)]
        for p in range(2):
            both = jnp.concatenate([part[:, p] for part in parts], axis=1)
            result[place, pl.ds(p * SPEC, SPEC)] = both.astype(jnp.bfloat16).reshape(rows, SPEC)
        copy = pltpu.make_async_copy(result.at[place], out_hbm.at[place], sems.at[piece])
        copy.start()
        return copy

    loads[0].wait()
    convert(0)
    load_taps.wait()
    loads[1].wait()
    load_table = load(table_hbm, table, chunks + 1)
    convert(1)
    for i in range(inputs):
        for j in range(FRAME // LANES):
            filter_group(0, i, j)
    loads[2].wait()
    load_table.wait()
    load_flags.wait()
    for i in range(inputs):
        transform(0, i)
    convert(2)
    for i in range(inputs):
        if i > 0:
            transform(1, i - 1)
        for j in range(FRAME // LANES):
            filter_group(1, i, j)
    transform(1, inputs - 1)
    for i in range(inputs):
        rate(i)
    copies = [pack(piece) for piece in range(pieces)]
    for copy in copies:
        copy.wait()


def channelize(samples, flags, order):
    inputs = samples.shape[0]
    tiles = samples.reshape(inputs, -1, LANES)
    tiles = with_layout_constraint(tiles, Layout(major_to_minor=(1, 0, 2)))
    tiles = tiles.transpose(1, 0, 2)
    tiles = tiles.reshape(-1, LANES)
    table = twiddle().reshape(len(order), SUB, 2, FRAME)[np.asarray(order)].transpose(0, 2, 1, 3)
    table = jnp.asarray(table.reshape(FRAME, FRAME), dtype=jnp.bfloat16)
    taps = jnp.asarray(prototype())
    hbm = pl.BlockSpec(memory_space=pltpu.HBM)
    return pl.pallas_call(
        channelize_kernel,
        out_shape=jax.ShapeDtypeStruct((FRAME, inputs * SPEC), jnp.bfloat16),
        in_specs=[hbm] * 4,
        out_specs=hbm,
        scratch_shapes=[
            pltpu.SMEM(flags.shape, flags.dtype),
            pltpu.VMEM(taps.shape, taps.dtype),
            pltpu.VMEM(table.shape, table.dtype),
            pltpu.VMEM(tiles.shape, tiles.dtype),
            pltpu.VMEM((inputs * FRAME // LANES * PITCH, LANES), jnp.float32),
            pltpu.VMEM((inputs, SPEC, FRAME), jnp.bfloat16),
            pltpu.VMEM((inputs, FRAME, SPEC), jnp.float32),
            pltpu.VMEM((inputs, CH, LANES), jnp.float32),
            pltpu.VMEM((FRAME, inputs * SPEC), jnp.bfloat16),
            pltpu.SemaphoreType.DMA((SPEC // GROUP + 4,)),
            pltpu.SemaphoreType.DMA((8,)),
        ],
        cost_estimate=pl.CostEstimate(
            flops=2 * inputs * SPEC * FRAME * (FRAME + TAPS),
            bytes_accessed=4 * inputs * SPEC * FRAME,
            transcendentals=0,
        ),
    )(flags, tiles, taps, table)


def correlate_kernel(pick_ref, arrived_ref, own_ref, other_ref, slots, *, order):
    share, block, _ = own_ref.shape
    blocks = pick_ref.shape[0]
    width = blocks * block
    held = arrived_ref.shape[0] // len(order)
    first = lax.axis_index("blk") == 0
    lane = lax.broadcasted_iota(jnp.int32, (width, 2 * width), 1)
    sign = jnp.where(lane < width, 1.0 / SPEC, -1.0 / SPEC)
    for n in range(blocks):
        places = [place for place, device in enumerate(order) if device % blocks == n]
        rows = [arrived_ref[pl.ds(place * held, held), :] for place in places]
        slots[n] = jnp.dot(
            pick_ref[n], jnp.concatenate(rows, axis=0), preferred_element_type=jnp.float32
        ).astype(jnp.bfloat16)
    for k in range(share):
        pair = jnp.concatenate(
            [
                slots[n, pl.ds(k * block, block), pl.ds(p * SPEC, SPEC)]
                for p in range(2)
                for n in range(blocks)
            ],
            axis=0,
        )
        gram = lax.dot_general(
            pair, pair, (((1,), (1,)), ((), ())), preferred_element_type=jnp.float32
        )
        part = gram[:width] * sign + pltpu.roll(gram[width:], width, 1) / SPEC
        own_ref[k] = jnp.where(first, part[:block], part[block:])
        other_ref[k] = jnp.where(first, part[block:], part[:block])


def picks(orders, inputs, order, share):
    blocks, block = orders.shape
    device, held = orders // inputs, orders % inputs
    rank = [np.argsort([d for d in order if d % blocks == n]) for n in range(blocks)]
    known = jnp.asarray(np.stack(rank), dtype=jnp.int32)
    match = device[:, :, None] == jnp.arange(known.shape[1], dtype=jnp.int32)
    place = jnp.sum(jnp.where(match, known[:, None, :], 0), axis=2)
    start = ((place * inputs + held) * share)[:, None, :]
    chan = jnp.arange(share, dtype=jnp.int32)[:, None]
    target = (start + chan).reshape(blocks, share * block, 1)
    column = lax.broadcasted_iota(jnp.int32, (1, 1, known.shape[1] * inputs * share), 2)
    return (column == target).astype(jnp.bfloat16)


def correlate(arrived, pick, order, share, block):
    blocks = pick.shape[0]
    vmem = pl.BlockSpec(memory_space=pltpu.VMEM)
    tile = jax.ShapeDtypeStruct((share, block, 2 * blocks * block), jnp.float32)
    return pl.pallas_call(
        functools.partial(correlate_kernel, order=order),
        out_shape=(tile, tile),
        in_specs=[vmem, vmem],
        out_specs=(vmem, vmem),
        scratch_shapes=[pltpu.VMEM((blocks, share * block, 2 * SPEC), jnp.bfloat16)],
        compiler_params=pltpu.CompilerParams(vmem_limit_bytes=VMEM_LIMIT),
        cost_estimate=pl.CostEstimate(
            flops=4 * pick.size * SPEC, bytes_accessed=4 * arrived.size, transcendentals=0
        ),
    )(pick, arrived)


def place_kernel(packed_ref, *refs, own):
    out_ref, parts, sems = refs[-3:]
    share, _, _, width = parts.shape
    me = lax.axis_index("blk")
    start = (me if own else 1 - me) * share
    copies = []
    count = share // sems.shape[0]
    for n in range(sems.shape[0]):
        for k in range(n * count, (n + 1) * count):
            parts[k, 0] = packed_ref[k, :, :width]
            parts[k, 1] = packed_ref[k, :, width:]
        target = out_ref.at[pl.ds(start + n * count, count)]
        copies.append(pltpu.make_async_copy(parts.at[pl.ds(n * count, count)], target, sems.at[n]))
        copies[-1].start()
    for copy in copies:
        copy.wait()


def place(packed, blocks, base=None):
    share, block, lanes = packed.shape
    width = lanes // 2
    anywhere = pl.BlockSpec(memory_space=pl.ANY)
    return pl.pallas_call(
        functools.partial(place_kernel, own=base is None),
        out_shape=jax.ShapeDtypeStruct((blocks * share, 2, block, width), packed.dtype),
        in_specs=[pl.BlockSpec(memory_space=pltpu.VMEM)] + ([] if base is None else [anywhere]),
        out_specs=anywhere,
        scratch_shapes=[
            pltpu.VMEM((share, 2, block, width), packed.dtype),
            pltpu.SemaphoreType.DMA((2,)),
        ],
        input_output_aliases={} if base is None else {1: 0},
        compiler_params=pltpu.CompilerParams(vmem_limit_bytes=VMEM_LIMIT),
        cost_estimate=pl.CostEstimate(flops=0, bytes_accessed=8 * packed.size, transcendentals=0),
    )(packed, *([] if base is None else [base]))


def split_channels(freq, blocks, samples, slot_order, flags):
    share = CH // (freq * blocks)
    inputs, block = samples.shape[0], slot_order.shape[1]
    axes = ("freq", "blk")
    plane = freq * blocks // 4
    order = [*reversed(range(plane, freq * blocks)), *range(plane)]
    me = lax.axis_index("blk").astype(jnp.int32)
    partner = lax.ppermute(slot_order, "blk", SWAP)
    orders = jnp.where(
        me == 0,
        jnp.concatenate([slot_order, partner]),
        jnp.concatenate([partner, slot_order]),
    )
    sent = channelize(samples, flags, order)
    arrived = lax.all_to_all(
        sent, axes, split_axis=0, concat_axis=0, axis_index_groups=[order], tiled=True
    )
    pick = picks(orders, inputs, order, share)
    own, other = correlate(arrived, pick, order, share, block)
    received = lax.ppermute(other, "blk", SWAP)
    return place(received, blocks, place(own, blocks))


def gather_blocks(freq, samples, slot_order, flags):
    inputs = samples.shape[0]
    taps = jnp.asarray(prototype())
    table = jnp.asarray(twiddle().reshape(2 * CH, FRAME), dtype=jnp.bfloat16)
    good = (1 - flags).astype(jnp.float32)
    frames = samples.reshape(inputs, SPEC + TAPS - 1, FRAME)
    total = jnp.zeros((inputs, SPEC, FRAME), jnp.float32)
    for tap in range(TAPS):
        window = frames[:, tap : tap + SPEC, :].astype(jnp.float32)
        total = total + taps[tap][None, None, :] * window
    fir = total.astype(jnp.bfloat16)
    spectra = jnp.einsum("kn,isn->kis", table, fir, preferred_element_type=jnp.float32)
    squares = jnp.sum(spectra * spectra, axis=2)
    power = jnp.sum(squares.reshape(CH, 2, inputs), axis=1) / SPEC
    scale = good[None, :] / jnp.sqrt(power + 1e-05)
    quantized = (spectra * jnp.repeat(scale, 2, axis=0)[:, :, None]).astype(jnp.bfloat16)
    arrived = lax.all_to_all(quantized, "freq", split_axis=0, concat_axis=1, tiled=True)
    share = CH // freq
    block = slot_order.shape[1]
    own = jnp.take(arrived.reshape(share, 2, block, SPEC), slot_order[0], axis=2)
    piece = lax.all_gather(own, "blk", axis=2, tiled=True)
    dot = functools.partial(jnp.einsum, "cas,cbs->cab", preferred_element_type=jnp.float32)
    real = dot(own[:, 0], piece[:, 0]) + dot(own[:, 1], piece[:, 1])
    imag = dot(own[:, 1], piece[:, 0]) - dot(own[:, 0], piece[:, 1])
    return jnp.stack([real / SPEC, imag / SPEC], axis=1)


def solution(mesh):
    freq, blocks = mesh.shape["freq"], mesh.shape["blk"]

    def body(samples, slot_order, flags):
        if blocks == 2 and CH == SUB * freq * blocks:
            return split_channels(freq, blocks, samples, slot_order, flags)
        return gather_blocks(freq, samples, slot_order, flags)

    in_specs = (P(("blk", "freq"), None), P("blk", None), P(("blk", "freq")))
    out_specs = P("freq", None, "blk", None)
    return jax.shard_map(body, mesh=mesh, in_specs=in_specs, out_specs=out_specs, check_vma=False)
```

```python
import functools
import math

import jax
import jax.numpy as jnp
import numpy as np
from jax import lax
from jax.experimental import pallas as pl
from jax.experimental.pallas import tpu as pltpu
from jax.experimental.layout import Layout, with_layout_constraint
from jax.sharding import PartitionSpec as P

CH = 256
TAPS = 12
SPEC = 512
FRAME = 2 * CH
LANES = 128
SUB = 8
GROUP = 256
STEP = GROUP // SUB
STRIDE = STEP + 1
PITCH = SPEC + 25
SWAP = [(0, 1), (1, 0)]
VMEM_LIMIT = 40 * 1024 * 1024


def prototype():
    count = TAPS * FRAME
    index = np.arange(count, dtype=np.float64)
    shifted = (index + 0.5) / FRAME - TAPS / 2.0
    window = 0.5 - 0.5 * np.cos(2.0 * math.pi * (index + 0.5) / count)
    return (np.sinc(shifted) * window).astype(np.float32).reshape(TAPS, FRAME)


def twiddle():
    chan = np.arange(CH, dtype=np.int64)[:, None]
    point = np.arange(FRAME, dtype=np.int64)[None, :]
    phase = (chan * point % FRAME).astype(np.float64) * (2.0 * math.pi / FRAME)
    return np.stack([np.cos(phase), -np.sin(phase)], axis=1).astype(np.float32)


def channelize_kernel(
    flags_hbm,
    x_hbm,
    taps_hbm,
    table_hbm,
    out_hbm,
    flags,
    taps_all,
    table,
    held,
    wide,
    fir,
    spectra,
    scales,
    result,
    load_sems,
    sems,
):
    inputs = fir.shape[0]
    frames = SPEC + TAPS - 1
    spread = inputs * FRAME // LANES
    groups = SPEC // GROUP
    pieces = sems.shape[0]
    rows = FRAME // pieces
    last = lax.broadcasted_iota(jnp.int32, (SUB, LANES), 0) == SUB - 1
    edges = [0, GROUP // 2] + [g * GROUP + TAPS for g in range(1, groups)] + [frames]

    def load(source, target, n):
        copy = pltpu.make_async_copy(source, target, load_sems.at[n])
        copy.start()
        return copy

    def span(n):
        return pl.ds(edges[n] * spread, (edges[n + 1] - edges[n]) * spread)

    chunks = len(edges) - 1
    loads = [load(x_hbm.at[span(n)], held.at[span(n)], n) for n in range(chunks)]
    load_taps = load(taps_hbm, taps_all, chunks)
    load_flags = load(flags_hbm, flags, chunks + 2)

    def convert(n):
        for f in range(edges[n], edges[n + 1], 2):
            count = min(2, frames - f)
            tile = held[pl.ds(f * spread, count * spread), :].astype(jnp.float32)
            for c in range(count):
                part = tile[c * spread : (c + 1) * spread]
                wide[pl.ds(f + c, spread, stride=PITCH), :] = part

    def filter_group(g, i, j):
        cols = pl.ds(j * LANES, LANES)
        taps = [jnp.broadcast_to(taps_all[pl.ds(t, 1), cols], (SUB, LANES)) for t in range(TAPS)]

        def take(b):
            first = (inputs * j + i) * PITCH + g * GROUP + b
            return wide[pl.ds(first, SUB, stride=STRIDE), :]

        def total(first, count):
            window = [take(first + b) for b in range(count + TAPS - 1)]
            out = [taps[0] * window[b] for b in range(count)]
            for t in range(1, TAPS):
                out = [out[b] + taps[t] * window[b + t] for b in range(count)]
            return out

        extra = total(STEP, 1)[0]
        for first in range(0, STEP, SUB):
            out = total(first, SUB)
            for b in range(SUB):
                past = first + b - (STEP - SUB + 1)
                if past >= 0:
                    out[b] = jnp.where(last, pltpu.roll(extra, SUB - 1 - past, 0), out[b])
            for b in range(0, SUB, 2):
                both = jnp.concatenate(out[b : b + 2], axis=0).astype(jnp.bfloat16)
                fir[i, pl.ds(g * GROUP + (first + b) * SUB, 2 * SUB), cols] = both

    def transform(g, i):
        part = pl.ds(g * GROUP, GROUP)
        spectra[i, :, part] = lax.dot_general(
            table[...],
            fir[i, part, :],
            (((1,), (1,)), ((), ())),
            preferred_element_type=jnp.float32,
        )

    def rate(i):
        good = (1 - flags[i]).astype(jnp.float32)
        for piece in range(pieces):
            pairs = spectra[i, pl.ds(piece * rows, rows), :]
            pairs = pairs.reshape(rows // (2 * SUB), 2, SUB, SPEC)
            squares = jnp.sum(pairs * pairs, axis=1)
            power = jnp.sum(squares, axis=2, keepdims=True) / SPEC
            scale = good / jnp.sqrt(power + 1e-05)
            place = pl.ds(piece * rows // 2, rows // 2)
            scales[i, place, :] = jnp.broadcast_to(scale.reshape(rows // 2, 1), (rows // 2, LANES))

    def scaled(i, piece):
        pairs = spectra[i, pl.ds(piece * rows, rows), :]
        pairs = pairs.reshape(rows // (2 * SUB), 2, SUB, SPEC)
        scale = scales[i, pl.ds(piece * rows // 2, rows // 2), :]
        scale = jnp.concatenate([scale] * (SPEC // LANES), axis=1)
        return pairs * scale.reshape(rows // (2 * SUB), 1, SUB, SPEC)

    def pack(piece):
        place = pl.ds(piece * rows, rows)
        parts = [scaled(i, piece) for i in range(inputs)]
        for p in range(2):
            both = jnp.concatenate([part[:, p] for part in parts], axis=1)
            result[place, pl.ds(p * SPEC, SPEC)] = both.astype(jnp.bfloat16).reshape(rows, SPEC)
        copy = pltpu.make_async_copy(result.at[place], out_hbm.at[place], sems.at[piece])
        copy.start()
        return copy

    loads[0].wait()
    convert(0)
    load_taps.wait()
    loads[1].wait()
    load_table = load(table_hbm, table, chunks + 1)
    convert(1)
    for i in range(inputs):
        for j in range(FRAME // LANES):
            filter_group(0, i, j)
    loads[2].wait()
    load_table.wait()
    load_flags.wait()
    for i in range(inputs):
        transform(0, i)
    convert(2)
    for i in range(inputs):
        if i > 0:
            transform(1, i - 1)
        for j in range(FRAME // LANES):
            filter_group(1, i, j)
    transform(1, inputs - 1)
    for i in range(inputs):
        rate(i)
    copies = [pack(piece) for piece in range(pieces)]
    for copy in copies:
        copy.wait()


def channelize(samples, flags, order):
    inputs = samples.shape[0]
    tiles = samples.reshape(inputs, -1, LANES)
    tiles = with_layout_constraint(tiles, Layout(major_to_minor=(1, 0, 2)))
    tiles = tiles.transpose(1, 0, 2)
    tiles = tiles.reshape(-1, LANES)
    table = twiddle().reshape(len(order), SUB, 2, FRAME)[np.asarray(order)].transpose(0, 2, 1, 3)
    table = jnp.asarray(table.reshape(FRAME, FRAME), dtype=jnp.bfloat16)
    taps = jnp.asarray(prototype())
    hbm = pl.BlockSpec(memory_space=pltpu.HBM)
    return pl.pallas_call(
        channelize_kernel,
        out_shape=jax.ShapeDtypeStruct((FRAME, inputs * SPEC), jnp.bfloat16),
        in_specs=[hbm] * 4,
        out_specs=hbm,
        scratch_shapes=[
            pltpu.SMEM(flags.shape, flags.dtype),
            pltpu.VMEM(taps.shape, taps.dtype),
            pltpu.VMEM(table.shape, table.dtype),
            pltpu.VMEM(tiles.shape, tiles.dtype),
            pltpu.VMEM((inputs * FRAME // LANES * PITCH, LANES), jnp.float32),
            pltpu.VMEM((inputs, SPEC, FRAME), jnp.bfloat16),
            pltpu.VMEM((inputs, FRAME, SPEC), jnp.float32),
            pltpu.VMEM((inputs, CH, LANES), jnp.float32),
            pltpu.VMEM((FRAME, inputs * SPEC), jnp.bfloat16),
            pltpu.SemaphoreType.DMA((SPEC // GROUP + 4,)),
            pltpu.SemaphoreType.DMA((8,)),
        ],
        cost_estimate=pl.CostEstimate(
            flops=2 * inputs * SPEC * FRAME * (FRAME + TAPS),
            bytes_accessed=4 * inputs * SPEC * FRAME,
            transcendentals=0,
        ),
    )(flags, tiles, taps, table)


def correlate_kernel(pick_ref, arrived_ref, own_ref, other_ref, slots, *, order):
    share, block, _ = own_ref.shape
    blocks = pick_ref.shape[0]
    width = blocks * block
    held = arrived_ref.shape[0] // len(order)
    first = lax.axis_index("blk") == 0
    lane = lax.broadcasted_iota(jnp.int32, (width, 2 * width), 1)
    sign = jnp.where(lane < width, 1.0 / SPEC, -1.0 / SPEC)
    for n in range(blocks):
        places = [place for place, device in enumerate(order) if device % blocks == n]
        rows = [arrived_ref[pl.ds(place * held, held), :] for place in places]
        slots[n] = jnp.dot(
            pick_ref[n], jnp.concatenate(rows, axis=0), preferred_element_type=jnp.float32
        ).astype(jnp.bfloat16)
    for k in range(share):
        pair = jnp.concatenate(
            [
                slots[n, pl.ds(k * block, block), pl.ds(p * SPEC, SPEC)]
                for p in range(2)
                for n in range(blocks)
            ],
            axis=0,
        )
        gram = lax.dot_general(
            pair, pair, (((1,), (1,)), ((), ())), preferred_element_type=jnp.float32
        )
        part = gram[:width] * sign + pltpu.roll(gram[width:], width, 1) / SPEC
        own_ref[k] = jnp.where(first, part[:block], part[block:])
        other_ref[k] = jnp.where(first, part[block:], part[:block])


def picks(orders, inputs, order, share):
    blocks, block = orders.shape
    device, held = orders // inputs, orders % inputs
    rank = [np.argsort([d for d in order if d % blocks == n]) for n in range(blocks)]
    known = jnp.asarray(np.stack(rank), dtype=jnp.int32)
    match = device[:, :, None] == jnp.arange(known.shape[1], dtype=jnp.int32)
    place = jnp.sum(jnp.where(match, known[:, None, :], 0), axis=2)
    start = ((place * inputs + held) * share)[:, None, :]
    chan = jnp.arange(share, dtype=jnp.int32)[:, None]
    target = (start + chan).reshape(blocks, share * block, 1)
    column = lax.broadcasted_iota(jnp.int32, (1, 1, known.shape[1] * inputs * share), 2)
    return (column == target).astype(jnp.bfloat16)


def correlate(arrived, pick, order, share, block):
    blocks = pick.shape[0]
    vmem = pl.BlockSpec(memory_space=pltpu.VMEM)
    tile = jax.ShapeDtypeStruct((share, block, 2 * blocks * block), jnp.float32)
    return pl.pallas_call(
        functools.partial(correlate_kernel, order=order),
        out_shape=(tile, tile),
        in_specs=[vmem, vmem],
        out_specs=(vmem, vmem),
        scratch_shapes=[pltpu.VMEM((blocks, share * block, 2 * SPEC), jnp.bfloat16)],
        compiler_params=pltpu.CompilerParams(vmem_limit_bytes=VMEM_LIMIT),
        cost_estimate=pl.CostEstimate(
            flops=4 * pick.size * SPEC, bytes_accessed=4 * arrived.size, transcendentals=0
        ),
    )(pick, arrived)


def place_kernel(packed_ref, *refs, own):
    out_ref, parts, sems = refs[-3:]
    share, _, _, width = parts.shape
    me = lax.axis_index("blk")
    start = (me if own else 1 - me) * share
    copies = []
    count = share // sems.shape[0]
    for n in range(sems.shape[0]):
        for k in range(n * count, (n + 1) * count):
            parts[k, 0] = packed_ref[k, :, :width]
            parts[k, 1] = packed_ref[k, :, width:]
        target = out_ref.at[pl.ds(start + n * count, count)]
        copies.append(pltpu.make_async_copy(parts.at[pl.ds(n * count, count)], target, sems.at[n]))
        copies[-1].start()
    for copy in copies:
        copy.wait()


def place(packed, blocks, base=None):
    share, block, lanes = packed.shape
    width = lanes // 2
    anywhere = pl.BlockSpec(memory_space=pl.ANY)
    return pl.pallas_call(
        functools.partial(place_kernel, own=base is None),
        out_shape=jax.ShapeDtypeStruct((blocks * share, 2, block, width), packed.dtype),
        in_specs=[pl.BlockSpec(memory_space=pltpu.VMEM)] + ([] if base is None else [anywhere]),
        out_specs=anywhere,
        scratch_shapes=[
            pltpu.VMEM((share, 2, block, width), packed.dtype),
            pltpu.SemaphoreType.DMA((2,)),
        ],
        input_output_aliases={} if base is None else {1: 0},
        compiler_params=pltpu.CompilerParams(vmem_limit_bytes=VMEM_LIMIT),
        cost_estimate=pl.CostEstimate(flops=0, bytes_accessed=8 * packed.size, transcendentals=0),
    )(packed, *([] if base is None else [base]))


def split_channels(freq, blocks, samples, slot_order, flags):
    share = CH // (freq * blocks)
    inputs, block = samples.shape[0], slot_order.shape[1]
    axes = ("freq", "blk")
    plane = freq * blocks // 4
    order = [d for z in (3, 2, 0, 1) for d in reversed(range(z * plane, (z + 1) * plane))]
    me = lax.axis_index("blk").astype(jnp.int32)
    partner = lax.ppermute(slot_order, "blk", SWAP)
    orders = jnp.where(
        me == 0,
        jnp.concatenate([slot_order, partner]),
        jnp.concatenate([partner, slot_order]),
    )
    sent = channelize(samples, flags, order)
    arrived = lax.all_to_all(
        sent, axes, split_axis=0, concat_axis=0, axis_index_groups=[order], tiled=True
    )
    pick = picks(orders, inputs, order, share)
    own, other = correlate(arrived, pick, order, share, block)
    received = lax.ppermute(other, "blk", SWAP)
    return place(received, blocks, place(own, blocks))


def gather_blocks(freq, samples, slot_order, flags):
    inputs = samples.shape[0]
    taps = jnp.asarray(prototype())
    table = jnp.asarray(twiddle().reshape(2 * CH, FRAME), dtype=jnp.bfloat16)
    good = (1 - flags).astype(jnp.float32)
    frames = samples.reshape(inputs, SPEC + TAPS - 1, FRAME)
    total = jnp.zeros((inputs, SPEC, FRAME), jnp.float32)
    for tap in range(TAPS):
        window = frames[:, tap : tap + SPEC, :].astype(jnp.float32)
        total = total + taps[tap][None, None, :] * window
    fir = total.astype(jnp.bfloat16)
    spectra = jnp.einsum("kn,isn->kis", table, fir, preferred_element_type=jnp.float32)
    squares = jnp.sum(spectra * spectra, axis=2)
    power = jnp.sum(squares.reshape(CH, 2, inputs), axis=1) / SPEC
    scale = good[None, :] / jnp.sqrt(power + 1e-05)
    quantized = (spectra * jnp.repeat(scale, 2, axis=0)[:, :, None]).astype(jnp.bfloat16)
    arrived = lax.all_to_all(quantized, "freq", split_axis=0, concat_axis=1, tiled=True)
    share = CH // freq
    block = slot_order.shape[1]
    own = jnp.take(arrived.reshape(share, 2, block, SPEC), slot_order[0], axis=2)
    piece = lax.all_gather(own, "blk", axis=2, tiled=True)
    dot = functools.partial(jnp.einsum, "cas,cbs->cab", preferred_element_type=jnp.float32)
    real = dot(own[:, 0], piece[:, 0]) + dot(own[:, 1], piece[:, 1])
    imag = dot(own[:, 1], piece[:, 0]) - dot(own[:, 0], piece[:, 1])
    return jnp.stack([real / SPEC, imag / SPEC], axis=1)


def solution(mesh):
    freq, blocks = mesh.shape["freq"], mesh.shape["blk"]

    def body(samples, slot_order, flags):
        if blocks == 2 and CH == SUB * freq * blocks:
            return split_channels(freq, blocks, samples, slot_order, flags)
        return gather_blocks(freq, samples, slot_order, flags)

    in_specs = (P(("blk", "freq"), None), P("blk", None), P(("blk", "freq")))
    out_specs = P("freq", None, "blk", None)
    return jax.shard_map(body, mesh=mesh, in_specs=in_specs, out_specs=out_specs, check_vma=False)
```

```python
import functools
import math

import jax
import jax.numpy as jnp
import numpy as np
from jax import lax
from jax.experimental import pallas as pl
from jax.experimental.pallas import tpu as pltpu
from jax.experimental.layout import Layout, with_layout_constraint
from jax.sharding import PartitionSpec as P

CH = 256
TAPS = 12
SPEC = 512
FRAME = 2 * CH
LANES = 128
SUB = 8
GROUP = 256
PART = 128
STEP = PART // SUB
STRIDE = STEP + 1
PITCH = SPEC + 25
SWAP = [(0, 1), (1, 0)]
VMEM_LIMIT = 40 * 1024 * 1024


def prototype():
    count = TAPS * FRAME
    index = np.arange(count, dtype=np.float64)
    shifted = (index + 0.5) / FRAME - TAPS / 2.0
    window = 0.5 - 0.5 * np.cos(2.0 * math.pi * (index + 0.5) / count)
    return (np.sinc(shifted) * window).astype(np.float32).reshape(TAPS, FRAME)


def twiddle():
    chan = np.arange(CH, dtype=np.int64)[:, None]
    point = np.arange(FRAME, dtype=np.int64)[None, :]
    phase = (chan * point % FRAME).astype(np.float64) * (2.0 * math.pi / FRAME)
    return np.stack([np.cos(phase), -np.sin(phase)], axis=1).astype(np.float32)


def channelize_kernel(
    flags_hbm,
    x_hbm,
    taps_hbm,
    table_hbm,
    out_hbm,
    flags,
    taps_all,
    table,
    held,
    wide,
    fir,
    spectra,
    result,
    load_sems,
    sems,
):
    inputs = fir.shape[0]
    frames = SPEC + TAPS - 1
    spread = inputs * FRAME // LANES
    groups = SPEC // GROUP
    parts = SPEC // PART
    pieces = sems.shape[1]
    rows = FRAME // pieces
    last = lax.broadcasted_iota(jnp.int32, (SUB, LANES), 0) == SUB - 1
    edges = [0] + [n * PART + TAPS for n in range(1, parts)] + [frames]

    def load(source, target, n):
        copy = pltpu.make_async_copy(source, target, load_sems.at[n])
        copy.start()
        return copy

    def span(n):
        return pl.ds(edges[n] * spread, (edges[n + 1] - edges[n]) * spread)

    chunks = len(edges) - 1
    loads = [load(x_hbm.at[span(n)], held.at[span(n)], n) for n in range(chunks)]
    load_taps = load(taps_hbm, taps_all, chunks)
    load_flags = load(flags_hbm, flags, chunks + 2)

    def convert(n):
        for f in range(edges[n], edges[n + 1], 2):
            count = min(2, frames - f)
            tile = held[pl.ds(f * spread, count * spread), :].astype(jnp.float32)
            for c in range(count):
                part = tile[c * spread : (c + 1) * spread]
                wide[pl.ds(f + c, spread, stride=PITCH), :] = part

    def filter_part(n, i, j):
        cols = pl.ds(j * LANES, LANES)
        good = (1 - flags[i]).astype(jnp.float32)
        taps = [
            jnp.broadcast_to(taps_all[pl.ds(t, 1), cols] * good, (SUB, LANES)) for t in range(TAPS)
        ]

        def take(b):
            first = (inputs * j + i) * PITCH + n * PART + b
            return wide[pl.ds(first, SUB, stride=STRIDE), :]

        def total(first, count):
            window = [take(first + b) for b in range(count + TAPS - 1)]
            out = [taps[0] * window[b] for b in range(count)]
            for t in range(1, TAPS):
                out = [out[b] + taps[t] * window[b + t] for b in range(count)]
            return out

        extra = total(STEP, 1)[0]
        for first in range(0, STEP, SUB):
            out = total(first, SUB)
            for b in range(SUB):
                past = first + b - (STEP - SUB + 1)
                if past >= 0:
                    out[b] = jnp.where(last, pltpu.roll(extra, SUB - 1 - past, 0), out[b])
            for b in range(0, SUB, 2):
                both = jnp.concatenate(out[b : b + 2], axis=0).astype(jnp.bfloat16)
                fir[i, pl.ds(n * PART + (first + b) * SUB, 2 * SUB), cols] = both

    def transform(g, i):
        part = pl.ds(g * GROUP, GROUP)
        spectra[g, i] = lax.dot_general(
            table[...],
            fir[i, part, :],
            (((1,), (1,)), ((), ())),
            preferred_element_type=jnp.float32,
        )

    def pack(g, piece):
        place = pl.ds(piece * rows, rows)
        shape = (rows // (2 * SUB), 2, SUB, GROUP)
        parts = [spectra[g, i, place, :].reshape(shape) for i in range(inputs)]
        for p in range(2):
            both = jnp.concatenate([part[:, p] for part in parts], axis=1)
            cols = pl.ds(p * SPEC + g * GROUP, GROUP)
            result[place, cols] = both.astype(jnp.bfloat16).reshape(rows, GROUP)

    def store(g, piece):
        copies = []
        for p in range(2):
            place = (pl.ds(piece * rows, rows), pl.ds(p * SPEC + g * GROUP, GROUP))
            sem = sems.at[g, piece, p]
            copies.append(pltpu.make_async_copy(result.at[place], out_hbm.at[place], sem))
            copies[-1].start()
        return copies

    def filter_input(n, i):
        for j in range(FRAME // LANES):
            filter_part(n, i, j)

    load_taps.wait()
    load_flags.wait()
    loads[0].wait()
    convert(0)
    for i in range(inputs):
        filter_input(0, i)
    loads[1].wait()
    load_table = load(table_hbm, table, chunks + 1)
    convert(1)
    for i in range(inputs):
        filter_input(1, i)
    loads[2].wait()
    loads[3].wait()
    load_table.wait()
    for i in range(inputs):
        transform(0, i)
    convert(2)
    convert(3)
    for i in range(inputs):
        if i > 0:
            transform(1, i - 1)
        filter_input(2, i)
        filter_input(3, i)
        if i == 0:
            for piece in range(pieces):
                pack(0, piece)
    copies = []
    for piece in range(pieces):
        copies += store(0, piece)
    transform(1, inputs - 1)
    for piece in range(pieces):
        pack(1, piece)
        copies += store(1, piece)
    for copy in copies:
        copy.wait()


def channelize(samples, flags, order):
    inputs = samples.shape[0]
    tiles = samples.reshape(inputs, -1, LANES)
    tiles = with_layout_constraint(tiles, Layout(major_to_minor=(1, 0, 2)))
    tiles = tiles.transpose(1, 0, 2)
    tiles = tiles.reshape(-1, LANES)
    table = twiddle().reshape(len(order), SUB, 2, FRAME)[np.asarray(order)].transpose(0, 2, 1, 3)
    table = jnp.asarray(table.reshape(FRAME, FRAME), dtype=jnp.bfloat16)
    taps = jnp.asarray(prototype())
    hbm = pl.BlockSpec(memory_space=pltpu.HBM)
    return pl.pallas_call(
        channelize_kernel,
        out_shape=jax.ShapeDtypeStruct((FRAME, inputs * SPEC), jnp.bfloat16),
        in_specs=[hbm] * 4,
        out_specs=hbm,
        scratch_shapes=[
            pltpu.SMEM(flags.shape, flags.dtype),
            pltpu.VMEM(taps.shape, taps.dtype),
            pltpu.VMEM(table.shape, table.dtype),
            pltpu.VMEM(tiles.shape, tiles.dtype),
            pltpu.VMEM((inputs * FRAME // LANES * PITCH, LANES), jnp.float32),
            pltpu.VMEM((inputs, SPEC, FRAME), jnp.bfloat16),
            pltpu.VMEM((SPEC // GROUP, inputs, FRAME, GROUP), jnp.float32),
            pltpu.VMEM((FRAME, inputs * SPEC), jnp.bfloat16),
            pltpu.SemaphoreType.DMA((SPEC // PART + 3,)),
            pltpu.SemaphoreType.DMA((SPEC // GROUP, 4, 2)),
        ],
        cost_estimate=pl.CostEstimate(
            flops=2 * inputs * SPEC * FRAME * (FRAME + TAPS),
            bytes_accessed=4 * inputs * SPEC * FRAME,
            transcendentals=0,
        ),
    )(flags, tiles, taps, table)


def correlate_kernel(pick_ref, arrived_ref, own_ref, other_ref, slots, grams, *, order):
    share, block, _ = own_ref.shape
    blocks = pick_ref.shape[0]
    width = blocks * block
    held = arrived_ref.shape[0] // len(order)
    first = lax.axis_index("blk") == 0
    lane = lax.broadcasted_iota(jnp.int32, (width, 2 * width), 1)
    sign = jnp.where(lane < width, 1.0, -1.0)
    diagonal = lane == lax.broadcasted_iota(jnp.int32, (width, 2 * width), 0)
    for n in range(blocks):
        places = [place for place, device in enumerate(order) if device % blocks == n]
        rows = [arrived_ref[pl.ds(place * held, held), :] for place in places]
        slots[n] = jnp.dot(
            pick_ref[n], jnp.concatenate(rows, axis=0), preferred_element_type=jnp.float32
        ).astype(jnp.bfloat16)
    for k in range(share):
        pair = jnp.concatenate(
            [
                slots[n, pl.ds(k * block, block), pl.ds(p * SPEC, SPEC)]
                for p in range(2)
                for n in range(blocks)
            ],
            axis=0,
        )
        gram = lax.dot_general(
            pair, pair, (((1,), (1,)), ((), ())), preferred_element_type=jnp.float32
        )
        grams[k] = gram[:width] * sign + pltpu.roll(gram[width:], width, 1)
    part = grams[...]
    square = jnp.where(diagonal[None], part, 0.0)
    across = jnp.sum(square, axis=1, keepdims=True)
    across = jnp.concatenate([across[:, :, :width], across[:, :, :width]], axis=2)
    down = jnp.sum(square, axis=2, keepdims=True)
    part = part * (lax.rsqrt(across / SPEC + 1e-05) / SPEC)
    part = part * lax.rsqrt(down / SPEC + 1e-05)
    own_ref[...] = jnp.where(first, part[:, :block], part[:, block:])
    other_ref[...] = jnp.where(first, part[:, block:], part[:, :block])


def picks(orders, inputs, order, share):
    blocks, block = orders.shape
    device, held = orders // inputs, orders % inputs
    rank = [np.argsort([d for d in order if d % blocks == n]) for n in range(blocks)]
    known = jnp.asarray(np.stack(rank), dtype=jnp.int32)
    match = device[:, :, None] == jnp.arange(known.shape[1], dtype=jnp.int32)
    place = jnp.sum(jnp.where(match, known[:, None, :], 0), axis=2)
    start = ((place * inputs + held) * share)[:, None, :]
    chan = jnp.arange(share, dtype=jnp.int32)[:, None]
    target = (start + chan).reshape(blocks, share * block, 1)
    column = lax.broadcasted_iota(jnp.int32, (1, 1, known.shape[1] * inputs * share), 2)
    return (column == target).astype(jnp.bfloat16)


def correlate(arrived, pick, order, share, block):
    blocks = pick.shape[0]
    vmem = pl.BlockSpec(memory_space=pltpu.VMEM)
    tile = jax.ShapeDtypeStruct((share, block, 2 * blocks * block), jnp.float32)
    return pl.pallas_call(
        functools.partial(correlate_kernel, order=order),
        out_shape=(tile, tile),
        in_specs=[vmem, vmem],
        out_specs=(vmem, vmem),
        scratch_shapes=[
            pltpu.VMEM((blocks, share * block, 2 * SPEC), jnp.bfloat16),
            pltpu.VMEM((share, blocks * block, 2 * blocks * block), jnp.float32),
        ],
        compiler_params=pltpu.CompilerParams(vmem_limit_bytes=VMEM_LIMIT),
        cost_estimate=pl.CostEstimate(
            flops=4 * pick.size * SPEC, bytes_accessed=4 * arrived.size, transcendentals=0
        ),
    )(pick, arrived)


def place_kernel(packed_ref, *refs, own):
    out_ref, parts, sems = refs[-3:]
    share, _, _, width = parts.shape
    me = lax.axis_index("blk")
    start = (me if own else 1 - me) * share
    copies = []
    count = share // sems.shape[0]
    for n in range(sems.shape[0]):
        for k in range(n * count, (n + 1) * count):
            parts[k, 0] = packed_ref[k, :, :width]
            parts[k, 1] = packed_ref[k, :, width:]
        target = out_ref.at[pl.ds(start + n * count, count)]
        copies.append(pltpu.make_async_copy(parts.at[pl.ds(n * count, count)], target, sems.at[n]))
        copies[-1].start()
    for copy in copies:
        copy.wait()


def place(packed, blocks, base=None):
    share, block, lanes = packed.shape
    width = lanes // 2
    anywhere = pl.BlockSpec(memory_space=pl.ANY)
    return pl.pallas_call(
        functools.partial(place_kernel, own=base is None),
        out_shape=jax.ShapeDtypeStruct((blocks * share, 2, block, width), packed.dtype),
        in_specs=[pl.BlockSpec(memory_space=pltpu.VMEM)] + ([] if base is None else [anywhere]),
        out_specs=anywhere,
        scratch_shapes=[
            pltpu.VMEM((share, 2, block, width), packed.dtype),
            pltpu.SemaphoreType.DMA((2,)),
        ],
        input_output_aliases={} if base is None else {1: 0},
        compiler_params=pltpu.CompilerParams(vmem_limit_bytes=VMEM_LIMIT),
        cost_estimate=pl.CostEstimate(flops=0, bytes_accessed=8 * packed.size, transcendentals=0),
    )(packed, *([] if base is None else [base]))


def split_channels(freq, blocks, samples, slot_order, flags):
    share = CH // (freq * blocks)
    inputs, block = samples.shape[0], slot_order.shape[1]
    axes = ("freq", "blk")
    plane = freq * blocks // 4
    order = [d for z in (3, 2, 0, 1) for d in reversed(range(z * plane, (z + 1) * plane))]
    me = lax.axis_index("blk").astype(jnp.int32)
    partner = lax.ppermute(slot_order, "blk", SWAP)
    orders = jnp.where(
        me == 0,
        jnp.concatenate([slot_order, partner]),
        jnp.concatenate([partner, slot_order]),
    )
    sent = channelize(samples, flags, order)
    arrived = lax.all_to_all(
        sent, axes, split_axis=0, concat_axis=0, axis_index_groups=[order], tiled=True
    )
    pick = picks(orders, inputs, order, share)
    own, other = correlate(arrived, pick, order, share, block)
    received = lax.ppermute(other, "blk", SWAP)
    return place(received, blocks, place(own, blocks))


def gather_blocks(freq, samples, slot_order, flags):
    inputs = samples.shape[0]
    taps = jnp.asarray(prototype())
    table = jnp.asarray(twiddle().reshape(2 * CH, FRAME), dtype=jnp.bfloat16)
    good = (1 - flags).astype(jnp.float32)
    frames = samples.reshape(inputs, SPEC + TAPS - 1, FRAME)
    total = jnp.zeros((inputs, SPEC, FRAME), jnp.float32)
    for tap in range(TAPS):
        window = frames[:, tap : tap + SPEC, :].astype(jnp.float32)
        total = total + taps[tap][None, None, :] * window
    fir = total.astype(jnp.bfloat16)
    spectra = jnp.einsum("kn,isn->kis", table, fir, preferred_element_type=jnp.float32)
    squares = jnp.sum(spectra * spectra, axis=2)
    power = jnp.sum(squares.reshape(CH, 2, inputs), axis=1) / SPEC
    scale = good[None, :] / jnp.sqrt(power + 1e-05)
    quantized = (spectra * jnp.repeat(scale, 2, axis=0)[:, :, None]).astype(jnp.bfloat16)
    arrived = lax.all_to_all(quantized, "freq", split_axis=0, concat_axis=1, tiled=True)
    share = CH // freq
    block = slot_order.shape[1]
    own = jnp.take(arrived.reshape(share, 2, block, SPEC), slot_order[0], axis=2)
    piece = lax.all_gather(own, "blk", axis=2, tiled=True)
    dot = functools.partial(jnp.einsum, "cas,cbs->cab", preferred_element_type=jnp.float32)
    real = dot(own[:, 0], piece[:, 0]) + dot(own[:, 1], piece[:, 1])
    imag = dot(own[:, 1], piece[:, 0]) - dot(own[:, 0], piece[:, 1])
    return jnp.stack([real / SPEC, imag / SPEC], axis=1)


def solution(mesh):
    freq, blocks = mesh.shape["freq"], mesh.shape["blk"]

    def body(samples, slot_order, flags):
        if blocks == 2 and CH == SUB * freq * blocks:
            return split_channels(freq, blocks, samples, slot_order, flags)
        return gather_blocks(freq, samples, slot_order, flags)

    in_specs = (P(("blk", "freq"), None), P("blk", None), P(("blk", "freq")))
    out_specs = P("freq", None, "blk", None)
    return jax.shard_map(body, mesh=mesh, in_specs=in_specs, out_specs=out_specs, check_vma=False)
```

```python
import functools
import math

import jax
import jax.numpy as jnp
import numpy as np
from jax import lax
from jax.experimental import pallas as pl
from jax.experimental.pallas import tpu as pltpu
from jax.experimental.layout import Layout, with_layout_constraint
from jax.sharding import PartitionSpec as P

CH = 256
TAPS = 12
SPEC = 512
FRAME = 2 * CH
LANES = 128
SUB = 8
GROUP = 256
STEP = GROUP // SUB
STRIDE = STEP + 1
PITCH = SPEC + 25
SWAP = [(0, 1), (1, 0)]
VMEM_LIMIT = 40 * 1024 * 1024


def prototype():
    count = TAPS * FRAME
    index = np.arange(count, dtype=np.float64)
    shifted = (index + 0.5) / FRAME - TAPS / 2.0
    window = 0.5 - 0.5 * np.cos(2.0 * math.pi * (index + 0.5) / count)
    return (np.sinc(shifted) * window).astype(np.float32).reshape(TAPS, FRAME)


def twiddle():
    chan = np.arange(CH, dtype=np.int64)[:, None]
    point = np.arange(FRAME, dtype=np.int64)[None, :]
    phase = (chan * point % FRAME).astype(np.float64) * (2.0 * math.pi / FRAME)
    return np.stack([np.cos(phase), -np.sin(phase)], axis=1).astype(np.float32)


def channelize_kernel(
    flags_hbm,
    x_hbm,
    taps_hbm,
    table_hbm,
    out_hbm,
    flags,
    taps_all,
    table,
    held,
    wide,
    fir,
    spectra,
    scales,
    result,
    load_sems,
    sems,
):
    inputs = fir.shape[0]
    frames = SPEC + TAPS - 1
    spread = inputs * FRAME // LANES
    groups = SPEC // GROUP
    pieces = sems.shape[0]
    rows = FRAME // pieces
    last = lax.broadcasted_iota(jnp.int32, (SUB, LANES), 0) == SUB - 1
    edges = [0, GROUP // 2] + [g * GROUP + TAPS for g in range(1, groups)] + [frames]

    def load(source, target, n):
        copy = pltpu.make_async_copy(source, target, load_sems.at[n])
        copy.start()
        return copy

    def span(n):
        return pl.ds(edges[n] * spread, (edges[n + 1] - edges[n]) * spread)

    chunks = len(edges) - 1
    loads = [load(x_hbm.at[span(n)], held.at[span(n)], n) for n in range(chunks)]
    load_taps = load(taps_hbm, taps_all, chunks)
    load_flags = load(flags_hbm, flags, chunks + 2)

    def convert(n):
        for f in range(edges[n], edges[n + 1], 2):
            count = min(2, frames - f)
            tile = held[pl.ds(f * spread, count * spread), :].astype(jnp.float32)
            for c in range(count):
                part = tile[c * spread : (c + 1) * spread]
                wide[pl.ds(f + c, spread, stride=PITCH), :] = part

    def filter_group(g, i, j):
        cols = pl.ds(j * LANES, LANES)
        taps = [jnp.broadcast_to(taps_all[pl.ds(t, 1), cols], (SUB, LANES)) for t in range(TAPS)]

        def take(b):
            first = (inputs * j + i) * PITCH + g * GROUP + b
            return wide[pl.ds(first, SUB, stride=STRIDE), :]

        def total(first, count):
            window = [take(first + b) for b in range(count + TAPS - 1)]
            out = [taps[0] * window[b] for b in range(count)]
            for t in range(1, TAPS):
                out = [out[b] + taps[t] * window[b + t] for b in range(count)]
            return out

        extra = total(STEP, 1)[0]
        for first in range(0, STEP, SUB):
            out = total(first, SUB)
            for b in range(SUB):
                past = first + b - (STEP - SUB + 1)
                if past >= 0:
                    out[b] = jnp.where(last, pltpu.roll(extra, SUB - 1 - past, 0), out[b])
            for b in range(0, SUB, 2):
                both = jnp.concatenate(out[b : b + 2], axis=0).astype(jnp.bfloat16)
                fir[i, pl.ds(g * GROUP + (first + b) * SUB, 2 * SUB), cols] = both

    def transform(g, i):
        part = pl.ds(g * GROUP, GROUP)
        spectra[i, :, part] = lax.dot_general(
            table[...],
            fir[i, part, :],
            (((1,), (1,)), ((), ())),
            preferred_element_type=jnp.float32,
        )

    def rate(i):
        good = (1 - flags[i]).astype(jnp.float32)
        for piece in range(pieces):
            pairs = spectra[i, pl.ds(piece * rows, rows), :]
            pairs = pairs.reshape(rows // (2 * SUB), 2, SUB, SPEC)
            squares = jnp.sum(pairs * pairs, axis=1)
            power = jnp.sum(squares, axis=2, keepdims=True) / SPEC
            scale = good / jnp.sqrt(power + 1e-05)
            place = pl.ds(piece * rows // 2, rows // 2)
            scales[i, place, :] = jnp.broadcast_to(scale.reshape(rows // 2, 1), (rows // 2, LANES))

    def scaled(i, piece):
        pairs = spectra[i, pl.ds(piece * rows, rows), :]
        pairs = pairs.reshape(rows // (2 * SUB), 2, SUB, SPEC)
        scale = scales[i, pl.ds(piece * rows // 2, rows // 2), :]
        scale = jnp.concatenate([scale] * (SPEC // LANES), axis=1)
        return pairs * scale.reshape(rows // (2 * SUB), 1, SUB, SPEC)

    def pack(piece):
        place = pl.ds(piece * rows, rows)
        parts = [scaled(i, piece) for i in range(inputs)]
        for p in range(2):
            both = jnp.concatenate([part[:, p] for part in parts], axis=1)
            result[place, pl.ds(p * SPEC, SPEC)] = both.astype(jnp.bfloat16).reshape(rows, SPEC)
        copy = pltpu.make_async_copy(result.at[place], out_hbm.at[place], sems.at[piece])
        copy.start()
        return copy

    loads[0].wait()
    convert(0)
    load_taps.wait()
    loads[1].wait()
    load_table = load(table_hbm, table, chunks + 1)
    convert(1)
    for i in range(inputs):
        for j in range(FRAME // LANES):
            filter_group(0, i, j)
    loads[2].wait()
    load_table.wait()
    load_flags.wait()
    for i in range(inputs):
        transform(0, i)
    convert(2)
    for i in range(inputs):
        if i > 0:
            transform(1, i - 1)
        for j in range(FRAME // LANES):
            filter_group(1, i, j)
    transform(1, inputs - 1)
    for i in range(inputs):
        rate(i)
    copies = [pack(piece) for piece in range(pieces)]
    for copy in copies:
        copy.wait()


def channelize(samples, flags, order):
    inputs = samples.shape[0]
    tiles = samples.reshape(inputs, -1, LANES)
    tiles = with_layout_constraint(tiles, Layout(major_to_minor=(1, 0, 2)))
    tiles = tiles.transpose(1, 0, 2)
    tiles = tiles.reshape(-1, LANES)
    table = twiddle().reshape(len(order), SUB, 2, FRAME)[np.asarray(order)].transpose(0, 2, 1, 3)
    table = jnp.asarray(table.reshape(FRAME, FRAME), dtype=jnp.bfloat16)
    taps = jnp.asarray(prototype())
    hbm = pl.BlockSpec(memory_space=pltpu.HBM)
    return pl.pallas_call(
        channelize_kernel,
        out_shape=jax.ShapeDtypeStruct((FRAME, inputs * SPEC), jnp.bfloat16),
        in_specs=[hbm] * 4,
        out_specs=hbm,
        scratch_shapes=[
            pltpu.SMEM(flags.shape, flags.dtype),
            pltpu.VMEM(taps.shape, taps.dtype),
            pltpu.VMEM(table.shape, table.dtype),
            pltpu.VMEM(tiles.shape, tiles.dtype),
            pltpu.VMEM((inputs * FRAME // LANES * PITCH, LANES), jnp.float32),
            pltpu.VMEM((inputs, SPEC, FRAME), jnp.bfloat16),
            pltpu.VMEM((inputs, FRAME, SPEC), jnp.float32),
            pltpu.VMEM((inputs, CH, LANES), jnp.float32),
            pltpu.VMEM((FRAME, inputs * SPEC), jnp.bfloat16),
            pltpu.SemaphoreType.DMA((SPEC // GROUP + 4,)),
            pltpu.SemaphoreType.DMA((8,)),
        ],
        cost_estimate=pl.CostEstimate(
            flops=2 * inputs * SPEC * FRAME * (FRAME + TAPS),
            bytes_accessed=4 * inputs * SPEC * FRAME,
            transcendentals=0,
        ),
    )(flags, tiles, taps, table)


def correlate_kernel(pick_ref, arrived_ref, own_ref, other_ref, slots, *, order):
    share, block, _ = own_ref.shape
    blocks = pick_ref.shape[0]
    width = blocks * block
    held = arrived_ref.shape[0] // len(order)
    first = lax.axis_index("blk") == 0
    lane = lax.broadcasted_iota(jnp.int32, (width, 2 * width), 1)
    sign = jnp.where(lane < width, 1.0 / SPEC, -1.0 / SPEC)
    for n in range(blocks):
        places = [place for place, device in enumerate(order) if device % blocks == n]
        rows = [arrived_ref[pl.ds(place * held, held), :] for place in places]
        slots[n] = jnp.dot(
            pick_ref[n], jnp.concatenate(rows, axis=0), preferred_element_type=jnp.float32
        ).astype(jnp.bfloat16)
    for k in range(share):
        pair = jnp.concatenate(
            [
                slots[n, pl.ds(k * block, block), pl.ds(p * SPEC, SPEC)]
                for p in range(2)
                for n in range(blocks)
            ],
            axis=0,
        )
        gram = lax.dot_general(
            pair, pair, (((1,), (1,)), ((), ())), preferred_element_type=jnp.float32
        )
        part = gram[:width] * sign + pltpu.roll(gram[width:], width, 1) / SPEC
        own_ref[k] = jnp.where(first, part[:block], part[block:])
        other_ref[k] = jnp.where(first, part[block:], part[:block])


def picks(orders, inputs, order, share):
    blocks, block = orders.shape
    device, held = orders // inputs, orders % inputs
    rank = [np.argsort([d for d in order if d % blocks == n]) for n in range(blocks)]
    known = jnp.asarray(np.stack(rank), dtype=jnp.int32)
    match = device[:, :, None] == jnp.arange(known.shape[1], dtype=jnp.int32)
    place = jnp.sum(jnp.where(match, known[:, None, :], 0), axis=2)
    start = ((place * inputs + held) * share)[:, None, :]
    chan = jnp.arange(share, dtype=jnp.int32)[:, None]
    target = (start + chan).reshape(blocks, share * block, 1)
    column = lax.broadcasted_iota(jnp.int32, (1, 1, known.shape[1] * inputs * share), 2)
    return (column == target).astype(jnp.bfloat16)


def correlate(arrived, pick, order, share, block):
    blocks = pick.shape[0]
    vmem = pl.BlockSpec(memory_space=pltpu.VMEM)
    tile = jax.ShapeDtypeStruct((share, block, 2 * blocks * block), jnp.float32)
    return pl.pallas_call(
        functools.partial(correlate_kernel, order=order),
        out_shape=(tile, tile),
        in_specs=[vmem, vmem],
        out_specs=(vmem, vmem),
        scratch_shapes=[pltpu.VMEM((blocks, share * block, 2 * SPEC), jnp.bfloat16)],
        compiler_params=pltpu.CompilerParams(vmem_limit_bytes=VMEM_LIMIT),
        cost_estimate=pl.CostEstimate(
            flops=4 * pick.size * SPEC, bytes_accessed=4 * arrived.size, transcendentals=0
        ),
    )(pick, arrived)


def place_kernel(packed_ref, *refs, own):
    out_ref, parts, sems = refs[-3:]
    share, _, _, width = parts.shape
    me = lax.axis_index("blk")
    start = (me if own else 1 - me) * share
    copies = []
    count = share // sems.shape[0]
    for n in range(sems.shape[0]):
        for k in range(n * count, (n + 1) * count):
            parts[k, 0] = packed_ref[k, :, :width]
            parts[k, 1] = packed_ref[k, :, width:]
        target = out_ref.at[pl.ds(start + n * count, count)]
        copies.append(pltpu.make_async_copy(parts.at[pl.ds(n * count, count)], target, sems.at[n]))
        copies[-1].start()
    for copy in copies:
        copy.wait()


def place(packed, blocks, base=None):
    share, block, lanes = packed.shape
    width = lanes // 2
    anywhere = pl.BlockSpec(memory_space=pl.ANY)
    return pl.pallas_call(
        functools.partial(place_kernel, own=base is None),
        out_shape=jax.ShapeDtypeStruct((blocks * share, 2, block, width), packed.dtype),
        in_specs=[pl.BlockSpec(memory_space=pltpu.VMEM)] + ([] if base is None else [anywhere]),
        out_specs=anywhere,
        scratch_shapes=[
            pltpu.VMEM((share, 2, block, width), packed.dtype),
            pltpu.SemaphoreType.DMA((2,)),
        ],
        input_output_aliases={} if base is None else {1: 0},
        compiler_params=pltpu.CompilerParams(vmem_limit_bytes=VMEM_LIMIT),
        cost_estimate=pl.CostEstimate(flops=0, bytes_accessed=8 * packed.size, transcendentals=0),
    )(packed, *([] if base is None else [base]))


def split_channels(freq, blocks, samples, slot_order, flags):
    share = CH // (freq * blocks)
    inputs, block = samples.shape[0], slot_order.shape[1]
    axes = ("freq", "blk")
    plane = freq * blocks // 4
    order = [
        z * plane + d
        for z in (3, 2, 0, 1)
        for core in reversed(range(blocks))
        for d in reversed(range(core, plane, blocks))
    ]
    me = lax.axis_index("blk").astype(jnp.int32)
    partner = lax.ppermute(slot_order, "blk", SWAP)
    orders = jnp.where(
        me == 0,
        jnp.concatenate([slot_order, partner]),
        jnp.concatenate([partner, slot_order]),
    )
    sent = channelize(samples, flags, order)
    arrived = lax.all_to_all(
        sent, axes, split_axis=0, concat_axis=0, axis_index_groups=[order], tiled=True
    )
    pick = picks(orders, inputs, order, share)
    own, other = correlate(arrived, pick, order, share, block)
    received = lax.ppermute(other, "blk", SWAP)
    return place(received, blocks, place(own, blocks))


def gather_blocks(freq, samples, slot_order, flags):
    inputs = samples.shape[0]
    taps = jnp.asarray(prototype())
    table = jnp.asarray(twiddle().reshape(2 * CH, FRAME), dtype=jnp.bfloat16)
    good = (1 - flags).astype(jnp.float32)
    frames = samples.reshape(inputs, SPEC + TAPS - 1, FRAME)
    total = jnp.zeros((inputs, SPEC, FRAME), jnp.float32)
    for tap in range(TAPS):
        window = frames[:, tap : tap + SPEC, :].astype(jnp.float32)
        total = total + taps[tap][None, None, :] * window
    fir = total.astype(jnp.bfloat16)
    spectra = jnp.einsum("kn,isn->kis", table, fir, preferred_element_type=jnp.float32)
    squares = jnp.sum(spectra * spectra, axis=2)
    power = jnp.sum(squares.reshape(CH, 2, inputs), axis=1) / SPEC
    scale = good[None, :] / jnp.sqrt(power + 1e-05)
    quantized = (spectra * jnp.repeat(scale, 2, axis=0)[:, :, None]).astype(jnp.bfloat16)
    arrived = lax.all_to_all(quantized, "freq", split_axis=0, concat_axis=1, tiled=True)
    share = CH // freq
    block = slot_order.shape[1]
    own = jnp.take(arrived.reshape(share, 2, block, SPEC), slot_order[0], axis=2)
    piece = lax.all_gather(own, "blk", axis=2, tiled=True)
    dot = functools.partial(jnp.einsum, "cas,cbs->cab", preferred_element_type=jnp.float32)
    real = dot(own[:, 0], piece[:, 0]) + dot(own[:, 1], piece[:, 1])
    imag = dot(own[:, 1], piece[:, 0]) - dot(own[:, 0], piece[:, 1])
    return jnp.stack([real / SPEC, imag / SPEC], axis=1)


def solution(mesh):
    freq, blocks = mesh.shape["freq"], mesh.shape["blk"]

    def body(samples, slot_order, flags):
        if blocks == 2 and CH == SUB * freq * blocks:
            return split_channels(freq, blocks, samples, slot_order, flags)
        return gather_blocks(freq, samples, slot_order, flags)

    in_specs = (P(("blk", "freq"), None), P("blk", None), P(("blk", "freq")))
    out_specs = P("freq", None, "blk", None)
    return jax.shard_map(body, mesh=mesh, in_specs=in_specs, out_specs=out_specs, check_vma=False)
```

```python
import functools
import math

import jax
import jax.numpy as jnp
import numpy as np
from jax import lax
from jax.experimental import pallas as pl
from jax.experimental.pallas import tpu as pltpu
from jax.experimental.layout import Layout, with_layout_constraint
from jax.sharding import PartitionSpec as P

CH = 256
TAPS = 12
SPEC = 512
FRAME = 2 * CH
LANES = 128
SUB = 8
GROUP = 256
STEP = GROUP // SUB
STRIDE = STEP + 1
PITCH = SPEC + 25
SWAP = [(0, 1), (1, 0)]
VMEM_LIMIT = 40 * 1024 * 1024


def prototype():
    count = TAPS * FRAME
    index = np.arange(count, dtype=np.float64)
    shifted = (index + 0.5) / FRAME - TAPS / 2.0
    window = 0.5 - 0.5 * np.cos(2.0 * math.pi * (index + 0.5) / count)
    return (np.sinc(shifted) * window).astype(np.float32).reshape(TAPS, FRAME)


def twiddle():
    chan = np.arange(CH, dtype=np.int64)[:, None]
    point = np.arange(FRAME, dtype=np.int64)[None, :]
    phase = (chan * point % FRAME).astype(np.float64) * (2.0 * math.pi / FRAME)
    return np.stack([np.cos(phase), -np.sin(phase)], axis=1).astype(np.float32)


def channelize_kernel(
    flags_hbm,
    x_hbm,
    taps_hbm,
    table_hbm,
    out_hbm,
    flags,
    taps_all,
    table,
    held,
    wide,
    fir,
    spectra,
    scales,
    result,
    load_sems,
    sems,
):
    inputs = fir.shape[0]
    frames = SPEC + TAPS - 1
    spread = inputs * FRAME // LANES
    groups = SPEC // GROUP
    pieces = sems.shape[0]
    rows = FRAME // pieces
    last = lax.broadcasted_iota(jnp.int32, (SUB, LANES), 0) == SUB - 1
    edges = [0, GROUP // 2] + [g * GROUP + TAPS for g in range(1, groups)] + [frames]

    def load(source, target, n):
        copy = pltpu.make_async_copy(source, target, load_sems.at[n])
        copy.start()
        return copy

    def span(n):
        return pl.ds(edges[n] * spread, (edges[n + 1] - edges[n]) * spread)

    chunks = len(edges) - 1
    loads = [load(x_hbm.at[span(n)], held.at[span(n)], n) for n in range(chunks)]
    load_taps = load(taps_hbm, taps_all, chunks)
    load_flags = load(flags_hbm, flags, chunks + 2)

    def convert(n):
        for f in range(edges[n], edges[n + 1], 2):
            count = min(2, frames - f)
            tile = held[pl.ds(f * spread, count * spread), :].astype(jnp.float32)
            for c in range(count):
                part = tile[c * spread : (c + 1) * spread]
                wide[pl.ds(f + c, spread, stride=PITCH), :] = part

    def filter_group(g, i, j):
        cols = pl.ds(j * LANES, LANES)
        taps = [jnp.broadcast_to(taps_all[pl.ds(t, 1), cols], (SUB, LANES)) for t in range(TAPS)]

        def take(b):
            first = (inputs * j + i) * PITCH + g * GROUP + b
            return wide[pl.ds(first, SUB, stride=STRIDE), :]

        def total(first, count):
            window = [take(first + b) for b in range(count + TAPS - 1)]
            out = [taps[0] * window[b] for b in range(count)]
            for t in range(1, TAPS):
                out = [out[b] + taps[t] * window[b + t] for b in range(count)]
            return out

        extra = total(STEP, 1)[0]
        for first in range(0, STEP, SUB):
            out = total(first, SUB)
            for b in range(SUB):
                past = first + b - (STEP - SUB + 1)
                if past >= 0:
                    out[b] = jnp.where(last, pltpu.roll(extra, SUB - 1 - past, 0), out[b])
            for b in range(0, SUB, 2):
                both = jnp.concatenate(out[b : b + 2], axis=0).astype(jnp.bfloat16)
                fir[i, pl.ds(g * GROUP + (first + b) * SUB, 2 * SUB), cols] = both

    def transform(g, i):
        part = pl.ds(g * GROUP, GROUP)
        spectra[i, :, part] = lax.dot_general(
            table[...],
            fir[i, part, :],
            (((1,), (1,)), ((), ())),
            preferred_element_type=jnp.float32,
        )

    def rate(i):
        good = (1 - flags[i]).astype(jnp.float32)
        for piece in range(pieces):
            pairs = spectra[i, pl.ds(piece * rows, rows), :]
            pairs = pairs.reshape(rows // (2 * SUB), 2, SUB, SPEC)
            squares = jnp.sum(pairs * pairs, axis=1)
            power = jnp.sum(squares, axis=2, keepdims=True) / SPEC
            scale = good / jnp.sqrt(power + 1e-05)
            place = pl.ds(piece * rows // 2, rows // 2)
            scales[i, place, :] = jnp.broadcast_to(scale.reshape(rows // 2, 1), (rows // 2, LANES))

    def scaled(i, piece):
        pairs = spectra[i, pl.ds(piece * rows, rows), :]
        pairs = pairs.reshape(rows // (2 * SUB), 2, SUB, SPEC)
        scale = scales[i, pl.ds(piece * rows // 2, rows // 2), :]
        scale = jnp.concatenate([scale] * (SPEC // LANES), axis=1)
        return pairs * scale.reshape(rows // (2 * SUB), 1, SUB, SPEC)

    def pack(piece):
        place = pl.ds(piece * rows, rows)
        parts = [scaled(i, piece) for i in range(inputs)]
        for p in range(2):
            both = jnp.concatenate([part[:, p] for part in parts], axis=1)
            result[place, pl.ds(p * SPEC, SPEC)] = both.astype(jnp.bfloat16).reshape(rows, SPEC)
        copy = pltpu.make_async_copy(result.at[place], out_hbm.at[place], sems.at[piece])
        copy.start()
        return copy

    loads[0].wait()
    convert(0)
    load_taps.wait()
    loads[1].wait()
    load_table = load(table_hbm, table, chunks + 1)
    convert(1)
    for i in range(inputs):
        for j in range(FRAME // LANES):
            filter_group(0, i, j)
    loads[2].wait()
    load_table.wait()
    load_flags.wait()
    for i in range(inputs):
        transform(0, i)
    convert(2)
    for i in range(inputs):
        if i > 0:
            transform(1, i - 1)
        for j in range(FRAME // LANES):
            filter_group(1, i, j)
    transform(1, inputs - 1)
    for i in range(inputs):
        rate(i)
    copies = [pack(piece) for piece in range(pieces)]
    for copy in copies:
        copy.wait()


def channelize(samples, flags, order):
    inputs = samples.shape[0]
    tiles = samples.reshape(inputs, -1, LANES)
    tiles = with_layout_constraint(tiles, Layout(major_to_minor=(1, 0, 2)))
    tiles = tiles.transpose(1, 0, 2)
    tiles = tiles.reshape(-1, LANES)
    table = twiddle().reshape(len(order), SUB, 2, FRAME)[np.asarray(order)].transpose(0, 2, 1, 3)
    table = jnp.asarray(table.reshape(FRAME, FRAME), dtype=jnp.bfloat16)
    taps = jnp.asarray(prototype())
    hbm = pl.BlockSpec(memory_space=pltpu.HBM)
    return pl.pallas_call(
        channelize_kernel,
        out_shape=jax.ShapeDtypeStruct((FRAME, inputs * SPEC), jnp.bfloat16),
        in_specs=[hbm] * 4,
        out_specs=hbm,
        scratch_shapes=[
            pltpu.SMEM(flags.shape, flags.dtype),
            pltpu.VMEM(taps.shape, taps.dtype),
            pltpu.VMEM(table.shape, table.dtype),
            pltpu.VMEM(tiles.shape, tiles.dtype),
            pltpu.VMEM((inputs * FRAME // LANES * PITCH, LANES), jnp.float32),
            pltpu.VMEM((inputs, SPEC, FRAME), jnp.bfloat16),
            pltpu.VMEM((inputs, FRAME, SPEC), jnp.float32),
            pltpu.VMEM((inputs, CH, LANES), jnp.float32),
            pltpu.VMEM((FRAME, inputs * SPEC), jnp.bfloat16),
            pltpu.SemaphoreType.DMA((SPEC // GROUP + 4,)),
            pltpu.SemaphoreType.DMA((8,)),
        ],
        cost_estimate=pl.CostEstimate(
            flops=2 * inputs * SPEC * FRAME * (FRAME + TAPS),
            bytes_accessed=4 * inputs * SPEC * FRAME,
            transcendentals=0,
        ),
    )(flags, tiles, taps, table)


def correlate_kernel(pick_ref, arrived_ref, own_ref, other_ref, slots, *, order):
    share, block, _ = own_ref.shape
    blocks = pick_ref.shape[0]
    width = blocks * block
    held = arrived_ref.shape[0] // len(order)
    first = lax.axis_index("blk") == 0
    lane = lax.broadcasted_iota(jnp.int32, (width, 2 * width), 1)
    sign = jnp.where(lane < width, 1.0 / SPEC, -1.0 / SPEC)
    for n in range(blocks):
        places = [place for place, device in enumerate(order) if device % blocks == n]
        rows = [arrived_ref[pl.ds(place * held, held), :] for place in places]
        slots[n] = jnp.dot(
            pick_ref[n], jnp.concatenate(rows, axis=0), preferred_element_type=jnp.float32
        ).astype(jnp.bfloat16)
    for k in range(share):
        pair = jnp.concatenate(
            [
                slots[n, pl.ds(k * block, block), pl.ds(p * SPEC, SPEC)]
                for p in range(2)
                for n in range(blocks)
            ],
            axis=0,
        )
        gram = lax.dot_general(
            pair, pair, (((1,), (1,)), ((), ())), preferred_element_type=jnp.float32
        )
        part = gram[:width] * sign + pltpu.roll(gram[width:], width, 1) / SPEC
        own_ref[k] = jnp.where(first, part[:block], part[block:])
        other_ref[k] = jnp.where(first, part[block:], part[:block])


def picks(orders, inputs, order, share):
    blocks, block = orders.shape
    device, held = orders // inputs, orders % inputs
    rank = [np.argsort([d for d in order if d % blocks == n]) for n in range(blocks)]
    known = jnp.asarray(np.stack(rank), dtype=jnp.int32)
    match = device[:, :, None] == jnp.arange(known.shape[1], dtype=jnp.int32)
    place = jnp.sum(jnp.where(match, known[:, None, :], 0), axis=2)
    start = ((place * inputs + held) * share)[:, None, :]
    chan = jnp.arange(share, dtype=jnp.int32)[:, None]
    target = (start + chan).reshape(blocks, share * block, 1)
    column = lax.broadcasted_iota(jnp.int32, (1, 1, known.shape[1] * inputs * share), 2)
    return (column == target).astype(jnp.bfloat16)


def correlate(arrived, pick, order, share, block):
    blocks = pick.shape[0]
    vmem = pl.BlockSpec(memory_space=pltpu.VMEM)
    tile = jax.ShapeDtypeStruct((share, block, 2 * blocks * block), jnp.float32)
    return pl.pallas_call(
        functools.partial(correlate_kernel, order=order),
        out_shape=(tile, tile),
        in_specs=[vmem, vmem],
        out_specs=(vmem, vmem),
        scratch_shapes=[pltpu.VMEM((blocks, share * block, 2 * SPEC), jnp.bfloat16)],
        compiler_params=pltpu.CompilerParams(vmem_limit_bytes=VMEM_LIMIT),
        cost_estimate=pl.CostEstimate(
            flops=4 * pick.size * SPEC, bytes_accessed=4 * arrived.size, transcendentals=0
        ),
    )(pick, arrived)


def place_kernel(packed_ref, *refs, own):
    out_ref, parts, sems = refs[-3:]
    share, _, _, width = parts.shape
    me = lax.axis_index("blk")
    start = (me if own else 1 - me) * share
    copies = []
    count = share // sems.shape[0]
    for n in range(sems.shape[0]):
        for k in range(n * count, (n + 1) * count):
            parts[k, 0] = packed_ref[k, :, :width]
            parts[k, 1] = packed_ref[k, :, width:]
        target = out_ref.at[pl.ds(start + n * count, count)]
        copies.append(pltpu.make_async_copy(parts.at[pl.ds(n * count, count)], target, sems.at[n]))
        copies[-1].start()
    for copy in copies:
        copy.wait()


def place(packed, blocks, base=None):
    share, block, lanes = packed.shape
    width = lanes // 2
    anywhere = pl.BlockSpec(memory_space=pl.ANY)
    return pl.pallas_call(
        functools.partial(place_kernel, own=base is None),
        out_shape=jax.ShapeDtypeStruct((blocks * share, 2, block, width), packed.dtype),
        in_specs=[pl.BlockSpec(memory_space=pltpu.VMEM)] + ([] if base is None else [anywhere]),
        out_specs=anywhere,
        scratch_shapes=[
            pltpu.VMEM((share, 2, block, width), packed.dtype),
            pltpu.SemaphoreType.DMA((2,)),
        ],
        input_output_aliases={} if base is None else {1: 0},
        compiler_params=pltpu.CompilerParams(vmem_limit_bytes=VMEM_LIMIT),
        cost_estimate=pl.CostEstimate(flops=0, bytes_accessed=8 * packed.size, transcendentals=0),
    )(packed, *([] if base is None else [base]))


def split_channels(freq, blocks, samples, slot_order, flags):
    share = CH // (freq * blocks)
    inputs, block = samples.shape[0], slot_order.shape[1]
    axes = ("freq", "blk")
    plane = freq * blocks // 4
    order = [
        z * plane + d
        for planes in ((3, 2), (0,), (1,))
        for core in reversed(range(blocks))
        for z in planes
        for d in reversed(range(core, plane, blocks))
    ]
    me = lax.axis_index("blk").astype(jnp.int32)
    partner = lax.ppermute(slot_order, "blk", SWAP)
    orders = jnp.where(
        me == 0,
        jnp.concatenate([slot_order, partner]),
        jnp.concatenate([partner, slot_order]),
    )
    sent = channelize(samples, flags, order)
    arrived = lax.all_to_all(
        sent, axes, split_axis=0, concat_axis=0, axis_index_groups=[order], tiled=True
    )
    pick = picks(orders, inputs, order, share)
    own, other = correlate(arrived, pick, order, share, block)
    received = lax.ppermute(other, "blk", SWAP)
    return place(received, blocks, place(own, blocks))


def gather_blocks(freq, samples, slot_order, flags):
    inputs = samples.shape[0]
    taps = jnp.asarray(prototype())
    table = jnp.asarray(twiddle().reshape(2 * CH, FRAME), dtype=jnp.bfloat16)
    good = (1 - flags).astype(jnp.float32)
    frames = samples.reshape(inputs, SPEC + TAPS - 1, FRAME)
    total = jnp.zeros((inputs, SPEC, FRAME), jnp.float32)
    for tap in range(TAPS):
        window = frames[:, tap : tap + SPEC, :].astype(jnp.float32)
        total = total + taps[tap][None, None, :] * window
    fir = total.astype(jnp.bfloat16)
    spectra = jnp.einsum("kn,isn->kis", table, fir, preferred_element_type=jnp.float32)
    squares = jnp.sum(spectra * spectra, axis=2)
    power = jnp.sum(squares.reshape(CH, 2, inputs), axis=1) / SPEC
    scale = good[None, :] / jnp.sqrt(power + 1e-05)
    quantized = (spectra * jnp.repeat(scale, 2, axis=0)[:, :, None]).astype(jnp.bfloat16)
    arrived = lax.all_to_all(quantized, "freq", split_axis=0, concat_axis=1, tiled=True)
    share = CH // freq
    block = slot_order.shape[1]
    own = jnp.take(arrived.reshape(share, 2, block, SPEC), slot_order[0], axis=2)
    piece = lax.all_gather(own, "blk", axis=2, tiled=True)
    dot = functools.partial(jnp.einsum, "cas,cbs->cab", preferred_element_type=jnp.float32)
    real = dot(own[:, 0], piece[:, 0]) + dot(own[:, 1], piece[:, 1])
    imag = dot(own[:, 1], piece[:, 0]) - dot(own[:, 0], piece[:, 1])
    return jnp.stack([real / SPEC, imag / SPEC], axis=1)


def solution(mesh):
    freq, blocks = mesh.shape["freq"], mesh.shape["blk"]

    def body(samples, slot_order, flags):
        if blocks == 2 and CH == SUB * freq * blocks:
            return split_channels(freq, blocks, samples, slot_order, flags)
        return gather_blocks(freq, samples, slot_order, flags)

    in_specs = (P(("blk", "freq"), None), P("blk", None), P(("blk", "freq")))
    out_specs = P("freq", None, "blk", None)
    return jax.shard_map(body, mesh=mesh, in_specs=in_specs, out_specs=out_specs, check_vma=False)
```

```python
import functools
import math

import jax
import jax.numpy as jnp
import numpy as np
from jax import lax
from jax.experimental import pallas as pl
from jax.experimental.pallas import tpu as pltpu
from jax.experimental.layout import Layout, with_layout_constraint
from jax.sharding import PartitionSpec as P

CH = 256
TAPS = 12
SPEC = 512
FRAME = 2 * CH
LANES = 128
SUB = 8
GROUP = 256
STEP = GROUP // SUB
STRIDE = STEP + 1
PITCH = SPEC + 25
SWAP = [(0, 1), (1, 0)]
VMEM_LIMIT = 40 * 1024 * 1024


def prototype():
    count = TAPS * FRAME
    index = np.arange(count, dtype=np.float64)
    shifted = (index + 0.5) / FRAME - TAPS / 2.0
    window = 0.5 - 0.5 * np.cos(2.0 * math.pi * (index + 0.5) / count)
    return (np.sinc(shifted) * window).astype(np.float32).reshape(TAPS, FRAME)


def twiddle():
    chan = np.arange(CH, dtype=np.int64)[:, None]
    point = np.arange(FRAME, dtype=np.int64)[None, :]
    phase = (chan * point % FRAME).astype(np.float64) * (2.0 * math.pi / FRAME)
    return np.stack([np.cos(phase), -np.sin(phase)], axis=1).astype(np.float32)


def channelize_kernel(
    flags_hbm,
    x_hbm,
    taps_hbm,
    table_hbm,
    out_hbm,
    flags,
    taps_all,
    table,
    held,
    wide,
    fir,
    spectra,
    scales,
    result,
    load_sems,
    sems,
):
    inputs = fir.shape[0]
    frames = SPEC + TAPS - 1
    spread = inputs * FRAME // LANES
    groups = SPEC // GROUP
    pieces = sems.shape[0]
    rows = FRAME // pieces
    last = lax.broadcasted_iota(jnp.int32, (SUB, LANES), 0) == SUB - 1
    edges = [0, GROUP // 2] + [g * GROUP + TAPS for g in range(1, groups)] + [frames]

    def load(source, target, n):
        copy = pltpu.make_async_copy(source, target, load_sems.at[n])
        copy.start()
        return copy

    def span(n):
        return pl.ds(edges[n] * spread, (edges[n + 1] - edges[n]) * spread)

    chunks = len(edges) - 1
    loads = [load(x_hbm.at[span(n)], held.at[span(n)], n) for n in range(chunks - 1)]
    load_taps = load(taps_hbm, taps_all, chunks)
    load_flags = load(flags_hbm, flags, chunks + 2)

    def convert(n):
        for f in range(edges[n], edges[n + 1], 2):
            count = min(2, frames - f)
            tile = held[pl.ds(f * spread, count * spread), :].astype(jnp.float32)
            for c in range(count):
                part = tile[c * spread : (c + 1) * spread]
                wide[pl.ds(f + c, spread, stride=PITCH), :] = part

    def filter_group(g, i, j):
        cols = pl.ds(j * LANES, LANES)
        taps = [jnp.broadcast_to(taps_all[pl.ds(t, 1), cols], (SUB, LANES)) for t in range(TAPS)]

        def take(b):
            first = (inputs * j + i) * PITCH + g * GROUP + b
            return wide[pl.ds(first, SUB, stride=STRIDE), :]

        def total(first, count):
            window = [take(first + b) for b in range(count + TAPS - 1)]
            out = [taps[0] * window[b] for b in range(count)]
            for t in range(1, TAPS):
                out = [out[b] + taps[t] * window[b + t] for b in range(count)]
            return out

        extra = total(STEP, 1)[0]
        for first in range(0, STEP, SUB):
            out = total(first, SUB)
            for b in range(SUB):
                past = first + b - (STEP - SUB + 1)
                if past >= 0:
                    out[b] = jnp.where(last, pltpu.roll(extra, SUB - 1 - past, 0), out[b])
            for b in range(0, SUB, 2):
                both = jnp.concatenate(out[b : b + 2], axis=0).astype(jnp.bfloat16)
                fir[i, pl.ds(g * GROUP + (first + b) * SUB, 2 * SUB), cols] = both

    def transform(g, i, points=pl.ds(0, FRAME), add=False):
        part = pl.ds(g * GROUP, GROUP)
        product = lax.dot_general(
            table[:, points],
            fir[i, part, points],
            (((1,), (1,)), ((), ())),
            preferred_element_type=jnp.float32,
        )
        spectra[i, :, part] = spectra[i, :, part] + product if add else product

    def rate(i):
        good = (1 - flags[i]).astype(jnp.float32)
        for piece in range(pieces):
            pairs = spectra[i, pl.ds(piece * rows, rows), :]
            pairs = pairs.reshape(rows // (2 * SUB), 2, SUB, SPEC)
            squares = jnp.sum(pairs * pairs, axis=1)
            power = jnp.sum(squares, axis=2, keepdims=True) / SPEC
            scale = good / jnp.sqrt(power + 1e-05)
            place = pl.ds(piece * rows // 2, rows // 2)
            scales[i, place, :] = jnp.broadcast_to(scale.reshape(rows // 2, 1), (rows // 2, LANES))

    def scaled(i, piece):
        pairs = spectra[i, pl.ds(piece * rows, rows), :]
        pairs = pairs.reshape(rows // (2 * SUB), 2, SUB, SPEC)
        scale = scales[i, pl.ds(piece * rows // 2, rows // 2), :]
        scale = jnp.concatenate([scale] * (SPEC // LANES), axis=1)
        return pairs * scale.reshape(rows // (2 * SUB), 1, SUB, SPEC)

    def pack(piece):
        place = pl.ds(piece * rows, rows)
        parts = [scaled(i, piece) for i in range(inputs)]
        for p in range(2):
            both = jnp.concatenate([part[:, p] for part in parts], axis=1)
            result[place, pl.ds(p * SPEC, SPEC)] = both.astype(jnp.bfloat16).reshape(rows, SPEC)
        copy = pltpu.make_async_copy(result.at[place], out_hbm.at[place], sems.at[piece])
        copy.start()
        return copy

    loads[0].wait()
    loads.append(load(x_hbm.at[span(chunks - 1)], held.at[span(chunks - 1)], chunks - 1))
    convert(0)
    load_taps.wait()
    loads[1].wait()
    load_table = load(table_hbm, table, chunks + 1)
    convert(1)
    for i in range(inputs):
        for j in range(FRAME // LANES):
            filter_group(0, i, j)
    loads[2].wait()
    load_table.wait()
    load_flags.wait()
    for i in range(inputs):
        transform(0, i)
    convert(2)
    halves = pl.ds(0, FRAME // 2), pl.ds(FRAME // 2, FRAME // 2)
    for i in range(inputs):
        if i > 0:
            transform(1, i - 1)
        for j in range(FRAME // LANES):
            if i == inputs - 1 and j == FRAME // LANES // 2:
                transform(1, i, halves[0])
            filter_group(1, i, j)
    transform(1, inputs - 1, halves[1], add=True)
    for i in range(inputs):
        rate(i)
    copies = [pack(piece) for piece in range(pieces)]
    for copy in copies:
        copy.wait()


def channelize(samples, flags, order):
    inputs = samples.shape[0]
    tiles = samples.reshape(inputs, -1, LANES)
    tiles = with_layout_constraint(tiles, Layout(major_to_minor=(1, 0, 2)))
    tiles = tiles.transpose(1, 0, 2)
    tiles = tiles.reshape(-1, LANES)
    table = twiddle().reshape(len(order), SUB, 2, FRAME)[np.asarray(order)].transpose(0, 2, 1, 3)
    table = jnp.asarray(table.reshape(FRAME, FRAME), dtype=jnp.bfloat16)
    taps = jnp.asarray(prototype())
    hbm = pl.BlockSpec(memory_space=pltpu.HBM)
    return pl.pallas_call(
        channelize_kernel,
        out_shape=jax.ShapeDtypeStruct((FRAME, inputs * SPEC), jnp.bfloat16),
        in_specs=[hbm] * 4,
        out_specs=hbm,
        scratch_shapes=[
            pltpu.SMEM(flags.shape, flags.dtype),
            pltpu.VMEM(taps.shape, taps.dtype),
            pltpu.VMEM(table.shape, table.dtype),
            pltpu.VMEM(tiles.shape, tiles.dtype),
            pltpu.VMEM((inputs * FRAME // LANES * PITCH, LANES), jnp.float32),
            pltpu.VMEM((inputs, SPEC, FRAME), jnp.bfloat16),
            pltpu.VMEM((inputs, FRAME, SPEC), jnp.float32),
            pltpu.VMEM((inputs, CH, LANES), jnp.float32),
            pltpu.VMEM((FRAME, inputs * SPEC), jnp.bfloat16),
            pltpu.SemaphoreType.DMA((SPEC // GROUP + 4,)),
            pltpu.SemaphoreType.DMA((8,)),
        ],
        cost_estimate=pl.CostEstimate(
            flops=2 * inputs * SPEC * FRAME * (FRAME + TAPS),
            bytes_accessed=4 * inputs * SPEC * FRAME,
            transcendentals=0,
        ),
    )(flags, tiles, taps, table)


def correlate_kernel(pick_ref, arrived_ref, own_ref, other_ref, slots, *, order):
    share, block, _ = own_ref.shape
    blocks = pick_ref.shape[0]
    width = blocks * block
    held = arrived_ref.shape[0] // len(order)
    first = lax.axis_index("blk") == 0
    lane = lax.broadcasted_iota(jnp.int32, (width, 2 * width), 1)
    sign = jnp.where(lane < width, 1.0 / SPEC, -1.0 / SPEC)
    for n in range(blocks):
        places = [place for place, device in enumerate(order) if device % blocks == n]
        rows = [arrived_ref[pl.ds(place * held, held), :] for place in places]
        slots[n] = jnp.dot(
            pick_ref[n], jnp.concatenate(rows, axis=0), preferred_element_type=jnp.float32
        ).astype(jnp.bfloat16)
    for k in range(share):
        pair = jnp.concatenate(
            [
                slots[n, pl.ds(k * block, block), pl.ds(p * SPEC, SPEC)]
                for p in range(2)
                for n in range(blocks)
            ],
            axis=0,
        )
        gram = lax.dot_general(
            pair, pair, (((1,), (1,)), ((), ())), preferred_element_type=jnp.float32
        )
        part = gram[:width] * sign + pltpu.roll(gram[width:], width, 1) / SPEC
        own_ref[k] = jnp.where(first, part[:block], part[block:])
        other_ref[k] = jnp.where(first, part[block:], part[:block])


def picks(orders, inputs, order, share):
    blocks, block = orders.shape
    device, held = orders // inputs, orders % inputs
    rank = [np.argsort([d for d in order if d % blocks == n]) for n in range(blocks)]
    known = jnp.asarray(np.stack(rank), dtype=jnp.int32)
    match = device[:, :, None] == jnp.arange(known.shape[1], dtype=jnp.int32)
    place = jnp.sum(jnp.where(match, known[:, None, :], 0), axis=2)
    start = ((place * inputs + held) * share)[:, None, :]
    chan = jnp.arange(share, dtype=jnp.int32)[:, None]
    target = (start + chan).reshape(blocks, share * block, 1)
    column = lax.broadcasted_iota(jnp.int32, (1, 1, known.shape[1] * inputs * share), 2)
    return (column == target).astype(jnp.bfloat16)


def correlate(arrived, pick, order, share, block):
    blocks = pick.shape[0]
    vmem = pl.BlockSpec(memory_space=pltpu.VMEM)
    tile = jax.ShapeDtypeStruct((share, block, 2 * blocks * block), jnp.float32)
    return pl.pallas_call(
        functools.partial(correlate_kernel, order=order),
        out_shape=(tile, tile),
        in_specs=[vmem, vmem],
        out_specs=(vmem, vmem),
        scratch_shapes=[pltpu.VMEM((blocks, share * block, 2 * SPEC), jnp.bfloat16)],
        compiler_params=pltpu.CompilerParams(vmem_limit_bytes=VMEM_LIMIT),
        cost_estimate=pl.CostEstimate(
            flops=4 * pick.size * SPEC, bytes_accessed=4 * arrived.size, transcendentals=0
        ),
    )(pick, arrived)


def place_kernel(packed_ref, *refs, own):
    out_ref, parts, sems = refs[-3:]
    share, _, _, width = parts.shape
    me = lax.axis_index("blk")
    start = (me if own else 1 - me) * share
    copies = []
    count = share // sems.shape[0]
    for n in range(sems.shape[0]):
        for k in range(n * count, (n + 1) * count):
            parts[k, 0] = packed_ref[k, :, :width]
            parts[k, 1] = packed_ref[k, :, width:]
        target = out_ref.at[pl.ds(start + n * count, count)]
        copies.append(pltpu.make_async_copy(parts.at[pl.ds(n * count, count)], target, sems.at[n]))
        copies[-1].start()
    for copy in copies:
        copy.wait()


def place(packed, blocks, base=None):
    share, block, lanes = packed.shape
    width = lanes // 2
    anywhere = pl.BlockSpec(memory_space=pl.ANY)
    return pl.pallas_call(
        functools.partial(place_kernel, own=base is None),
        out_shape=jax.ShapeDtypeStruct((blocks * share, 2, block, width), packed.dtype),
        in_specs=[pl.BlockSpec(memory_space=pltpu.VMEM)] + ([] if base is None else [anywhere]),
        out_specs=anywhere,
        scratch_shapes=[
            pltpu.VMEM((share, 2, block, width), packed.dtype),
            pltpu.SemaphoreType.DMA((2,)),
        ],
        input_output_aliases={} if base is None else {1: 0},
        compiler_params=pltpu.CompilerParams(vmem_limit_bytes=VMEM_LIMIT),
        cost_estimate=pl.CostEstimate(flops=0, bytes_accessed=8 * packed.size, transcendentals=0),
    )(packed, *([] if base is None else [base]))


def split_channels(freq, blocks, samples, slot_order, flags):
    share = CH // (freq * blocks)
    inputs, block = samples.shape[0], slot_order.shape[1]
    axes = ("freq", "blk")
    plane = freq * blocks // 4
    order = [
        z * plane + d
        for z in (3, 2, 0, 1)
        for core in reversed(range(blocks))
        for d in reversed(range(core, plane, blocks))
    ]
    me = lax.axis_index("blk").astype(jnp.int32)
    partner = lax.ppermute(slot_order, "blk", SWAP)
    orders = jnp.where(
        me == 0,
        jnp.concatenate([slot_order, partner]),
        jnp.concatenate([partner, slot_order]),
    )
    sent = channelize(samples, flags, order)
    arrived = lax.all_to_all(
        sent, axes, split_axis=0, concat_axis=0, axis_index_groups=[order], tiled=True
    )
    pick = picks(orders, inputs, order, share)
    own, other = correlate(arrived, pick, order, share, block)
    received = lax.ppermute(other, "blk", SWAP)
    return place(received, blocks, place(own, blocks))


def gather_blocks(freq, samples, slot_order, flags):
    inputs = samples.shape[0]
    taps = jnp.asarray(prototype())
    table = jnp.asarray(twiddle().reshape(2 * CH, FRAME), dtype=jnp.bfloat16)
    good = (1 - flags).astype(jnp.float32)
    frames = samples.reshape(inputs, SPEC + TAPS - 1, FRAME)
    total = jnp.zeros((inputs, SPEC, FRAME), jnp.float32)
    for tap in range(TAPS):
        window = frames[:, tap : tap + SPEC, :].astype(jnp.float32)
        total = total + taps[tap][None, None, :] * window
    fir = total.astype(jnp.bfloat16)
    spectra = jnp.einsum("kn,isn->kis", table, fir, preferred_element_type=jnp.float32)
    squares = jnp.sum(spectra * spectra, axis=2)
    power = jnp.sum(squares.reshape(CH, 2, inputs), axis=1) / SPEC
    scale = good[None, :] / jnp.sqrt(power + 1e-05)
    quantized = (spectra * jnp.repeat(scale, 2, axis=0)[:, :, None]).astype(jnp.bfloat16)
    arrived = lax.all_to_all(quantized, "freq", split_axis=0, concat_axis=1, tiled=True)
    share = CH // freq
    block = slot_order.shape[1]
    own = jnp.take(arrived.reshape(share, 2, block, SPEC), slot_order[0], axis=2)
    piece = lax.all_gather(own, "blk", axis=2, tiled=True)
    dot = functools.partial(jnp.einsum, "cas,cbs->cab", preferred_element_type=jnp.float32)
    real = dot(own[:, 0], piece[:, 0]) + dot(own[:, 1], piece[:, 1])
    imag = dot(own[:, 1], piece[:, 0]) - dot(own[:, 0], piece[:, 1])
    return jnp.stack([real / SPEC, imag / SPEC], axis=1)


def solution(mesh):
    freq, blocks = mesh.shape["freq"], mesh.shape["blk"]

    def body(samples, slot_order, flags):
        if blocks == 2 and CH == SUB * freq * blocks:
            return split_channels(freq, blocks, samples, slot_order, flags)
        return gather_blocks(freq, samples, slot_order, flags)

    in_specs = (P(("blk", "freq"), None), P("blk", None), P(("blk", "freq")))
    out_specs = P("freq", None, "blk", None)
    return jax.shard_map(body, mesh=mesh, in_specs=in_specs, out_specs=out_specs, check_vma=False)
```

```python
import functools
import math

import jax
import jax.numpy as jnp
import numpy as np
from jax import lax
from jax.experimental import pallas as pl
from jax.experimental.pallas import tpu as pltpu
from jax.experimental.layout import Layout, with_layout_constraint
from jax.sharding import PartitionSpec as P

CH = 256
TAPS = 12
SPEC = 512
FRAME = 2 * CH
LANES = 128
SUB = 8
GROUP = 256
STEP = GROUP // SUB
STRIDE = STEP + 1
PITCH = SPEC + 25
SWAP = [(0, 1), (1, 0)]
VMEM_LIMIT = 40 * 1024 * 1024


def prototype():
    count = TAPS * FRAME
    index = np.arange(count, dtype=np.float64)
    shifted = (index + 0.5) / FRAME - TAPS / 2.0
    window = 0.5 - 0.5 * np.cos(2.0 * math.pi * (index + 0.5) / count)
    return (np.sinc(shifted) * window).astype(np.float32).reshape(TAPS, FRAME)


def twiddle():
    chan = np.arange(CH, dtype=np.int64)[:, None]
    point = np.arange(FRAME, dtype=np.int64)[None, :]
    phase = (chan * point % FRAME).astype(np.float64) * (2.0 * math.pi / FRAME)
    return np.stack([np.cos(phase), -np.sin(phase)], axis=1).astype(np.float32)


def channelize_kernel(
    flags_hbm,
    x_hbm,
    taps_hbm,
    table_hbm,
    out_hbm,
    flags,
    taps_all,
    table,
    held,
    wide,
    fir,
    spectra,
    scales,
    result,
    load_sems,
    sems,
):
    inputs = fir.shape[0]
    frames = SPEC + TAPS - 1
    spread = inputs * FRAME // LANES
    groups = SPEC // GROUP
    pieces = sems.shape[0]
    rows = FRAME // pieces
    last = lax.broadcasted_iota(jnp.int32, (SUB, LANES), 0) == SUB - 1
    edges = [0, GROUP // 2] + [g * GROUP + TAPS for g in range(1, groups)] + [frames]

    def load(source, target, n):
        copy = pltpu.make_async_copy(source, target, load_sems.at[n])
        copy.start()
        return copy

    def span(n):
        return pl.ds(edges[n] * spread, (edges[n + 1] - edges[n]) * spread)

    chunks = len(edges) - 1
    loads = [load(x_hbm.at[span(n)], held.at[span(n)], n) for n in range(chunks)]
    load_taps = load(taps_hbm, taps_all, chunks)
    load_flags = load(flags_hbm, flags, chunks + 2)

    def convert(n):
        for f in range(edges[n], edges[n + 1], 2):
            count = min(2, frames - f)
            tile = held[pl.ds(f * spread, count * spread), :].astype(jnp.float32)
            for c in range(count):
                part = tile[c * spread : (c + 1) * spread]
                wide[pl.ds(f + c, spread, stride=PITCH), :] = part

    def filter_group(g, i, j):
        cols = pl.ds(j * LANES, LANES)
        taps = [jnp.broadcast_to(taps_all[pl.ds(t, 1), cols], (SUB, LANES)) for t in range(TAPS)]

        def take(b):
            first = (inputs * j + i) * PITCH + g * GROUP + b
            return wide[pl.ds(first, SUB, stride=STRIDE), :]

        window = []

        def total(first, count):
            while len(window) < first + count + TAPS - 1:
                window.append(take(len(window)))
            out = [taps[0] * window[first + b] for b in range(count)]
            for t in range(1, TAPS):
                out = [out[b] + taps[t] * window[first + b + t] for b in range(count)]
            return out

        for first in range(0, STEP, SUB):
            final = first + SUB == STEP
            out = total(first, SUB + 1 if final else SUB)
            for m in range(SUB - 1 if final else 0):
                moved = pltpu.roll(out[SUB], SUB - 1 - m, 0)
                out[m + 1] = jnp.where(last, moved, out[m + 1])
            for b in range(0, SUB, 2):
                both = jnp.concatenate(out[b : b + 2], axis=0).astype(jnp.bfloat16)
                fir[i, pl.ds(g * GROUP + (first + b) * SUB, 2 * SUB), cols] = both

    def transform(g, i):
        part = pl.ds(g * GROUP, GROUP)
        spectra[i, :, part] = lax.dot_general(
            table[...],
            fir[i, part, :],
            (((1,), (1,)), ((), ())),
            preferred_element_type=jnp.float32,
        )

    def rate(i):
        good = (1 - flags[i]).astype(jnp.float32)
        for piece in range(pieces):
            pairs = spectra[i, pl.ds(piece * rows, rows), :]
            pairs = pairs.reshape(rows // (2 * SUB), 2, SUB, SPEC)
            squares = jnp.sum(pairs * pairs, axis=1)
            power = jnp.sum(squares, axis=2, keepdims=True) / SPEC
            scale = good / jnp.sqrt(power + 1e-05)
            place = pl.ds(piece * rows // 2, rows // 2)
            scales[i, place, :] = jnp.broadcast_to(scale.reshape(rows // 2, 1), (rows // 2, LANES))

    def scaled(i, piece):
        pairs = spectra[i, pl.ds(piece * rows, rows), :]
        pairs = pairs.reshape(rows // (2 * SUB), 2, SUB, SPEC)
        scale = scales[i, pl.ds(piece * rows // 2, rows // 2), :]
        scale = jnp.concatenate([scale] * (SPEC // LANES), axis=1)
        return pairs * scale.reshape(rows // (2 * SUB), 1, SUB, SPEC)

    def pack(piece):
        place = pl.ds(piece * rows, rows)
        parts = [scaled(i, piece) for i in range(inputs)]
        for p in range(2):
            both = jnp.concatenate([part[:, p] for part in parts], axis=1)
            result[place, pl.ds(p * SPEC, SPEC)] = both.astype(jnp.bfloat16).reshape(rows, SPEC)
        copy = pltpu.make_async_copy(result.at[place], out_hbm.at[place], sems.at[piece])
        copy.start()
        return copy

    loads[0].wait()
    convert(0)
    load_taps.wait()
    loads[1].wait()
    load_table = load(table_hbm, table, chunks + 1)
    convert(1)
    for i in range(inputs):
        for j in range(FRAME // LANES):
            filter_group(0, i, j)
    loads[2].wait()
    load_table.wait()
    load_flags.wait()
    for i in range(inputs):
        transform(0, i)
    convert(2)
    for i in range(inputs):
        if i > 0:
            transform(1, i - 1)
        for j in range(FRAME // LANES):
            filter_group(1, i, j)
    transform(1, inputs - 1)
    for i in range(inputs):
        rate(i)
    copies = [pack(piece) for piece in range(pieces)]
    for copy in copies:
        copy.wait()


def channelize(samples, flags, order):
    inputs = samples.shape[0]
    tiles = samples.reshape(inputs, -1, LANES)
    tiles = with_layout_constraint(tiles, Layout(major_to_minor=(1, 0, 2)))
    tiles = tiles.transpose(1, 0, 2)
    tiles = tiles.reshape(-1, LANES)
    table = twiddle().reshape(len(order), SUB, 2, FRAME)[np.asarray(order)].transpose(0, 2, 1, 3)
    table = jnp.asarray(table.reshape(FRAME, FRAME), dtype=jnp.bfloat16)
    taps = jnp.asarray(prototype())
    hbm = pl.BlockSpec(memory_space=pltpu.HBM)
    return pl.pallas_call(
        channelize_kernel,
        out_shape=jax.ShapeDtypeStruct((FRAME, inputs * SPEC), jnp.bfloat16),
        in_specs=[hbm] * 4,
        out_specs=hbm,
        scratch_shapes=[
            pltpu.SMEM(flags.shape, flags.dtype),
            pltpu.VMEM(taps.shape, taps.dtype),
            pltpu.VMEM(table.shape, table.dtype),
            pltpu.VMEM(tiles.shape, tiles.dtype),
            pltpu.VMEM((inputs * FRAME // LANES * PITCH, LANES), jnp.float32),
            pltpu.VMEM((inputs, SPEC, FRAME), jnp.bfloat16),
            pltpu.VMEM((inputs, FRAME, SPEC), jnp.float32),
            pltpu.VMEM((inputs, CH, LANES), jnp.float32),
            pltpu.VMEM((FRAME, inputs * SPEC), jnp.bfloat16),
            pltpu.SemaphoreType.DMA((SPEC // GROUP + 4,)),
            pltpu.SemaphoreType.DMA((8,)),
        ],
        cost_estimate=pl.CostEstimate(
            flops=2 * inputs * SPEC * FRAME * (FRAME + TAPS),
            bytes_accessed=4 * inputs * SPEC * FRAME,
            transcendentals=0,
        ),
    )(flags, tiles, taps, table)


def correlate_kernel(pick_ref, arrived_ref, own_ref, other_ref, slots, *, order):
    share, block, _ = own_ref.shape
    blocks = pick_ref.shape[0]
    width = blocks * block
    held = arrived_ref.shape[0] // len(order)
    first = lax.axis_index("blk") == 0
    lane = lax.broadcasted_iota(jnp.int32, (width, 2 * width), 1)
    sign = jnp.where(lane < width, 1.0 / SPEC, -1.0 / SPEC)
    for n in range(blocks):
        places = [place for place, device in enumerate(order) if device % blocks == n]
        rows = [arrived_ref[pl.ds(place * held, held), :] for place in places]
        slots[n] = jnp.dot(
            pick_ref[n], jnp.concatenate(rows, axis=0), preferred_element_type=jnp.float32
        ).astype(jnp.bfloat16)
    for k in range(share):
        pair = jnp.concatenate(
            [
                slots[n, pl.ds(k * block, block), pl.ds(p * SPEC, SPEC)]
                for p in range(2)
                for n in range(blocks)
            ],
            axis=0,
        )
        gram = lax.dot_general(
            pair, pair, (((1,), (1,)), ((), ())), preferred_element_type=jnp.float32
        )
        part = gram[:width] * sign + pltpu.roll(gram[width:], width, 1) / SPEC
        own_ref[k] = jnp.where(first, part[:block], part[block:])
        other_ref[k] = jnp.where(first, part[block:], part[:block])


def picks(orders, inputs, order, share):
    blocks, block = orders.shape
    device, held = orders // inputs, orders % inputs
    rank = [np.argsort([d for d in order if d % blocks == n]) for n in range(blocks)]
    known = jnp.asarray(np.stack(rank), dtype=jnp.int32)
    match = device[:, :, None] == jnp.arange(known.shape[1], dtype=jnp.int32)
    place = jnp.sum(jnp.where(match, known[:, None, :], 0), axis=2)
    start = ((place * inputs + held) * share)[:, None, :]
    chan = jnp.arange(share, dtype=jnp.int32)[:, None]
    target = (start + chan).reshape(blocks, share * block, 1)
    column = lax.broadcasted_iota(jnp.int32, (1, 1, known.shape[1] * inputs * share), 2)
    return (column == target).astype(jnp.bfloat16)


def correlate(arrived, pick, order, share, block):
    blocks = pick.shape[0]
    vmem = pl.BlockSpec(memory_space=pltpu.VMEM)
    tile = jax.ShapeDtypeStruct((share, block, 2 * blocks * block), jnp.float32)
    return pl.pallas_call(
        functools.partial(correlate_kernel, order=order),
        out_shape=(tile, tile),
        in_specs=[vmem, vmem],
        out_specs=(vmem, vmem),
        scratch_shapes=[pltpu.VMEM((blocks, share * block, 2 * SPEC), jnp.bfloat16)],
        compiler_params=pltpu.CompilerParams(vmem_limit_bytes=VMEM_LIMIT),
        cost_estimate=pl.CostEstimate(
            flops=4 * pick.size * SPEC, bytes_accessed=4 * arrived.size, transcendentals=0
        ),
    )(pick, arrived)


def place_kernel(packed_ref, *refs, own):
    out_ref, parts, sems = refs[-3:]
    share, _, _, width = parts.shape
    me = lax.axis_index("blk")
    start = (me if own else 1 - me) * share
    copies = []
    count = share // sems.shape[0]
    for n in range(sems.shape[0]):
        for k in range(n * count, (n + 1) * count):
            parts[k, 0] = packed_ref[k, :, :width]
            parts[k, 1] = packed_ref[k, :, width:]
        target = out_ref.at[pl.ds(start + n * count, count)]
        copies.append(pltpu.make_async_copy(parts.at[pl.ds(n * count, count)], target, sems.at[n]))
        copies[-1].start()
    for copy in copies:
        copy.wait()


def place(packed, blocks, base=None):
    share, block, lanes = packed.shape
    width = lanes // 2
    anywhere = pl.BlockSpec(memory_space=pl.ANY)
    return pl.pallas_call(
        functools.partial(place_kernel, own=base is None),
        out_shape=jax.ShapeDtypeStruct((blocks * share, 2, block, width), packed.dtype),
        in_specs=[pl.BlockSpec(memory_space=pltpu.VMEM)] + ([] if base is None else [anywhere]),
        out_specs=anywhere,
        scratch_shapes=[
            pltpu.VMEM((share, 2, block, width), packed.dtype),
            pltpu.SemaphoreType.DMA((2,)),
        ],
        input_output_aliases={} if base is None else {1: 0},
        compiler_params=pltpu.CompilerParams(vmem_limit_bytes=VMEM_LIMIT),
        cost_estimate=pl.CostEstimate(flops=0, bytes_accessed=8 * packed.size, transcendentals=0),
    )(packed, *([] if base is None else [base]))


def split_channels(freq, blocks, samples, slot_order, flags):
    share = CH // (freq * blocks)
    inputs, block = samples.shape[0], slot_order.shape[1]
    axes = ("freq", "blk")
    plane = freq * blocks // 4
    order = [
        z * plane + d
        for z in (3, 2, 0, 1)
        for core in reversed(range(blocks))
        for d in reversed(range(core, plane, blocks))
    ]
    me = lax.axis_index("blk").astype(jnp.int32)
    partner = lax.ppermute(slot_order, "blk", SWAP)
    orders = jnp.where(
        me == 0,
        jnp.concatenate([slot_order, partner]),
        jnp.concatenate([partner, slot_order]),
    )
    sent = channelize(samples, flags, order)
    arrived = lax.all_to_all(
        sent, axes, split_axis=0, concat_axis=0, axis_index_groups=[order], tiled=True
    )
    pick = picks(orders, inputs, order, share)
    own, other = correlate(arrived, pick, order, share, block)
    received = lax.ppermute(other, "blk", SWAP)
    return place(received, blocks, place(own, blocks))


def gather_blocks(freq, samples, slot_order, flags):
    inputs = samples.shape[0]
    taps = jnp.asarray(prototype())
    table = jnp.asarray(twiddle().reshape(2 * CH, FRAME), dtype=jnp.bfloat16)
    good = (1 - flags).astype(jnp.float32)
    frames = samples.reshape(inputs, SPEC + TAPS - 1, FRAME)
    total = jnp.zeros((inputs, SPEC, FRAME), jnp.float32)
    for tap in range(TAPS):
        window = frames[:, tap : tap + SPEC, :].astype(jnp.float32)
        total = total + taps[tap][None, None, :] * window
    fir = total.astype(jnp.bfloat16)
    spectra = jnp.einsum("kn,isn->kis", table, fir, preferred_element_type=jnp.float32)
    squares = jnp.sum(spectra * spectra, axis=2)
    power = jnp.sum(squares.reshape(CH, 2, inputs), axis=1) / SPEC
    scale = good[None, :] / jnp.sqrt(power + 1e-05)
    quantized = (spectra * jnp.repeat(scale, 2, axis=0)[:, :, None]).astype(jnp.bfloat16)
    arrived = lax.all_to_all(quantized, "freq", split_axis=0, concat_axis=1, tiled=True)
    share = CH // freq
    block = slot_order.shape[1]
    own = jnp.take(arrived.reshape(share, 2, block, SPEC), slot_order[0], axis=2)
    piece = lax.all_gather(own, "blk", axis=2, tiled=True)
    dot = functools.partial(jnp.einsum, "cas,cbs->cab", preferred_element_type=jnp.float32)
    real = dot(own[:, 0], piece[:, 0]) + dot(own[:, 1], piece[:, 1])
    imag = dot(own[:, 1], piece[:, 0]) - dot(own[:, 0], piece[:, 1])
    return jnp.stack([real / SPEC, imag / SPEC], axis=1)


def solution(mesh):
    freq, blocks = mesh.shape["freq"], mesh.shape["blk"]

    def body(samples, slot_order, flags):
        if blocks == 2 and CH == SUB * freq * blocks:
            return split_channels(freq, blocks, samples, slot_order, flags)
        return gather_blocks(freq, samples, slot_order, flags)

    in_specs = (P(("blk", "freq"), None), P("blk", None), P(("blk", "freq")))
    out_specs = P("freq", None, "blk", None)
    return jax.shard_map(body, mesh=mesh, in_specs=in_specs, out_specs=out_specs, check_vma=False)
```

```python
import functools
import math

import jax
import jax.numpy as jnp
import numpy as np
from jax import lax
from jax.experimental import pallas as pl
from jax.experimental.pallas import tpu as pltpu
from jax.experimental.layout import Layout, with_layout_constraint
from jax.sharding import PartitionSpec as P

CH = 256
TAPS = 12
SPEC = 512
FRAME = 2 * CH
LANES = 128
SUB = 8
GROUP = 256
STEP = GROUP // SUB
STRIDE = STEP + 1
PITCH = SPEC + 25
SWAP = [(0, 1), (1, 0)]
VMEM_LIMIT = 40 * 1024 * 1024


def prototype():
    count = TAPS * FRAME
    index = np.arange(count, dtype=np.float64)
    shifted = (index + 0.5) / FRAME - TAPS / 2.0
    window = 0.5 - 0.5 * np.cos(2.0 * math.pi * (index + 0.5) / count)
    return (np.sinc(shifted) * window).astype(np.float32).reshape(TAPS, FRAME)


def twiddle():
    chan = np.arange(CH, dtype=np.int64)[:, None]
    point = np.arange(FRAME, dtype=np.int64)[None, :]
    phase = (chan * point % FRAME).astype(np.float64) * (2.0 * math.pi / FRAME)
    return np.stack([np.cos(phase), -np.sin(phase)], axis=1).astype(np.float32)


def channelize_kernel(
    flags_hbm,
    x_hbm,
    taps_hbm,
    table_hbm,
    out_hbm,
    flags,
    taps_all,
    table,
    held,
    wide,
    fir,
    spectra,
    scales,
    result,
    load_sems,
    sems,
):
    inputs = fir.shape[0]
    frames = SPEC + TAPS - 1
    spread = inputs * FRAME // LANES
    groups = SPEC // GROUP
    pieces = sems.shape[0]
    rows = FRAME // pieces
    last = lax.broadcasted_iota(jnp.int32, (SUB, LANES), 0) == SUB - 1
    edges = [0, GROUP // 2] + [g * GROUP + TAPS for g in range(1, groups)] + [frames]

    def load(source, target, n):
        copy = pltpu.make_async_copy(source, target, load_sems.at[n])
        copy.start()
        return copy

    def span(n):
        return pl.ds(edges[n] * spread, (edges[n + 1] - edges[n]) * spread)

    chunks = len(edges) - 1
    loads = [load(x_hbm.at[span(n)], held.at[span(n)], n) for n in range(chunks)]
    load_taps = load(taps_hbm, taps_all, chunks)
    load_flags = load(flags_hbm, flags, chunks + 2)
    load_table = load(table_hbm, table, chunks + 1)

    def convert(n):
        for f in range(edges[n], edges[n + 1], 2):
            count = min(2, frames - f)
            tile = held[pl.ds(f * spread, count * spread), :].astype(jnp.float32)
            for c in range(count):
                part = tile[c * spread : (c + 1) * spread]
                wide[pl.ds(f + c, spread, stride=PITCH), :] = part

    def filter_group(g, i, j):
        cols = pl.ds(j * LANES, LANES)
        taps = [jnp.broadcast_to(taps_all[pl.ds(t, 1), cols], (SUB, LANES)) for t in range(TAPS)]

        def take(b):
            first = (inputs * j + i) * PITCH + g * GROUP + b
            return wide[pl.ds(first, SUB, stride=STRIDE), :]

        window = []

        def total(first, count):
            while len(window) < first + count + TAPS - 1:
                window.append(take(len(window)))
            out = [taps[0] * window[first + b] for b in range(count)]
            for t in range(1, TAPS):
                out = [out[b] + taps[t] * window[first + b + t] for b in range(count)]
            return out

        for first in range(0, STEP, SUB):
            final = first + SUB == STEP
            out = total(first, SUB + 1 if final else SUB)
            for m in range(SUB - 1 if final else 0):
                moved = pltpu.roll(out[SUB], SUB - 1 - m, 0)
                out[m + 1] = jnp.where(last, moved, out[m + 1])
            for b in range(0, SUB, 2):
                both = jnp.concatenate(out[b : b + 2], axis=0).astype(jnp.bfloat16)
                fir[i, pl.ds(g * GROUP + (first + b) * SUB, 2 * SUB), cols] = both

    def transform(g, i):
        part = pl.ds(g * GROUP, GROUP)
        spectra[i, :, part] = lax.dot_general(
            table[...],
            fir[i, part, :],
            (((1,), (1,)), ((), ())),
            preferred_element_type=jnp.float32,
        )

    def rate(i):
        good = (1 - flags[i]).astype(jnp.float32)
        for piece in range(pieces):
            pairs = spectra[i, pl.ds(piece * rows, rows), :]
            pairs = pairs.reshape(rows // (2 * SUB), 2, SUB, SPEC)
            squares = jnp.sum(pairs * pairs, axis=1)
            power = jnp.sum(squares, axis=2, keepdims=True) / SPEC
            scale = good / jnp.sqrt(power + 1e-05)
            place = pl.ds(piece * rows // 2, rows // 2)
            scales[i, place, :] = jnp.broadcast_to(scale.reshape(rows // 2, 1), (rows // 2, LANES))

    def scaled(i, piece):
        pairs = spectra[i, pl.ds(piece * rows, rows), :]
        pairs = pairs.reshape(rows // (2 * SUB), 2, SUB, SPEC)
        scale = scales[i, pl.ds(piece * rows // 2, rows // 2), :]
        scale = jnp.concatenate([scale] * (SPEC // LANES), axis=1)
        return pairs * scale.reshape(rows // (2 * SUB), 1, SUB, SPEC)

    def pack(piece):
        place = pl.ds(piece * rows, rows)
        parts = [scaled(i, piece) for i in range(inputs)]
        for p in range(2):
            both = jnp.concatenate([part[:, p] for part in parts], axis=1)
            result[place, pl.ds(p * SPEC, SPEC)] = both.astype(jnp.bfloat16).reshape(rows, SPEC)
        copy = pltpu.make_async_copy(result.at[place], out_hbm.at[place], sems.at[piece])
        copy.start()
        return copy

    for copy in [*loads, load_taps, load_flags, load_table]:
        copy.wait()
    convert(0)
    convert(1)
    for i in range(inputs):
        for j in range(FRAME // LANES):
            filter_group(0, i, j)
    for i in range(inputs):
        transform(0, i)
    convert(2)
    for i in range(inputs):
        if i > 0:
            transform(1, i - 1)
        for j in range(FRAME // LANES):
            filter_group(1, i, j)
    transform(1, inputs - 1)
    for i in range(inputs):
        rate(i)
    copies = [pack(piece) for piece in range(pieces)]
    for copy in copies:
        copy.wait()


def channelize(samples, flags, order):
    inputs = samples.shape[0]
    tiles = samples.reshape(inputs, -1, LANES)
    tiles = with_layout_constraint(tiles, Layout(major_to_minor=(1, 0, 2)))
    tiles = tiles.transpose(1, 0, 2)
    tiles = tiles.reshape(-1, LANES)
    table = twiddle().reshape(len(order), SUB, 2, FRAME)[np.asarray(order)].transpose(0, 2, 1, 3)
    table = jnp.asarray(table.reshape(FRAME, FRAME), dtype=jnp.bfloat16)
    taps = jnp.asarray(prototype())
    hbm = pl.BlockSpec(memory_space=pltpu.HBM)
    return pl.pallas_call(
        channelize_kernel,
        out_shape=jax.ShapeDtypeStruct((FRAME, inputs * SPEC), jnp.bfloat16),
        in_specs=[hbm] * 4,
        out_specs=hbm,
        scratch_shapes=[
            pltpu.SMEM(flags.shape, flags.dtype),
            pltpu.VMEM(taps.shape, taps.dtype),
            pltpu.VMEM(table.shape, table.dtype),
            pltpu.VMEM(tiles.shape, tiles.dtype),
            pltpu.VMEM((inputs * FRAME // LANES * PITCH, LANES), jnp.float32),
            pltpu.VMEM((inputs, SPEC, FRAME), jnp.bfloat16),
            pltpu.VMEM((inputs, FRAME, SPEC), jnp.float32),
            pltpu.VMEM((inputs, CH, LANES), jnp.float32),
            pltpu.VMEM((FRAME, inputs * SPEC), jnp.bfloat16),
            pltpu.SemaphoreType.DMA((SPEC // GROUP + 4,)),
            pltpu.SemaphoreType.DMA((8,)),
        ],
        cost_estimate=pl.CostEstimate(
            flops=2 * inputs * SPEC * FRAME * (FRAME + TAPS),
            bytes_accessed=4 * inputs * SPEC * FRAME,
            transcendentals=0,
        ),
    )(flags, tiles, taps, table)


def correlate_kernel(pick_ref, arrived_ref, own_ref, other_ref, slots, *, order):
    share, block, _ = own_ref.shape
    blocks = pick_ref.shape[0]
    width = blocks * block
    held = arrived_ref.shape[0] // len(order)
    first = lax.axis_index("blk") == 0
    lane = lax.broadcasted_iota(jnp.int32, (width, 2 * width), 1)
    sign = jnp.where(lane < width, 1.0 / SPEC, -1.0 / SPEC)
    for n in range(blocks):
        places = [place for place, device in enumerate(order) if device % blocks == n]
        rows = [arrived_ref[pl.ds(place * held, held), :] for place in places]
        slots[n] = jnp.dot(
            pick_ref[n], jnp.concatenate(rows, axis=0), preferred_element_type=jnp.float32
        ).astype(jnp.bfloat16)
    for k in range(share):
        pair = jnp.concatenate(
            [
                slots[n, pl.ds(k * block, block), pl.ds(p * SPEC, SPEC)]
                for p in range(2)
                for n in range(blocks)
            ],
            axis=0,
        )
        gram = lax.dot_general(
            pair, pair, (((1,), (1,)), ((), ())), preferred_element_type=jnp.float32
        )
        part = gram[:width] * sign + pltpu.roll(gram[width:], width, 1) / SPEC
        own_ref[k] = jnp.where(first, part[:block], part[block:])
        other_ref[k] = jnp.where(first, part[block:], part[:block])


def picks(orders, inputs, order, share):
    blocks, block = orders.shape
    device, held = orders // inputs, orders % inputs
    rank = [np.argsort([d for d in order if d % blocks == n]) for n in range(blocks)]
    known = jnp.asarray(np.stack(rank), dtype=jnp.int32)
    match = device[:, :, None] == jnp.arange(known.shape[1], dtype=jnp.int32)
    place = jnp.sum(jnp.where(match, known[:, None, :], 0), axis=2)
    start = ((place * inputs + held) * share)[:, None, :]
    chan = jnp.arange(share, dtype=jnp.int32)[:, None]
    target = (start + chan).reshape(blocks, share * block, 1)
    column = lax.broadcasted_iota(jnp.int32, (1, 1, known.shape[1] * inputs * share), 2)
    return (column == target).astype(jnp.bfloat16)


def correlate(arrived, pick, order, share, block):
    blocks = pick.shape[0]
    vmem = pl.BlockSpec(memory_space=pltpu.VMEM)
    tile = jax.ShapeDtypeStruct((share, block, 2 * blocks * block), jnp.float32)
    return pl.pallas_call(
        functools.partial(correlate_kernel, order=order),
        out_shape=(tile, tile),
        in_specs=[vmem, vmem],
        out_specs=(vmem, vmem),
        scratch_shapes=[pltpu.VMEM((blocks, share * block, 2 * SPEC), jnp.bfloat16)],
        compiler_params=pltpu.CompilerParams(vmem_limit_bytes=VMEM_LIMIT),
        cost_estimate=pl.CostEstimate(
            flops=4 * pick.size * SPEC, bytes_accessed=4 * arrived.size, transcendentals=0
        ),
    )(pick, arrived)


def place_kernel(packed_ref, *refs, own):
    out_ref, parts, sems = refs[-3:]
    share, _, _, width = parts.shape
    me = lax.axis_index("blk")
    start = (me if own else 1 - me) * share
    copies = []
    count = share // sems.shape[0]
    for n in range(sems.shape[0]):
        for k in range(n * count, (n + 1) * count):
            parts[k, 0] = packed_ref[k, :, :width]
            parts[k, 1] = packed_ref[k, :, width:]
        target = out_ref.at[pl.ds(start + n * count, count)]
        copies.append(pltpu.make_async_copy(parts.at[pl.ds(n * count, count)], target, sems.at[n]))
        copies[-1].start()
    for copy in copies:
        copy.wait()


def place(packed, blocks, base=None):
    share, block, lanes = packed.shape
    width = lanes // 2
    anywhere = pl.BlockSpec(memory_space=pl.ANY)
    return pl.pallas_call(
        functools.partial(place_kernel, own=base is None),
        out_shape=jax.ShapeDtypeStruct((blocks * share, 2, block, width), packed.dtype),
        in_specs=[pl.BlockSpec(memory_space=pltpu.VMEM)] + ([] if base is None else [anywhere]),
        out_specs=anywhere,
        scratch_shapes=[
            pltpu.VMEM((share, 2, block, width), packed.dtype),
            pltpu.SemaphoreType.DMA((2,)),
        ],
        input_output_aliases={} if base is None else {1: 0},
        compiler_params=pltpu.CompilerParams(vmem_limit_bytes=VMEM_LIMIT),
        cost_estimate=pl.CostEstimate(flops=0, bytes_accessed=8 * packed.size, transcendentals=0),
    )(packed, *([] if base is None else [base]))


def split_channels(freq, blocks, samples, slot_order, flags):
    share = CH // (freq * blocks)
    inputs, block = samples.shape[0], slot_order.shape[1]
    axes = ("freq", "blk")
    plane = freq * blocks // 4
    order = [
        z * plane + d
        for z in (3, 2, 0, 1)
        for core in reversed(range(blocks))
        for d in reversed(range(core, plane, blocks))
    ]
    me = lax.axis_index("blk").astype(jnp.int32)
    partner = lax.ppermute(slot_order, "blk", SWAP)
    orders = jnp.where(
        me == 0,
        jnp.concatenate([slot_order, partner]),
        jnp.concatenate([partner, slot_order]),
    )
    sent = channelize(samples, flags, order)
    arrived = lax.all_to_all(
        sent, axes, split_axis=0, concat_axis=0, axis_index_groups=[order], tiled=True
    )
    pick = picks(orders, inputs, order, share)
    own, other = correlate(arrived, pick, order, share, block)
    received = lax.ppermute(other, "blk", SWAP)
    return place(received, blocks, place(own, blocks))


def gather_blocks(freq, samples, slot_order, flags):
    inputs = samples.shape[0]
    taps = jnp.asarray(prototype())
    table = jnp.asarray(twiddle().reshape(2 * CH, FRAME), dtype=jnp.bfloat16)
    good = (1 - flags).astype(jnp.float32)
    frames = samples.reshape(inputs, SPEC + TAPS - 1, FRAME)
    total = jnp.zeros((inputs, SPEC, FRAME), jnp.float32)
    for tap in range(TAPS):
        window = frames[:, tap : tap + SPEC, :].astype(jnp.float32)
        total = total + taps[tap][None, None, :] * window
    fir = total.astype(jnp.bfloat16)
    spectra = jnp.einsum("kn,isn->kis", table, fir, preferred_element_type=jnp.float32)
    squares = jnp.sum(spectra * spectra, axis=2)
    power = jnp.sum(squares.reshape(CH, 2, inputs), axis=1) / SPEC
    scale = good[None, :] / jnp.sqrt(power + 1e-05)
    quantized = (spectra * jnp.repeat(scale, 2, axis=0)[:, :, None]).astype(jnp.bfloat16)
    arrived = lax.all_to_all(quantized, "freq", split_axis=0, concat_axis=1, tiled=True)
    share = CH // freq
    block = slot_order.shape[1]
    own = jnp.take(arrived.reshape(share, 2, block, SPEC), slot_order[0], axis=2)
    piece = lax.all_gather(own, "blk", axis=2, tiled=True)
    dot = functools.partial(jnp.einsum, "cas,cbs->cab", preferred_element_type=jnp.float32)
    real = dot(own[:, 0], piece[:, 0]) + dot(own[:, 1], piece[:, 1])
    imag = dot(own[:, 1], piece[:, 0]) - dot(own[:, 0], piece[:, 1])
    return jnp.stack([real / SPEC, imag / SPEC], axis=1)


def solution(mesh):
    freq, blocks = mesh.shape["freq"], mesh.shape["blk"]

    def body(samples, slot_order, flags):
        if blocks == 2 and CH == SUB * freq * blocks:
            return split_channels(freq, blocks, samples, slot_order, flags)
        return gather_blocks(freq, samples, slot_order, flags)

    in_specs = (P(("blk", "freq"), None), P("blk", None), P(("blk", "freq")))
    out_specs = P("freq", None, "blk", None)
    return jax.shard_map(body, mesh=mesh, in_specs=in_specs, out_specs=out_specs, check_vma=False)
```

```python
import functools
import math

import jax
import jax.numpy as jnp
import numpy as np
from jax import lax
from jax.experimental import pallas as pl
from jax.experimental.pallas import tpu as pltpu
from jax.experimental.layout import Layout, with_layout_constraint
from jax.sharding import PartitionSpec as P

CH = 256
TAPS = 12
SPEC = 512
FRAME = 2 * CH
LANES = 128
SUB = 8
GROUP = 256
STEP = GROUP // SUB
STRIDE = STEP + 1
PITCH = SPEC + 25
SWAP = [(0, 1), (1, 0)]
VMEM_LIMIT = 40 * 1024 * 1024


def prototype():
    count = TAPS * FRAME
    index = np.arange(count, dtype=np.float64)
    shifted = (index + 0.5) / FRAME - TAPS / 2.0
    window = 0.5 - 0.5 * np.cos(2.0 * math.pi * (index + 0.5) / count)
    return (np.sinc(shifted) * window).astype(np.float32).reshape(TAPS, FRAME)


def twiddle():
    chan = np.arange(CH, dtype=np.int64)[:, None]
    point = np.arange(FRAME, dtype=np.int64)[None, :]
    phase = (chan * point % FRAME).astype(np.float64) * (2.0 * math.pi / FRAME)
    return np.stack([np.cos(phase), -np.sin(phase)], axis=1).astype(np.float32)


def channelize_kernel(
    flags_hbm,
    x_hbm,
    taps_hbm,
    table_hbm,
    out_hbm,
    flags,
    taps_all,
    table,
    held,
    wide,
    fir,
    spectra,
    scales,
    result,
    load_sems,
    sems,
):
    inputs = fir.shape[0]
    frames = SPEC + TAPS - 1
    spread = inputs * FRAME // LANES
    groups = SPEC // GROUP
    pieces = sems.shape[1]
    rows = FRAME // pieces
    last = lax.broadcasted_iota(jnp.int32, (SUB, LANES), 0) == SUB - 1
    edges = [0, GROUP // 2] + [g * GROUP + TAPS for g in range(1, groups)] + [frames]

    def load(source, target, n):
        copy = pltpu.make_async_copy(source, target, load_sems.at[n])
        copy.start()
        return copy

    def span(n):
        return pl.ds(edges[n] * spread, (edges[n + 1] - edges[n]) * spread)

    chunks = len(edges) - 1
    loads = [load(x_hbm.at[span(n)], held.at[span(n)], n) for n in range(chunks)]
    load_taps = load(taps_hbm, taps_all, chunks)
    load_flags = load(flags_hbm, flags, chunks + 2)

    def convert(n):
        for f in range(edges[n], edges[n + 1], 2):
            count = min(2, frames - f)
            tile = held[pl.ds(f * spread, count * spread), :].astype(jnp.float32)
            for c in range(count):
                part = tile[c * spread : (c + 1) * spread]
                wide[pl.ds(f + c, spread, stride=PITCH), :] = part

    def filter_group(g, i, j):
        cols = pl.ds(j * LANES, LANES)
        taps = [jnp.broadcast_to(taps_all[pl.ds(t, 1), cols], (SUB, LANES)) for t in range(TAPS)]

        def take(b):
            first = (inputs * j + i) * PITCH + g * GROUP + b
            return wide[pl.ds(first, SUB, stride=STRIDE), :]

        window = []

        def total(first, count):
            while len(window) < first + count + TAPS - 1:
                window.append(take(len(window)))
            out = [taps[0] * window[first + b] for b in range(count)]
            for t in range(1, TAPS):
                out = [out[b] + taps[t] * window[first + b + t] for b in range(count)]
            return out

        for first in range(0, STEP, SUB):
            final = first + SUB == STEP
            out = total(first, SUB + 1 if final else SUB)
            for m in range(SUB - 1 if final else 0):
                moved = pltpu.roll(out[SUB], SUB - 1 - m, 0)
                out[m + 1] = jnp.where(last, moved, out[m + 1])
            for b in range(0, SUB, 2):
                both = jnp.concatenate(out[b : b + 2], axis=0).astype(jnp.bfloat16)
                fir[i, pl.ds(g * GROUP + (first + b) * SUB, 2 * SUB), cols] = both

    def transform(g, i):
        part = pl.ds(g * GROUP, GROUP)
        spectra[i, :, part] = lax.dot_general(
            table[...],
            fir[i, part, :],
            (((1,), (1,)), ((), ())),
            preferred_element_type=jnp.float32,
        )

    def rate(i):
        good = (1 - flags[i]).astype(jnp.float32)
        for piece in range(pieces):
            pairs = spectra[i, pl.ds(piece * rows, rows), :]
            pairs = pairs.reshape(rows // (2 * SUB), 2, SUB, SPEC)
            squares = jnp.sum(pairs * pairs, axis=1)
            power = jnp.sum(squares, axis=2, keepdims=True) / SPEC
            scale = good / jnp.sqrt(power + 1e-05)
            place = pl.ds(piece * rows // 2, rows // 2)
            scales[i, place, :] = jnp.broadcast_to(scale.reshape(rows // 2, 1), (rows // 2, LANES))

    def scaled(i, piece):
        pairs = spectra[i, pl.ds(piece * rows, rows), :]
        pairs = pairs.reshape(rows // (2 * SUB), 2, SUB, SPEC)
        scale = scales[i, pl.ds(piece * rows // 2, rows // 2), :]
        scale = jnp.concatenate([scale] * (SPEC // LANES), axis=1)
        return pairs * scale.reshape(rows // (2 * SUB), 1, SUB, SPEC)

    def pack(i, piece):
        part = scaled(i, piece).astype(jnp.bfloat16)
        for p in range(2):
            place = (pl.ds(piece * rows // 2, rows // 2), pl.ds((2 * i + p) * SPEC, SPEC))
            result[place] = part[:, p].reshape(rows // 2, SPEC)

    def store(i, piece):
        place = (pl.ds(piece * rows // 2, rows // 2), pl.ds(2 * i * SPEC, 2 * SPEC))
        copy = pltpu.make_async_copy(result.at[place], out_hbm.at[place], sems.at[i, piece])
        copy.start()
        return copy

    loads[0].wait()
    convert(0)
    load_taps.wait()
    loads[1].wait()
    load_table = load(table_hbm, table, chunks + 1)
    convert(1)
    for i in range(inputs):
        for j in range(FRAME // LANES):
            filter_group(0, i, j)
    loads[2].wait()
    load_table.wait()
    load_flags.wait()
    for i in range(inputs):
        transform(0, i)
    convert(2)
    copies = []
    for i in range(inputs):
        if i > 0:
            transform(1, i - 1)
        for j in range(FRAME // LANES):
            filter_group(1, i, j)
        if i > 0:
            rate(i - 1)
            for piece in range(pieces):
                pack(i - 1, piece)
            copies += [store(i - 1, piece) for piece in range(pieces)]
    transform(1, inputs - 1)
    rate(inputs - 1)
    for piece in range(pieces):
        pack(inputs - 1, piece)
        copies.append(store(inputs - 1, piece))
    for copy in copies:
        copy.wait()


def channelize(samples, flags, order):
    inputs = samples.shape[0]
    tiles = samples.reshape(inputs, -1, LANES)
    tiles = with_layout_constraint(tiles, Layout(major_to_minor=(1, 0, 2)))
    tiles = tiles.transpose(1, 0, 2)
    tiles = tiles.reshape(-1, LANES)
    table = twiddle().reshape(len(order), SUB, 2, FRAME)[np.asarray(order)].transpose(0, 2, 1, 3)
    table = jnp.asarray(table.reshape(FRAME, FRAME), dtype=jnp.bfloat16)
    taps = jnp.asarray(prototype())
    hbm = pl.BlockSpec(memory_space=pltpu.HBM)
    return pl.pallas_call(
        channelize_kernel,
        out_shape=jax.ShapeDtypeStruct((CH, inputs * 2 * SPEC), jnp.bfloat16),
        in_specs=[hbm] * 4,
        out_specs=hbm,
        scratch_shapes=[
            pltpu.SMEM(flags.shape, flags.dtype),
            pltpu.VMEM(taps.shape, taps.dtype),
            pltpu.VMEM(table.shape, table.dtype),
            pltpu.VMEM(tiles.shape, tiles.dtype),
            pltpu.VMEM((inputs * FRAME // LANES * PITCH, LANES), jnp.float32),
            pltpu.VMEM((inputs, SPEC, FRAME), jnp.bfloat16),
            pltpu.VMEM((inputs, FRAME, SPEC), jnp.float32),
            pltpu.VMEM((inputs, CH, LANES), jnp.float32),
            pltpu.VMEM((CH, inputs * 2 * SPEC), jnp.bfloat16),
            pltpu.SemaphoreType.DMA((SPEC // GROUP + 4,)),
            pltpu.SemaphoreType.DMA((inputs, 4)),
        ],
        cost_estimate=pl.CostEstimate(
            flops=2 * inputs * SPEC * FRAME * (FRAME + TAPS),
            bytes_accessed=4 * inputs * SPEC * FRAME,
            transcendentals=0,
        ),
    )(flags, tiles, taps, table)


def correlate_kernel(pick_ref, arrived_ref, own_ref, other_ref, slots, *, order):
    share, block, _ = own_ref.shape
    blocks = pick_ref.shape[0]
    width = blocks * block
    first = lax.axis_index("blk") == 0
    lane = lax.broadcasted_iota(jnp.int32, (width, 2 * width), 1)
    sign = jnp.where(lane < width, 1.0 / SPEC, -1.0 / SPEC)
    for n in range(blocks):
        places = [place for place, device in enumerate(order) if device % blocks == n]
        rows = [
            arrived_ref[pl.ds(place * share, 2 * share), pl.ds(2 * i * SPEC, 2 * SPEC)]
            for i in range(arrived_ref.shape[1] // (2 * SPEC))
            for place in places[::2]
        ]
        slots[n] = jnp.dot(
            pick_ref[n], jnp.concatenate(rows, axis=0), preferred_element_type=jnp.float32
        ).astype(jnp.bfloat16)
    for k in range(share):
        pair = jnp.concatenate(
            [
                slots[n, pl.ds(k * block, block), pl.ds(p * SPEC, SPEC)]
                for p in range(2)
                for n in range(blocks)
            ],
            axis=0,
        )
        gram = lax.dot_general(
            pair, pair, (((1,), (1,)), ((), ())), preferred_element_type=jnp.float32
        )
        part = gram[:width] * sign + pltpu.roll(gram[width:], width, 1) / SPEC
        own_ref[k] = jnp.where(first, part[:block], part[block:])
        other_ref[k] = jnp.where(first, part[block:], part[:block])


def picks(orders, inputs, order, share):
    blocks, block = orders.shape
    device, held = orders // inputs, orders % inputs
    rank = [np.argsort([d for d in order if d % blocks == n]) for n in range(blocks)]
    known = jnp.asarray(np.stack(rank), dtype=jnp.int32)
    match = device[:, :, None] == jnp.arange(known.shape[1], dtype=jnp.int32)
    place = jnp.sum(jnp.where(match, known[:, None, :], 0), axis=2)
    start = ((held * known.shape[1] + place) * share)[:, None, :]
    chan = jnp.arange(share, dtype=jnp.int32)[:, None]
    target = (start + chan).reshape(blocks, share * block, 1)
    column = lax.broadcasted_iota(jnp.int32, (1, 1, known.shape[1] * inputs * share), 2)
    return (column == target).astype(jnp.bfloat16)


def correlate(arrived, pick, order, share, block):
    blocks = pick.shape[0]
    vmem = pl.BlockSpec(memory_space=pltpu.VMEM)
    tile = jax.ShapeDtypeStruct((share, block, 2 * blocks * block), jnp.float32)
    return pl.pallas_call(
        functools.partial(correlate_kernel, order=order),
        out_shape=(tile, tile),
        in_specs=[vmem, vmem],
        out_specs=(vmem, vmem),
        scratch_shapes=[pltpu.VMEM((blocks, share * block, 2 * SPEC), jnp.bfloat16)],
        compiler_params=pltpu.CompilerParams(vmem_limit_bytes=VMEM_LIMIT),
        cost_estimate=pl.CostEstimate(
            flops=4 * pick.size * SPEC, bytes_accessed=4 * arrived.size, transcendentals=0
        ),
    )(pick, arrived)


def place_kernel(packed_ref, *refs, own):
    out_ref, parts, sems = refs[-3:]
    share, _, _, width = parts.shape
    me = lax.axis_index("blk")
    start = (me if own else 1 - me) * share
    copies = []
    count = share // sems.shape[0]
    for n in range(sems.shape[0]):
        for k in range(n * count, (n + 1) * count):
            parts[k, 0] = packed_ref[k, :, :width]
            parts[k, 1] = packed_ref[k, :, width:]
        target = out_ref.at[pl.ds(start + n * count, count)]
        copies.append(pltpu.make_async_copy(parts.at[pl.ds(n * count, count)], target, sems.at[n]))
        copies[-1].start()
    for copy in copies:
        copy.wait()


def place(packed, blocks, base=None):
    share, block, lanes = packed.shape
    width = lanes // 2
    anywhere = pl.BlockSpec(memory_space=pl.ANY)
    return pl.pallas_call(
        functools.partial(place_kernel, own=base is None),
        out_shape=jax.ShapeDtypeStruct((blocks * share, 2, block, width), packed.dtype),
        in_specs=[pl.BlockSpec(memory_space=pltpu.VMEM)] + ([] if base is None else [anywhere]),
        out_specs=anywhere,
        scratch_shapes=[
            pltpu.VMEM((share, 2, block, width), packed.dtype),
            pltpu.SemaphoreType.DMA((2,)),
        ],
        input_output_aliases={} if base is None else {1: 0},
        compiler_params=pltpu.CompilerParams(vmem_limit_bytes=VMEM_LIMIT),
        cost_estimate=pl.CostEstimate(flops=0, bytes_accessed=8 * packed.size, transcendentals=0),
    )(packed, *([] if base is None else [base]))


def split_channels(freq, blocks, samples, slot_order, flags):
    share = CH // (freq * blocks)
    inputs, block = samples.shape[0], slot_order.shape[1]
    axes = ("freq", "blk")
    plane = freq * blocks // 4
    order = [
        z * plane + d
        for z in (3, 2, 0, 1)
        for core in reversed(range(blocks))
        for d in reversed(range(core, plane, blocks))
    ]
    me = lax.axis_index("blk").astype(jnp.int32)
    partner = lax.ppermute(slot_order, "blk", SWAP)
    orders = jnp.where(
        me == 0,
        jnp.concatenate([slot_order, partner]),
        jnp.concatenate([partner, slot_order]),
    )
    sent = channelize(samples, flags, order)
    arrived = lax.all_to_all(
        sent, axes, split_axis=0, concat_axis=0, axis_index_groups=[order], tiled=True
    )
    pick = picks(orders, inputs, order, share)
    own, other = correlate(arrived, pick, order, share, block)
    received = lax.ppermute(other, "blk", SWAP)
    return place(received, blocks, place(own, blocks))


def gather_blocks(freq, samples, slot_order, flags):
    inputs = samples.shape[0]
    taps = jnp.asarray(prototype())
    table = jnp.asarray(twiddle().reshape(2 * CH, FRAME), dtype=jnp.bfloat16)
    good = (1 - flags).astype(jnp.float32)
    frames = samples.reshape(inputs, SPEC + TAPS - 1, FRAME)
    total = jnp.zeros((inputs, SPEC, FRAME), jnp.float32)
    for tap in range(TAPS):
        window = frames[:, tap : tap + SPEC, :].astype(jnp.float32)
        total = total + taps[tap][None, None, :] * window
    fir = total.astype(jnp.bfloat16)
    spectra = jnp.einsum("kn,isn->kis", table, fir, preferred_element_type=jnp.float32)
    squares = jnp.sum(spectra * spectra, axis=2)
    power = jnp.sum(squares.reshape(CH, 2, inputs), axis=1) / SPEC
    scale = good[None, :] / jnp.sqrt(power + 1e-05)
    quantized = (spectra * jnp.repeat(scale, 2, axis=0)[:, :, None]).astype(jnp.bfloat16)
    arrived = lax.all_to_all(quantized, "freq", split_axis=0, concat_axis=1, tiled=True)
    share = CH // freq
    block = slot_order.shape[1]
    own = jnp.take(arrived.reshape(share, 2, block, SPEC), slot_order[0], axis=2)
    piece = lax.all_gather(own, "blk", axis=2, tiled=True)
    dot = functools.partial(jnp.einsum, "cas,cbs->cab", preferred_element_type=jnp.float32)
    real = dot(own[:, 0], piece[:, 0]) + dot(own[:, 1], piece[:, 1])
    imag = dot(own[:, 1], piece[:, 0]) - dot(own[:, 0], piece[:, 1])
    return jnp.stack([real / SPEC, imag / SPEC], axis=1)


def solution(mesh):
    freq, blocks = mesh.shape["freq"], mesh.shape["blk"]

    def body(samples, slot_order, flags):
        if blocks == 2 and CH == SUB * freq * blocks:
            return split_channels(freq, blocks, samples, slot_order, flags)
        return gather_blocks(freq, samples, slot_order, flags)

    in_specs = (P(("blk", "freq"), None), P("blk", None), P(("blk", "freq")))
    out_specs = P("freq", None, "blk", None)
    return jax.shard_map(body, mesh=mesh, in_specs=in_specs, out_specs=out_specs, check_vma=False)
```

```python
import functools
import math

import jax
import jax.numpy as jnp
import numpy as np
from jax import lax
from jax.experimental import pallas as pl
from jax.experimental.pallas import tpu as pltpu
from jax.experimental.layout import Layout, with_layout_constraint
from jax.sharding import PartitionSpec as P

CH = 256
TAPS = 12
SPEC = 512
FRAME = 2 * CH
LANES = 128
SUB = 8
GROUP = 256
STEP = GROUP // SUB
STRIDE = STEP + 1
PITCH = SPEC + 25
SWAP = [(0, 1), (1, 0)]
VMEM_LIMIT = 40 * 1024 * 1024


def prototype():
    count = TAPS * FRAME
    index = np.arange(count, dtype=np.float64)
    shifted = (index + 0.5) / FRAME - TAPS / 2.0
    window = 0.5 - 0.5 * np.cos(2.0 * math.pi * (index + 0.5) / count)
    return (np.sinc(shifted) * window).astype(np.float32).reshape(TAPS, FRAME)


def twiddle():
    chan = np.arange(CH, dtype=np.int64)[:, None]
    point = np.arange(FRAME, dtype=np.int64)[None, :]
    phase = (chan * point % FRAME).astype(np.float64) * (2.0 * math.pi / FRAME)
    return np.stack([np.cos(phase), -np.sin(phase)], axis=1).astype(np.float32)


def channelize_kernel(
    flags_hbm,
    x_hbm,
    taps_hbm,
    table_hbm,
    out_hbm,
    flags,
    taps_all,
    table,
    held,
    wide,
    fir,
    spectra,
    scales,
    result,
    load_sems,
    sems,
):
    inputs = fir.shape[0]
    frames = SPEC + TAPS - 1
    spread = inputs * FRAME // LANES
    groups = SPEC // GROUP
    pieces = sems.shape[1]
    rows = FRAME // pieces
    last = lax.broadcasted_iota(jnp.int32, (SUB, LANES), 0) == SUB - 1
    edges = [0, GROUP // 2] + [g * GROUP + TAPS for g in range(1, groups)] + [frames]

    def load(source, target, n):
        copy = pltpu.make_async_copy(source, target, load_sems.at[n])
        copy.start()
        return copy

    def span(n):
        return pl.ds(edges[n] * spread, (edges[n + 1] - edges[n]) * spread)

    chunks = len(edges) - 1
    loads = [load(x_hbm.at[span(n)], held.at[span(n)], n) for n in range(chunks)]
    load_taps = load(taps_hbm, taps_all, chunks)
    load_flags = load(flags_hbm, flags, chunks + 2)

    def convert(n):
        for f in range(edges[n], edges[n + 1], 2):
            count = min(2, frames - f)
            tile = held[pl.ds(f * spread, count * spread), :].astype(jnp.float32)
            for c in range(count):
                part = tile[c * spread : (c + 1) * spread]
                wide[pl.ds(f + c, spread, stride=PITCH), :] = part

    def filter_group(g, i, j):
        cols = pl.ds(j * LANES, LANES)
        taps = [jnp.broadcast_to(taps_all[pl.ds(t, 1), cols], (SUB, LANES)) for t in range(TAPS)]

        def take(b):
            first = (inputs * j + i) * PITCH + g * GROUP + b
            return wide[pl.ds(first, SUB, stride=STRIDE), :]

        window = []

        def total(first, count):
            while len(window) < first + count + TAPS - 1:
                window.append(take(len(window)))
            out = [taps[0] * window[first + b] for b in range(count)]
            for t in range(1, TAPS):
                out = [out[b] + taps[t] * window[first + b + t] for b in range(count)]
            return out

        for first in range(0, STEP, SUB):
            final = first + SUB == STEP
            out = total(first, SUB + 1 if final else SUB)
            for m in range(SUB - 1 if final else 0):
                moved = pltpu.roll(out[SUB], SUB - 1 - m, 0)
                out[m + 1] = jnp.where(last, moved, out[m + 1])
            for b in range(0, SUB, 2):
                both = jnp.concatenate(out[b : b + 2], axis=0).astype(jnp.bfloat16)
                fir[i, pl.ds(g * GROUP + (first + b) * SUB, 2 * SUB), cols] = both

    def transform(g, i):
        part = pl.ds(g * GROUP, GROUP)
        spectra[i, :, part] = lax.dot_general(
            table[...],
            fir[i, part, :],
            (((1,), (1,)), ((), ())),
            preferred_element_type=jnp.float32,
        )

    def rate(i):
        good = (1 - flags[i]).astype(jnp.float32)
        for piece in range(pieces):
            pairs = spectra[i, pl.ds(piece * rows, rows), :]
            pairs = pairs.reshape(rows // (2 * SUB), 2, SUB, SPEC)
            squares = jnp.sum(pairs * pairs, axis=1)
            power = jnp.sum(squares, axis=2, keepdims=True) / SPEC
            scale = good / jnp.sqrt(power + 1e-05)
            place = pl.ds(piece * rows // 2, rows // 2)
            scales[i, place, :] = jnp.broadcast_to(scale.reshape(rows // 2, 1), (rows // 2, LANES))

    def scaled(i, piece):
        pairs = spectra[i, pl.ds(piece * rows, rows), :]
        pairs = pairs.reshape(rows // (2 * SUB), 2, SUB, SPEC)
        scale = scales[i, pl.ds(piece * rows // 2, rows // 2), :]
        scale = jnp.concatenate([scale] * (SPEC // LANES), axis=1)
        return pairs * scale.reshape(rows // (2 * SUB), 1, SUB, SPEC)

    def pack(i, piece):
        part = scaled(i, piece).astype(jnp.bfloat16)
        for p in range(2):
            place = (pl.ds(piece * rows // 2, rows // 2), pl.ds((2 * i + p) * SPEC, SPEC))
            result[place] = part[:, p].reshape(rows // 2, SPEC)

    def store(i, piece):
        place = (pl.ds(piece * rows // 2, rows // 2), pl.ds(2 * i * SPEC, 2 * SPEC))
        copy = pltpu.make_async_copy(result.at[place], out_hbm.at[place], sems.at[i, piece])
        copy.start()
        return copy

    loads[0].wait()
    convert(0)
    load_taps.wait()
    loads[1].wait()
    load_table = load(table_hbm, table, chunks + 1)
    convert(1)
    for i in range(inputs):
        for j in range(FRAME // LANES):
            filter_group(0, i, j)
    loads[2].wait()
    load_table.wait()
    load_flags.wait()
    for i in range(inputs):
        transform(0, i)
    convert(2)
    copies = []
    for i in range(inputs):
        if i > 0:
            transform(1, i - 1)
        for j in range(FRAME // LANES):
            filter_group(1, i, j)
        if i > 0:
            rate(i - 1)
            for piece in range(pieces):
                pack(i - 1, piece)
            copies += [store(i - 1, piece) for piece in range(pieces)]
    transform(1, inputs - 1)
    rate(inputs - 1)
    for piece in range(pieces):
        pack(inputs - 1, piece)
        copies.append(store(inputs - 1, piece))
    for copy in copies:
        copy.wait()


def channelize(samples, flags, order):
    inputs = samples.shape[0]
    tiles = samples.reshape(inputs, -1, LANES)
    tiles = with_layout_constraint(tiles, Layout(major_to_minor=(1, 0, 2)))
    tiles = tiles.transpose(1, 0, 2)
    tiles = tiles.reshape(-1, LANES)
    table = twiddle().reshape(len(order), SUB, 2, FRAME)[np.asarray(order)].transpose(0, 2, 1, 3)
    table = jnp.asarray(table.reshape(FRAME, FRAME), dtype=jnp.bfloat16)
    taps = jnp.asarray(prototype())
    hbm = pl.BlockSpec(memory_space=pltpu.HBM)
    return pl.pallas_call(
        channelize_kernel,
        out_shape=jax.ShapeDtypeStruct((CH, inputs * 2 * SPEC), jnp.bfloat16),
        in_specs=[hbm] * 4,
        out_specs=hbm,
        scratch_shapes=[
            pltpu.SMEM(flags.shape, flags.dtype),
            pltpu.VMEM(taps.shape, taps.dtype),
            pltpu.VMEM(table.shape, table.dtype),
            pltpu.VMEM(tiles.shape, tiles.dtype),
            pltpu.VMEM((inputs * FRAME // LANES * PITCH, LANES), jnp.float32),
            pltpu.VMEM((inputs, SPEC, FRAME), jnp.bfloat16),
            pltpu.VMEM((inputs, FRAME, SPEC), jnp.float32),
            pltpu.VMEM((inputs, CH, LANES), jnp.float32),
            pltpu.VMEM((CH, inputs * 2 * SPEC), jnp.bfloat16),
            pltpu.SemaphoreType.DMA((SPEC // GROUP + 4,)),
            pltpu.SemaphoreType.DMA((inputs, 4)),
        ],
        cost_estimate=pl.CostEstimate(
            flops=2 * inputs * SPEC * FRAME * (FRAME + TAPS),
            bytes_accessed=4 * inputs * SPEC * FRAME,
            transcendentals=0,
        ),
    )(flags, tiles, taps, table)


def correlate_kernel(pick_ref, arrived_ref, own_ref, other_ref, slots, *, order):
    share, block, _ = own_ref.shape
    blocks = pick_ref.shape[0]
    width = blocks * block
    first = lax.axis_index("blk") == 0
    lane = lax.broadcasted_iota(jnp.int32, (width, 2 * width), 1)
    sign = jnp.where(lane < width, 1.0 / SPEC, -1.0 / SPEC)
    for n in range(blocks):
        places = [place for place, device in enumerate(order) if device % blocks == n]
        rows = [
            arrived_ref[pl.ds(place * share, 2 * share), pl.ds(2 * i * SPEC, 2 * SPEC)]
            for i in range(arrived_ref.shape[1] // (2 * SPEC))
            for place in places[::2]
        ]
        slots[n] = jnp.dot(
            pick_ref[n], jnp.concatenate(rows, axis=0), preferred_element_type=jnp.float32
        ).astype(jnp.bfloat16)
    for k in range(share):
        pair = jnp.concatenate(
            [
                slots[n, pl.ds(k * block, block), pl.ds(p * SPEC, SPEC)]
                for p in range(2)
                for n in range(blocks)
            ],
            axis=0,
        )
        gram = lax.dot_general(
            pair, pair, (((1,), (1,)), ((), ())), preferred_element_type=jnp.float32
        )
        part = gram[:width] * sign + pltpu.roll(gram[width:], width, 1) / SPEC
        own_ref[k] = jnp.where(first, part[:block], part[block:])
        other_ref[k] = jnp.where(first, part[block:], part[:block])


def picks(orders, inputs, order, share):
    blocks, block = orders.shape
    device, held = orders // inputs, orders % inputs
    rank = [np.argsort([d for d in order if d % blocks == n]) for n in range(blocks)]
    known = jnp.asarray(np.stack(rank), dtype=jnp.int32)
    match = device[:, :, None] == jnp.arange(known.shape[1], dtype=jnp.int32)
    place = jnp.sum(jnp.where(match, known[:, None, :], 0), axis=2)
    start = ((held * known.shape[1] + place) * share)[:, None, :]
    chan = jnp.arange(share, dtype=jnp.int32)[:, None]
    target = (start + chan).reshape(blocks, share * block, 1)
    column = lax.broadcasted_iota(jnp.int32, (1, 1, known.shape[1] * inputs * share), 2)
    return (column == target).astype(jnp.bfloat16)


def correlate(arrived, pick, order, share, block):
    blocks = pick.shape[0]
    vmem = pl.BlockSpec(memory_space=pltpu.VMEM)
    tile = jax.ShapeDtypeStruct((share, block, 2 * blocks * block), jnp.float32)
    return pl.pallas_call(
        functools.partial(correlate_kernel, order=order),
        out_shape=(tile, tile),
        in_specs=[vmem, vmem],
        out_specs=(vmem, vmem),
        scratch_shapes=[pltpu.VMEM((blocks, share * block, 2 * SPEC), jnp.bfloat16)],
        compiler_params=pltpu.CompilerParams(vmem_limit_bytes=VMEM_LIMIT),
        cost_estimate=pl.CostEstimate(
            flops=4 * pick.size * SPEC, bytes_accessed=4 * arrived.size, transcendentals=0
        ),
    )(pick, arrived)


def place_kernel(packed_ref, *refs, own):
    out_ref, parts, sems = refs[-3:]
    share, _, _, width = parts.shape
    me = lax.axis_index("blk")
    start = (me if own else 1 - me) * share
    copies = []
    count = share // sems.shape[0]
    for n in range(sems.shape[0]):
        for k in range(n * count, (n + 1) * count):
            parts[k, 0] = packed_ref[k, :, :width]
            parts[k, 1] = packed_ref[k, :, width:]
        target = out_ref.at[pl.ds(start + n * count, count)]
        copies.append(pltpu.make_async_copy(parts.at[pl.ds(n * count, count)], target, sems.at[n]))
        copies[-1].start()
    for copy in copies:
        copy.wait()


def place(packed, blocks, base=None):
    share, block, lanes = packed.shape
    width = lanes // 2
    anywhere = pl.BlockSpec(memory_space=pl.ANY)
    return pl.pallas_call(
        functools.partial(place_kernel, own=base is None),
        out_shape=jax.ShapeDtypeStruct((blocks * share, 2, block, width), packed.dtype),
        in_specs=[pl.BlockSpec(memory_space=pltpu.VMEM)] + ([] if base is None else [anywhere]),
        out_specs=anywhere,
        scratch_shapes=[
            pltpu.VMEM((share, 2, block, width), packed.dtype),
            pltpu.SemaphoreType.DMA((2,)),
        ],
        input_output_aliases={} if base is None else {1: 0},
        compiler_params=pltpu.CompilerParams(vmem_limit_bytes=VMEM_LIMIT),
        cost_estimate=pl.CostEstimate(flops=0, bytes_accessed=8 * packed.size, transcendentals=0),
    )(packed, *([] if base is None else [base]))


def split_channels(freq, blocks, samples, slot_order, flags):
    share = CH // (freq * blocks)
    inputs, block = samples.shape[0], slot_order.shape[1]
    axes = ("freq", "blk")
    plane = freq * blocks // 4
    order = [
        z * plane + d
        for z in (3, 2, 0, 1)
        for core in reversed(range(blocks))
        for half in reversed(range(blocks))
        for d in reversed(range(core + half * blocks, plane, 2 * blocks))
    ]
    me = lax.axis_index("blk").astype(jnp.int32)
    partner = lax.ppermute(slot_order, "blk", SWAP)
    orders = jnp.where(
        me == 0,
        jnp.concatenate([slot_order, partner]),
        jnp.concatenate([partner, slot_order]),
    )
    sent = channelize(samples, flags, order)
    arrived = lax.all_to_all(
        sent, axes, split_axis=0, concat_axis=0, axis_index_groups=[order], tiled=True
    )
    pick = picks(orders, inputs, order, share)
    own, other = correlate(arrived, pick, order, share, block)
    received = lax.ppermute(other, "blk", SWAP)
    return place(received, blocks, place(own, blocks))


def gather_blocks(freq, samples, slot_order, flags):
    inputs = samples.shape[0]
    taps = jnp.asarray(prototype())
    table = jnp.asarray(twiddle().reshape(2 * CH, FRAME), dtype=jnp.bfloat16)
    good = (1 - flags).astype(jnp.float32)
    frames = samples.reshape(inputs, SPEC + TAPS - 1, FRAME)
    total = jnp.zeros((inputs, SPEC, FRAME), jnp.float32)
    for tap in range(TAPS):
        window = frames[:, tap : tap + SPEC, :].astype(jnp.float32)
        total = total + taps[tap][None, None, :] * window
    fir = total.astype(jnp.bfloat16)
    spectra = jnp.einsum("kn,isn->kis", table, fir, preferred_element_type=jnp.float32)
    squares = jnp.sum(spectra * spectra, axis=2)
    power = jnp.sum(squares.reshape(CH, 2, inputs), axis=1) / SPEC
    scale = good[None, :] / jnp.sqrt(power + 1e-05)
    quantized = (spectra * jnp.repeat(scale, 2, axis=0)[:, :, None]).astype(jnp.bfloat16)
    arrived = lax.all_to_all(quantized, "freq", split_axis=0, concat_axis=1, tiled=True)
    share = CH // freq
    block = slot_order.shape[1]
    own = jnp.take(arrived.reshape(share, 2, block, SPEC), slot_order[0], axis=2)
    piece = lax.all_gather(own, "blk", axis=2, tiled=True)
    dot = functools.partial(jnp.einsum, "cas,cbs->cab", preferred_element_type=jnp.float32)
    real = dot(own[:, 0], piece[:, 0]) + dot(own[:, 1], piece[:, 1])
    imag = dot(own[:, 1], piece[:, 0]) - dot(own[:, 0], piece[:, 1])
    return jnp.stack([real / SPEC, imag / SPEC], axis=1)


def solution(mesh):
    freq, blocks = mesh.shape["freq"], mesh.shape["blk"]

    def body(samples, slot_order, flags):
        if blocks == 2 and CH == SUB * freq * blocks:
            return split_channels(freq, blocks, samples, slot_order, flags)
        return gather_blocks(freq, samples, slot_order, flags)

    in_specs = (P(("blk", "freq"), None), P("blk", None), P(("blk", "freq")))
    out_specs = P("freq", None, "blk", None)
    return jax.shard_map(body, mesh=mesh, in_specs=in_specs, out_specs=out_specs, check_vma=False)
```

```python
import functools
import math

import jax
import jax.numpy as jnp
import numpy as np
from jax import lax
from jax.experimental import pallas as pl
from jax.experimental.pallas import tpu as pltpu
from jax.experimental.layout import Layout, with_layout_constraint
from jax.sharding import PartitionSpec as P

CH = 256
TAPS = 12
SPEC = 512
FRAME = 2 * CH
LANES = 128
SUB = 8
GROUP = 256
STEP = GROUP // SUB
STRIDE = STEP + 1
PITCH = SPEC + 25
SWAP = [(0, 1), (1, 0)]
VMEM_LIMIT = 40 * 1024 * 1024


def prototype():
    count = TAPS * FRAME
    index = np.arange(count, dtype=np.float64)
    shifted = (index + 0.5) / FRAME - TAPS / 2.0
    window = 0.5 - 0.5 * np.cos(2.0 * math.pi * (index + 0.5) / count)
    return (np.sinc(shifted) * window).astype(np.float32).reshape(TAPS, FRAME)


def twiddle():
    chan = np.arange(CH, dtype=np.int64)[:, None]
    point = np.arange(FRAME, dtype=np.int64)[None, :]
    phase = (chan * point % FRAME).astype(np.float64) * (2.0 * math.pi / FRAME)
    return np.stack([np.cos(phase), -np.sin(phase)], axis=1).astype(np.float32)


def channelize_kernel(
    flags_hbm,
    x_hbm,
    taps_hbm,
    table_hbm,
    out_hbm,
    flags,
    taps_all,
    table,
    held,
    wide,
    fir,
    spectra,
    scales,
    result,
    load_sems,
    sems,
):
    inputs = fir.shape[0]
    frames = SPEC + TAPS - 1
    spread = inputs * FRAME // LANES
    groups = SPEC // GROUP
    pieces = sems.shape[1]
    rows = FRAME // pieces
    last = lax.broadcasted_iota(jnp.int32, (SUB, LANES), 0) == SUB - 1
    edges = [0, GROUP // 2] + [g * GROUP + TAPS for g in range(1, groups)] + [frames]

    def load(source, target, n):
        copy = pltpu.make_async_copy(source, target, load_sems.at[n])
        copy.start()
        return copy

    def span(n):
        return pl.ds(edges[n] * spread, (edges[n + 1] - edges[n]) * spread)

    chunks = len(edges) - 1
    loads = [load(x_hbm.at[span(n)], held.at[span(n)], n) for n in range(chunks)]
    load_taps = load(taps_hbm, taps_all, chunks)
    load_flags = load(flags_hbm, flags, chunks + 2)

    def convert(n):
        for f in range(edges[n], edges[n + 1], 2):
            count = min(2, frames - f)
            tile = held[pl.ds(f * spread, count * spread), :].astype(jnp.float32)
            for c in range(count):
                part = tile[c * spread : (c + 1) * spread]
                wide[pl.ds(f + c, spread, stride=PITCH), :] = part

    def filter_group(g, i, j):
        cols = pl.ds(j * LANES, LANES)
        taps = [jnp.broadcast_to(taps_all[pl.ds(t, 1), cols], (SUB, LANES)) for t in range(TAPS)]

        def take(b):
            first = (inputs * j + i) * PITCH + g * GROUP + b
            return wide[pl.ds(first, SUB, stride=STRIDE), :]

        window = []

        def total(first, count):
            while len(window) < first + count + TAPS - 1:
                window.append(take(len(window)))
            out = [taps[0] * window[first + b] for b in range(count)]
            for t in range(1, TAPS):
                out = [out[b] + taps[t] * window[first + b + t] for b in range(count)]
            return out

        for first in range(0, STEP, SUB):
            final = first + SUB == STEP
            out = total(first, SUB + 1 if final else SUB)
            for m in range(SUB - 1 if final else 0):
                moved = pltpu.roll(out[SUB], SUB - 1 - m, 0)
                out[m + 1] = jnp.where(last, moved, out[m + 1])
            for b in range(0, SUB, 2):
                both = jnp.concatenate(out[b : b + 2], axis=0).astype(jnp.bfloat16)
                fir[i, pl.ds(g * GROUP + (first + b) * SUB, 2 * SUB), cols] = both

    def transform(g, i):
        part = pl.ds(g * GROUP, GROUP)
        spectra[i, :, part] = lax.dot_general(
            table[...],
            fir[i, part, :],
            (((1,), (1,)), ((), ())),
            preferred_element_type=jnp.float32,
        )

    def rate(i):
        good = (1 - flags[i]).astype(jnp.float32)
        for piece in range(pieces):
            pairs = spectra[i, pl.ds(piece * rows, rows), :]
            pairs = pairs.reshape(rows // (2 * SUB), 2, SUB, SPEC)
            squares = jnp.sum(pairs * pairs, axis=1)
            power = jnp.sum(squares, axis=2, keepdims=True) / SPEC
            scale = good / jnp.sqrt(power + 1e-05)
            place = pl.ds(piece * rows // 2, rows // 2)
            scales[i, place, :] = jnp.broadcast_to(scale.reshape(rows // 2, 1), (rows // 2, LANES))

    def scaled(i, piece):
        pairs = spectra[i, pl.ds(piece * rows, rows), :]
        pairs = pairs.reshape(rows // (2 * SUB), 2, SUB, SPEC)
        scale = scales[i, pl.ds(piece * rows // 2, rows // 2), :]
        scale = jnp.concatenate([scale] * (SPEC // LANES), axis=1)
        return pairs * scale.reshape(rows // (2 * SUB), 1, SUB, SPEC)

    def pack(i, piece):
        part = scaled(i, piece).astype(jnp.bfloat16)
        for p in range(2):
            place = (pl.ds(piece * rows // 2, rows // 2), pl.ds((2 * i + p) * SPEC, SPEC))
            result[place] = part[:, p].reshape(rows // 2, SPEC)

    def store(i, piece):
        place = (pl.ds(piece * rows // 2, rows // 2), pl.ds(2 * i * SPEC, 2 * SPEC))
        copy = pltpu.make_async_copy(result.at[place], out_hbm.at[place], sems.at[i, piece])
        copy.start()
        return copy

    loads[0].wait()
    convert(0)
    load_taps.wait()
    loads[1].wait()
    load_table = load(table_hbm, table, chunks + 1)
    convert(1)
    for i in range(inputs):
        for j in range(FRAME // LANES):
            filter_group(0, i, j)
    loads[2].wait()
    load_table.wait()
    load_flags.wait()
    for i in range(inputs):
        transform(0, i)
    convert(2)
    copies = []
    for i in range(inputs):
        if i > 0:
            transform(1, i - 1)
        for j in range(FRAME // LANES):
            filter_group(1, i, j)
        if i > 0:
            rate(i - 1)
            for piece in range(pieces):
                pack(i - 1, piece)
            copies += [store(i - 1, piece) for piece in range(pieces)]
    transform(1, inputs - 1)
    rate(inputs - 1)
    for piece in range(pieces):
        pack(inputs - 1, piece)
        copies.append(store(inputs - 1, piece))
    for copy in copies:
        copy.wait()


def channelize(samples, flags, order):
    inputs = samples.shape[0]
    tiles = samples.reshape(inputs, -1, LANES)
    tiles = with_layout_constraint(tiles, Layout(major_to_minor=(1, 0, 2)))
    tiles = tiles.transpose(1, 0, 2)
    tiles = tiles.reshape(-1, LANES)
    table = twiddle().reshape(len(order), SUB, 2, FRAME)[np.asarray(order)].transpose(0, 2, 1, 3)
    table = jnp.asarray(table.reshape(FRAME, FRAME), dtype=jnp.bfloat16)
    taps = jnp.asarray(prototype())
    hbm = pl.BlockSpec(memory_space=pltpu.HBM)
    return pl.pallas_call(
        channelize_kernel,
        out_shape=jax.ShapeDtypeStruct((CH, inputs * 2 * SPEC), jnp.bfloat16),
        in_specs=[hbm] * 4,
        out_specs=hbm,
        scratch_shapes=[
            pltpu.SMEM(flags.shape, flags.dtype),
            pltpu.VMEM(taps.shape, taps.dtype),
            pltpu.VMEM(table.shape, table.dtype),
            pltpu.VMEM(tiles.shape, tiles.dtype),
            pltpu.VMEM((inputs * FRAME // LANES * PITCH, LANES), jnp.float32),
            pltpu.VMEM((inputs, SPEC, FRAME), jnp.bfloat16),
            pltpu.VMEM((inputs, FRAME, SPEC), jnp.float32),
            pltpu.VMEM((inputs, CH, LANES), jnp.float32),
            pltpu.VMEM((CH, inputs * 2 * SPEC), jnp.bfloat16),
            pltpu.SemaphoreType.DMA((SPEC // GROUP + 4,)),
            pltpu.SemaphoreType.DMA((inputs, 4)),
        ],
        cost_estimate=pl.CostEstimate(
            flops=2 * inputs * SPEC * FRAME * (FRAME + TAPS),
            bytes_accessed=4 * inputs * SPEC * FRAME,
            transcendentals=0,
        ),
    )(flags, tiles, taps, table)


def correlate_kernel(pick_ref, arrived_ref, own_ref, other_ref, slots, *, order):
    share, block, _ = own_ref.shape
    blocks = pick_ref.shape[0]
    width = blocks * block
    first = lax.axis_index("blk") == 0
    lane = lax.broadcasted_iota(jnp.int32, (width, 2 * width), 1)
    sign = jnp.where(lane < width, 1.0 / SPEC, -1.0 / SPEC)
    for n in range(blocks):
        places = [place for place, device in enumerate(order) if device % blocks == n]
        rows = [
            arrived_ref[pl.ds(place * share, 2 * share), pl.ds(2 * i * SPEC, 2 * SPEC)]
            for i in range(arrived_ref.shape[1] // (2 * SPEC))
            for place in places[::2]
        ]
        slots[n] = jnp.dot(
            pick_ref[n], jnp.concatenate(rows, axis=0), preferred_element_type=jnp.float32
        ).astype(jnp.bfloat16)
    for k in range(share):
        pair = jnp.concatenate(
            [
                slots[n, pl.ds(k * block, block), pl.ds(p * SPEC, SPEC)]
                for p in range(2)
                for n in range(blocks)
            ],
            axis=0,
        )
        gram = lax.dot_general(
            pair, pair, (((1,), (1,)), ((), ())), preferred_element_type=jnp.float32
        )
        part = gram[:width] * sign + pltpu.roll(gram[width:], width, 1) / SPEC
        own_ref[k] = jnp.where(first, part[:block], part[block:])
        other_ref[k] = jnp.where(first, part[block:], part[:block])


def picks(orders, inputs, order, share):
    blocks, block = orders.shape
    device, held = orders // inputs, orders % inputs
    rank = [np.argsort([d for d in order if d % blocks == n]) for n in range(blocks)]
    known = jnp.asarray(np.stack(rank), dtype=jnp.int32)
    match = device[:, :, None] == jnp.arange(known.shape[1], dtype=jnp.int32)
    place = jnp.sum(jnp.where(match, known[:, None, :], 0), axis=2)
    start = ((held * known.shape[1] + place) * share)[:, None, :]
    chan = jnp.arange(share, dtype=jnp.int32)[:, None]
    target = (start + chan).reshape(blocks, share * block, 1)
    column = lax.broadcasted_iota(jnp.int32, (1, 1, known.shape[1] * inputs * share), 2)
    return (column == target).astype(jnp.bfloat16)


def correlate(arrived, pick, order, share, block):
    blocks = pick.shape[0]
    vmem = pl.BlockSpec(memory_space=pltpu.VMEM)
    tile = jax.ShapeDtypeStruct((share, block, 2 * blocks * block), jnp.float32)
    return pl.pallas_call(
        functools.partial(correlate_kernel, order=order),
        out_shape=(tile, tile),
        in_specs=[vmem, vmem],
        out_specs=(vmem, vmem),
        scratch_shapes=[pltpu.VMEM((blocks, share * block, 2 * SPEC), jnp.bfloat16)],
        compiler_params=pltpu.CompilerParams(vmem_limit_bytes=VMEM_LIMIT),
        cost_estimate=pl.CostEstimate(
            flops=4 * pick.size * SPEC, bytes_accessed=4 * arrived.size, transcendentals=0
        ),
    )(pick, arrived)


def place_kernel(packed_ref, *refs, own):
    out_ref, parts, sems = refs[-3:]
    share, _, _, width = parts.shape
    me = lax.axis_index("blk")
    start = (me if own else 1 - me) * share
    copies = []
    count = share // sems.shape[0]
    for n in range(sems.shape[0]):
        for k in range(n * count, (n + 1) * count):
            parts[k, 0] = packed_ref[k, :, :width]
            parts[k, 1] = packed_ref[k, :, width:]
        target = out_ref.at[pl.ds(start + n * count, count)]
        copies.append(pltpu.make_async_copy(parts.at[pl.ds(n * count, count)], target, sems.at[n]))
        copies[-1].start()
    for copy in copies:
        copy.wait()


def place(packed, blocks, base=None):
    share, block, lanes = packed.shape
    width = lanes // 2
    anywhere = pl.BlockSpec(memory_space=pl.ANY)
    return pl.pallas_call(
        functools.partial(place_kernel, own=base is None),
        out_shape=jax.ShapeDtypeStruct((blocks * share, 2, block, width), packed.dtype),
        in_specs=[pl.BlockSpec(memory_space=pltpu.VMEM)] + ([] if base is None else [anywhere]),
        out_specs=anywhere,
        scratch_shapes=[
            pltpu.VMEM((share, 2, block, width), packed.dtype),
            pltpu.SemaphoreType.DMA((2,)),
        ],
        input_output_aliases={} if base is None else {1: 0},
        compiler_params=pltpu.CompilerParams(vmem_limit_bytes=VMEM_LIMIT),
        cost_estimate=pl.CostEstimate(flops=0, bytes_accessed=8 * packed.size, transcendentals=0),
    )(packed, *([] if base is None else [base]))


def split_channels(freq, blocks, samples, slot_order, flags):
    share = CH // (freq * blocks)
    inputs, block = samples.shape[0], slot_order.shape[1]
    axes = ("freq", "blk")
    plane = freq * blocks // 4
    near = [6, 2, 4, 0, 7, 3, 5, 1]
    order = [
        z * plane + d
        for z in (3, 2, 0, 1)
        for d in (near if z == 0 else [7, 5, 3, 1, 6, 4, 2, 0])
    ]
    me = lax.axis_index("blk").astype(jnp.int32)
    partner = lax.ppermute(slot_order, "blk", SWAP)
    orders = jnp.where(
        me == 0,
        jnp.concatenate([slot_order, partner]),
        jnp.concatenate([partner, slot_order]),
    )
    sent = channelize(samples, flags, order)
    arrived = lax.all_to_all(
        sent, axes, split_axis=0, concat_axis=0, axis_index_groups=[order], tiled=True
    )
    pick = picks(orders, inputs, order, share)
    own, other = correlate(arrived, pick, order, share, block)
    received = lax.ppermute(other, "blk", SWAP)
    return place(received, blocks, place(own, blocks))


def gather_blocks(freq, samples, slot_order, flags):
    inputs = samples.shape[0]
    taps = jnp.asarray(prototype())
    table = jnp.asarray(twiddle().reshape(2 * CH, FRAME), dtype=jnp.bfloat16)
    good = (1 - flags).astype(jnp.float32)
    frames = samples.reshape(inputs, SPEC + TAPS - 1, FRAME)
    total = jnp.zeros((inputs, SPEC, FRAME), jnp.float32)
    for tap in range(TAPS):
        window = frames[:, tap : tap + SPEC, :].astype(jnp.float32)
        total = total + taps[tap][None, None, :] * window
    fir = total.astype(jnp.bfloat16)
    spectra = jnp.einsum("kn,isn->kis", table, fir, preferred_element_type=jnp.float32)
    squares = jnp.sum(spectra * spectra, axis=2)
    power = jnp.sum(squares.reshape(CH, 2, inputs), axis=1) / SPEC
    scale = good[None, :] / jnp.sqrt(power + 1e-05)
    quantized = (spectra * jnp.repeat(scale, 2, axis=0)[:, :, None]).astype(jnp.bfloat16)
    arrived = lax.all_to_all(quantized, "freq", split_axis=0, concat_axis=1, tiled=True)
    share = CH // freq
    block = slot_order.shape[1]
    own = jnp.take(arrived.reshape(share, 2, block, SPEC), slot_order[0], axis=2)
    piece = lax.all_gather(own, "blk", axis=2, tiled=True)
    dot = functools.partial(jnp.einsum, "cas,cbs->cab", preferred_element_type=jnp.float32)
    real = dot(own[:, 0], piece[:, 0]) + dot(own[:, 1], piece[:, 1])
    imag = dot(own[:, 1], piece[:, 0]) - dot(own[:, 0], piece[:, 1])
    return jnp.stack([real / SPEC, imag / SPEC], axis=1)


def solution(mesh):
    freq, blocks = mesh.shape["freq"], mesh.shape["blk"]

    def body(samples, slot_order, flags):
        if blocks == 2 and CH == SUB * freq * blocks:
            return split_channels(freq, blocks, samples, slot_order, flags)
        return gather_blocks(freq, samples, slot_order, flags)

    in_specs = (P(("blk", "freq"), None), P("blk", None), P(("blk", "freq")))
    out_specs = P("freq", None, "blk", None)
    return jax.shard_map(body, mesh=mesh, in_specs=in_specs, out_specs=out_specs, check_vma=False)
```

```python
import functools
import math

import jax
import jax.numpy as jnp
import numpy as np
from jax import lax
from jax.experimental import pallas as pl
from jax.experimental.pallas import tpu as pltpu
from jax.experimental.layout import Layout, with_layout_constraint
from jax.sharding import PartitionSpec as P

CH = 256
TAPS = 12
SPEC = 512
FRAME = 2 * CH
LANES = 128
SUB = 8
GROUP = 256
STEP = GROUP // SUB
STRIDE = STEP + 1
PITCH = SPEC + 25
SWAP = [(0, 1), (1, 0)]
VMEM_LIMIT = 40 * 1024 * 1024


def prototype():
    count = TAPS * FRAME
    index = np.arange(count, dtype=np.float64)
    shifted = (index + 0.5) / FRAME - TAPS / 2.0
    window = 0.5 - 0.5 * np.cos(2.0 * math.pi * (index + 0.5) / count)
    return (np.sinc(shifted) * window).astype(np.float32).reshape(TAPS, FRAME)


def twiddle():
    chan = np.arange(CH, dtype=np.int64)[:, None]
    point = np.arange(FRAME, dtype=np.int64)[None, :]
    phase = (chan * point % FRAME).astype(np.float64) * (2.0 * math.pi / FRAME)
    return np.stack([np.cos(phase), -np.sin(phase)], axis=1).astype(np.float32)


def channelize_kernel(
    flags_hbm,
    x_hbm,
    taps_hbm,
    table_hbm,
    out_hbm,
    flags,
    taps_all,
    table,
    held,
    wide,
    fir,
    spectra,
    scales,
    result,
    load_sems,
    sems,
):
    inputs = fir.shape[0]
    frames = SPEC + TAPS - 1
    spread = inputs * FRAME // LANES
    groups = SPEC // GROUP
    pieces = sems.shape[1]
    rows = FRAME // pieces
    last = lax.broadcasted_iota(jnp.int32, (SUB, LANES), 0) == SUB - 1
    edges = [0, GROUP // 2] + [g * GROUP + TAPS for g in range(1, groups)] + [frames]

    def load(source, target, n):
        copy = pltpu.make_async_copy(source, target, load_sems.at[n])
        copy.start()
        return copy

    def span(n):
        return pl.ds(edges[n] * spread, (edges[n + 1] - edges[n]) * spread)

    chunks = len(edges) - 1
    loads = [load(x_hbm.at[span(n)], held.at[span(n)], n) for n in range(chunks)]
    load_taps = load(taps_hbm, taps_all, chunks)
    load_flags = load(flags_hbm, flags, chunks + 2)

    def convert(n):
        for f in range(edges[n], edges[n + 1], 2):
            count = min(2, frames - f)
            tile = held[pl.ds(f * spread, count * spread), :].astype(jnp.float32)
            for c in range(count):
                part = tile[c * spread : (c + 1) * spread]
                wide[pl.ds(f + c, spread, stride=PITCH), :] = part

    def filter_group(g, i, j):
        cols = pl.ds(j * LANES, LANES)
        taps = [jnp.broadcast_to(taps_all[pl.ds(t, 1), cols], (SUB, LANES)) for t in range(TAPS)]

        def take(b):
            first = (inputs * j + i) * PITCH + g * GROUP + b
            return wide[pl.ds(first, SUB, stride=STRIDE), :]

        window = []

        def total(first, count):
            while len(window) < first + count + TAPS - 1:
                window.append(take(len(window)))
            out = [taps[0] * window[first + b] for b in range(count)]
            for t in range(1, TAPS):
                out = [out[b] + taps[t] * window[first + b + t] for b in range(count)]
            return out

        for first in range(0, STEP, SUB):
            final = first + SUB == STEP
            out = total(first, SUB + 1 if final else SUB)
            for m in range(SUB - 1 if final else 0):
                moved = pltpu.roll(out[SUB], SUB - 1 - m, 0)
                out[m + 1] = jnp.where(last, moved, out[m + 1])
            for b in range(0, SUB, 2):
                both = jnp.concatenate(out[b : b + 2], axis=0).astype(jnp.bfloat16)
                fir[i, pl.ds(g * GROUP + (first + b) * SUB, 2 * SUB), cols] = both

    def transform(g, i):
        part = pl.ds(g * GROUP, GROUP)
        spectra[i, :, part] = lax.dot_general(
            table[...],
            fir[i, part, :],
            (((1,), (1,)), ((), ())),
            preferred_element_type=jnp.float32,
        )

    def rate(i):
        good = (1 - flags[i]).astype(jnp.float32)
        for piece in range(pieces):
            pairs = spectra[i, pl.ds(piece * rows, rows), :]
            pairs = pairs.reshape(rows // (2 * SUB), 2, SUB, SPEC)
            squares = jnp.sum(pairs * pairs, axis=1)
            power = jnp.sum(squares, axis=2, keepdims=True) / SPEC
            scale = good / jnp.sqrt(power + 1e-05)
            place = pl.ds(piece * rows // 2, rows // 2)
            scales[i, place, :] = jnp.broadcast_to(scale.reshape(rows // 2, 1), (rows // 2, LANES))

    def scaled(i, piece):
        pairs = spectra[i, pl.ds(piece * rows, rows), :]
        pairs = pairs.reshape(rows // (2 * SUB), 2, SUB, SPEC)
        scale = scales[i, pl.ds(piece * rows // 2, rows // 2), :]
        scale = jnp.concatenate([scale] * (SPEC // LANES), axis=1)
        return pairs * scale.reshape(rows // (2 * SUB), 1, SUB, SPEC)

    def pack(i, piece):
        part = scaled(i, piece).astype(jnp.bfloat16)
        for p in range(2):
            place = (pl.ds(piece * rows // 2, rows // 2), pl.ds((2 * i + p) * SPEC, SPEC))
            result[place] = part[:, p].reshape(rows // 2, SPEC)

    def store(i, piece):
        place = (pl.ds(piece * rows // 2, rows // 2), pl.ds(2 * i * SPEC, 2 * SPEC))
        copy = pltpu.make_async_copy(result.at[place], out_hbm.at[place], sems.at[i, piece])
        copy.start()
        return copy

    loads[0].wait()
    convert(0)
    load_taps.wait()
    loads[1].wait()
    load_table = load(table_hbm, table, chunks + 1)
    convert(1)
    for i in range(inputs):
        for j in range(FRAME // LANES):
            filter_group(0, i, j)
    loads[2].wait()
    load_table.wait()
    load_flags.wait()
    for i in range(inputs):
        transform(0, i)
    convert(2)
    copies = []
    for i in range(inputs):
        if i > 0:
            transform(1, i - 1)
        for j in range(FRAME // LANES):
            filter_group(1, i, j)
        if i > 0:
            rate(i - 1)
            for piece in range(pieces):
                pack(i - 1, piece)
            copies += [store(i - 1, piece) for piece in range(pieces)]
    transform(1, inputs - 1)
    rate(inputs - 1)
    for piece in range(pieces):
        pack(inputs - 1, piece)
        copies.append(store(inputs - 1, piece))
    for copy in copies:
        copy.wait()


def channelize(samples, flags, order):
    inputs = samples.shape[0]
    tiles = samples.reshape(inputs, -1, LANES)
    tiles = with_layout_constraint(tiles, Layout(major_to_minor=(1, 0, 2)))
    tiles = tiles.transpose(1, 0, 2)
    tiles = tiles.reshape(-1, LANES)
    table = twiddle().reshape(len(order), SUB, 2, FRAME)[np.asarray(order)].transpose(0, 2, 1, 3)
    table = jnp.asarray(table.reshape(FRAME, FRAME), dtype=jnp.bfloat16)
    taps = jnp.asarray(prototype())
    hbm = pl.BlockSpec(memory_space=pltpu.HBM)
    return pl.pallas_call(
        channelize_kernel,
        out_shape=jax.ShapeDtypeStruct((CH, inputs * 2 * SPEC), jnp.bfloat16),
        in_specs=[hbm] * 4,
        out_specs=hbm,
        scratch_shapes=[
            pltpu.SMEM(flags.shape, flags.dtype),
            pltpu.VMEM(taps.shape, taps.dtype),
            pltpu.VMEM(table.shape, table.dtype),
            pltpu.VMEM(tiles.shape, tiles.dtype),
            pltpu.VMEM((inputs * FRAME // LANES * PITCH, LANES), jnp.float32),
            pltpu.VMEM((inputs, SPEC, FRAME), jnp.bfloat16),
            pltpu.VMEM((inputs, FRAME, SPEC), jnp.float32),
            pltpu.VMEM((inputs, CH, LANES), jnp.float32),
            pltpu.VMEM((CH, inputs * 2 * SPEC), jnp.bfloat16),
            pltpu.SemaphoreType.DMA((SPEC // GROUP + 4,)),
            pltpu.SemaphoreType.DMA((inputs, 4)),
        ],
        cost_estimate=pl.CostEstimate(
            flops=2 * inputs * SPEC * FRAME * (FRAME + TAPS),
            bytes_accessed=4 * inputs * SPEC * FRAME,
            transcendentals=0,
        ),
    )(flags, tiles, taps, table)


def correlate_kernel(pick_ref, arrived_ref, own_ref, other_ref, slots, *, order):
    share, block, _ = own_ref.shape
    blocks = pick_ref.shape[0]
    width = blocks * block
    first = lax.axis_index("blk") == 0
    lane = lax.broadcasted_iota(jnp.int32, (width, 2 * width), 1)
    sign = jnp.where(lane < width, 1.0 / SPEC, -1.0 / SPEC)
    for n in range(blocks):
        places = [place for place, device in enumerate(order) if device % blocks == n]
        rows = [
            arrived_ref[pl.ds(place * share, 2 * share), pl.ds(2 * i * SPEC, 2 * SPEC)]
            for i in range(arrived_ref.shape[1] // (2 * SPEC))
            for place in places[::2]
        ]
        slots[n] = jnp.dot(
            pick_ref[n], jnp.concatenate(rows, axis=0), preferred_element_type=jnp.float32
        ).astype(jnp.bfloat16)
    for k in range(share):
        pair = jnp.concatenate(
            [
                slots[n, pl.ds(k * block, block), pl.ds(p * SPEC, SPEC)]
                for p in range(2)
                for n in range(blocks)
            ],
            axis=0,
        )
        gram = lax.dot_general(
            pair, pair, (((1,), (1,)), ((), ())), preferred_element_type=jnp.float32
        )
        part = gram[:width] * sign + pltpu.roll(gram[width:], width, 1) / SPEC
        own_ref[k] = jnp.where(first, part[:block], part[block:])
        other_ref[k] = jnp.where(first, part[block:], part[:block])


def picks(orders, inputs, order, share):
    blocks, block = orders.shape
    device, held = orders // inputs, orders % inputs
    rank = [np.argsort([d for d in order if d % blocks == n]) for n in range(blocks)]
    known = jnp.asarray(np.stack(rank), dtype=jnp.int32)
    match = device[:, :, None] == jnp.arange(known.shape[1], dtype=jnp.int32)
    place = jnp.sum(jnp.where(match, known[:, None, :], 0), axis=2)
    start = ((held * known.shape[1] + place) * share)[:, None, :]
    chan = jnp.arange(share, dtype=jnp.int32)[:, None]
    target = (start + chan).reshape(blocks, share * block, 1)
    column = lax.broadcasted_iota(jnp.int32, (1, 1, known.shape[1] * inputs * share), 2)
    return (column == target).astype(jnp.bfloat16)


def correlate(arrived, pick, order, share, block):
    blocks = pick.shape[0]
    vmem = pl.BlockSpec(memory_space=pltpu.VMEM)
    tile = jax.ShapeDtypeStruct((share, block, 2 * blocks * block), jnp.float32)
    return pl.pallas_call(
        functools.partial(correlate_kernel, order=order),
        out_shape=(tile, tile),
        in_specs=[vmem, vmem],
        out_specs=(vmem, vmem),
        scratch_shapes=[pltpu.VMEM((blocks, share * block, 2 * SPEC), jnp.bfloat16)],
        compiler_params=pltpu.CompilerParams(vmem_limit_bytes=VMEM_LIMIT),
        cost_estimate=pl.CostEstimate(
            flops=4 * pick.size * SPEC, bytes_accessed=4 * arrived.size, transcendentals=0
        ),
    )(pick, arrived)


def place_kernel(packed_ref, *refs, own):
    out_ref, parts, sems = refs[-3:]
    share, _, _, width = parts.shape
    me = lax.axis_index("blk")
    start = (me if own else 1 - me) * share
    copies = []
    count = share // sems.shape[0]
    for n in range(sems.shape[0]):
        for k in range(n * count, (n + 1) * count):
            parts[k, 0] = packed_ref[k, :, :width]
            parts[k, 1] = packed_ref[k, :, width:]
        target = out_ref.at[pl.ds(start + n * count, count)]
        copies.append(pltpu.make_async_copy(parts.at[pl.ds(n * count, count)], target, sems.at[n]))
        copies[-1].start()
    for copy in copies:
        copy.wait()


def place(packed, blocks, base=None):
    share, block, lanes = packed.shape
    width = lanes // 2
    anywhere = pl.BlockSpec(memory_space=pl.ANY)
    return pl.pallas_call(
        functools.partial(place_kernel, own=base is None),
        out_shape=jax.ShapeDtypeStruct((blocks * share, 2, block, width), packed.dtype),
        in_specs=[pl.BlockSpec(memory_space=pltpu.VMEM)] + ([] if base is None else [anywhere]),
        out_specs=anywhere,
        scratch_shapes=[
            pltpu.VMEM((share, 2, block, width), packed.dtype),
            pltpu.SemaphoreType.DMA((2,)),
        ],
        input_output_aliases={} if base is None else {1: 0},
        compiler_params=pltpu.CompilerParams(vmem_limit_bytes=VMEM_LIMIT),
        cost_estimate=pl.CostEstimate(flops=0, bytes_accessed=8 * packed.size, transcendentals=0),
    )(packed, *([] if base is None else [base]))


def split_channels(freq, blocks, samples, slot_order, flags):
    share = CH // (freq * blocks)
    inputs, block = samples.shape[0], slot_order.shape[1]
    axes = ("freq", "blk")
    plane = freq * blocks // 4
    order = [
        z * plane + d
        for z in (2, 3, 0, 1)
        for core in reversed(range(blocks))
        for d in reversed(range(core, plane, blocks))
    ]
    me = lax.axis_index("blk").astype(jnp.int32)
    partner = lax.ppermute(slot_order, "blk", SWAP)
    orders = jnp.where(
        me == 0,
        jnp.concatenate([slot_order, partner]),
        jnp.concatenate([partner, slot_order]),
    )
    sent = channelize(samples, flags, order)
    arrived = lax.all_to_all(
        sent, axes, split_axis=0, concat_axis=0, axis_index_groups=[order], tiled=True
    )
    pick = picks(orders, inputs, order, share)
    own, other = correlate(arrived, pick, order, share, block)
    received = lax.ppermute(other, "blk", SWAP)
    return place(received, blocks, place(own, blocks))


def gather_blocks(freq, samples, slot_order, flags):
    inputs = samples.shape[0]
    taps = jnp.asarray(prototype())
    table = jnp.asarray(twiddle().reshape(2 * CH, FRAME), dtype=jnp.bfloat16)
    good = (1 - flags).astype(jnp.float32)
    frames = samples.reshape(inputs, SPEC + TAPS - 1, FRAME)
    total = jnp.zeros((inputs, SPEC, FRAME), jnp.float32)
    for tap in range(TAPS):
        window = frames[:, tap : tap + SPEC, :].astype(jnp.float32)
        total = total + taps[tap][None, None, :] * window
    fir = total.astype(jnp.bfloat16)
    spectra = jnp.einsum("kn,isn->kis", table, fir, preferred_element_type=jnp.float32)
    squares = jnp.sum(spectra * spectra, axis=2)
    power = jnp.sum(squares.reshape(CH, 2, inputs), axis=1) / SPEC
    scale = good[None, :] / jnp.sqrt(power + 1e-05)
    quantized = (spectra * jnp.repeat(scale, 2, axis=0)[:, :, None]).astype(jnp.bfloat16)
    arrived = lax.all_to_all(quantized, "freq", split_axis=0, concat_axis=1, tiled=True)
    share = CH // freq
    block = slot_order.shape[1]
    own = jnp.take(arrived.reshape(share, 2, block, SPEC), slot_order[0], axis=2)
    piece = lax.all_gather(own, "blk", axis=2, tiled=True)
    dot = functools.partial(jnp.einsum, "cas,cbs->cab", preferred_element_type=jnp.float32)
    real = dot(own[:, 0], piece[:, 0]) + dot(own[:, 1], piece[:, 1])
    imag = dot(own[:, 1], piece[:, 0]) - dot(own[:, 0], piece[:, 1])
    return jnp.stack([real / SPEC, imag / SPEC], axis=1)


def solution(mesh):
    freq, blocks = mesh.shape["freq"], mesh.shape["blk"]

    def body(samples, slot_order, flags):
        if blocks == 2 and CH == SUB * freq * blocks:
            return split_channels(freq, blocks, samples, slot_order, flags)
        return gather_blocks(freq, samples, slot_order, flags)

    in_specs = (P(("blk", "freq"), None), P("blk", None), P(("blk", "freq")))
    out_specs = P("freq", None, "blk", None)
    return jax.shard_map(body, mesh=mesh, in_specs=in_specs, out_specs=out_specs, check_vma=False)
```

```python
import functools
import math

import jax
import jax.numpy as jnp
import numpy as np
from jax import lax
from jax.experimental import pallas as pl
from jax.experimental.pallas import tpu as pltpu
from jax.experimental.layout import Layout, with_layout_constraint
from jax.sharding import PartitionSpec as P

CH = 256
TAPS = 12
SPEC = 512
FRAME = 2 * CH
LANES = 128
SUB = 8
GROUP = 256
STEP = GROUP // SUB
STRIDE = STEP + 1
PITCH = SPEC + 25
SWAP = [(0, 1), (1, 0)]
VMEM_LIMIT = 40 * 1024 * 1024


def prototype():
    count = TAPS * FRAME
    index = np.arange(count, dtype=np.float64)
    shifted = (index + 0.5) / FRAME - TAPS / 2.0
    window = 0.5 - 0.5 * np.cos(2.0 * math.pi * (index + 0.5) / count)
    return (np.sinc(shifted) * window).astype(np.float32).reshape(TAPS, FRAME)


def twiddle():
    chan = np.arange(CH, dtype=np.int64)[:, None]
    point = np.arange(FRAME, dtype=np.int64)[None, :]
    phase = (chan * point % FRAME).astype(np.float64) * (2.0 * math.pi / FRAME)
    return np.stack([np.cos(phase), -np.sin(phase)], axis=1).astype(np.float32)


def channelize_kernel(
    flags_hbm,
    x_hbm,
    taps_hbm,
    table_hbm,
    out_hbm,
    flags,
    taps_all,
    table,
    held,
    wide,
    fir,
    spectra,
    scales,
    result,
    load_sems,
    sems,
):
    inputs = fir.shape[0]
    frames = SPEC + TAPS - 1
    spread = inputs * FRAME // LANES
    groups = SPEC // GROUP
    pieces = sems.shape[1]
    rows = FRAME // pieces
    last = lax.broadcasted_iota(jnp.int32, (SUB, LANES), 0) == SUB - 1
    edges = [0, GROUP // 2] + [g * GROUP + TAPS for g in range(1, groups)] + [frames]

    def load(source, target, n):
        copy = pltpu.make_async_copy(source, target, load_sems.at[n])
        copy.start()
        return copy

    def span(n):
        return pl.ds(edges[n] * spread, (edges[n + 1] - edges[n]) * spread)

    chunks = len(edges) - 1
    loads = [load(x_hbm.at[span(n)], held.at[span(n)], n) for n in range(chunks)]
    load_taps = load(taps_hbm, taps_all, chunks)
    load_flags = load(flags_hbm, flags, chunks + 2)

    def convert(n):
        for f in range(edges[n], edges[n + 1], 2):
            count = min(2, frames - f)
            tile = held[pl.ds(f * spread, count * spread), :].astype(jnp.float32)
            for c in range(count):
                part = tile[c * spread : (c + 1) * spread]
                wide[pl.ds(f + c, spread, stride=PITCH), :] = part

    def filter_group(g, i, j):
        cols = pl.ds(j * LANES, LANES)
        taps = [jnp.broadcast_to(taps_all[pl.ds(t, 1), cols], (SUB, LANES)) for t in range(TAPS)]

        def take(b):
            first = (inputs * j + i) * PITCH + g * GROUP + b
            return wide[pl.ds(first, SUB, stride=STRIDE), :]

        window = []

        def total(first, count):
            while len(window) < first + count + TAPS - 1:
                window.append(take(len(window)))
            out = [taps[0] * window[first + b] for b in range(count)]
            for t in range(1, TAPS):
                out = [out[b] + taps[t] * window[first + b + t] for b in range(count)]
            return out

        for first in range(0, STEP, SUB):
            final = first + SUB == STEP
            out = total(first, SUB + 1 if final else SUB)
            for m in range(SUB - 1 if final else 0):
                moved = pltpu.roll(out[SUB], SUB - 1 - m, 0)
                out[m + 1] = jnp.where(last, moved, out[m + 1])
            for b in range(0, SUB, 2):
                both = jnp.concatenate(out[b : b + 2], axis=0).astype(jnp.bfloat16)
                fir[i, pl.ds(g * GROUP + (first + b) * SUB, 2 * SUB), cols] = both

    def transform(g, i, points=pl.ds(0, FRAME), add=False):
        part = pl.ds(g * GROUP, GROUP)
        product = lax.dot_general(
            table[:, points],
            fir[i, part, points],
            (((1,), (1,)), ((), ())),
            preferred_element_type=jnp.float32,
        )
        spectra[i, :, part] = spectra[i, :, part] + product if add else product

    def rate(i):
        good = (1 - flags[i]).astype(jnp.float32)
        for piece in range(pieces):
            pairs = spectra[i, pl.ds(piece * rows, rows), :]
            pairs = pairs.reshape(rows // (2 * SUB), 2, SUB, SPEC)
            squares = jnp.sum(pairs * pairs, axis=1)
            power = jnp.sum(squares, axis=2, keepdims=True) / SPEC
            scale = good / jnp.sqrt(power + 1e-05)
            place = pl.ds(piece * rows // 2, rows // 2)
            scales[i, place, :] = jnp.broadcast_to(scale.reshape(rows // 2, 1), (rows // 2, LANES))

    def scaled(i, piece):
        pairs = spectra[i, pl.ds(piece * rows, rows), :]
        pairs = pairs.reshape(rows // (2 * SUB), 2, SUB, SPEC)
        scale = scales[i, pl.ds(piece * rows // 2, rows // 2), :]
        scale = jnp.concatenate([scale] * (SPEC // LANES), axis=1)
        return pairs * scale.reshape(rows // (2 * SUB), 1, SUB, SPEC)

    def pack(i, piece):
        part = scaled(i, piece).astype(jnp.bfloat16)
        for p in range(2):
            place = (pl.ds(piece * rows // 2, rows // 2), pl.ds((2 * i + p) * SPEC, SPEC))
            result[place] = part[:, p].reshape(rows // 2, SPEC)

    def store(i, piece):
        place = (pl.ds(piece * rows // 2, rows // 2), pl.ds(2 * i * SPEC, 2 * SPEC))
        copy = pltpu.make_async_copy(result.at[place], out_hbm.at[place], sems.at[i, piece])
        copy.start()
        return copy

    loads[0].wait()
    convert(0)
    load_taps.wait()
    loads[1].wait()
    load_table = load(table_hbm, table, chunks + 1)
    convert(1)
    for i in range(inputs):
        for j in range(FRAME // LANES):
            filter_group(0, i, j)
    loads[2].wait()
    load_table.wait()
    load_flags.wait()
    for i in range(inputs):
        transform(0, i)
    convert(2)
    halves = pl.ds(0, FRAME // 2), pl.ds(FRAME // 2, FRAME // 2)
    copies = []
    for i in range(inputs):
        if i > 0:
            transform(1, i - 1)
        for j in range(FRAME // LANES):
            if i == inputs - 1 and j == FRAME // LANES // 2:
                transform(1, i, halves[0])
            filter_group(1, i, j)
        if i > 0:
            rate(i - 1)
            for piece in range(pieces):
                pack(i - 1, piece)
            copies += [store(i - 1, piece) for piece in range(pieces)]
    transform(1, inputs - 1, halves[1], add=True)
    rate(inputs - 1)
    for piece in range(pieces):
        pack(inputs - 1, piece)
        copies.append(store(inputs - 1, piece))
    for copy in copies:
        copy.wait()


def channelize(samples, flags, order):
    inputs = samples.shape[0]
    tiles = samples.reshape(inputs, -1, LANES)
    tiles = with_layout_constraint(tiles, Layout(major_to_minor=(1, 0, 2)))
    tiles = tiles.transpose(1, 0, 2)
    tiles = tiles.reshape(-1, LANES)
    table = twiddle().reshape(len(order), SUB, 2, FRAME)[np.asarray(order)].transpose(0, 2, 1, 3)
    table = jnp.asarray(table.reshape(FRAME, FRAME), dtype=jnp.bfloat16)
    taps = jnp.asarray(prototype())
    hbm = pl.BlockSpec(memory_space=pltpu.HBM)
    return pl.pallas_call(
        channelize_kernel,
        out_shape=jax.ShapeDtypeStruct((CH, inputs * 2 * SPEC), jnp.bfloat16),
        in_specs=[hbm] * 4,
        out_specs=hbm,
        scratch_shapes=[
            pltpu.SMEM(flags.shape, flags.dtype),
            pltpu.VMEM(taps.shape, taps.dtype),
            pltpu.VMEM(table.shape, table.dtype),
            pltpu.VMEM(tiles.shape, tiles.dtype),
            pltpu.VMEM((inputs * FRAME // LANES * PITCH, LANES), jnp.float32),
            pltpu.VMEM((inputs, SPEC, FRAME), jnp.bfloat16),
            pltpu.VMEM((inputs, FRAME, SPEC), jnp.float32),
            pltpu.VMEM((inputs, CH, LANES), jnp.float32),
            pltpu.VMEM((CH, inputs * 2 * SPEC), jnp.bfloat16),
            pltpu.SemaphoreType.DMA((SPEC // GROUP + 4,)),
            pltpu.SemaphoreType.DMA((inputs, 4)),
        ],
        cost_estimate=pl.CostEstimate(
            flops=2 * inputs * SPEC * FRAME * (FRAME + TAPS),
            bytes_accessed=4 * inputs * SPEC * FRAME,
            transcendentals=0,
        ),
    )(flags, tiles, taps, table)


def correlate_kernel(pick_ref, arrived_ref, own_ref, other_ref, slots, *, order):
    share, block, _ = own_ref.shape
    blocks = pick_ref.shape[0]
    width = blocks * block
    first = lax.axis_index("blk") == 0
    lane = lax.broadcasted_iota(jnp.int32, (width, 2 * width), 1)
    sign = jnp.where(lane < width, 1.0 / SPEC, -1.0 / SPEC)
    for n in range(blocks):
        places = [place for place, device in enumerate(order) if device % blocks == n]
        rows = [
            arrived_ref[pl.ds(place * share, 2 * share), pl.ds(2 * i * SPEC, 2 * SPEC)]
            for i in range(arrived_ref.shape[1] // (2 * SPEC))
            for place in places[::2]
        ]
        slots[n] = jnp.dot(
            pick_ref[n], jnp.concatenate(rows, axis=0), preferred_element_type=jnp.float32
        ).astype(jnp.bfloat16)
    for k in range(share):
        pair = jnp.concatenate(
            [
                slots[n, pl.ds(k * block, block), pl.ds(p * SPEC, SPEC)]
                for p in range(2)
                for n in range(blocks)
            ],
            axis=0,
        )
        gram = lax.dot_general(
            pair, pair, (((1,), (1,)), ((), ())), preferred_element_type=jnp.float32
        )
        part = gram[:width] * sign + pltpu.roll(gram[width:], width, 1) / SPEC
        own_ref[k] = jnp.where(first, part[:block], part[block:])
        other_ref[k] = jnp.where(first, part[block:], part[:block])


def picks(orders, inputs, order, share):
    blocks, block = orders.shape
    device, held = orders // inputs, orders % inputs
    rank = [np.argsort([d for d in order if d % blocks == n]) for n in range(blocks)]
    known = jnp.asarray(np.stack(rank), dtype=jnp.int32)
    match = device[:, :, None] == jnp.arange(known.shape[1], dtype=jnp.int32)
    place = jnp.sum(jnp.where(match, known[:, None, :], 0), axis=2)
    start = ((held * known.shape[1] + place) * share)[:, None, :]
    chan = jnp.arange(share, dtype=jnp.int32)[:, None]
    target = (start + chan).reshape(blocks, share * block, 1)
    column = lax.broadcasted_iota(jnp.int32, (1, 1, known.shape[1] * inputs * share), 2)
    return (column == target).astype(jnp.bfloat16)


def correlate(arrived, pick, order, share, block):
    blocks = pick.shape[0]
    vmem = pl.BlockSpec(memory_space=pltpu.VMEM)
    tile = jax.ShapeDtypeStruct((share, block, 2 * blocks * block), jnp.float32)
    return pl.pallas_call(
        functools.partial(correlate_kernel, order=order),
        out_shape=(tile, tile),
        in_specs=[vmem, vmem],
        out_specs=(vmem, vmem),
        scratch_shapes=[pltpu.VMEM((blocks, share * block, 2 * SPEC), jnp.bfloat16)],
        compiler_params=pltpu.CompilerParams(vmem_limit_bytes=VMEM_LIMIT),
        cost_estimate=pl.CostEstimate(
            flops=4 * pick.size * SPEC, bytes_accessed=4 * arrived.size, transcendentals=0
        ),
    )(pick, arrived)


def place_kernel(packed_ref, *refs, own):
    out_ref, parts, sems = refs[-3:]
    share, _, _, width = parts.shape
    me = lax.axis_index("blk")
    start = (me if own else 1 - me) * share
    copies = []
    count = share // sems.shape[0]
    for n in range(sems.shape[0]):
        for k in range(n * count, (n + 1) * count):
            parts[k, 0] = packed_ref[k, :, :width]
            parts[k, 1] = packed_ref[k, :, width:]
        target = out_ref.at[pl.ds(start + n * count, count)]
        copies.append(pltpu.make_async_copy(parts.at[pl.ds(n * count, count)], target, sems.at[n]))
        copies[-1].start()
    for copy in copies:
        copy.wait()


def place(packed, blocks, base=None):
    share, block, lanes = packed.shape
    width = lanes // 2
    anywhere = pl.BlockSpec(memory_space=pl.ANY)
    return pl.pallas_call(
        functools.partial(place_kernel, own=base is None),
        out_shape=jax.ShapeDtypeStruct((blocks * share, 2, block, width), packed.dtype),
        in_specs=[pl.BlockSpec(memory_space=pltpu.VMEM)] + ([] if base is None else [anywhere]),
        out_specs=anywhere,
        scratch_shapes=[
            pltpu.VMEM((share, 2, block, width), packed.dtype),
            pltpu.SemaphoreType.DMA((2,)),
        ],
        input_output_aliases={} if base is None else {1: 0},
        compiler_params=pltpu.CompilerParams(vmem_limit_bytes=VMEM_LIMIT),
        cost_estimate=pl.CostEstimate(flops=0, bytes_accessed=8 * packed.size, transcendentals=0),
    )(packed, *([] if base is None else [base]))


def split_channels(freq, blocks, samples, slot_order, flags):
    share = CH // (freq * blocks)
    inputs, block = samples.shape[0], slot_order.shape[1]
    axes = ("freq", "blk")
    plane = freq * blocks // 4
    order = [
        z * plane + d
        for z in (3, 2, 0, 1)
        for core in reversed(range(blocks))
        for d in reversed(range(core, plane, blocks))
    ]
    me = lax.axis_index("blk").astype(jnp.int32)
    partner = lax.ppermute(slot_order, "blk", SWAP)
    orders = jnp.where(
        me == 0,
        jnp.concatenate([slot_order, partner]),
        jnp.concatenate([partner, slot_order]),
    )
    sent = channelize(samples, flags, order)
    arrived = lax.all_to_all(
        sent, axes, split_axis=0, concat_axis=0, axis_index_groups=[order], tiled=True
    )
    pick = picks(orders, inputs, order, share)
    own, other = correlate(arrived, pick, order, share, block)
    received = lax.ppermute(other, "blk", SWAP)
    return place(received, blocks, place(own, blocks))


def gather_blocks(freq, samples, slot_order, flags):
    inputs = samples.shape[0]
    taps = jnp.asarray(prototype())
    table = jnp.asarray(twiddle().reshape(2 * CH, FRAME), dtype=jnp.bfloat16)
    good = (1 - flags).astype(jnp.float32)
    frames = samples.reshape(inputs, SPEC + TAPS - 1, FRAME)
    total = jnp.zeros((inputs, SPEC, FRAME), jnp.float32)
    for tap in range(TAPS):
        window = frames[:, tap : tap + SPEC, :].astype(jnp.float32)
        total = total + taps[tap][None, None, :] * window
    fir = total.astype(jnp.bfloat16)
    spectra = jnp.einsum("kn,isn->kis", table, fir, preferred_element_type=jnp.float32)
    squares = jnp.sum(spectra * spectra, axis=2)
    power = jnp.sum(squares.reshape(CH, 2, inputs), axis=1) / SPEC
    scale = good[None, :] / jnp.sqrt(power + 1e-05)
    quantized = (spectra * jnp.repeat(scale, 2, axis=0)[:, :, None]).astype(jnp.bfloat16)
    arrived = lax.all_to_all(quantized, "freq", split_axis=0, concat_axis=1, tiled=True)
    share = CH // freq
    block = slot_order.shape[1]
    own = jnp.take(arrived.reshape(share, 2, block, SPEC), slot_order[0], axis=2)
    piece = lax.all_gather(own, "blk", axis=2, tiled=True)
    dot = functools.partial(jnp.einsum, "cas,cbs->cab", preferred_element_type=jnp.float32)
    real = dot(own[:, 0], piece[:, 0]) + dot(own[:, 1], piece[:, 1])
    imag = dot(own[:, 1], piece[:, 0]) - dot(own[:, 0], piece[:, 1])
    return jnp.stack([real / SPEC, imag / SPEC], axis=1)


def solution(mesh):
    freq, blocks = mesh.shape["freq"], mesh.shape["blk"]

    def body(samples, slot_order, flags):
        if blocks == 2 and CH == SUB * freq * blocks:
            return split_channels(freq, blocks, samples, slot_order, flags)
        return gather_blocks(freq, samples, slot_order, flags)

    in_specs = (P(("blk", "freq"), None), P("blk", None), P(("blk", "freq")))
    out_specs = P("freq", None, "blk", None)
    return jax.shard_map(body, mesh=mesh, in_specs=in_specs, out_specs=out_specs, check_vma=False)
```
